32 devices in a mesh: dom: 8 (over z, x), rep: 4 (over y, core).
Axes of the slice: x: 2, y: 2, z: 4, core: 2. Of those that a mesh axis runs over, the one named last changes fastest.
Arguments:
- features: bfloat16 [131072, 100], P(('dom', 'rep')), may hold values from -6 to 6
- labels: int32 [65536], P(('dom', 'rep')), may hold values from 0 to 46
- seed_rows: int32 [65536], P(('dom', 'rep')), may hold values from 0 to 4095
- seed_mask: int32 [65536], P(('dom', 'rep')), may hold values from 0 to 1
- send_rows: int32 [1024, 16], P(('dom', 'rep')), may hold values from 0 to 4095
- neighbors_one: int32 [131072, 15], P(('dom', 'rep')), may hold values from 0 to 4607, as said below
- neighbors_two: int32 [131072, 10], P(('dom', 'rep')), may hold values from 0 to 4607, as said below
- neighbors_three: int32 [131072, 5], P(('dom', 'rep')), may hold values from 0 to 4607, as said below
- weight_one: float32 [200, 256], replicated, may hold values from -0.625 to 0.625
- weight_two: float32 [512, 256], replicated, may hold values from -6 to 6
- weight_three: float32 [512, 47], replicated, may hold values from -12 to 12
- left_one: float32 [200, 200], replicated, as said below
- right_one: float32 [256, 256], replicated, as said below
- left_two: float32 [512, 512], replicated, as said below
- right_two: float32 [256, 256], replicated, as said below
- left_three: float32 [512, 512], replicated, as said below
- right_three: float32 [47, 47], replicated, as said below
- first_one: float32 [200, 256], replicated
- first_two: float32 [512, 256], replicated
- first_three: float32 [512, 47], replicated
- second_one: float32 [200, 256], replicated
- second_two: float32 [512, 256], replicated, may hold values from 1.5258789e-12 to 6.1035157e-12
- second_three: float32 [512, 47], replicated, may hold values from 1.5258789e-12 to 6.1035157e-12
- bias_all: float32 [559], replicated, may hold values from -0.6 to 0.6
- bias_first: float32 [559], replicated
- bias_second: float32 [559], replicated, may hold values from 1.5258789e-10 to 6.1035155e-10
Outputs:
- new_weight_one: float32 [200, 256], replicated
- new_first_one: float32 [200, 256], replicated
- new_second_one: float32 [200, 256], replicated
- new_weight_two: float32 [512, 256], replicated
- new_first_two: float32 [512, 256], replicated
- new_second_two: float32 [512, 256], replicated
- new_weight_three: float32 [512, 47], replicated
- new_first_three: float32 [512, 47], replicated
- new_second_three: float32 [512, 47], replicated
- new_bias: float32 [559], replicated
- new_bias_first: float32 [559], replicated
- new_bias_second: float32 [559], replicated
- loss_sum: float32 [], replicated
- seed_total: float32 [], replicated
The draws below stay inside these ranges and needn't reach their ends.
Inputs may be any that keep to these rules, and one draw needn't show every extreme that they name: `neighbors_one`: entries below 4096 name the part's own nodes, the others its halo rows; column 0 of a part's lists names every halo row of that part at least once. `neighbors_two`: as for neighbors_one. `neighbors_three`: as for neighbors_one. `left_one`: Orthogonal. `right_one`: Orthogonal. `left_two`: Orthogonal. `right_two`: Orthogonal. `left_three`: Orthogonal. `right_three`: Orthogonal.
All inputs are finite; a program needn't handle non-finite values.
Results may differ from the reference program's by a relative error of at most 0.0085.
Values may be sent and summed in bfloat16 or wider, within the bound.
A program may use at most 256 MiB of HBM per device.

```python
import math
import jax
import jax.numpy as jnp
from jax import lax

FEAT = 100
HID = 256
CLASSES = 47
FAN1 = 15
FAN2 = 10
FAN3 = 5
NODES_DEV = 4096
HALO = 16
STEP = 10
SEEDS_DEV = 2048
PART_COUNT = 32
NODES = 131072
N_DOM = 8
N_REP = 4


def neighbor_lists(key, fanout):
    parts = N_DOM * N_REP
    halo_rows = parts * HALO
    random_part = jax.random.randint(key, (parts * NODES_DEV, fanout), 0, NODES_DEV + halo_rows)
    offsets = jax.random.randint(jax.random.fold_in(key, 7), (parts, 1), 0, halo_rows)
    local = jnp.arange(NODES_DEV, dtype=jnp.int32)[None, :]
    covering = NODES_DEV + (local + offsets) % halo_rows
    return random_part.at[:, 0].set(covering.reshape(-1).astype(jnp.int32))


def basis(key, order):
    vector = jax.random.normal(key, (order,), jnp.float32)
    return jnp.eye(order, dtype=jnp.float32) - 2.0 * vector[:, None] * vector[None, :] / jnp.sum(vector * vector)


def moment(key, shape, factor):
    scale = factor / math.sqrt(N_DOM * N_REP * NODES_DEV)
    return scale * jax.random.normal(key, shape, jnp.float32)


def spread_moment(key, shape, low_factor, high_factor):
    base = 2e-07 / (N_DOM * N_REP * NODES_DEV)
    ticket = jax.random.uniform(key, shape, jnp.float32)
    return base * jnp.exp(math.log(low_factor) + (math.log(high_factor) - math.log(low_factor)) * ticket)


def draw_seed_mask(key, part):
    key = jax.random.fold_in(key, 1)
    parts = N_DOM * N_REP
    index = jnp.arange(parts * SEEDS_DEV, dtype=jnp.int32) // SEEDS_DEV
    dom_index = index // N_REP
    rep_index = index % N_REP
    keep = 9 * (N_DOM - 1 + 2 * dom_index) * (N_REP - 1 + 2 * rep_index)
    ticket = jax.random.randint(key, (parts * SEEDS_DEV,), 0, 90 * (N_DOM - 1) * (N_REP - 1))
    return (ticket < keep).astype(jnp.int32)


def draw_neighbors_one(key, part):
    return neighbor_lists(jax.random.fold_in(key, 2), FAN1)


def draw_neighbors_two(key, part):
    return neighbor_lists(jax.random.fold_in(key, 3), FAN2)


def draw_neighbors_three(key, part):
    return neighbor_lists(jax.random.fold_in(key, 4), FAN3)


def draw_left_one(key, part):
    return basis(jax.random.fold_in(key, 5), 2 * FEAT)


def draw_right_one(key, part):
    return basis(jax.random.fold_in(key, 6), HID)


def draw_left_two(key, part):
    return basis(jax.random.fold_in(key, 8), 2 * HID)


def draw_right_two(key, part):
    return basis(jax.random.fold_in(key, 9), HID)


def draw_left_three(key, part):
    return basis(jax.random.fold_in(key, 10), 2 * HID)


def draw_right_three(key, part):
    return basis(jax.random.fold_in(key, 11), CLASSES)


def draw_first_one(key, part):
    return moment(jax.random.fold_in(key, 12), (2 * FEAT, HID), 0.0016)


def draw_first_two(key, part):
    return moment(jax.random.fold_in(key, 13), (2 * HID, HID), 0.0016)


def draw_first_three(key, part):
    return moment(jax.random.fold_in(key, 14), (2 * HID, CLASSES), 0.0016)


def draw_bias_first(key, part):
    return moment(jax.random.fold_in(key, 15), (2 * HID + CLASSES,), 0.016)


def draw_second_one(key, part):
    key = jax.random.fold_in(key, 16)
    return spread_moment(key, (2 * FEAT, HID), 0.5, 8.0)


def place_ends(drawn, stream_key, least, largest):
    extent = drawn.shape
    index_at = [jax.random.randint(jax.random.fold_in(stream_key, axis), (), 0, extent[axis]) for axis in range(len(extent))]
    drawn = drawn.at[tuple(index_at)].set(least)
    longest = extent.index(max(extent))
    index_at[longest] = (index_at[longest] + 1) % extent[longest]
    return drawn.at[tuple(index_at)].set(largest)


def block_levels(own_key, extent, shards, least, top_value):
    gain = 1.0
    for axis_at, shards_of in shards:
        heights = jax.random.uniform(jax.random.fold_in(jax.random.fold_in(own_key, 6), axis_at), (shards_of,), jnp.float32, least / len(shards), top_value / len(shards))
        gain = gain * jnp.repeat(jnp.exp(heights), extent[axis_at] // shards_of).reshape((-1,) + (1,) * (len(extent) - 1 - axis_at))
    return gain


def scatter_about(rng, dims, spread, limit, pieces=(), held_as=jnp.bfloat16):
    entries = jax.random.normal(rng, dims, jnp.float32) * spread
    if len(pieces) > 0:
        entries = block_levels(rng, dims, pieces, -0.22, 0.18) * entries
    return jnp.clip(entries, min=-limit, max=limit).astype(held_as)


def setup_inputs(seed: int = 0) -> dict:
    arg_keys = jax.random.split(jax.random.key(seed), 27)
    features = scatter_about(arg_keys[0], (NODES, FEAT), 1.0, 6.0, ((0, 32),))
    labels = place_ends(jax.random.randint(arg_keys[1], (SEEDS_DEV * PART_COUNT,), 0, CLASSES), jax.random.fold_in(arg_keys[1], 1), 0, CLASSES - 1).astype(jnp.int32)
    seed_rows = place_ends(jax.random.randint(arg_keys[2], (SEEDS_DEV * PART_COUNT,), 0, NODES_DEV), jax.random.fold_in(arg_keys[2], 1), 0, NODES_DEV - 1).astype(jnp.int32)
    seed_mask = draw_seed_mask(jax.random.fold_in(arg_keys[26], 71), 0)
    send_rows = place_ends(jax.random.randint(arg_keys[4], (PART_COUNT * PART_COUNT, HALO), 0, NODES_DEV), jax.random.fold_in(arg_keys[4], 1), 0, NODES_DEV - 1).astype(jnp.int32)
    neighbors_one = draw_neighbors_one(jax.random.fold_in(arg_keys[26], 71), 0)
    neighbors_two = draw_neighbors_two(jax.random.fold_in(arg_keys[26], 71), 0)
    neighbors_three = draw_neighbors_three(jax.random.fold_in(arg_keys[26], 71), 0)
    weight_one = scatter_about(arg_keys[8], (2 * FEAT, HID), FEAT ** -0.5, 0.625, (), jnp.float32)
    weight_two = scatter_about(arg_keys[9], (2 * HID, HID), 1.0, 6.0, (), jnp.float32)
    weight_three = scatter_about(arg_keys[10], (2 * HID, CLASSES), 2.0, 12.0, (), jnp.float32)
    left_one = draw_left_one(jax.random.fold_in(arg_keys[26], 71), 0)
    right_one = draw_right_one(jax.random.fold_in(arg_keys[26], 71), 0)
    left_two = draw_left_two(jax.random.fold_in(arg_keys[26], 71), 0)
    right_two = draw_right_two(jax.random.fold_in(arg_keys[26], 71), 0)
    left_three = draw_left_three(jax.random.fold_in(arg_keys[26], 71), 0)
    right_three = draw_right_three(jax.random.fold_in(arg_keys[26], 71), 0)
    first_one = draw_first_one(jax.random.fold_in(arg_keys[26], 71), 0)
    first_two = draw_first_two(jax.random.fold_in(arg_keys[26], 71), 0)
    first_three = draw_first_three(jax.random.fold_in(arg_keys[26], 71), 0)
    second_one = draw_second_one(jax.random.fold_in(arg_keys[26], 71), 0)
    second_two = jnp.clip(jnp.exp(jax.random.uniform(arg_keys[21], (2 * HID, HID), jnp.float32, math.log(1.5258789240815696e-12), math.log(6.103515696326278e-12))), 1.5258789240815696e-12, 6.103515696326278e-12)
    second_three = jnp.clip(jnp.exp(jax.random.uniform(arg_keys[22], (2 * HID, CLASSES), jnp.float32, math.log(1.5258789240815696e-12), math.log(6.103515696326278e-12))), 1.5258789240815696e-12, 6.103515696326278e-12)
    bias_all = scatter_about(arg_keys[23], (2 * HID + CLASSES,), 0.1, 0.6, (), jnp.float32)
    bias_first = draw_bias_first(jax.random.fold_in(arg_keys[26], 71), 0)
    bias_second = jnp.clip(jnp.exp(jax.random.uniform(arg_keys[25], (2 * HID + CLASSES,), jnp.float32, math.log(1.5258788677030566e-10), math.log(6.103515470812226e-10))), 1.5258788677030566e-10, 6.103515470812226e-10)
    return {"features": features, "labels": labels, "seed_rows": seed_rows, "seed_mask": seed_mask, "send_rows": send_rows, "neighbors_one": neighbors_one, "neighbors_two": neighbors_two, "neighbors_three": neighbors_three, "weight_one": weight_one, "weight_two": weight_two, "weight_three": weight_three, "left_one": left_one, "right_one": right_one, "left_two": left_two, "right_two": right_two, "left_three": left_three, "right_three": right_three, "first_one": first_one, "first_two": first_two, "first_three": first_three, "second_one": second_one, "second_two": second_two, "second_three": second_three, "bias_all": bias_all, "bias_first": bias_first, "bias_second": bias_second}


@jax.custom_vjp
def low(v):
    return lax.optimization_barrier(v.astype(jnp.bfloat16)).astype(jnp.float32)

@jax.custom_vjp
def low_back(v):
    return v

def low_keep(v):
    return (low(v), None)

def low_pass(kept, grad):
    return (grad,)

def back_keep(v):
    return (v, None)

def back_low(kept, grad):
    return (low(grad),)
low.defvjp(low_keep, low_pass)
low_back.defvjp(back_keep, back_low)
beta_one = 0.9
beta_two = 0.999
epsilon = 1e-08
step_rates = (0.05, 0.5, 1.0)
bias_rate = 0.05
weight_decay = 0.01

def product(left, right):
    return jnp.dot(left, right, precision=lax.Precision.HIGHEST, preferred_element_type=jnp.float32)

def activate(preact):
    active = jax.nn.silu(preact)
    return active * lax.rsqrt(lax.optimization_barrier(jnp.sum(active * active, axis=-1, keepdims=True)) + 1e-06)

def layer_pass(states, weight, bias_part, neighbors, send_rows, last):
    rounded = low(states)
    in_width = rounded.shape[2]
    sent = jax.vmap(lambda source, picks: source[picks])(rounded, send_rows)
    received = low_back(jnp.swapaxes(sent, 0, 1).reshape(PART_COUNT, -1, in_width))
    lookup = jnp.concatenate([rounded, received], axis=1)
    fanout = neighbors.shape[2]
    summed = jnp.zeros(rounded.shape, jnp.float32)
    for column in range(fanout):
        summed = summed + jax.vmap(lambda table, picks: table[picks])(lookup, neighbors[:, :, column])
    mean = low(summed / fanout)
    weight_low = low(weight)
    preact = jnp.einsum('pnk,kc->pnc', rounded, weight_low[:in_width], precision=lax.Precision.HIGHEST)
    preact = preact + jnp.einsum('pnk,kc->pnc', mean, weight_low[in_width:], precision=lax.Precision.HIGHEST)
    preact = low_back(preact + bias_part)
    if last:
        return preact
    return activate(preact)

def forward_loss(weight_one, weight_two, weight_three, bias_all, features, send_rows, neighbor_list, seed_rows, labels, seed_float):
    biases = (bias_all[:HID], bias_all[HID:2 * HID], bias_all[2 * HID:])
    weights = (weight_one, weight_two, weight_three)
    states = features
    for layer in range(3):
        states = layer_pass(states, weights[layer], biases[layer], neighbor_list[layer], send_rows, layer == 2)
    picked_rows = jax.vmap(lambda logits, picks: logits[picks])(states, seed_rows)
    normer = jax.scipy.special.logsumexp(picked_rows, axis=-1)
    target = jnp.take_along_axis(picked_rows, labels[:, :, None], axis=-1)[:, :, 0]
    return jnp.sum((normer - target) * seed_float)

def rotate_adam(weight, grad, first, second, left_basis, right_basis, rate):
    turned = product(product(left_basis.T, grad), right_basis)
    first = beta_one * first + (1.0 - beta_one) * turned
    second = beta_two * second + (1.0 - beta_two) * turned * turned
    update = first / (1.0 - beta_one ** STEP) / (jnp.sqrt(second / (1.0 - beta_two ** STEP)) + epsilon)
    return (weight - rate * product(product(left_basis, update), right_basis.T), first, second)

def reference(features, labels, seed_rows, seed_mask, send_rows, neighbors_one, neighbors_two, neighbors_three, weight_one, weight_two, weight_three, left_one, right_one, left_two, right_two, left_three, right_three, first_one, first_two, first_three, second_one, second_two, second_three, bias_all, bias_first, bias_second):
    feats = features.astype(jnp.float32).reshape(PART_COUNT, NODES_DEV, FEAT)
    sends = send_rows.reshape(PART_COUNT, PART_COUNT, HALO)
    neighbor_list = (neighbors_one.reshape(PART_COUNT, NODES_DEV, -1), neighbors_two.reshape(PART_COUNT, NODES_DEV, -1), neighbors_three.reshape(PART_COUNT, NODES_DEV, -1))
    seeds = seed_rows.reshape(PART_COUNT, -1)
    label_grid = labels.reshape(PART_COUNT, -1)
    seed_float = seed_mask.reshape(PART_COUNT, -1).astype(jnp.float32)
    seed_total = jnp.sum(seed_float)

    def objective(w_one, w_two, w_three, biases):
        summed = forward_loss(w_one, w_two, w_three, biases, feats, sends, neighbor_list, seeds, label_grid, seed_float)
        return (summed / seed_total, summed)
    (loss_mean, loss_sum), pullback = jax.vjp(objective, weight_one, weight_two, weight_three, bias_all)
    grads = pullback((jnp.float32(1.0), jnp.float32(0.0)))
    out_one = rotate_adam(weight_one, grads[0], first_one, second_one, left_one, right_one, step_rates[0])
    out_two = rotate_adam(weight_two, grads[1], first_two, second_two, left_two, right_two, step_rates[1])
    out_three = rotate_adam(weight_three, grads[2], first_three, second_three, left_three, right_three, step_rates[2])
    bias_m = beta_one * bias_first + (1.0 - beta_one) * grads[3]
    bias_v = beta_two * bias_second + (1.0 - beta_two) * grads[3] * grads[3]
    bias_update = bias_m / (1.0 - beta_one ** STEP) / (jnp.sqrt(bias_v / (1.0 - beta_two ** STEP)) + epsilon)
    new_bias = bias_all - bias_rate * (bias_update + weight_decay * bias_all)
    return (out_one[0], out_one[1], out_one[2], out_two[0], out_two[1], out_two[2], out_three[0], out_three[1], out_three[2], new_bias, bias_m, bias_v, loss_sum, seed_total)
```

```python
import functools

import jax
import jax.numpy as jnp
from jax import lax
from jax.experimental import pallas as pl
from jax.experimental.pallas import tpu as pltpu
from jax.sharding import PartitionSpec as P

STEP = 10


beta_one = 0.9
beta_two = 0.999
epsilon = 1e-08
step_rates = (0.05, 0.5, 1.0)
bias_rate = 0.05
weight_decay = 0.01

axes = ("dom", "rep")
WORDS = 4
SLOTS = 8
GROUPS = WORDS * SLOTS
BLOCK = 512
VMEM_BYTES = 56 * 1024 * 1024
TRANS_LEFT = (((0,), (0,)), ((), ()))
TRANS_RIGHT = (((1,), (1,)), ((), ()))


def dot(left, right, dims=(((1,), (0,)), ((), ()))):
    return lax.dot_general(left, right, dims, preferred_element_type=jnp.float32)


def params():
    return pltpu.CompilerParams(
        dimension_semantics=("arbitrary",), vmem_limit_bytes=VMEM_BYTES
    )


def whole(shape):
    return pl.BlockSpec(shape, lambda i: (0,) * len(shape))


def lanes(rows, width):
    return pl.BlockSpec((rows, width), lambda i: (0, i))


def words_layer(near_ref, out_ref, place_ref, field_ref):
    fanout, block = near_ref.shape
    span = out_ref.shape[0] // WORDS
    near = near_ref[...]
    group = ((near.astype(jnp.float32) + 0.5) * (1.0 / span)).astype(jnp.int32)
    place = near - group * span
    word = group >> 3
    bit = jnp.left_shift(jnp.int32(1), (group & 7) * 4)
    parts = [jnp.where(word == k, bit, 0) for k in range(WORDS)]
    totals = [jnp.zeros_like(bit) for _ in range(WORDS)]
    for g in range(fanout):
        same = place == place[g : g + 1]
        for k in range(WORDS):
            totals[k] = totals[k] + jnp.where(same, parts[k][g : g + 1], 0)
    place_ref[:fanout, :] = place
    for k in range(WORDS):
        field_ref[k, :fanout, :] = totals[k]
    chunk = 48
    for tile in range(0, block, 128):
        cols = slice(tile, tile + 128)
        for start in range(0, span, chunk):
            rows = lax.broadcasted_iota(jnp.int32, (chunk, 128), 0) + start
            sums = [jnp.zeros((chunk, 128), jnp.int32) for _ in range(WORDS)]
            for g in range(fanout):
                hit = rows == place_ref[g : g + 1, cols]
                for k in range(WORDS):
                    sums[k] = jnp.where(hit, field_ref[k, g : g + 1, cols], sums[k])
            for k in range(WORDS):
                out_ref[k * span + start : k * span + start + chunk, cols] = sums[k]


def words_kernel(one_ref, two_ref, three_ref, out_one, out_two, out_three, place_ref, field_ref):
    words_layer(one_ref, out_one, place_ref, field_ref)
    words_layer(two_ref, out_two, place_ref, field_ref)
    words_layer(three_ref, out_three, place_ref, field_ref)


def count_words(near, table):
    nodes = near[0].shape[1]
    height = table // SLOTS
    return pl.pallas_call(
        words_kernel,
        grid=(nodes // BLOCK,),
        in_specs=[lanes(n.shape[0], BLOCK) for n in near],
        out_specs=[lanes(height, BLOCK)] * 3,
        out_shape=[jax.ShapeDtypeStruct((height, nodes), jnp.int32)] * 3,
        scratch_shapes=[
            pltpu.VMEM((16, BLOCK), jnp.int32),
            pltpu.VMEM((WORDS, 16, BLOCK), jnp.int32),
        ],
        compiler_params=params(),
        name="count_words",
    )(*near)


def field(words, slot):
    if slot == SLOTS - 1:
        picked = lax.shift_right_logical(words, 4 * slot)
    else:
        picked = words & (15 << (4 * slot))
    return picked.astype(jnp.float32).astype(jnp.bfloat16)


def slot_scale(slot):
    return 1.0 if slot == SLOTS - 1 else 2.0 ** (-4 * slot)


def spread_counts(words_ref, counts_ref, group, span):
    word, slot = divmod(group, SLOTS)
    width = words_ref.shape[1]
    for tile in range(0, width, 128):
        cols = slice(tile, tile + 128)
        for start in range(0, span, 48):
            counts_ref[group * span + start : group * span + start + 48, cols] = field(
                words_ref[word * span + start : word * span + start + 48, cols], slot
            )


def gather_product(table_ref, words_ref, counts_ref):
    table = table_ref.shape[1]
    span = table // GROUPS
    total = None
    done = 0
    step = 512
    for group in range(GROUPS):
        spread_counts(words_ref, counts_ref, group, span)
        ready = (group + 1) * span
        while ready - done >= step or (group == GROUPS - 1 and done < table):
            stop = min(done + step, table)
            term = dot(table_ref[:, done:stop], counts_ref[done:stop, :])
            total = term if total is None else total + term
            done = stop
    return total


def scaled_table(own, got, scale, table_ref):
    width, nodes = own.shape
    table_ref[:width, :nodes] = (own.astype(jnp.float32) * scale[:, :nodes]).astype(jnp.bfloat16)
    table_ref[:width, nodes:] = (got.astype(jnp.float32) * scale[:, nodes:]).astype(jnp.bfloat16)


def hidden_kernel(
    fanout,
    words_ref,
    own_ref,
    own_block,
    got_ref,
    scale_ref,
    self_ref,
    near_ref,
    bias_ref,
    send_ref,
    state_ref,
    preact_ref,
    sent_ref,
    extra_ref,
    table_ref,
    counts_ref,
    picked_ref,
):
    step = pl.program_id(0)
    width = own_ref.shape[0]

    @pl.when(step == 0)
    def _():
        if table_ref.shape[0] > width:
            table_ref[...] = jnp.zeros_like(table_ref)
        got = got_ref[...].T
        scaled_table(own_ref[...], got, scale_ref[...], table_ref)
        if width == state_ref.shape[0]:
            extra_ref[:, : own_ref.shape[1]] = own_ref[...]
            extra_ref[:, own_ref.shape[1] :] = got
        picked_ref[...] = jnp.zeros_like(picked_ref)

    mean = (gather_product(table_ref, words_ref, counts_ref) / fanout).astype(jnp.bfloat16)
    if width != state_ref.shape[0]:
        extra_ref[...] = mean
    preact = dot(self_ref[...], own_block[...]) + dot(near_ref[...], mean) + bias_ref[...]
    preact_ref[...] = preact
    active = preact * jax.nn.sigmoid(preact)
    norm = lax.rsqrt(jnp.sum(active * active, axis=0, keepdims=True) + 1e-06)
    state = (active * norm).astype(jnp.bfloat16)
    state_ref[...] = state
    block = state.shape[1]
    node = lax.broadcasted_iota(jnp.int32, (1, block), 1) + step * block
    chosen = jnp.where(send_ref[...] == node, 1.0, 0.0).astype(jnp.bfloat16)
    picked_ref[...] += dot(chosen, state, TRANS_RIGHT)

    @pl.when(step == pl.num_programs(0) - 1)
    def _():
        sent_ref[...] = picked_ref[...].astype(jnp.bfloat16)


def hidden_layer(words, own, got, scale, weight_self, weight_near, bias_col, send_col, fanout):
    width, nodes = own.shape
    halo = got.shape[0]
    table = nodes + halo
    units = weight_self.shape[0]
    padded = weight_near.shape[1]
    if width == units:
        extra_shape, extra_spec = (units, table), whole((units, table))
    else:
        extra_shape, extra_spec = (padded, nodes), lanes(padded, BLOCK)
    return pl.pallas_call(
        functools.partial(hidden_kernel, fanout),
        grid=(nodes // BLOCK,),
        in_specs=[
            lanes(words.shape[0], BLOCK),
            whole(own.shape),
            lanes(width, BLOCK),
            whole(got.shape),
            whole(scale.shape),
            whole(weight_self.shape),
            whole(weight_near.shape),
            whole(bias_col.shape),
            whole(send_col.shape),
        ],
        out_specs=[
            lanes(units, BLOCK),
            lanes(units, BLOCK),
            whole((halo, units)),
            extra_spec,
        ],
        out_shape=[
            jax.ShapeDtypeStruct((units, nodes), jnp.bfloat16),
            jax.ShapeDtypeStruct((units, nodes), jnp.float32),
            jax.ShapeDtypeStruct((halo, units), jnp.bfloat16),
            jax.ShapeDtypeStruct(extra_shape, jnp.bfloat16),
        ],
        scratch_shapes=[
            pltpu.VMEM((padded, table), jnp.bfloat16),
            pltpu.VMEM((table, BLOCK), jnp.bfloat16),
            pltpu.VMEM((halo, units), jnp.float32),
        ],
        compiler_params=params(),
        name="hidden_layer",
    )(words, own, own, got, scale, weight_self, weight_near, bias_col, send_col)


def seed_kernel(rows_ref, labels_ref, mask_ref, out_ref):
    step = pl.program_id(0)
    classes, block = out_ref.shape
    slots = rows_ref.shape[0]
    kind = lax.broadcasted_iota(jnp.int32, (classes, slots), 0)
    marked = jnp.where((kind == labels_ref[...]) & (mask_ref[...] != 0), 1.0, 0.0)
    node = lax.broadcasted_iota(jnp.int32, (1, block), 1) + step * block
    chosen = jnp.where(rows_ref[...] == node, 1.0, 0.0).astype(jnp.bfloat16)
    out_ref[...] = dot(marked.astype(jnp.bfloat16), chosen)


def seed_counts(rows_col, labels_row, mask_row, nodes, classes):
    return pl.pallas_call(
        seed_kernel,
        grid=(nodes // BLOCK,),
        in_specs=[whole(rows_col.shape), whole(labels_row.shape), whole(mask_row.shape)],
        out_specs=lanes(classes, BLOCK),
        out_shape=jax.ShapeDtypeStruct((classes, nodes), jnp.float32),
        compiler_params=params(),
        name="seed_counts",
    )(rows_col, labels_row, mask_row)


def last_kernel(
    fanout,
    words_ref,
    own_ref,
    own_block,
    got_ref,
    scale_ref,
    self_ref,
    near_ref,
    bias_ref,
    seeds_ref,
    grad_ref,
    sums_ref,
    table_out,
    reduced_ref,
    counts_ref,
):
    step = pl.program_id(0)
    classes = self_ref.shape[0]
    nodes = own_ref.shape[1]

    @pl.when(step == 0)
    def _():
        table_out[:, :nodes] = own_ref[...]
        table_out[:, nodes:] = got_ref[...].T
        reduced = dot(near_ref[...], table_out[...]) * scale_ref[...]
        high = reduced.astype(jnp.bfloat16)
        reduced_ref[:classes, :] = high
        reduced_ref[classes:, :] = (reduced - high.astype(jnp.float32)).astype(jnp.bfloat16)
        sums_ref[...] = jnp.zeros_like(sums_ref)

    both = gather_product(reduced_ref, words_ref, counts_ref)
    near_part = (both[:classes] + both[classes:]) / fanout
    logits = dot(self_ref[...], own_block[...]) + near_part + bias_ref[...]
    top = jnp.max(logits, axis=0, keepdims=True)
    powers = jnp.exp(logits - top)
    total = jnp.sum(powers, axis=0, keepdims=True)
    normer = jnp.log(total) + top
    seeds = seeds_ref[...]
    uses = jnp.sum(seeds, axis=0, keepdims=True)
    grad = (powers / total * uses - seeds).astype(jnp.bfloat16)
    grad_ref[...] = grad
    loss = uses * normer - jnp.sum(seeds * logits, axis=0, keepdims=True)
    sums_ref[:classes, :] += jnp.sum(grad.astype(jnp.float32), axis=1, keepdims=True)
    sums_ref[classes:, :] += jnp.sum(loss)


def last_layer(words, own, got, scale, weight_self, weight_near, bias_col, seeds, fanout):
    width, nodes = own.shape
    table = nodes + got.shape[0]
    classes = weight_self.shape[0]
    return pl.pallas_call(
        functools.partial(last_kernel, fanout),
        grid=(nodes // BLOCK,),
        in_specs=[
            lanes(words.shape[0], BLOCK),
            whole(own.shape),
            lanes(width, BLOCK),
            whole(got.shape),
            whole(scale.shape),
            whole(weight_self.shape),
            whole(weight_near.shape),
            whole(bias_col.shape),
            lanes(classes, BLOCK),
        ],
        out_specs=[
            lanes(classes, BLOCK),
            whole((classes + 8, 128)),
            whole((width, table)),
        ],
        out_shape=[
            jax.ShapeDtypeStruct((classes, nodes), jnp.bfloat16),
            jax.ShapeDtypeStruct((classes + 8, 128), jnp.float32),
            jax.ShapeDtypeStruct((width, table), jnp.bfloat16),
        ],
        scratch_shapes=[
            pltpu.VMEM((2 * classes, table), jnp.bfloat16),
            pltpu.VMEM((table, BLOCK), jnp.bfloat16),
        ],
        compiler_params=params(),
        name="last_layer",
    )(words, own, own, got, scale, weight_self, weight_near, bias_col, seeds)


def scatter_kernel(
    fanout,
    words_ref,
    grad_ref,
    table_ref,
    self_ref,
    near_ref,
    state_ref,
    weight_ref,
    rows_ref,
    padded_ref,
    counts_ref,
    sums_ref,
):
    step = pl.program_id(0)
    units, nodes = grad_ref.shape
    span = words_ref.shape[0]
    part = span * SLOTS

    @pl.when(step == 0)
    def _():
        rows_ref[...] = grad_ref[...].T
        for k in range(WORDS):
            start = k * part
            stop = min(start + part, nodes)
            if stop > start:
                padded_ref[k, :, : stop - start] = grad_ref[:, start:stop]
            if stop < start + part:
                left = max(stop - start, 0)
                padded_ref[k, :, left:] = jnp.zeros((units, part - left), jnp.bfloat16)
        weight_ref[...] = jnp.zeros_like(weight_ref)

    pair = 2
    for slot in range(0, SLOTS, pair):
        for one in range(slot, slot + pair):
            spread_slot(words_ref, counts_ref, one, span)
        added = dot(counts_ref[slot * span : (slot + pair) * span, :], rows_ref[...])
        for one in range(slot, slot + pair):
            piece = added[(one - slot) * span : (one - slot + 1) * span, :]
            sums_ref[one * span : (one + 1) * span, :] = (
                piece * (slot_scale(one) / fanout)
            ).astype(jnp.bfloat16)
    sums = sums_ref[...]
    own_grad = padded_ref[step]
    state_ref[...] = dot(near_ref[...], sums, TRANS_RIGHT) + dot(self_ref[...], own_grad)
    width = table_ref.shape[0]
    weight_ref[:width, :] += dot(table_ref[...], own_grad, TRANS_RIGHT)
    weight_ref[width:, :] += dot(table_ref[...], sums)


def spread_slot(words_ref, counts_ref, slot, span):
    for tile in range(0, words_ref.shape[1], 128):
        cols = slice(tile, tile + 128)
        for start in range(0, span, 48):
            counts_ref[slot * span + start : slot * span + start + 48, cols] = field(
                words_ref[start : start + 48, cols], slot
            )


def scatter_layer(words, grad, table, weight_self, weight_near, fanout):
    units, nodes = grad.shape
    width, rows = table.shape
    span = rows // GROUPS
    part = rows // WORDS
    return pl.pallas_call(
        functools.partial(scatter_kernel, fanout),
        grid=(WORDS,),
        in_specs=[
            pl.BlockSpec((span, nodes), lambda i: (i, 0)),
            whole(grad.shape),
            lanes(width, part),
            whole(weight_self.shape),
            whole(weight_near.shape),
        ],
        out_specs=[lanes(width, part), whole((2 * width, units))],
        out_shape=[
            jax.ShapeDtypeStruct((width, rows), jnp.float32),
            jax.ShapeDtypeStruct((2 * width, units), jnp.float32),
        ],
        scratch_shapes=[
            pltpu.VMEM((nodes, units), jnp.bfloat16),
            pltpu.VMEM((WORDS, units, part), jnp.bfloat16),
            pltpu.VMEM((part, nodes), jnp.bfloat16),
            pltpu.VMEM((part, units), jnp.bfloat16),
        ],
        compiler_params=params(),
        name="scatter_layer",
    )(words, grad, table, weight_self, weight_near)


def active_kernel(first, state_ref, preact_ref, returned_ref, send_ref, *refs):
    if first:
        own_block, mean_block, grad_ref, sums_ref, weight_ref = refs
    else:
        grad_ref, sums_ref = refs
    step = pl.program_id(0)
    block = state_ref.shape[1]
    node = lax.broadcasted_iota(jnp.int32, (1, block), 1) + step * block
    chosen = jnp.where(send_ref[...] == node, 1.0, 0.0).astype(jnp.bfloat16)
    upper = state_ref[...] + dot(returned_ref[...], chosen, TRANS_LEFT)
    preact = preact_ref[...]
    gate = jax.nn.sigmoid(preact)
    active = preact * gate
    norm = lax.rsqrt(jnp.sum(active * active, axis=0, keepdims=True) + 1e-06)
    along = jnp.sum(active * upper, axis=0, keepdims=True)
    inner = norm * upper - active * (norm * norm * norm * along)
    grad = (inner * (gate * (1.0 + preact * (1.0 - gate)))).astype(jnp.bfloat16)
    grad_ref[...] = grad

    @pl.when(step == 0)
    def _():
        sums_ref[...] = jnp.zeros_like(sums_ref)
        if first:
            weight_ref[...] = jnp.zeros_like(weight_ref)

    sums_ref[...] += jnp.sum(grad.astype(jnp.float32), axis=1, keepdims=True)
    if first:
        width = own_block.shape[0]
        weight_ref[0, :width, :] += dot(own_block[...], grad, TRANS_RIGHT)
        weight_ref[1] += dot(mean_block[...], grad, TRANS_RIGHT)


def active_layer(state_grad, preact, returned, send_col, own=None, mean=None):
    units, nodes = preact.shape
    first = own is not None
    in_specs = [
        lanes(units, BLOCK),
        lanes(units, BLOCK),
        whole(returned.shape),
        whole(send_col.shape),
    ]
    out_specs = [lanes(units, BLOCK), whole((units, 128))]
    out_shape = [
        jax.ShapeDtypeStruct((units, nodes), jnp.bfloat16),
        jax.ShapeDtypeStruct((units, 128), jnp.float32),
    ]
    operands = [state_grad, preact, returned, send_col]
    if first:
        padded = mean.shape[0]
        in_specs += [lanes(own.shape[0], BLOCK), lanes(padded, BLOCK)]
        out_specs.append(whole((2, padded, units)))
        out_shape.append(jax.ShapeDtypeStruct((2, padded, units), jnp.float32))
        operands += [own, mean]
    return pl.pallas_call(
        functools.partial(active_kernel, first),
        grid=(nodes // BLOCK,),
        in_specs=in_specs,
        out_specs=out_specs,
        out_shape=out_shape,
        compiler_params=params(),
        name="active_layer",
    )(*operands)


def product(left, right):
    return jnp.dot(left, right, precision=lax.Precision.HIGHEST, preferred_element_type=jnp.float32)


def exchange(rows):
    return lax.all_to_all(rows, axes, split_axis=0, concat_axis=0, tiled=True)


def rotate_adam(weight, grad, first, second, left_basis, right_basis, rate):
    turned = product(product(left_basis.T, grad), right_basis)
    first = beta_one * first + (1.0 - beta_one) * turned
    second = beta_two * second + (1.0 - beta_two) * turned * turned
    update = first / (1.0 - beta_one**STEP) / (jnp.sqrt(second / (1.0 - beta_two**STEP)) + epsilon)
    return (weight - rate * product(product(left_basis, update), right_basis.T), first, second)


def on_device(
    features,
    labels,
    seed_rows,
    seed_mask,
    send_rows,
    neighbors_one,
    neighbors_two,
    neighbors_three,
    weight_one,
    weight_two,
    weight_three,
    left_one,
    right_one,
    left_two,
    right_two,
    left_three,
    right_three,
    first_one,
    first_two,
    first_three,
    second_one,
    second_two,
    second_three,
    bias_all,
    bias_first,
    bias_second,
):
    nodes, width = features.shape
    units = weight_one.shape[1]
    classes = weight_three.shape[1]
    halo = send_rows.size
    table = nodes + halo
    span = table // GROUPS
    low = jnp.bfloat16
    fans = (neighbors_one.shape[1], neighbors_two.shape[1], neighbors_three.shape[1])
    near = (neighbors_one.T, neighbors_two.T, neighbors_three.T)
    feats = features.T
    slot_of = (jnp.arange(table, dtype=jnp.int32) // span) % SLOTS
    scale = jnp.where(slot_of == SLOTS - 1, 1.0, 0.0)
    for slot in range(SLOTS - 1):
        scale = jnp.where(slot_of == slot, slot_scale(slot), scale)
    scale = scale.astype(jnp.float32)[None, :]
    send_col = send_rows.reshape(halo, 1)

    got_one = exchange(features[send_rows.reshape(-1)])
    words = count_words(near, table)
    padded_classes = -(-classes // 16) * 16
    more = padded_classes - classes
    seeds = seed_counts(
        seed_rows.reshape(-1, 1),
        labels.reshape(1, -1),
        seed_mask.reshape(1, -1),
        nodes,
        padded_classes,
    )
    seed_float = seed_mask.astype(jnp.float32)

    padded = -(-width // 16) * 16
    self_one = weight_one[:width].T.astype(low)
    near_one = jnp.pad(weight_one[width:].T, ((0, 0), (0, padded - width))).astype(low)
    self_two = weight_two[:units].astype(low)
    near_two = weight_two[units:].astype(low)
    wide_three = jnp.pad(weight_three, ((0, 0), (0, more))).astype(low)
    self_three = wide_three[:units]
    near_three = wide_three[units:]
    bias_three = jnp.pad(bias_all[2 * units :], (0, more), constant_values=-1e30)

    state_one, preact_one, sent_two, mean_one = hidden_layer(
        words[0],
        feats,
        got_one,
        scale,
        self_one,
        near_one,
        bias_all[:units].reshape(-1, 1),
        send_col,
        fans[0],
    )
    got_two = exchange(sent_two)
    state_two, preact_two, sent_three, table_two = hidden_layer(
        words[1],
        state_one,
        got_two,
        scale,
        self_two.T,
        near_two.T,
        bias_all[units : 2 * units].reshape(-1, 1),
        send_col,
        fans[1],
    )
    got_three = exchange(sent_three)
    grad_three, sums_three, table_three = last_layer(
        words[2],
        state_two,
        got_three,
        scale,
        self_three.T,
        near_three.T,
        bias_three.reshape(-1, 1),
        seeds,
        fans[2],
    )
    state_grad, weight_grad_three = scatter_layer(
        words[2], grad_three, table_three, self_three, near_three, fans[2]
    )
    returned = exchange(state_grad[:, nodes:].T.astype(low))
    grad_two, sums_two = active_layer(state_grad, preact_two, returned, send_col)
    state_grad, weight_grad_two = scatter_layer(
        words[1], grad_two, table_two, self_two, near_two, fans[1]
    )
    returned = exchange(state_grad[:, nodes:].T.astype(low))
    _, sums_one, weight_grad_one = active_layer(
        state_grad, preact_one, returned, send_col, feats, mean_one
    )
    small = jnp.concatenate(
        [
            sums_one[:, 0],
            sums_two[:, 0],
            sums_three[:classes, 0],
            sums_three[padded_classes : padded_classes + 1, 0],
            jnp.sum(seed_float)[None],
        ]
    )
    weight_grad_one = weight_grad_one[:, :width].reshape(2 * width, units)
    summed = lax.psum((weight_grad_one, weight_grad_two, weight_grad_three, small), axes)
    loss_sum = summed[3][-2]
    seed_total = summed[3][-1]
    share = 1.0 / seed_total
    bias_grad = summed[3][:-2] * share
    out_one = rotate_adam(
        weight_one, summed[0] * share, first_one, second_one, left_one, right_one, step_rates[0]
    )
    out_two = rotate_adam(
        weight_two, summed[1] * share, first_two, second_two, left_two, right_two, step_rates[1]
    )
    out_three = rotate_adam(
        weight_three,
        summed[2][:, :classes] * share,
        first_three,
        second_three,
        left_three,
        right_three,
        step_rates[2],
    )
    bias_m = beta_one * bias_first + (1.0 - beta_one) * bias_grad
    bias_v = beta_two * bias_second + (1.0 - beta_two) * bias_grad * bias_grad
    bias_update = (
        bias_m / (1.0 - beta_one**STEP) / (jnp.sqrt(bias_v / (1.0 - beta_two**STEP)) + epsilon)
    )
    new_bias = bias_all - bias_rate * (bias_update + weight_decay * bias_all)
    return (*out_one, *out_two, *out_three, new_bias, bias_m, bias_v, loss_sum, seed_total)


def solution(mesh):
    split = P(axes)
    rows = P(axes, None)
    placed = (rows, split, split, split, rows, rows, rows, rows) + (P(),) * 18
    return jax.shard_map(
        on_device,
        mesh=mesh,
        in_specs=placed,
        out_specs=(P(),) * 14,
        check_vma=False,
    )
```

```python
import functools

import jax
import jax.numpy as jnp
from jax import lax
from jax.experimental import pallas as pl
from jax.experimental.pallas import tpu as pltpu
from jax.sharding import PartitionSpec as P

STEP = 10


beta_one = 0.9
beta_two = 0.999
epsilon = 1e-08
step_rates = (0.05, 0.5, 1.0)
bias_rate = 0.05
weight_decay = 0.01

axes = ("dom", "rep")
WORDS = 4
SLOTS = 8
GROUPS = WORDS * SLOTS
BLOCK = 512
VMEM_BYTES = 56 * 1024 * 1024
TRANS_LEFT = (((0,), (0,)), ((), ()))
TRANS_RIGHT = (((1,), (1,)), ((), ()))


def dot(left, right, dims=(((1,), (0,)), ((), ()))):
    return lax.dot_general(left, right, dims, preferred_element_type=jnp.float32)


def params():
    return pltpu.CompilerParams(
        dimension_semantics=("arbitrary",), vmem_limit_bytes=VMEM_BYTES
    )


def whole(shape):
    return pl.BlockSpec(shape, lambda i: (0,) * len(shape))


def lanes(rows, width):
    return pl.BlockSpec((rows, width), lambda i: (0, i))


def words_layer(near_ref, out_ref, place_ref, field_ref):
    fanout, block = near_ref.shape
    span = out_ref.shape[0] // WORDS
    near = near_ref[...]
    group = ((near.astype(jnp.float32) + 0.5) * (1.0 / span)).astype(jnp.int32)
    place = near - group * span
    word = group >> 3
    bit = jnp.left_shift(jnp.int32(1), (group & 7) * 4)
    parts = [jnp.where(word == k, bit, 0) for k in range(WORDS)]
    totals = [jnp.zeros_like(bit) for _ in range(WORDS)]
    for g in range(fanout):
        same = place == place[g : g + 1]
        for k in range(WORDS):
            totals[k] = totals[k] + jnp.where(same, parts[k][g : g + 1], 0)
    place_ref[:fanout, :] = place
    for k in range(WORDS):
        field_ref[k, :fanout, :] = totals[k]
    chunk = 48
    for tile in range(0, block, 128):
        cols = slice(tile, tile + 128)
        for start in range(0, span, chunk):
            rows = lax.broadcasted_iota(jnp.int32, (chunk, 128), 0) + start
            sums = [jnp.zeros((chunk, 128), jnp.int32) for _ in range(WORDS)]
            for g in range(fanout):
                hit = rows == place_ref[g : g + 1, cols]
                for k in range(WORDS):
                    sums[k] = jnp.where(hit, field_ref[k, g : g + 1, cols], sums[k])
            for k in range(WORDS):
                out_ref[k * span + start : k * span + start + chunk, cols] = sums[k]


def words_kernel(near_ref, out_ref, place_ref, field_ref):
    words_layer(near_ref, out_ref, place_ref, field_ref)


def count_words(near, table):
    fanout, nodes = near.shape
    height = table // SLOTS
    return pl.pallas_call(
        words_kernel,
        grid=(nodes // BLOCK,),
        in_specs=[lanes(fanout, BLOCK)],
        out_specs=lanes(height, BLOCK),
        out_shape=jax.ShapeDtypeStruct((height, nodes), jnp.int32),
        scratch_shapes=[
            pltpu.VMEM((16, BLOCK), jnp.int32),
            pltpu.VMEM((WORDS, 16, BLOCK), jnp.int32),
        ],
        compiler_params=params(),
        name="count_words",
    )(near)


def field(words, slot):
    if slot == SLOTS - 1:
        picked = lax.shift_right_logical(words, 4 * slot)
    else:
        picked = words & (15 << (4 * slot))
    return picked.astype(jnp.float32).astype(jnp.bfloat16)


def slot_scale(slot):
    return 1.0 if slot == SLOTS - 1 else 2.0 ** (-4 * slot)


def spread_counts(words_ref, counts_ref, group, span):
    word, slot = divmod(group, SLOTS)
    width = words_ref.shape[1]
    for tile in range(0, width, 128):
        cols = slice(tile, tile + 128)
        for start in range(0, span, 48):
            counts_ref[group * span + start : group * span + start + 48, cols] = field(
                words_ref[word * span + start : word * span + start + 48, cols], slot
            )


def gather_product(table_ref, words_ref, counts_ref):
    table = table_ref.shape[1]
    span = table // GROUPS
    total = None
    done = 0
    step = 512
    for group in range(GROUPS):
        spread_counts(words_ref, counts_ref, group, span)
        ready = (group + 1) * span
        while ready - done >= step or (group == GROUPS - 1 and done < table):
            stop = min(done + step, table)
            term = dot(table_ref[:, done:stop], counts_ref[done:stop, :])
            total = term if total is None else total + term
            done = stop
    return total


def scaled_table(own, got, scale, table_ref):
    width, nodes = own.shape
    table_ref[:width, :nodes] = (own.astype(jnp.float32) * scale[:, :nodes]).astype(jnp.bfloat16)
    table_ref[:width, nodes:] = (got.astype(jnp.float32) * scale[:, nodes:]).astype(jnp.bfloat16)


def late(rows, width):
    return pl.BlockSpec((rows, width), lambda i: (0, jnp.maximum(i - 1, 0)))


def now(rows, width, steps):
    return pl.BlockSpec((rows, width), lambda i: (0, jnp.minimum(i, steps - 1)))


def hidden_kernel(
    fanout,
    words_ref,
    own_ref,
    own_block,
    got_ref,
    scale_ref,
    self_ref,
    near_ref,
    bias_ref,
    send_ref,
    state_ref,
    preact_ref,
    sent_ref,
    extra_ref,
    table_ref,
    counts_ref,
    picked_ref,
    mean_ref,
):
    step = pl.program_id(0)
    last = pl.num_programs(0) - 1
    width = own_ref.shape[0]
    units, block = state_ref.shape

    @pl.when(step == 0)
    def _():
        if table_ref.shape[0] > width:
            table_ref[...] = jnp.zeros_like(table_ref)
        got = got_ref[...].T
        scaled_table(own_ref[...], got, scale_ref[...], table_ref)
        if width == units:
            extra_ref[:, : own_ref.shape[1]] = own_ref[...]
            extra_ref[:, own_ref.shape[1] :] = got
        mean_ref[...] = jnp.zeros_like(mean_ref)
        picked_ref[...] = jnp.zeros_like(picked_ref)

    def finish():
        mean = mean_ref[...]
        if width != units:
            extra_ref[...] = mean
        preact = dot(self_ref[...], own_block[...]) + dot(near_ref[...], mean) + bias_ref[...]
        preact_ref[...] = preact
        active = preact * jax.nn.sigmoid(preact)
        norm = lax.rsqrt(jnp.sum(active * active, axis=0, keepdims=True) + 1e-06)
        state = (active * norm).astype(jnp.bfloat16)
        state_ref[...] = state
        node = lax.broadcasted_iota(jnp.int32, (1, block), 1) + (step - 1) * block
        chosen = jnp.where(send_ref[...] == node, 1.0, 0.0).astype(jnp.bfloat16)
        picked_ref[...] += dot(chosen, state, TRANS_RIGHT)

    @pl.when(step < last)
    def _():
        finish()
        total = gather_product(table_ref, words_ref, counts_ref)
        mean_ref[...] = (total / fanout).astype(jnp.bfloat16)

    @pl.when(step == last)
    def _():
        finish()
        sent_ref[...] = picked_ref[...].astype(jnp.bfloat16)


def hidden_layer(words, own, got, scale, weight_self, weight_near, bias_col, send_col, fanout):
    width, nodes = own.shape
    halo = got.shape[0]
    table = nodes + halo
    units = weight_self.shape[0]
    padded = weight_near.shape[1]
    steps = nodes // BLOCK
    if width == units:
        extra_shape, extra_spec = (units, table), whole((units, table))
    else:
        extra_shape, extra_spec = (padded, nodes), late(padded, BLOCK)
    return pl.pallas_call(
        functools.partial(hidden_kernel, fanout),
        grid=(steps + 1,),
        in_specs=[
            now(words.shape[0], BLOCK, steps),
            whole(own.shape),
            late(width, BLOCK),
            whole(got.shape),
            whole(scale.shape),
            whole(weight_self.shape),
            whole(weight_near.shape),
            whole(bias_col.shape),
            whole(send_col.shape),
        ],
        out_specs=[
            late(units, BLOCK),
            late(units, BLOCK),
            whole((halo, units)),
            extra_spec,
        ],
        out_shape=[
            jax.ShapeDtypeStruct((units, nodes), jnp.bfloat16),
            jax.ShapeDtypeStruct((units, nodes), jnp.float32),
            jax.ShapeDtypeStruct((halo, units), jnp.bfloat16),
            jax.ShapeDtypeStruct(extra_shape, jnp.bfloat16),
        ],
        scratch_shapes=[
            pltpu.VMEM((padded, table), jnp.bfloat16),
            pltpu.VMEM((table, BLOCK), jnp.bfloat16),
            pltpu.VMEM((halo, units), jnp.float32),
            pltpu.VMEM((padded, BLOCK), jnp.bfloat16),
        ],
        compiler_params=params(),
        name="hidden_layer",
    )(words, own, own, got, scale, weight_self, weight_near, bias_col, send_col)


def seed_kernel(rows_ref, labels_ref, mask_ref, out_ref):
    step = pl.program_id(0)
    classes, block = out_ref.shape
    slots = rows_ref.shape[0]
    kind = lax.broadcasted_iota(jnp.int32, (classes, slots), 0)
    marked = jnp.where((kind == labels_ref[...]) & (mask_ref[...] != 0), 1.0, 0.0)
    node = lax.broadcasted_iota(jnp.int32, (1, block), 1) + step * block
    chosen = jnp.where(rows_ref[...] == node, 1.0, 0.0).astype(jnp.bfloat16)
    out_ref[...] = dot(marked.astype(jnp.bfloat16), chosen)


def seed_counts(rows_col, labels_row, mask_row, nodes, classes):
    return pl.pallas_call(
        seed_kernel,
        grid=(nodes // BLOCK,),
        in_specs=[whole(rows_col.shape), whole(labels_row.shape), whole(mask_row.shape)],
        out_specs=lanes(classes, BLOCK),
        out_shape=jax.ShapeDtypeStruct((classes, nodes), jnp.float32),
        compiler_params=params(),
        name="seed_counts",
    )(rows_col, labels_row, mask_row)


def last_kernel(
    fanout,
    words_ref,
    own_ref,
    own_block,
    got_ref,
    scale_ref,
    self_ref,
    near_ref,
    bias_ref,
    seeds_ref,
    grad_ref,
    sums_ref,
    table_out,
    reduced_ref,
    counts_ref,
    both_ref,
):
    step = pl.program_id(0)
    last = pl.num_programs(0) - 1
    classes = self_ref.shape[0]
    nodes = own_ref.shape[1]

    @pl.when(step == 0)
    def _():
        table_out[:, :nodes] = own_ref[...]
        table_out[:, nodes:] = got_ref[...].T
        reduced = dot(near_ref[...], table_out[...]) * scale_ref[...]
        high = reduced.astype(jnp.bfloat16)
        reduced_ref[:classes, :] = high
        reduced_ref[classes:, :] = (reduced - high.astype(jnp.float32)).astype(jnp.bfloat16)
        both_ref[...] = jnp.zeros_like(both_ref)

    @pl.when(step <= 1)
    def _():
        sums_ref[...] = jnp.zeros_like(sums_ref)

    def finish():
        near_part = (both_ref[:classes, :] + both_ref[classes:, :]) / fanout
        logits = dot(self_ref[...], own_block[...]) + near_part + bias_ref[...]
        top = jnp.max(logits, axis=0, keepdims=True)
        powers = jnp.exp(logits - top)
        total = jnp.sum(powers, axis=0, keepdims=True)
        normer = jnp.log(total) + top
        seeds = seeds_ref[...]
        uses = jnp.sum(seeds, axis=0, keepdims=True)
        grad = (powers / total * uses - seeds).astype(jnp.bfloat16)
        grad_ref[...] = grad
        loss = uses * normer - jnp.sum(seeds * logits, axis=0, keepdims=True)
        sums_ref[:classes, :] += jnp.sum(grad.astype(jnp.float32), axis=1, keepdims=True)
        sums_ref[classes:, :] += jnp.sum(loss)

    @pl.when(step < last)
    def _():
        finish()
        both_ref[...] = gather_product(reduced_ref, words_ref, counts_ref)

    @pl.when(step == last)
    def _():
        finish()


def last_layer(words, own, got, scale, weight_self, weight_near, bias_col, seeds, fanout):
    width, nodes = own.shape
    table = nodes + got.shape[0]
    classes = weight_self.shape[0]
    steps = nodes // BLOCK
    return pl.pallas_call(
        functools.partial(last_kernel, fanout),
        grid=(steps + 1,),
        in_specs=[
            now(words.shape[0], BLOCK, steps),
            whole(own.shape),
            late(width, BLOCK),
            whole(got.shape),
            whole(scale.shape),
            whole(weight_self.shape),
            whole(weight_near.shape),
            whole(bias_col.shape),
            late(classes, BLOCK),
        ],
        out_specs=[
            late(classes, BLOCK),
            whole((classes + 8, 128)),
            whole((width, table)),
        ],
        out_shape=[
            jax.ShapeDtypeStruct((classes, nodes), jnp.bfloat16),
            jax.ShapeDtypeStruct((classes + 8, 128), jnp.float32),
            jax.ShapeDtypeStruct((width, table), jnp.bfloat16),
        ],
        scratch_shapes=[
            pltpu.VMEM((2 * classes, table), jnp.bfloat16),
            pltpu.VMEM((table, BLOCK), jnp.bfloat16),
            pltpu.VMEM((2 * classes, BLOCK), jnp.float32),
        ],
        compiler_params=params(),
        name="last_layer",
    )(words, own, own, got, scale, weight_self, weight_near, bias_col, seeds)


def spread_slot(words_ref, word_row, counts_ref, count_row, slot, span):
    for tile in range(0, words_ref.shape[1], 128):
        cols = slice(tile, tile + 128)
        for start in range(0, span, 48):
            counts_ref[count_row + start : count_row + start + 48, cols] = field(
                words_ref[word_row + start : word_row + start + 48, cols], slot
            )


def halo_kernel(
    fanout,
    first_group,
    skip,
    words_ref,
    grad_ref,
    near_ref,
    rows_ref,
    sums_ref,
    halo_ref,
    counts_ref,
    all_ref,
):
    span = counts_ref.shape[0] // (GROUPS - first_group)
    rows_ref[...] = grad_ref[...].T
    for group in range(first_group, GROUPS):
        word, slot = divmod(group, SLOTS)
        row = (group - first_group) * span
        spread_slot(words_ref, word * span, counts_ref, row, slot, span)
        added = dot(counts_ref[row : row + span, :], rows_ref[...])
        all_ref[row : row + span, :] = (added * (slot_scale(slot) / fanout)).astype(jnp.bfloat16)
    sums = all_ref[skip:, :]
    sums_ref[...] = sums
    halo_ref[...] = dot(sums, near_ref[...], TRANS_RIGHT).astype(jnp.bfloat16)


def halo_scatter(words, grad, weight_near, halo, fanout):
    units, nodes = grad.shape
    width = weight_near.shape[0]
    span = (nodes + halo) // GROUPS
    first_group = nodes // span
    skip = nodes - first_group * span
    height = (GROUPS - first_group) * span
    return pl.pallas_call(
        functools.partial(halo_kernel, fanout, first_group, skip),
        grid=(1,),
        in_specs=[whole(words.shape), whole(grad.shape), whole(weight_near.shape)],
        out_specs=[whole((nodes, units)), whole((halo, units)), whole((halo, width))],
        out_shape=[
            jax.ShapeDtypeStruct((nodes, units), jnp.bfloat16),
            jax.ShapeDtypeStruct((halo, units), jnp.bfloat16),
            jax.ShapeDtypeStruct((halo, width), jnp.bfloat16),
        ],
        scratch_shapes=[
            pltpu.VMEM((height, nodes), jnp.bfloat16),
            pltpu.VMEM((height, units), jnp.bfloat16),
        ],
        compiler_params=params(),
        name="halo_scatter",
    )(words, grad, weight_near)


def scatter_kernel(
    fanout,
    words_ref,
    grad_ref,
    rows_ref,
    far_ref,
    table_ref,
    far_table,
    self_ref,
    near_ref,
    state_ref,
    weight_ref,
    padded_ref,
    counts_ref,
    sums_ref,
):
    step = pl.program_id(0)
    units, nodes = grad_ref.shape
    width = table_ref.shape[0]
    span = words_ref.shape[0]
    part = span * SLOTS

    @pl.when(step == 0)
    def _():
        for k in range(padded_ref.shape[0]):
            start = k * part
            stop = min(start + part, nodes)
            padded_ref[k, :, : stop - start] = grad_ref[:, start:stop]
            if stop < start + part:
                padded_ref[k, :, stop - start :] = jnp.zeros(
                    (units, start + part - stop), jnp.bfloat16
                )
        weight_ref[:width, :] = jnp.zeros((width, units), jnp.float32)
        weight_ref[width:, :] = dot(far_table[...], far_ref[...])
        sums_ref[...] = jnp.zeros_like(sums_ref)

    pair = 2
    steps = -(-nodes // part)

    def add(slot):
        for one in range(slot, slot + pair):
            spread_slot(words_ref, 0, counts_ref, one * span, one, span)
        added = dot(counts_ref[slot * span : (slot + pair) * span, :], rows_ref[...])
        for one in range(slot, slot + pair):
            piece = added[(one - slot) * span : (one - slot + 1) * span, :]
            piece = (piece * (slot_scale(one) / fanout)).astype(jnp.bfloat16)
            sums_ref[one * span : (one + 1) * span, :] = piece

    beyond = nodes - (steps - 1) * part
    ending = -(-beyond // (pair * span)) * pair
    for slot in range(0, ending, pair):
        add(slot)
    if ending < SLOTS:

        @pl.when(step < steps - 1)
        def _():
            for slot in range(ending, SLOTS, pair):
                add(slot)

    if beyond < part:

        @pl.when(step == steps - 1)
        def _():
            sums_ref[beyond:, :] = jnp.zeros((part - beyond, units), jnp.bfloat16)

    sums = sums_ref[...]
    own_grad = padded_ref[step]
    state_ref[...] = dot(near_ref[...], sums, TRANS_RIGHT) + dot(self_ref[...], own_grad)
    weight_ref[:width, :] += dot(table_ref[...], own_grad, TRANS_RIGHT)
    weight_ref[width:, :] += dot(table_ref[...], sums)


def scatter_layer(words, grad, rows, far, table, weight_self, weight_near, fanout):
    units, nodes = grad.shape
    width, total = table.shape
    span = total // GROUPS
    part = total // WORDS
    steps = -(-nodes // part)
    far_table = table[:, nodes:]
    return pl.pallas_call(
        functools.partial(scatter_kernel, fanout),
        grid=(steps,),
        in_specs=[
            pl.BlockSpec((span, nodes), lambda i: (i, 0)),
            whole(grad.shape),
            whole(rows.shape),
            whole(far.shape),
            lanes(width, part),
            whole(far_table.shape),
            whole(weight_self.shape),
            whole(weight_near.shape),
        ],
        out_specs=[lanes(width, part), whole((2 * width, units))],
        out_shape=[
            jax.ShapeDtypeStruct((width, total), jnp.float32),
            jax.ShapeDtypeStruct((2 * width, units), jnp.float32),
        ],
        scratch_shapes=[
            pltpu.VMEM((steps, units, part), jnp.bfloat16),
            pltpu.VMEM((part, nodes), jnp.bfloat16),
            pltpu.VMEM((part, units), jnp.bfloat16),
        ],
        compiler_params=params(),
        name="scatter_layer",
    )(words, grad, rows, far, table, far_table, weight_self, weight_near)


def active_kernel(first, state_ref, preact_ref, returned_ref, send_ref, *refs):
    if first:
        own_block, mean_block, grad_ref, sums_ref, weight_ref = refs
    else:
        grad_ref, sums_ref = refs
    step = pl.program_id(0)
    block = state_ref.shape[1]
    node = lax.broadcasted_iota(jnp.int32, (1, block), 1) + step * block
    chosen = jnp.where(send_ref[...] == node, 1.0, 0.0).astype(jnp.bfloat16)
    upper = state_ref[...] + dot(returned_ref[...], chosen, TRANS_LEFT)
    preact = preact_ref[...]
    gate = jax.nn.sigmoid(preact)
    active = preact * gate
    norm = lax.rsqrt(jnp.sum(active * active, axis=0, keepdims=True) + 1e-06)
    along = jnp.sum(active * upper, axis=0, keepdims=True)
    inner = norm * upper - active * (norm * norm * norm * along)
    grad = (inner * (gate * (1.0 + preact * (1.0 - gate)))).astype(jnp.bfloat16)
    grad_ref[...] = grad

    @pl.when(step == 0)
    def _():
        sums_ref[...] = jnp.zeros_like(sums_ref)
        if first:
            weight_ref[...] = jnp.zeros_like(weight_ref)

    sums_ref[...] += jnp.sum(grad.astype(jnp.float32), axis=1, keepdims=True)
    if first:
        width = own_block.shape[0]
        weight_ref[0, :width, :] += dot(own_block[...], grad, TRANS_RIGHT)
        weight_ref[1] += dot(mean_block[...], grad, TRANS_RIGHT)


def active_layer(state_grad, preact, returned, send_col, own=None, mean=None):
    units, nodes = preact.shape
    first = own is not None
    in_specs = [
        lanes(units, BLOCK),
        lanes(units, BLOCK),
        whole(returned.shape),
        whole(send_col.shape),
    ]
    out_specs = [lanes(units, BLOCK), whole((units, 128))]
    out_shape = [
        jax.ShapeDtypeStruct((units, nodes), jnp.bfloat16),
        jax.ShapeDtypeStruct((units, 128), jnp.float32),
    ]
    operands = [state_grad, preact, returned, send_col]
    if first:
        padded = mean.shape[0]
        in_specs += [lanes(own.shape[0], BLOCK), lanes(padded, BLOCK)]
        out_specs.append(whole((2, padded, units)))
        out_shape.append(jax.ShapeDtypeStruct((2, padded, units), jnp.float32))
        operands += [own, mean]
    return pl.pallas_call(
        functools.partial(active_kernel, first),
        grid=(nodes // BLOCK,),
        in_specs=in_specs,
        out_specs=out_specs,
        out_shape=out_shape,
        compiler_params=params(),
        name="active_layer",
    )(*operands)


def product(left, right):
    return jnp.dot(left, right, precision=lax.Precision.HIGHEST, preferred_element_type=jnp.float32)


def exchange(rows):
    return lax.all_to_all(rows, axes, split_axis=0, concat_axis=0, tiled=True)


def pad_count(rows, parts):
    return jnp.pad(rows, ((0, -rows.shape[0] % parts), (0, 0)))


def pad_rows(flat, width):
    return jnp.pad(flat, (0, -flat.size % width)).reshape(-1, width)


def in_terms(values):
    terms = []
    for _ in range(3):
        term = lax.reduce_precision(values, 8, 7)
        terms.append(term)
        values = values - term
    return jnp.stack(terms).astype(jnp.bfloat16)


def rotate_adam(weight, grad, first, second, left_basis, right_basis, rate):
    turned = product(product(left_basis.T, grad), right_basis)
    first = beta_one * first + (1.0 - beta_one) * turned
    second = beta_two * second + (1.0 - beta_two) * turned * turned
    update = first / (1.0 - beta_one**STEP) / (jnp.sqrt(second / (1.0 - beta_two**STEP)) + epsilon)
    return (weight - rate * product(product(left_basis, update), right_basis.T), first, second)


def on_device(
    features,
    labels,
    seed_rows,
    seed_mask,
    send_rows,
    neighbors_one,
    neighbors_two,
    neighbors_three,
    weight_one,
    weight_two,
    weight_three,
    left_one,
    right_one,
    left_two,
    right_two,
    left_three,
    right_three,
    first_one,
    first_two,
    first_three,
    second_one,
    second_two,
    second_three,
    bias_all,
    bias_first,
    bias_second,
):
    nodes, width = features.shape
    units = weight_one.shape[1]
    classes = weight_three.shape[1]
    halo = send_rows.size
    table = nodes + halo
    span = table // GROUPS
    low = jnp.bfloat16
    fans = (neighbors_one.shape[1], neighbors_two.shape[1], neighbors_three.shape[1])
    near = (neighbors_one.T, neighbors_two.T, neighbors_three.T)
    feats = features.T
    slot_of = (jnp.arange(table, dtype=jnp.int32) // span) % SLOTS
    scale = jnp.where(slot_of == SLOTS - 1, 1.0, 0.0)
    for slot in range(SLOTS - 1):
        scale = jnp.where(slot_of == slot, slot_scale(slot), scale)
    scale = scale.astype(jnp.float32)[None, :]
    send_col = send_rows.reshape(halo, 1)

    got_one = exchange(features[send_rows.reshape(-1)])
    words_one = count_words(near[0], table)
    padded_classes = -(-classes // 16) * 16
    more = padded_classes - classes
    seed_float = seed_mask.astype(jnp.float32)

    padded = -(-width // 16) * 16
    self_one = weight_one[:width].T.astype(low)
    near_one = jnp.pad(weight_one[width:].T, ((0, 0), (0, padded - width))).astype(low)
    self_two = weight_two[:units].astype(low)
    near_two = weight_two[units:].astype(low)
    wide_three = jnp.pad(weight_three, ((0, 0), (0, more))).astype(low)
    self_three = wide_three[:units]
    near_three = wide_three[units:]
    bias_three = jnp.pad(bias_all[2 * units :], (0, more), constant_values=-1e30)

    state_one, preact_one, sent_two, mean_one = hidden_layer(
        words_one,
        feats,
        got_one,
        scale,
        self_one,
        near_one,
        bias_all[:units].reshape(-1, 1),
        send_col,
        fans[0],
    )
    near_lists, sent_two = lax.optimization_barrier((near[1], sent_two))
    got_two = exchange(sent_two)
    words_two = count_words(near_lists, table)
    state_two, preact_two, sent_three, table_two = hidden_layer(
        words_two,
        state_one,
        got_two,
        scale,
        self_two.T,
        near_two.T,
        bias_all[units : 2 * units].reshape(-1, 1),
        send_col,
        fans[1],
    )
    near_lists, slots, sent_three = lax.optimization_barrier((near[2], seed_rows, sent_three))
    got_three = exchange(sent_three)
    words_three = count_words(near_lists, table)
    seeds = seed_counts(
        slots.reshape(-1, 1),
        labels.reshape(1, -1),
        seed_mask.reshape(1, -1),
        nodes,
        padded_classes,
    )
    grad_three, sums_three, table_three = last_layer(
        words_three,
        state_two,
        got_three,
        scale,
        self_three.T,
        near_three.T,
        bias_three.reshape(-1, 1),
        seeds,
        fans[2],
    )
    rows, far, halo_grad = halo_scatter(words_three, grad_three, near_three, halo, fans[2])
    returned = exchange(halo_grad)
    state_grad, weight_grad_three = scatter_layer(
        words_three, grad_three, rows, far, table_three, self_three, near_three, fans[2]
    )
    grad_two, sums_two = active_layer(state_grad, preact_two, returned, send_col)
    rows, far, halo_grad = halo_scatter(words_two, grad_two, near_two, halo, fans[1])
    returned = exchange(halo_grad)
    state_grad, weight_grad_two = scatter_layer(
        words_two, grad_two, rows, far, table_two, self_two, near_two, fans[1]
    )
    parts = lax.axis_size(axes)
    early = jnp.concatenate([weight_grad_two, weight_grad_three], axis=1).astype(low)
    early = early.reshape(parts, -1, early.shape[1])
    early_sum = jnp.sum(exchange(early).astype(jnp.float32), axis=0).astype(low)
    _, sums_one, weight_grad_one = active_layer(
        state_grad, preact_one, returned, send_col, feats, mean_one
    )
    bias_parts = jnp.concatenate([sums_one[:, 0], sums_two[:, 0], sums_three[:classes, 0]])
    scalars = jnp.stack([sums_three[padded_classes, 0], jnp.sum(seed_float)])
    late_rows = jnp.concatenate([weight_grad_one.reshape(-1, units), pad_rows(bias_parts, units)])
    late_rows = pad_count(late_rows, parts).astype(low).reshape(parts, -1)
    early_width = early_sum.size
    late_width = late_rows.shape[1]
    mixed = jnp.concatenate(
        [
            jnp.broadcast_to(early_sum.reshape(1, -1), (parts, early_width)),
            late_rows,
            jnp.broadcast_to(in_terms(scalars).reshape(1, -1), (parts, 6)),
        ],
        axis=1,
    )
    mixed = exchange(mixed)
    early_all = mixed[:, :early_width].reshape(2 * units, -1).astype(jnp.float32)
    late_sum = jnp.sum(
        mixed[:, early_width : early_width + late_width].astype(jnp.float32), axis=0
    ).astype(low)
    terms = mixed[:, early_width + late_width :].astype(jnp.float32)
    loss_sum, seed_total = jnp.sum(terms.reshape(parts, 3, 2), axis=(0, 1))
    late_all = exchange(jnp.broadcast_to(late_sum[None], (parts, late_width)))
    late_all = late_all.reshape(-1, units).astype(jnp.float32)
    share = 1.0 / seed_total
    out_two = rotate_adam(
        weight_two,
        early_all[:, :units] * share,
        first_two,
        second_two,
        left_two,
        right_two,
        step_rates[1],
    )
    out_three = rotate_adam(
        weight_three,
        early_all[:, units : units + classes] * share,
        first_three,
        second_three,
        left_three,
        right_three,
        step_rates[2],
    )
    sum_one = jnp.concatenate([late_all[:width], late_all[padded : padded + width]])
    out_one = rotate_adam(
        weight_one, sum_one * share, first_one, second_one, left_one, right_one, step_rates[0]
    )
    bias_grad = late_all[2 * padded :].reshape(-1)[: bias_all.size] * share
    bias_m = beta_one * bias_first + (1.0 - beta_one) * bias_grad
    bias_v = beta_two * bias_second + (1.0 - beta_two) * bias_grad * bias_grad
    bias_update = (
        bias_m / (1.0 - beta_one**STEP) / (jnp.sqrt(bias_v / (1.0 - beta_two**STEP)) + epsilon)
    )
    new_bias = bias_all - bias_rate * (bias_update + weight_decay * bias_all)
    return (*out_one, *out_two, *out_three, new_bias, bias_m, bias_v, loss_sum, seed_total)


def solution(mesh):
    split = P(axes)
    rows = P(axes, None)
    placed = (rows, split, split, split, rows, rows, rows, rows) + (P(),) * 18
    return jax.shard_map(
        on_device,
        mesh=mesh,
        in_specs=placed,
        out_specs=(P(),) * 14,
        check_vma=False,
    )
```

```python
import functools

import jax
import jax.numpy as jnp
from jax import lax
from jax.experimental import pallas as pl
from jax.experimental.pallas import tpu as pltpu
from jax.sharding import PartitionSpec as P

STEP = 10


beta_one = 0.9
beta_two = 0.999
epsilon = 1e-08
step_rates = (0.05, 0.5, 1.0)
bias_rate = 0.05
weight_decay = 0.01

axes = ("dom", "rep")
WORDS = 4
SLOTS = 8
GROUPS = WORDS * SLOTS
BLOCK = 512
VMEM_BYTES = 56 * 1024 * 1024
TRANS_LEFT = (((0,), (0,)), ((), ()))
TRANS_RIGHT = (((1,), (1,)), ((), ()))


def dot(left, right, dims=(((1,), (0,)), ((), ()))):
    return lax.dot_general(left, right, dims, preferred_element_type=jnp.float32)


def params():
    return pltpu.CompilerParams(
        dimension_semantics=("arbitrary",), vmem_limit_bytes=VMEM_BYTES
    )


def whole(shape):
    return pl.BlockSpec(shape, lambda i: (0,) * len(shape))


def lanes(rows, width):
    return pl.BlockSpec((rows, width), lambda i: (0, i))


def words_layer(near_ref, out_ref, place_ref, field_ref):
    fanout, block = near_ref.shape
    span = out_ref.shape[0] // WORDS
    near = near_ref[...]
    group = ((near.astype(jnp.float32) + 0.5) * (1.0 / span)).astype(jnp.int32)
    place = near - group * span
    word = group >> 3
    bit = jnp.left_shift(jnp.int32(1), (group & 7) * 4)
    parts = [jnp.where(word == k, bit, 0) for k in range(WORDS)]
    totals = [jnp.zeros_like(bit) for _ in range(WORDS)]
    for g in range(fanout):
        same = place == place[g : g + 1]
        for k in range(WORDS):
            totals[k] = totals[k] + jnp.where(same, parts[k][g : g + 1], 0)
    place_ref[:fanout, :] = place
    for k in range(WORDS):
        field_ref[k, :fanout, :] = totals[k]
    chunk = 48
    for tile in range(0, block, 128):
        cols = slice(tile, tile + 128)
        for start in range(0, span, chunk):
            rows = lax.broadcasted_iota(jnp.int32, (chunk, 128), 0) + start
            sums = [jnp.zeros((chunk, 128), jnp.int32) for _ in range(WORDS)]
            for g in range(fanout):
                hit = rows == place_ref[g : g + 1, cols]
                for k in range(WORDS):
                    sums[k] = jnp.where(hit, field_ref[k, g : g + 1, cols], sums[k])
            for k in range(WORDS):
                out_ref[k * span + start : k * span + start + chunk, cols] = sums[k]


def ring(mesh_sizes):
    across, along = mesh_sizes
    parts = across * along
    me = lax.axis_index(axes[0]) * along + lax.axis_index(axes[1])

    def peer(ahead):
        index = lax.rem(me + ahead, parts)
        return index, (index // along, lax.rem(index, along))

    return parts, me, peer


def greet(mesh_sizes):
    parts, _, peer = ring(mesh_sizes)
    barrier = pltpu.get_barrier_semaphore()

    def tell(ahead, carry):
        pl.semaphore_signal(
            barrier, inc=1, device_id=peer(ahead)[1], device_id_type=pl.DeviceIdType.MESH
        )
        return carry

    lax.fori_loop(1, parts, tell, 0)


def all_greeted(mesh_sizes):
    pl.semaphore_wait(pltpu.get_barrier_semaphore(), ring(mesh_sizes)[0] - 1)


def block_copy(mesh_sizes, out_ref, in_ref, send_sem, recv_sem, ahead):
    _, me, peer = ring(mesh_sizes)
    index, where = peer(ahead)
    return pltpu.make_async_remote_copy(
        src_ref=out_ref.at[index],
        dst_ref=in_ref.at[me],
        send_sem=send_sem.at[index],
        recv_sem=recv_sem.at[me],
        device_id=where,
        device_id_type=pl.DeviceIdType.MESH,
    )


def send_blocks(mesh_sizes, out_ref, in_ref, send_sem, recv_sem):
    parts = ring(mesh_sizes)[0]

    def send(ahead, carry):
        block_copy(mesh_sizes, out_ref, in_ref, send_sem, recv_sem, ahead).start()
        return carry

    lax.fori_loop(1, parts, send, 0)


def wait_blocks(mesh_sizes, out_ref, in_ref, send_sem, recv_sem):
    parts, me, peer = ring(mesh_sizes)

    def wait(ahead, carry):
        block_copy(mesh_sizes, out_ref, in_ref, send_sem, recv_sem, ahead).wait_send()
        index, where = peer(ahead)
        pltpu.make_async_remote_copy(
            src_ref=out_ref.at[index],
            dst_ref=in_ref.at[index],
            send_sem=send_sem.at[index],
            recv_sem=recv_sem.at[index],
            device_id=where,
            device_id_type=pl.DeviceIdType.MESH,
        ).wait_recv()
        return carry

    lax.fori_loop(1, parts, wait, 0)


def words_kernel(
    mesh_sizes,
    near_ref,
    sent_ref,
    out_ref,
    got_ref,
    place_ref,
    field_ref,
    land_ref,
    send_sem,
    recv_sem,
):
    step = pl.program_id(0)
    moves = (mesh_sizes, sent_ref, land_ref, send_sem, recv_sem)

    @pl.when(step == 0)
    def _():
        greet(mesh_sizes)

    @pl.when(step == 1)
    def _():
        all_greeted(mesh_sizes)
        send_blocks(*moves)

    words_layer(near_ref, out_ref, place_ref, field_ref)

    @pl.when(step == pl.num_programs(0) - 1)
    def _():
        me = ring(mesh_sizes)[1]
        wait_blocks(*moves)
        land_ref[me] = sent_ref[me]
        got_ref[...] = land_ref[...]


def count_words(near, sent, mesh_sizes, collective):
    fanout, nodes = near.shape
    halo, width = sent.shape
    parts = mesh_sizes[0] * mesh_sizes[1]
    blocks = (parts, halo // parts, width)
    height = (nodes + halo) // SLOTS
    words, got = pl.pallas_call(
        functools.partial(words_kernel, mesh_sizes),
        grid=(nodes // BLOCK,),
        in_specs=[lanes(fanout, BLOCK), whole(blocks)],
        out_specs=[lanes(height, BLOCK), whole(blocks)],
        out_shape=[
            jax.ShapeDtypeStruct((height, nodes), jnp.int32),
            jax.ShapeDtypeStruct(blocks, sent.dtype),
        ],
        scratch_shapes=[
            pltpu.VMEM((16, BLOCK), jnp.int32),
            pltpu.VMEM((WORDS, 16, BLOCK), jnp.int32),
            pltpu.VMEM(blocks, sent.dtype),
            pltpu.SemaphoreType.DMA((parts,)),
            pltpu.SemaphoreType.DMA((parts,)),
        ],
        compiler_params=pltpu.CompilerParams(
            dimension_semantics=("arbitrary",),
            vmem_limit_bytes=VMEM_BYTES,
            collective_id=collective,
            has_side_effects=True,
        ),
        name="count_words",
    )(near, sent.reshape(blocks))
    return words, got.reshape(halo, width)


def field(words, slot):
    if slot == SLOTS - 1:
        picked = lax.shift_right_logical(words, 4 * slot)
    else:
        picked = words & (15 << (4 * slot))
    return picked.astype(jnp.float32).astype(jnp.bfloat16)


def slot_scale(slot):
    return 1.0 if slot == SLOTS - 1 else 2.0 ** (-4 * slot)


def spread_counts(words_ref, counts_ref, group, span):
    word, slot = divmod(group, SLOTS)
    width = words_ref.shape[1]
    for tile in range(0, width, 128):
        cols = slice(tile, tile + 128)
        for start in range(0, span, 48):
            counts_ref[group * span + start : group * span + start + 48, cols] = field(
                words_ref[word * span + start : word * span + start + 48, cols], slot
            )


def gather_product(table_ref, words_ref, counts_ref):
    table = table_ref.shape[1]
    span = table // GROUPS
    total = None
    done = 0
    step = 512
    for group in range(GROUPS):
        spread_counts(words_ref, counts_ref, group, span)
        ready = (group + 1) * span
        while ready - done >= step or (group == GROUPS - 1 and done < table):
            stop = min(done + step, table)
            term = dot(table_ref[:, done:stop], counts_ref[done:stop, :])
            total = term if total is None else total + term
            done = stop
    return total


def scaled_table(own, got, scale, table_ref):
    width, nodes = own.shape
    table_ref[:width, :nodes] = (own.astype(jnp.float32) * scale[:, :nodes]).astype(jnp.bfloat16)
    table_ref[:width, nodes:] = (got.astype(jnp.float32) * scale[:, nodes:]).astype(jnp.bfloat16)


def late(rows, width):
    return pl.BlockSpec((rows, width), lambda i: (0, jnp.maximum(i - 1, 0)))


def now(rows, width, steps):
    return pl.BlockSpec((rows, width), lambda i: (0, jnp.minimum(i, steps - 1)))


def hidden_kernel(
    fanout,
    words_ref,
    own_ref,
    own_block,
    got_ref,
    scale_ref,
    self_ref,
    near_ref,
    bias_ref,
    send_ref,
    state_ref,
    preact_ref,
    sent_ref,
    extra_ref,
    table_ref,
    counts_ref,
    picked_ref,
    mean_ref,
):
    step = pl.program_id(0)
    last = pl.num_programs(0) - 1
    width = own_ref.shape[0]
    units, block = state_ref.shape

    @pl.when(step == 0)
    def _():
        if table_ref.shape[0] > width:
            table_ref[...] = jnp.zeros_like(table_ref)
        got = got_ref[...].T[:width]
        scaled_table(own_ref[...], got, scale_ref[...], table_ref)
        if width == units:
            extra_ref[:, : own_ref.shape[1]] = own_ref[...]
            extra_ref[:, own_ref.shape[1] :] = got
        mean_ref[...] = jnp.zeros_like(mean_ref)
        picked_ref[...] = jnp.zeros_like(picked_ref)

    def finish():
        mean = mean_ref[...]
        if width != units:
            extra_ref[...] = mean
        preact = dot(self_ref[...], own_block[...]) + dot(near_ref[...], mean) + bias_ref[...]
        preact_ref[...] = preact
        active = preact * jax.nn.sigmoid(preact)
        norm = lax.rsqrt(jnp.sum(active * active, axis=0, keepdims=True) + 1e-06)
        state = (active * norm).astype(jnp.bfloat16)
        state_ref[...] = state
        node = lax.broadcasted_iota(jnp.int32, (1, block), 1) + (step - 1) * block
        chosen = jnp.where(send_ref[...] == node, 1.0, 0.0).astype(jnp.bfloat16)
        picked_ref[...] += dot(chosen, state, TRANS_RIGHT)

    @pl.when(step < last)
    def _():
        finish()
        total = gather_product(table_ref, words_ref, counts_ref)
        mean_ref[...] = (total / fanout).astype(jnp.bfloat16)

    @pl.when(step == last)
    def _():
        finish()
        sent_ref[...] = picked_ref[...].astype(jnp.bfloat16)


def hidden_layer(words, own, got, scale, weight_self, weight_near, bias_col, send_col, fanout):
    width, nodes = own.shape
    halo = got.shape[0]
    table = nodes + halo
    units = weight_self.shape[0]
    padded = weight_near.shape[1]
    steps = nodes // BLOCK
    if width == units:
        extra_shape, extra_spec = (units, table), whole((units, table))
    else:
        extra_shape, extra_spec = (padded, nodes), late(padded, BLOCK)
    return pl.pallas_call(
        functools.partial(hidden_kernel, fanout),
        grid=(steps + 1,),
        in_specs=[
            now(words.shape[0], BLOCK, steps),
            whole(own.shape),
            late(width, BLOCK),
            whole(got.shape),
            whole(scale.shape),
            whole(weight_self.shape),
            whole(weight_near.shape),
            whole(bias_col.shape),
            whole(send_col.shape),
        ],
        out_specs=[
            late(units, BLOCK),
            late(units, BLOCK),
            whole((halo, units)),
            extra_spec,
        ],
        out_shape=[
            jax.ShapeDtypeStruct((units, nodes), jnp.bfloat16),
            jax.ShapeDtypeStruct((units, nodes), jnp.float32),
            jax.ShapeDtypeStruct((halo, units), jnp.bfloat16),
            jax.ShapeDtypeStruct(extra_shape, jnp.bfloat16),
        ],
        scratch_shapes=[
            pltpu.VMEM((padded, table), jnp.bfloat16),
            pltpu.VMEM((table, BLOCK), jnp.bfloat16),
            pltpu.VMEM((halo, units), jnp.float32),
            pltpu.VMEM((padded, BLOCK), jnp.bfloat16),
        ],
        compiler_params=params(),
        name="hidden_layer",
    )(words, own, own, got, scale, weight_self, weight_near, bias_col, send_col)


def seed_kernel(rows_ref, labels_ref, mask_ref, out_ref):
    step = pl.program_id(0)
    classes, block = out_ref.shape
    slots = rows_ref.shape[0]
    kind = lax.broadcasted_iota(jnp.int32, (classes, slots), 0)
    marked = jnp.where((kind == labels_ref[...]) & (mask_ref[...] != 0), 1.0, 0.0)
    node = lax.broadcasted_iota(jnp.int32, (1, block), 1) + step * block
    chosen = jnp.where(rows_ref[...] == node, 1.0, 0.0).astype(jnp.bfloat16)
    out_ref[...] = dot(marked.astype(jnp.bfloat16), chosen)


def seed_counts(rows_col, labels_row, mask_row, nodes, classes):
    return pl.pallas_call(
        seed_kernel,
        grid=(nodes // BLOCK,),
        in_specs=[whole(rows_col.shape), whole(labels_row.shape), whole(mask_row.shape)],
        out_specs=lanes(classes, BLOCK),
        out_shape=jax.ShapeDtypeStruct((classes, nodes), jnp.float32),
        compiler_params=params(),
        name="seed_counts",
    )(rows_col, labels_row, mask_row)


def last_kernel(
    fanout,
    words_ref,
    own_ref,
    own_block,
    got_ref,
    scale_ref,
    self_ref,
    near_ref,
    bias_ref,
    seeds_ref,
    grad_ref,
    sums_ref,
    table_out,
    reduced_ref,
    counts_ref,
    both_ref,
):
    step = pl.program_id(0)
    last = pl.num_programs(0) - 1
    classes = self_ref.shape[0]
    nodes = own_ref.shape[1]

    @pl.when(step == 0)
    def _():
        table_out[:, :nodes] = own_ref[...]
        table_out[:, nodes:] = got_ref[...].T
        reduced = dot(near_ref[...], table_out[...]) * scale_ref[...]
        high = reduced.astype(jnp.bfloat16)
        reduced_ref[:classes, :] = high
        reduced_ref[classes:, :] = (reduced - high.astype(jnp.float32)).astype(jnp.bfloat16)
        both_ref[...] = jnp.zeros_like(both_ref)

    @pl.when(step <= 1)
    def _():
        sums_ref[...] = jnp.zeros_like(sums_ref)

    def finish():
        near_part = (both_ref[:classes, :] + both_ref[classes:, :]) / fanout
        logits = dot(self_ref[...], own_block[...]) + near_part + bias_ref[...]
        top = jnp.max(logits, axis=0, keepdims=True)
        powers = jnp.exp(logits - top)
        total = jnp.sum(powers, axis=0, keepdims=True)
        normer = jnp.log(total) + top
        seeds = seeds_ref[...]
        uses = jnp.sum(seeds, axis=0, keepdims=True)
        grad = (powers / total * uses - seeds).astype(jnp.bfloat16)
        grad_ref[...] = grad
        loss = uses * normer - jnp.sum(seeds * logits, axis=0, keepdims=True)
        sums_ref[:classes, :] += jnp.sum(grad.astype(jnp.float32), axis=1, keepdims=True)
        sums_ref[classes:, :] += jnp.sum(loss)

    @pl.when(step < last)
    def _():
        finish()
        both_ref[...] = gather_product(reduced_ref, words_ref, counts_ref)

    @pl.when(step == last)
    def _():
        finish()


def last_layer(words, own, got, scale, weight_self, weight_near, bias_col, seeds, fanout):
    width, nodes = own.shape
    table = nodes + got.shape[0]
    classes = weight_self.shape[0]
    steps = nodes // BLOCK
    return pl.pallas_call(
        functools.partial(last_kernel, fanout),
        grid=(steps + 1,),
        in_specs=[
            now(words.shape[0], BLOCK, steps),
            whole(own.shape),
            late(width, BLOCK),
            whole(got.shape),
            whole(scale.shape),
            whole(weight_self.shape),
            whole(weight_near.shape),
            whole(bias_col.shape),
            late(classes, BLOCK),
        ],
        out_specs=[
            late(classes, BLOCK),
            whole((classes + 8, 128)),
            whole((width, table)),
        ],
        out_shape=[
            jax.ShapeDtypeStruct((classes, nodes), jnp.bfloat16),
            jax.ShapeDtypeStruct((classes + 8, 128), jnp.float32),
            jax.ShapeDtypeStruct((width, table), jnp.bfloat16),
        ],
        scratch_shapes=[
            pltpu.VMEM((2 * classes, table), jnp.bfloat16),
            pltpu.VMEM((table, BLOCK), jnp.bfloat16),
            pltpu.VMEM((2 * classes, BLOCK), jnp.float32),
        ],
        compiler_params=params(),
        name="last_layer",
    )(words, own, own, got, scale, weight_self, weight_near, bias_col, seeds)


def spread_slot(words_ref, word_row, counts_ref, count_row, slot, span):
    for tile in range(0, words_ref.shape[1], 128):
        cols = slice(tile, tile + 128)
        for start in range(0, span, 48):
            counts_ref[count_row + start : count_row + start + 48, cols] = field(
                words_ref[word_row + start : word_row + start + 48, cols], slot
            )


def halo_kernel(
    fanout,
    first_group,
    skip,
    words_ref,
    grad_ref,
    near_ref,
    rows_ref,
    sums_ref,
    halo_ref,
    counts_ref,
    all_ref,
):
    span = counts_ref.shape[0] // (GROUPS - first_group)
    rows_ref[...] = grad_ref[...].T
    for group in range(first_group, GROUPS):
        word, slot = divmod(group, SLOTS)
        row = (group - first_group) * span
        spread_slot(words_ref, word * span, counts_ref, row, slot, span)
        added = dot(counts_ref[row : row + span, :], rows_ref[...])
        all_ref[row : row + span, :] = (added * (slot_scale(slot) / fanout)).astype(jnp.bfloat16)
    sums = all_ref[skip:, :]
    sums_ref[...] = sums
    halo_ref[...] = dot(sums, near_ref[...], TRANS_RIGHT).astype(jnp.bfloat16)


def halo_scatter(words, grad, weight_near, halo, fanout):
    units, nodes = grad.shape
    width = weight_near.shape[0]
    span = (nodes + halo) // GROUPS
    first_group = nodes // span
    skip = nodes - first_group * span
    height = (GROUPS - first_group) * span
    return pl.pallas_call(
        functools.partial(halo_kernel, fanout, first_group, skip),
        grid=(1,),
        in_specs=[whole(words.shape), whole(grad.shape), whole(weight_near.shape)],
        out_specs=[whole((nodes, units)), whole((halo, units)), whole((halo, width))],
        out_shape=[
            jax.ShapeDtypeStruct((nodes, units), jnp.bfloat16),
            jax.ShapeDtypeStruct((halo, units), jnp.bfloat16),
            jax.ShapeDtypeStruct((halo, width), jnp.bfloat16),
        ],
        scratch_shapes=[
            pltpu.VMEM((height, nodes), jnp.bfloat16),
            pltpu.VMEM((height, units), jnp.bfloat16),
        ],
        compiler_params=params(),
        name="halo_scatter",
    )(words, grad, weight_near)


def scatter_kernel(
    fanout,
    words_ref,
    grad_ref,
    rows_ref,
    far_ref,
    table_ref,
    far_table,
    self_ref,
    near_ref,
    state_ref,
    weight_ref,
    padded_ref,
    counts_ref,
    sums_ref,
):
    step = pl.program_id(0)
    units, nodes = grad_ref.shape
    width = table_ref.shape[0]
    span = words_ref.shape[0]
    part = span * SLOTS

    @pl.when(step == 0)
    def _():
        for k in range(padded_ref.shape[0]):
            start = k * part
            stop = min(start + part, nodes)
            padded_ref[k, :, : stop - start] = grad_ref[:, start:stop]
            if stop < start + part:
                padded_ref[k, :, stop - start :] = jnp.zeros(
                    (units, start + part - stop), jnp.bfloat16
                )
        weight_ref[:width, :] = jnp.zeros((width, units), jnp.float32)
        weight_ref[width:, :] = dot(far_table[...], far_ref[...])
        sums_ref[...] = jnp.zeros_like(sums_ref)

    pair = 2
    steps = -(-nodes // part)

    def add(slot):
        for one in range(slot, slot + pair):
            spread_slot(words_ref, 0, counts_ref, one * span, one, span)
        added = dot(counts_ref[slot * span : (slot + pair) * span, :], rows_ref[...])
        for one in range(slot, slot + pair):
            piece = added[(one - slot) * span : (one - slot + 1) * span, :]
            piece = (piece * (slot_scale(one) / fanout)).astype(jnp.bfloat16)
            sums_ref[one * span : (one + 1) * span, :] = piece

    beyond = nodes - (steps - 1) * part
    ending = -(-beyond // (pair * span)) * pair
    for slot in range(0, ending, pair):
        add(slot)
    if ending < SLOTS:

        @pl.when(step < steps - 1)
        def _():
            for slot in range(ending, SLOTS, pair):
                add(slot)

    if beyond < part:

        @pl.when(step == steps - 1)
        def _():
            sums_ref[beyond:, :] = jnp.zeros((part - beyond, units), jnp.bfloat16)

    sums = sums_ref[...]
    own_grad = padded_ref[step]
    state_ref[...] = dot(near_ref[...], sums, TRANS_RIGHT) + dot(self_ref[...], own_grad)
    weight_ref[:width, :] += dot(table_ref[...], own_grad, TRANS_RIGHT)
    weight_ref[width:, :] += dot(table_ref[...], sums)


def scatter_layer(words, grad, rows, far, table, weight_self, weight_near, fanout):
    units, nodes = grad.shape
    width, total = table.shape
    span = total // GROUPS
    part = total // WORDS
    steps = -(-nodes // part)
    far_table = table[:, nodes:]
    return pl.pallas_call(
        functools.partial(scatter_kernel, fanout),
        grid=(steps,),
        in_specs=[
            pl.BlockSpec((span, nodes), lambda i: (i, 0)),
            whole(grad.shape),
            whole(rows.shape),
            whole(far.shape),
            lanes(width, part),
            whole(far_table.shape),
            whole(weight_self.shape),
            whole(weight_near.shape),
        ],
        out_specs=[lanes(width, part), whole((2 * width, units))],
        out_shape=[
            jax.ShapeDtypeStruct((width, total), jnp.float32),
            jax.ShapeDtypeStruct((2 * width, units), jnp.float32),
        ],
        scratch_shapes=[
            pltpu.VMEM((steps, units, part), jnp.bfloat16),
            pltpu.VMEM((part, nodes), jnp.bfloat16),
            pltpu.VMEM((part, units), jnp.bfloat16),
        ],
        compiler_params=params(),
        name="scatter_layer",
    )(words, grad, rows, far, table, far_table, weight_self, weight_near)


def active_kernel(first, state_ref, preact_ref, returned_ref, send_ref, *refs):
    if first:
        own_block, mean_block, grad_ref, sums_ref, weight_ref = refs
    else:
        grad_ref, sums_ref = refs
    step = pl.program_id(0)
    block = state_ref.shape[1]
    node = lax.broadcasted_iota(jnp.int32, (1, block), 1) + step * block
    chosen = jnp.where(send_ref[...] == node, 1.0, 0.0).astype(jnp.bfloat16)
    upper = state_ref[...] + dot(returned_ref[...], chosen, TRANS_LEFT)
    preact = preact_ref[...]
    gate = jax.nn.sigmoid(preact)
    active = preact * gate
    norm = lax.rsqrt(jnp.sum(active * active, axis=0, keepdims=True) + 1e-06)
    along = jnp.sum(active * upper, axis=0, keepdims=True)
    inner = norm * upper - active * (norm * norm * norm * along)
    grad = (inner * (gate * (1.0 + preact * (1.0 - gate)))).astype(jnp.bfloat16)
    grad_ref[...] = grad

    @pl.when(step == 0)
    def _():
        sums_ref[...] = jnp.zeros_like(sums_ref)
        if first:
            weight_ref[...] = jnp.zeros_like(weight_ref)

    sums_ref[...] += jnp.sum(grad.astype(jnp.float32), axis=1, keepdims=True)
    if first:
        width = own_block.shape[0]
        weight_ref[0, :width, :] += dot(own_block[...], grad, TRANS_RIGHT)
        weight_ref[1] += dot(mean_block[...], grad, TRANS_RIGHT)


def active_layer(state_grad, preact, returned, send_col, own=None, mean=None):
    units, nodes = preact.shape
    first = own is not None
    in_specs = [
        lanes(units, BLOCK),
        lanes(units, BLOCK),
        whole(returned.shape),
        whole(send_col.shape),
    ]
    out_specs = [lanes(units, BLOCK), whole((units, 128))]
    out_shape = [
        jax.ShapeDtypeStruct((units, nodes), jnp.bfloat16),
        jax.ShapeDtypeStruct((units, 128), jnp.float32),
    ]
    operands = [state_grad, preact, returned, send_col]
    if first:
        padded = mean.shape[0]
        in_specs += [lanes(own.shape[0], BLOCK), lanes(padded, BLOCK)]
        out_specs.append(whole((2, padded, units)))
        out_shape.append(jax.ShapeDtypeStruct((2, padded, units), jnp.float32))
        operands += [own, mean]
    return pl.pallas_call(
        functools.partial(active_kernel, first),
        grid=(nodes // BLOCK,),
        in_specs=in_specs,
        out_specs=out_specs,
        out_shape=out_shape,
        compiler_params=params(),
        name="active_layer",
    )(*operands)


def product(left, right):
    return jnp.dot(left, right, precision=lax.Precision.HIGHEST, preferred_element_type=jnp.float32)


def exchange(rows):
    return lax.all_to_all(rows, axes, split_axis=0, concat_axis=0, tiled=True)


def pad_count(rows, parts):
    return jnp.pad(rows, ((0, -rows.shape[0] % parts), (0, 0)))


def pad_rows(flat, width):
    return jnp.pad(flat, (0, -flat.size % width)).reshape(-1, width)


def in_terms(values):
    terms = []
    for _ in range(3):
        term = lax.reduce_precision(values, 8, 7)
        terms.append(term)
        values = values - term
    return jnp.stack(terms).astype(jnp.bfloat16)


def rotate_adam(weight, grad, first, second, left_basis, right_basis, rate):
    turned = product(product(left_basis.T, grad), right_basis)
    first = beta_one * first + (1.0 - beta_one) * turned
    second = beta_two * second + (1.0 - beta_two) * turned * turned
    update = first / (1.0 - beta_one**STEP) / (jnp.sqrt(second / (1.0 - beta_two**STEP)) + epsilon)
    return (weight - rate * product(product(left_basis, update), right_basis.T), first, second)


def on_device(
    features,
    labels,
    seed_rows,
    seed_mask,
    send_rows,
    neighbors_one,
    neighbors_two,
    neighbors_three,
    weight_one,
    weight_two,
    weight_three,
    left_one,
    right_one,
    left_two,
    right_two,
    left_three,
    right_three,
    first_one,
    first_two,
    first_three,
    second_one,
    second_two,
    second_three,
    bias_all,
    bias_first,
    bias_second,
):
    nodes, width = features.shape
    units = weight_one.shape[1]
    classes = weight_three.shape[1]
    halo = send_rows.size
    table = nodes + halo
    span = table // GROUPS
    low = jnp.bfloat16
    fans = (neighbors_one.shape[1], neighbors_two.shape[1], neighbors_three.shape[1])
    near = (neighbors_one.T, neighbors_two.T, neighbors_three.T)
    feats = features.T
    slot_of = (jnp.arange(table, dtype=jnp.int32) // span) % SLOTS
    scale = jnp.where(slot_of == SLOTS - 1, 1.0, 0.0)
    for slot in range(SLOTS - 1):
        scale = jnp.where(slot_of == slot, slot_scale(slot), scale)
    scale = scale.astype(jnp.float32)[None, :]
    send_col = send_rows.reshape(halo, 1)

    mesh_sizes = (lax.axis_size(axes[0]), lax.axis_size(axes[1]))
    sent_one = jnp.pad(features[send_rows.reshape(-1)], ((0, 0), (0, -width % 128)))
    words_one, got_one = count_words(near[0], sent_one, mesh_sizes, 0)
    padded_classes = -(-classes // 16) * 16
    more = padded_classes - classes
    seed_float = seed_mask.astype(jnp.float32)

    padded = -(-width // 16) * 16
    self_one = weight_one[:width].T.astype(low)
    near_one = jnp.pad(weight_one[width:].T, ((0, 0), (0, padded - width))).astype(low)
    self_two = weight_two[:units].astype(low)
    near_two = weight_two[units:].astype(low)
    wide_three = jnp.pad(weight_three, ((0, 0), (0, more))).astype(low)
    self_three = wide_three[:units]
    near_three = wide_three[units:]
    bias_three = jnp.pad(bias_all[2 * units :], (0, more), constant_values=-1e30)

    state_one, preact_one, sent_two, mean_one = hidden_layer(
        words_one,
        feats,
        got_one,
        scale,
        self_one,
        near_one,
        bias_all[:units].reshape(-1, 1),
        send_col,
        fans[0],
    )
    words_two, got_two = count_words(near[1], sent_two, mesh_sizes, 1)
    state_two, preact_two, sent_three, table_two = hidden_layer(
        words_two,
        state_one,
        got_two,
        scale,
        self_two.T,
        near_two.T,
        bias_all[units : 2 * units].reshape(-1, 1),
        send_col,
        fans[1],
    )
    words_three, got_three = count_words(near[2], sent_three, mesh_sizes, 2)
    seeds = seed_counts(
        seed_rows.reshape(-1, 1),
        labels.reshape(1, -1),
        seed_mask.reshape(1, -1),
        nodes,
        padded_classes,
    )
    grad_three, sums_three, table_three = last_layer(
        words_three,
        state_two,
        got_three,
        scale,
        self_three.T,
        near_three.T,
        bias_three.reshape(-1, 1),
        seeds,
        fans[2],
    )
    rows, far, halo_grad = halo_scatter(words_three, grad_three, near_three, halo, fans[2])
    returned = exchange(halo_grad)
    state_grad, weight_grad_three = scatter_layer(
        words_three, grad_three, rows, far, table_three, self_three, near_three, fans[2]
    )
    grad_two, sums_two = active_layer(state_grad, preact_two, returned, send_col)
    rows, far, halo_grad = halo_scatter(words_two, grad_two, near_two, halo, fans[1])
    returned = exchange(halo_grad)
    state_grad, weight_grad_two = scatter_layer(
        words_two, grad_two, rows, far, table_two, self_two, near_two, fans[1]
    )
    parts = lax.axis_size(axes)
    early = jnp.concatenate([weight_grad_two, weight_grad_three], axis=1).astype(low)
    early = early.reshape(parts, -1, early.shape[1])
    early_sum = jnp.sum(exchange(early).astype(jnp.float32), axis=0).astype(low)
    _, sums_one, weight_grad_one = active_layer(
        state_grad, preact_one, returned, send_col, feats, mean_one
    )
    bias_parts = jnp.concatenate([sums_one[:, 0], sums_two[:, 0], sums_three[:classes, 0]])
    scalars = jnp.stack([sums_three[padded_classes, 0], jnp.sum(seed_float)])
    late_rows = jnp.concatenate([weight_grad_one.reshape(-1, units), pad_rows(bias_parts, units)])
    late_rows = pad_count(late_rows, parts).astype(low).reshape(parts, -1)
    early_width = early_sum.size
    late_width = late_rows.shape[1]
    mixed = jnp.concatenate(
        [
            jnp.broadcast_to(early_sum.reshape(1, -1), (parts, early_width)),
            late_rows,
            jnp.broadcast_to(in_terms(scalars).reshape(1, -1), (parts, 6)),
        ],
        axis=1,
    )
    mixed = exchange(mixed)
    early_all = mixed[:, :early_width].reshape(2 * units, -1).astype(jnp.float32)
    late_sum = jnp.sum(
        mixed[:, early_width : early_width + late_width].astype(jnp.float32), axis=0
    ).astype(low)
    terms = mixed[:, early_width + late_width :].astype(jnp.float32)
    loss_sum, seed_total = jnp.sum(terms.reshape(parts, 3, 2), axis=(0, 1))
    late_all = exchange(jnp.broadcast_to(late_sum[None], (parts, late_width)))
    late_all = late_all.reshape(-1, units).astype(jnp.float32)
    share = 1.0 / seed_total
    out_two = rotate_adam(
        weight_two,
        early_all[:, :units] * share,
        first_two,
        second_two,
        left_two,
        right_two,
        step_rates[1],
    )
    out_three = rotate_adam(
        weight_three,
        early_all[:, units : units + classes] * share,
        first_three,
        second_three,
        left_three,
        right_three,
        step_rates[2],
    )
    sum_one = jnp.concatenate([late_all[:width], late_all[padded : padded + width]])
    out_one = rotate_adam(
        weight_one, sum_one * share, first_one, second_one, left_one, right_one, step_rates[0]
    )
    bias_grad = late_all[2 * padded :].reshape(-1)[: bias_all.size] * share
    bias_m = beta_one * bias_first + (1.0 - beta_one) * bias_grad
    bias_v = beta_two * bias_second + (1.0 - beta_two) * bias_grad * bias_grad
    bias_update = (
        bias_m / (1.0 - beta_one**STEP) / (jnp.sqrt(bias_v / (1.0 - beta_two**STEP)) + epsilon)
    )
    new_bias = bias_all - bias_rate * (bias_update + weight_decay * bias_all)
    return (*out_one, *out_two, *out_three, new_bias, bias_m, bias_v, loss_sum, seed_total)


def solution(mesh):
    split = P(axes)
    rows = P(axes, None)
    placed = (rows, split, split, split, rows, rows, rows, rows) + (P(),) * 18
    return jax.shard_map(
        on_device,
        mesh=mesh,
        in_specs=placed,
        out_specs=(P(),) * 14,
        check_vma=False,
    )
```

```python
import functools

import jax
import jax.numpy as jnp
from jax import lax
from jax.experimental import pallas as pl
from jax.experimental.pallas import tpu as pltpu
from jax.sharding import PartitionSpec as P

STEP = 10


beta_one = 0.9
beta_two = 0.999
epsilon = 1e-08
step_rates = (0.05, 0.5, 1.0)
bias_rate = 0.05
weight_decay = 0.01

axes = ("dom", "rep")
WORDS = 4
SLOTS = 8
GROUPS = WORDS * SLOTS
BLOCK = 512
VMEM_BYTES = 56 * 1024 * 1024
TRANS_LEFT = (((0,), (0,)), ((), ()))
TRANS_RIGHT = (((1,), (1,)), ((), ()))


def dot(left, right, dims=(((1,), (0,)), ((), ()))):
    return lax.dot_general(left, right, dims, preferred_element_type=jnp.float32)


def params(collective=None):
    remote = {} if collective is None else dict(collective_id=collective, has_side_effects=True)
    return pltpu.CompilerParams(
        dimension_semantics=("arbitrary",), vmem_limit_bytes=VMEM_BYTES, **remote
    )


def whole(shape):
    return pl.BlockSpec(shape, lambda i: (0,) * len(shape))


def lanes(rows, width):
    return pl.BlockSpec((rows, width), lambda i: (0, i))


def words_layer(near_ref, out_ref, place_ref, field_ref):
    fanout, block = near_ref.shape
    span = out_ref.shape[0] // WORDS
    near = near_ref[...]
    group = ((near.astype(jnp.float32) + 0.5) * (1.0 / span)).astype(jnp.int32)
    place = near - group * span
    word = group >> 3
    bit = jnp.left_shift(jnp.int32(1), (group & 7) * 4)
    parts = [jnp.where(word == k, bit, 0) for k in range(WORDS)]
    totals = [jnp.zeros_like(bit) for _ in range(WORDS)]
    for g in range(fanout):
        same = place == place[g : g + 1]
        for k in range(WORDS):
            totals[k] = totals[k] + jnp.where(same, parts[k][g : g + 1], 0)
    place_ref[:fanout, :] = place
    for k in range(WORDS):
        field_ref[k, :fanout, :] = totals[k]
    chunk = 48
    for tile in range(0, block, 128):
        cols = slice(tile, tile + 128)
        for start in range(0, span, chunk):
            rows = lax.broadcasted_iota(jnp.int32, (chunk, 128), 0) + start
            sums = [jnp.zeros((chunk, 128), jnp.int32) for _ in range(WORDS)]
            for g in range(fanout):
                hit = rows == place_ref[g : g + 1, cols]
                for k in range(WORDS):
                    sums[k] = jnp.where(hit, field_ref[k, g : g + 1, cols], sums[k])
            for k in range(WORDS):
                out_ref[k * span + start : k * span + start + chunk, cols] = sums[k]


def ring(mesh_sizes):
    across, along = mesh_sizes
    parts = across * along
    me = lax.axis_index(axes[0]) * along + lax.axis_index(axes[1])

    def peer(ahead):
        index = lax.rem(me + ahead, parts)
        return index, (index // along, lax.rem(index, along))

    return parts, me, peer


def greet(mesh_sizes):
    parts, _, peer = ring(mesh_sizes)
    barrier = pltpu.get_barrier_semaphore()

    def tell(ahead, carry):
        pl.semaphore_signal(
            barrier, inc=1, device_id=peer(ahead)[1], device_id_type=pl.DeviceIdType.MESH
        )
        return carry

    lax.fori_loop(1, parts, tell, 0)


def all_greeted(mesh_sizes):
    pl.semaphore_wait(pltpu.get_barrier_semaphore(), ring(mesh_sizes)[0] - 1)


def block_copy(mesh_sizes, out_ref, in_ref, send_sem, recv_sem, ahead):
    _, me, peer = ring(mesh_sizes)
    index, where = peer(ahead)
    return pltpu.make_async_remote_copy(
        src_ref=out_ref.at[index],
        dst_ref=in_ref.at[me],
        send_sem=send_sem.at[index],
        recv_sem=recv_sem.at[me],
        device_id=where,
        device_id_type=pl.DeviceIdType.MESH,
    )


def send_blocks(mesh_sizes, out_ref, in_ref, send_sem, recv_sem):
    parts = ring(mesh_sizes)[0]

    def send(ahead, carry):
        block_copy(mesh_sizes, out_ref, in_ref, send_sem, recv_sem, ahead).start()
        return carry

    lax.fori_loop(1, parts, send, 0)


def wait_blocks(mesh_sizes, out_ref, in_ref, send_sem, recv_sem):
    parts, me, peer = ring(mesh_sizes)

    def wait(ahead, carry):
        block_copy(mesh_sizes, out_ref, in_ref, send_sem, recv_sem, ahead).wait_send()
        index, where = peer(ahead)
        pltpu.make_async_remote_copy(
            src_ref=out_ref.at[index],
            dst_ref=in_ref.at[index],
            send_sem=send_sem.at[index],
            recv_sem=recv_sem.at[index],
            device_id=where,
            device_id_type=pl.DeviceIdType.MESH,
        ).wait_recv()
        return carry

    lax.fori_loop(1, parts, wait, 0)


def send_all(mesh_sizes, own_ref, in_ref, send_sem, recv_sem):
    parts, me, peer = ring(mesh_sizes)

    def send(ahead, carry):
        index, where = peer(ahead)
        pltpu.make_async_remote_copy(
            src_ref=own_ref,
            dst_ref=in_ref.at[me],
            send_sem=send_sem.at[index],
            recv_sem=recv_sem.at[me],
            device_id=where,
            device_id_type=pl.DeviceIdType.MESH,
        ).start()
        return carry

    lax.fori_loop(1, parts, send, 0)


def wait_all(mesh_sizes, own_ref, in_ref, send_sem, recv_sem):
    parts, _, peer = ring(mesh_sizes)

    def wait(ahead, carry):
        index, where = peer(ahead)
        copy = pltpu.make_async_remote_copy(
            src_ref=own_ref,
            dst_ref=in_ref.at[index],
            send_sem=send_sem.at[index],
            recv_sem=recv_sem.at[index],
            device_id=where,
            device_id_type=pl.DeviceIdType.MESH,
        )
        copy.wait_send()
        copy.wait_recv()
        return carry

    lax.fori_loop(1, parts, wait, 0)


def semaphores(parts):
    return [pltpu.SemaphoreType.DMA((parts,)), pltpu.SemaphoreType.DMA((parts,))]


def chosen_nodes(send_row, start, count):
    node = lax.broadcasted_iota(jnp.int32, (count, send_row.shape[1]), 0) + start
    return jnp.where(node == send_row, 1.0, 0.0).astype(jnp.bfloat16)


def words_kernel(mesh_sizes, kind, near_ref, *refs):
    refs = list(refs)
    if kind == "features":
        feats_ref, send_ref, out_ref, got_ref, sent_ref = refs[:5]
        refs = refs[5:]
    elif kind == "seeds":
        sent_ref, slots_ref, labels_ref, mask_ref, out_ref, got_ref, seeds_ref = refs[:7]
        refs = refs[7:]
    else:
        sent_ref, out_ref, got_ref = refs[:3]
        refs = refs[3:]
    place_ref, field_ref, land_ref, send_sem, recv_sem = refs
    step = pl.program_id(0)
    block = near_ref.shape[1]
    moves = (mesh_sizes, sent_ref, land_ref, send_sem, recv_sem)

    @pl.when(step == 0)
    def _():
        greet(mesh_sizes)

    if kind == "features":

        @pl.when(step == 0)
        def _():
            width, nodes = feats_ref.shape
            halo = send_ref.shape[1]
            total = jnp.zeros((width, halo), jnp.float32)
            for start in range(0, nodes, block):
                chosen = chosen_nodes(send_ref[...], start, block)
                total = total + dot(feats_ref[:, start : start + block], chosen)
            padded = sent_ref.shape[2]
            total = jnp.concatenate([total, jnp.zeros((padded - width, halo), jnp.float32)])
            sent_ref[...] = total.T.astype(jnp.bfloat16).reshape(sent_ref.shape)

    words_layer(near_ref, out_ref, place_ref, field_ref)

    @pl.when(step == 0)
    def _():
        all_greeted(mesh_sizes)
        send_blocks(*moves)

    if kind == "seeds":
        classes = seeds_ref.shape[0]
        slots = slots_ref.shape[1]
        label = lax.broadcasted_iota(jnp.int32, (classes, slots), 0)
        marked = jnp.where((label == labels_ref[...]) & (mask_ref[...] != 0), 1.0, 0.0)
        chosen = chosen_nodes(slots_ref[...], step * block, block)
        seeds_ref[...] = dot(marked.astype(jnp.bfloat16), chosen, TRANS_RIGHT)

    @pl.when(step == pl.num_programs(0) - 1)
    def _():
        me = ring(mesh_sizes)[1]
        wait_blocks(*moves)
        land_ref[me] = sent_ref[me]
        got_ref[...] = land_ref[...]


def count_words(near, mesh_sizes, collective, halo, sent=None, feats=None, send_row=None, seeds=None):
    fanout, nodes = near.shape
    parts = mesh_sizes[0] * mesh_sizes[1]
    height = (nodes + halo) // SLOTS
    in_specs = [lanes(fanout, BLOCK)]
    operands = [near]
    scratch = []
    if sent is None:
        kind = "features"
        blocks = (parts, halo // parts, -(-feats.shape[0] // 128) * 128)
        in_specs += [whole(feats.shape), whole(send_row.shape)]
        operands += [feats, send_row]
        scratch.append(pltpu.VMEM(blocks, jnp.bfloat16))
    else:
        kind = "plain"
        blocks = (parts, halo // parts, sent.shape[1])
        in_specs.append(whole(blocks))
        operands.append(sent.reshape(blocks))
    out_specs = [lanes(height, BLOCK), whole(blocks)]
    out_shape = [
        jax.ShapeDtypeStruct((height, nodes), jnp.int32),
        jax.ShapeDtypeStruct(blocks, jnp.bfloat16),
    ]
    if seeds is not None:
        kind = "seeds"
        classes, slots, labels, mask = seeds
        in_specs += [whole(slots.shape)] * 3
        operands += [slots, labels, mask]
        out_specs.append(lanes(classes, BLOCK))
        out_shape.append(jax.ShapeDtypeStruct((classes, nodes), jnp.float32))
    return pl.pallas_call(
        functools.partial(words_kernel, mesh_sizes, kind),
        grid=(nodes // BLOCK,),
        in_specs=in_specs,
        out_specs=out_specs,
        out_shape=out_shape,
        scratch_shapes=scratch
        + [
            pltpu.VMEM((16, BLOCK), jnp.int32),
            pltpu.VMEM((WORDS, 16, BLOCK), jnp.int32),
            pltpu.VMEM(blocks, jnp.bfloat16),
        ]
        + semaphores(parts),
        compiler_params=params(collective),
        name="count_words",
    )(*operands)


def field(words, slot):
    if slot == SLOTS - 1:
        picked = lax.shift_right_logical(words, 4 * slot)
    else:
        picked = words & (15 << (4 * slot))
    return picked.astype(jnp.float32).astype(jnp.bfloat16)


def slot_scale(slot):
    return 1.0 if slot == SLOTS - 1 else 2.0 ** (-4 * slot)


def spread_counts(words_ref, counts_ref, group, span):
    word, slot = divmod(group, SLOTS)
    width = words_ref.shape[1]
    for tile in range(0, width, 128):
        cols = slice(tile, tile + 128)
        for start in range(0, span, 48):
            counts_ref[group * span + start : group * span + start + 48, cols] = field(
                words_ref[word * span + start : word * span + start + 48, cols], slot
            )


def gather_product(table_ref, words_ref, counts_ref):
    table = table_ref.shape[1]
    span = table // GROUPS
    total = None
    done = 0
    step = 512
    for group in range(GROUPS):
        spread_counts(words_ref, counts_ref, group, span)
        ready = (group + 1) * span
        while ready - done >= step or (group == GROUPS - 1 and done < table):
            stop = min(done + step, table)
            term = dot(table_ref[:, done:stop], counts_ref[done:stop, :])
            total = term if total is None else total + term
            done = stop
    return total


def scale_row(table):
    column = lax.broadcasted_iota(jnp.int32, (1, table), 1)
    group = ((column.astype(jnp.float32) + 0.5) * (GROUPS / table)).astype(jnp.int32)
    slot = group & (SLOTS - 1)
    scale = jnp.ones((1, table), jnp.float32)
    for k in range(SLOTS - 1):
        scale = jnp.where(slot == k, slot_scale(k), scale)
    return scale


def column_of(row):
    return jnp.broadcast_to(row, (128, row.shape[1])).T


def late(rows, width):
    return pl.BlockSpec((rows, width), lambda i: (0, jnp.maximum(i - 1, 0)))


def now(rows, width, steps):
    return pl.BlockSpec((rows, width), lambda i: (0, jnp.minimum(i, steps - 1)))


def hidden_kernel(
    fanout,
    bias_start,
    words_ref,
    own_ref,
    own_block,
    got_ref,
    weight_ref,
    bias_ref,
    send_ref,
    state_ref,
    preact_ref,
    sent_ref,
    extra_ref,
    table_ref,
    counts_ref,
    picked_ref,
    mean_ref,
    self_ref,
    near_ref,
    bias_col,
):
    step = pl.program_id(0)
    last = pl.num_programs(0) - 1
    width, nodes = own_ref.shape
    units, block = state_ref.shape
    padded = mean_ref.shape[0]

    @pl.when(step == 0)
    def _():
        if table_ref.shape[0] > width:
            table_ref[...] = jnp.zeros_like(table_ref)
        got = got_ref[...].reshape(-1, got_ref.shape[2]).T[:width]
        scale = scale_row(table_ref.shape[1])
        own = own_ref[...].astype(jnp.float32) * scale[:, :nodes]
        table_ref[:width, :nodes] = own.astype(jnp.bfloat16)
        far = got.astype(jnp.float32) * scale[:, nodes:]
        table_ref[:width, nodes:] = far.astype(jnp.bfloat16)
        if width == units:
            extra_ref[:, :nodes] = own_ref[...]
            extra_ref[:, nodes:] = got
        mean_ref[...] = jnp.zeros_like(mean_ref)
        picked_ref[...] = jnp.zeros_like(picked_ref)
        self_ref[...] = weight_ref[:width, :].T.astype(jnp.bfloat16)
        if padded > width:
            near_ref[...] = jnp.zeros_like(near_ref)
        near_ref[:, :width] = weight_ref[width:, :].T.astype(jnp.bfloat16)
        bias_col[...] = column_of(bias_ref[:, bias_start : bias_start + units])

    def finish():
        mean = mean_ref[...]
        if width != units:
            extra_ref[...] = mean
        preact = dot(self_ref[...], own_block[...]) + dot(near_ref[...], mean) + bias_col[:, :1]
        preact_ref[...] = preact
        active = preact * jax.nn.sigmoid(preact)
        norm = lax.rsqrt(jnp.sum(active * active, axis=0, keepdims=True) + 1e-06)
        state = (active * norm).astype(jnp.bfloat16)
        state_ref[...] = state
        picked_ref[...] += dot(state, chosen_nodes(send_ref[...], (step - 1) * block, block))

    @pl.when(step < last)
    def _():
        finish()
        total = gather_product(table_ref, words_ref, counts_ref)
        mean_ref[...] = (total[:padded] / fanout).astype(jnp.bfloat16)

    @pl.when(step == last)
    def _():
        finish()
        sent_ref[...] = picked_ref[...].T.astype(jnp.bfloat16)


def hidden_layer(words, own, got, weight, bias_row, bias_start, send_row, fanout):
    width, nodes = own.shape
    halo = send_row.shape[1]
    table = nodes + halo
    units = weight.shape[1]
    padded = -(-width // 16) * 16
    tall = max(padded, 3 * units // 4)
    steps = nodes // BLOCK
    if width == units:
        extra_shape, extra_spec = (units, table), whole((units, table))
    else:
        extra_shape, extra_spec = (padded, nodes), late(padded, BLOCK)
    return pl.pallas_call(
        functools.partial(hidden_kernel, fanout, bias_start),
        grid=(steps + 1,),
        in_specs=[
            now(words.shape[0], BLOCK, steps),
            whole(own.shape),
            late(width, BLOCK),
            whole(got.shape),
            whole(weight.shape),
            whole(bias_row.shape),
            whole(send_row.shape),
        ],
        out_specs=[
            late(units, BLOCK),
            late(units, BLOCK),
            whole((halo, units)),
            extra_spec,
        ],
        out_shape=[
            jax.ShapeDtypeStruct((units, nodes), jnp.bfloat16),
            jax.ShapeDtypeStruct((units, nodes), jnp.float32),
            jax.ShapeDtypeStruct((halo, units), jnp.bfloat16),
            jax.ShapeDtypeStruct(extra_shape, jnp.bfloat16),
        ],
        scratch_shapes=[
            pltpu.VMEM((tall, table), jnp.bfloat16),
            pltpu.VMEM((table, BLOCK), jnp.bfloat16),
            pltpu.VMEM((units, halo), jnp.float32),
            pltpu.VMEM((padded, BLOCK), jnp.bfloat16),
            pltpu.VMEM((units, width), jnp.bfloat16),
            pltpu.VMEM((units, padded), jnp.bfloat16),
            pltpu.VMEM((units, 128), jnp.float32),
        ],
        compiler_params=params(),
        name="hidden_layer",
    )(words, own, own, got, weight, bias_row, send_row)


def far_groups(nodes, halo):
    span = (nodes + halo) // GROUPS
    first = nodes // span
    return span, first, nodes - first * span


def far_finish(fanout, nodes, far_sums, far_ref, halo_ref, near_right):
    halo = far_ref.shape[0]
    span, first, skip = far_groups(nodes, halo)
    pieces = []
    for group in range(first, GROUPS):
        row = (group - first) * span
        pieces.append(far_sums[row : row + span, :] * (slot_scale(group % SLOTS) / fanout))
    sums = jnp.concatenate(pieces).astype(jnp.bfloat16)[skip:]
    far_ref[...] = sums
    halo_ref[...] = dot(sums, near_right).astype(jnp.bfloat16)


def last_kernel(
    fanout,
    bias_start,
    words_ref,
    own_ref,
    own_block,
    got_ref,
    weight_ref,
    bias_ref,
    seeds_ref,
    grad_ref,
    rows_ref,
    sums_ref,
    notes_ref,
    table_out,
    far_ref,
    halo_ref,
    reduced_ref,
    counts_ref,
    both_ref,
    self_ref,
    near_ref,
    bias_col,
    far_sums,
):
    step = pl.program_id(0)
    last = pl.num_programs(0) - 1
    classes = self_ref.shape[0]
    width, nodes = own_ref.shape
    kinds = weight_ref.shape[0]
    halo = far_ref.shape[0]
    span, first, skip = far_groups(nodes, halo)

    @pl.when(step == 0)
    def _():
        table_out[:, :nodes] = own_ref[...]
        table_out[:, nodes:] = got_ref[...].reshape(halo, width).T
        more = jnp.zeros((classes - kinds, 2 * width), jnp.float32)
        weight = jnp.concatenate([weight_ref[...], more]).astype(jnp.bfloat16)
        self_ref[...] = weight[:, :width]
        near_ref[...] = weight[:, width:]
        rest = jnp.full((1, classes - kinds), -1e30, jnp.float32)
        bias_col[...] = column_of(
            jnp.concatenate([bias_ref[:, bias_start : bias_start + kinds], rest], axis=1)
        )
        reduced = dot(near_ref[...], table_out[...]) * scale_row(table_out.shape[1])
        high = reduced.astype(jnp.bfloat16)
        reduced_ref[:classes, :] = high
        reduced_ref[classes:, :] = (reduced - high.astype(jnp.float32)).astype(jnp.bfloat16)
        both_ref[...] = jnp.zeros_like(both_ref)
        counts_ref[first * span :, :] = jnp.zeros_like(counts_ref[first * span :, :])

    @pl.when(step <= 1)
    def _():
        sums_ref[...] = jnp.zeros_like(sums_ref)
        notes_ref[...] = jnp.zeros_like(notes_ref)
        far_sums[...] = jnp.zeros_like(far_sums)

    def finish():
        near_part = (both_ref[:classes, :] + both_ref[classes:, :]) / fanout
        logits = dot(self_ref[...], own_block[...]) + near_part + bias_col[:, :1]
        top = jnp.max(logits, axis=0, keepdims=True)
        powers = jnp.exp(logits - top)
        total = jnp.sum(powers, axis=0, keepdims=True)
        normer = jnp.log(total) + top
        seeds = seeds_ref[...]
        uses = jnp.sum(seeds, axis=0, keepdims=True)
        grad = (powers / total * uses - seeds).astype(jnp.bfloat16)
        grad_ref[...] = grad
        loss = uses * normer - jnp.sum(seeds * logits, axis=0, keepdims=True)
        sums_ref[...] += jnp.sum(grad.astype(jnp.float32), axis=1, keepdims=True)
        notes_ref[:8, :] += jnp.sum(loss)
        notes_ref[8:, :] += jnp.sum(uses)
        rows = grad.T
        rows_ref[...] = rows
        far_sums[...] += dot(counts_ref[first * span :, :], rows)

    @pl.when(step < last)
    def _():
        finish()
        both_ref[...] = gather_product(reduced_ref, words_ref, counts_ref)

    @pl.when(step == last)
    def _():
        finish()
        far_finish(fanout, nodes, far_sums, far_ref, halo_ref, near_ref[...])


def last_layer(words, own, got, weight, bias_row, bias_start, seeds, fanout):
    width, nodes = own.shape
    halo = got.shape[0] * got.shape[1]
    table = nodes + halo
    classes = seeds.shape[0]
    steps = nodes // BLOCK
    span, first, _ = far_groups(nodes, halo)
    far_height = (GROUPS - first) * span
    return pl.pallas_call(
        functools.partial(last_kernel, fanout, bias_start),
        grid=(steps + 1,),
        in_specs=[
            now(words.shape[0], BLOCK, steps),
            whole(own.shape),
            late(width, BLOCK),
            whole(got.shape),
            whole(weight.shape),
            whole(bias_row.shape),
            late(classes, BLOCK),
        ],
        out_specs=[
            late(classes, BLOCK),
            pl.BlockSpec((BLOCK, classes), lambda i: (jnp.maximum(i - 1, 0), 0)),
            whole((classes, 128)),
            whole((16, 128)),
            whole((width, table)),
            whole((halo, classes)),
            whole((halo, width)),
        ],
        out_shape=[
            jax.ShapeDtypeStruct((classes, nodes), jnp.bfloat16),
            jax.ShapeDtypeStruct((nodes, classes), jnp.bfloat16),
            jax.ShapeDtypeStruct((classes, 128), jnp.float32),
            jax.ShapeDtypeStruct((16, 128), jnp.float32),
            jax.ShapeDtypeStruct((width, table), jnp.bfloat16),
            jax.ShapeDtypeStruct((halo, classes), jnp.bfloat16),
            jax.ShapeDtypeStruct((halo, width), jnp.bfloat16),
        ],
        scratch_shapes=[
            pltpu.VMEM((2 * classes, table), jnp.bfloat16),
            pltpu.VMEM((table, BLOCK), jnp.bfloat16),
            pltpu.VMEM((2 * classes, BLOCK), jnp.float32),
            pltpu.VMEM((classes, width), jnp.bfloat16),
            pltpu.VMEM((classes, width), jnp.bfloat16),
            pltpu.VMEM((classes, 128), jnp.float32),
            pltpu.VMEM((far_height, classes), jnp.float32),
        ],
        compiler_params=params(),
        name="last_layer",
    )(words, own, own, got, weight, bias_row, seeds)


def spread_slot(words_ref, word_row, counts_ref, count_row, slot, span):
    for start in range(0, span, 48):
        for tile in range(0, words_ref.shape[1], 512):
            cols = slice(tile, tile + 512)
            counts_ref[count_row + start : count_row + start + 48, cols] = field(
                words_ref[word_row + start : word_row + start + 48, cols], slot
            )


def scatter_kernel(
    mesh_sizes,
    fanout,
    flipped,
    words_ref,
    grad_ref,
    rows_ref,
    far_ref,
    table_ref,
    far_table,
    weight_in,
    halo_ref,
    other_ref,
    state_ref,
    weight_ref,
    got_ref,
    *refs,
):
    if flipped:
        notes_ref, padded_ref, counts_ref, sums_ref, self_ref, near_ref, land_ref = refs[:7]
        send_sem, recv_sem, notes_land, notes_send, notes_recv = refs[7:]
        total_ref = weight_ref
    else:
        padded_ref, counts_ref, sums_ref, self_ref, near_ref, total_ref, land_ref = refs[:7]
        send_sem, recv_sem = refs[7:]
    step = pl.program_id(0)
    units, nodes = grad_ref.shape
    width = table_ref.shape[0]
    span = words_ref.shape[0]
    part = span * SLOTS
    steps = -(-nodes // part)
    moves = (mesh_sizes, halo_ref, land_ref, send_sem, recv_sem)

    @pl.when(step == 0)
    def _():
        greet(mesh_sizes)
        for k in range(steps):
            start = k * part
            stop = min(start + part, nodes)
            padded_ref[k, :, : stop - start] = grad_ref[:, start:stop]
            if stop < start + part:
                padded_ref[k, :, stop - start :] = jnp.zeros(
                    (units, start + part - stop), jnp.bfloat16
                )
        if flipped:
            weight = weight_in[...]
            more = jnp.zeros((units - weight.shape[0], 2 * width), jnp.float32)
            weight = jnp.concatenate([weight, more]).T
        else:
            weight = weight_in[...]
        self_ref[...] = weight[:width].astype(jnp.bfloat16)
        near_ref[...] = weight[width:].astype(jnp.bfloat16)
        total_ref[:width, :] = jnp.zeros((width, units), jnp.float32)
        total_ref[width:, :] = dot(far_table[...], far_ref[...])
        sums_ref[...] = jnp.zeros_like(sums_ref)

    pair = 2

    def add(slot):
        for one in range(slot, slot + pair):
            spread_slot(words_ref, 0, counts_ref, one * span, one, span)
        added = dot(counts_ref[slot * span : (slot + pair) * span, :], rows_ref[...])
        for one in range(slot, slot + pair):
            piece = added[(one - slot) * span : (one - slot + 1) * span, :]
            piece = (piece * (slot_scale(one) / fanout)).astype(jnp.bfloat16)
            sums_ref[one * span : (one + 1) * span, :] = piece

    beyond = nodes - (steps - 1) * part
    ending = -(-beyond // (pair * span)) * pair
    for slot in range(0, ending, pair):
        add(slot)
    if ending < SLOTS:

        @pl.when(step < steps - 1)
        def _():
            for slot in range(ending, SLOTS, pair):
                add(slot)

    if beyond < part:

        @pl.when(step == steps - 1)
        def _():
            sums_ref[beyond:, :] = jnp.zeros((part - beyond, units), jnp.bfloat16)

    sums = sums_ref[...]
    own_grad = padded_ref[step]
    state_ref[...] = dot(near_ref[...], sums, TRANS_RIGHT) + dot(self_ref[...], own_grad)
    total_ref[:width, :] += dot(table_ref[...], own_grad, TRANS_RIGHT)
    total_ref[width:, :] += dot(table_ref[...], sums)

    @pl.when(step == 0)
    def _():
        all_greeted(mesh_sizes)
        send_blocks(*moves)
        if flipped:
            send_all(mesh_sizes, other_ref, notes_land, notes_send, notes_recv)

    @pl.when(step == steps - 1)
    def _():
        me = ring(mesh_sizes)[1]
        wait_blocks(*moves)
        land_ref[me] = halo_ref[me]
        got_ref[...] = land_ref[...]
        if flipped:
            wait_all(mesh_sizes, other_ref, notes_land, notes_send, notes_recv)
            notes_land[me] = other_ref[...]
            notes_ref[...] = jnp.sum(notes_land[...], axis=0)
        else:
            weight_ref[:, :units] = total_ref[...].astype(jnp.bfloat16)
            weight_ref[:, units:] = jnp.zeros_like(weight_ref[:, units:])
            narrow = other_ref.shape[1]
            weight_ref[:, units : units + narrow] = other_ref[...].astype(jnp.bfloat16)


def scatter_layer(words, grad, rows, far, table, weight, halo_rows, other, mesh_sizes, collective, fanout):
    units, nodes = grad.shape
    width, total = table.shape
    parts = mesh_sizes[0] * mesh_sizes[1]
    flipped = weight.shape[1] == 2 * width
    span = total // GROUPS
    part = total // WORDS
    steps = -(-nodes // part)
    far_table = table[:, nodes:]
    blocks = (parts, halo_rows.shape[0] // parts, width)
    out_specs = [lanes(width, part)]
    out_shape = [jax.ShapeDtypeStruct((width, total), jnp.float32)]
    if flipped:
        sums_shape, sums_type = (2 * width, units), jnp.float32
    else:
        wide = units + -(-other.shape[1] // 128) * 128
        sums_shape, sums_type = (2 * width, wide), jnp.bfloat16
    out_specs += [whole(sums_shape), whole(blocks)]
    out_shape += [
        jax.ShapeDtypeStruct(sums_shape, sums_type),
        jax.ShapeDtypeStruct(blocks, jnp.bfloat16),
    ]
    scratch = [
        pltpu.VMEM((steps, units, part), jnp.bfloat16),
        pltpu.VMEM((part, nodes), jnp.bfloat16),
        pltpu.VMEM((part, units), jnp.bfloat16),
        pltpu.VMEM((width, units), jnp.bfloat16),
        pltpu.VMEM((width, units), jnp.bfloat16),
    ]
    if not flipped:
        scratch.append(pltpu.VMEM((2 * width, units), jnp.float32))
    scratch += [pltpu.VMEM(blocks, jnp.bfloat16)] + semaphores(parts)
    if flipped:
        out_specs.append(whole(other.shape))
        out_shape.append(jax.ShapeDtypeStruct(other.shape, other.dtype))
        scratch += [pltpu.VMEM((parts,) + other.shape, other.dtype)] + semaphores(parts)
    return pl.pallas_call(
        functools.partial(scatter_kernel, mesh_sizes, fanout, flipped),
        grid=(steps,),
        in_specs=[
            pl.BlockSpec((span, nodes), lambda i: (i, 0)),
            whole(grad.shape),
            whole(rows.shape),
            whole(far.shape),
            lanes(width, part),
            whole(far_table.shape),
            whole(weight.shape),
            whole(blocks),
            whole(other.shape),
        ],
        out_specs=out_specs,
        out_shape=out_shape,
        scratch_shapes=scratch,
        compiler_params=params(collective),
        name="scatter_layer",
    )(words, grad, rows, far, table, far_table, weight, halo_rows.reshape(blocks), other)


def active_grad(step, state_ref, preact_ref, back_ref, send_ref):
    block = state_ref.shape[1]
    chosen = chosen_nodes(send_ref[...], step * block, block)
    upper = state_ref[...] + dot(back_ref[...], chosen, TRANS_RIGHT)
    preact = preact_ref[...]
    gate = jax.nn.sigmoid(preact)
    active = preact * gate
    norm = lax.rsqrt(jnp.sum(active * active, axis=0, keepdims=True) + 1e-06)
    along = jnp.sum(active * upper, axis=0, keepdims=True)
    inner = norm * upper - active * (norm * norm * norm * along)
    return (inner * (gate * (1.0 + preact * (1.0 - gate)))).astype(jnp.bfloat16)


def middle_kernel(
    fanout,
    state_ref,
    preact_ref,
    returned_ref,
    send_ref,
    words_ref,
    weight_ref,
    grad_ref,
    rows_ref,
    sums_ref,
    far_ref,
    halo_ref,
    back_ref,
    counts_ref,
    far_sums,
):
    step = pl.program_id(0)
    units, block = state_ref.shape
    halo = far_ref.shape[0]
    nodes = block * pl.num_programs(0)
    span, first, skip = far_groups(nodes, halo)

    @pl.when(step == 0)
    def _():
        back_ref[...] = returned_ref[...].reshape(halo, units).T
        sums_ref[...] = jnp.zeros_like(sums_ref)
        far_sums[...] = jnp.zeros_like(far_sums)

    base = first // SLOTS * SLOTS
    for group in range(first, GROUPS):
        word = group // SLOTS - base // SLOTS
        spread_slot(
            words_ref, word * span, counts_ref, (group - first) * span, group % SLOTS, span
        )
    grad = active_grad(step, state_ref, preact_ref, back_ref, send_ref)
    grad_ref[...] = grad
    sums_ref[...] += jnp.sum(grad.astype(jnp.float32), axis=1, keepdims=True)
    rows = grad.T
    rows_ref[...] = rows
    far_sums[...] += dot(counts_ref[...], rows)

    @pl.when(step == pl.num_programs(0) - 1)
    def _():
        near = weight_ref[units:, :].T.astype(jnp.bfloat16)
        far_finish(fanout, nodes, far_sums, far_ref, halo_ref, near)


def middle_layer(state_grad, preact, returned, send_row, words, weight, fanout):
    units, nodes = preact.shape
    halo = send_row.shape[1]
    span, first, _ = far_groups(nodes, halo)
    far_words = WORDS - first // SLOTS
    far_height = (GROUPS - first) * span
    return pl.pallas_call(
        functools.partial(middle_kernel, fanout),
        grid=(nodes // BLOCK,),
        in_specs=[
            lanes(units, BLOCK),
            lanes(units, BLOCK),
            whole(returned.shape),
            whole(send_row.shape),
            pl.BlockSpec((far_words * span, BLOCK), lambda i: (WORDS // far_words - 1, i)),
            whole(weight.shape),
        ],
        out_specs=[
            lanes(units, BLOCK),
            pl.BlockSpec((BLOCK, units), lambda i: (i, 0)),
            whole((units, 128)),
            whole((halo, units)),
            whole((halo, units)),
        ],
        out_shape=[
            jax.ShapeDtypeStruct((units, nodes), jnp.bfloat16),
            jax.ShapeDtypeStruct((nodes, units), jnp.bfloat16),
            jax.ShapeDtypeStruct((units, 128), jnp.float32),
            jax.ShapeDtypeStruct((halo, units), jnp.bfloat16),
            jax.ShapeDtypeStruct((halo, units), jnp.bfloat16),
        ],
        scratch_shapes=[
            pltpu.VMEM((units, halo), jnp.bfloat16),
            pltpu.VMEM((far_height, BLOCK), jnp.bfloat16),
            pltpu.VMEM((far_height, units), jnp.float32),
        ],
        compiler_params=params(),
        name="middle_layer",
    )(state_grad, preact, returned, send_row, words, weight)


def bottom_kernel(
    mesh_sizes,
    state_ref,
    preact_ref,
    returned_ref,
    send_ref,
    own_block,
    mean_block,
    sums_two,
    sums_three,
    early_ref,
    late_ref,
    early_sum,
    back_ref,
    sums_ref,
    weight_ref,
    land_ref,
    send_sem,
    recv_sem,
):
    step = pl.program_id(0)
    units = state_ref.shape[0]
    halo = send_ref.shape[1]
    moves = (mesh_sizes, early_ref, land_ref, send_sem, recv_sem)

    @pl.when(step == 0)
    def _():
        greet(mesh_sizes)
        back_ref[...] = returned_ref[...].reshape(halo, units).T
        sums_ref[...] = jnp.zeros_like(sums_ref)
        weight_ref[...] = jnp.zeros_like(weight_ref)

    grad = active_grad(step, state_ref, preact_ref, back_ref, send_ref)
    sums_ref[...] += jnp.sum(grad.astype(jnp.float32), axis=1, keepdims=True)
    width = own_block.shape[0]
    weight_ref[0, :width, :] += dot(own_block[...], grad, TRANS_RIGHT)
    weight_ref[1] += dot(mean_block[...], grad, TRANS_RIGHT)

    @pl.when(step == 0)
    def _():
        all_greeted(mesh_sizes)
        send_blocks(*moves)

    @pl.when(step == pl.num_programs(0) - 1)
    def _():
        me = ring(mesh_sizes)[1]
        padded = weight_ref.shape[1]
        row = 0
        for start in range(0, units, 128):
            for half in range(2):
                late_ref[row : row + padded, :] = weight_ref[half, :, start : start + 128].astype(
                    jnp.bfloat16
                )
                row += padded
        pieces = []
        for sums in (sums_ref, sums_two, sums_three):
            flat = sums[...].T[:1]
            for start in range(0, flat.shape[1], 128):
                piece = flat[:, start : start + 128]
                pieces.append(piece)
        narrow = pieces[-1].shape[1]
        pieces[-1] = jnp.concatenate(
            [pieces[-1], jnp.zeros((1, 128 - narrow), jnp.float32)], axis=1
        )
        rest = late_ref.shape[0] - row
        pieces.append(jnp.zeros((rest - len(pieces), 128), jnp.float32))
        late_ref[row:, :] = jnp.concatenate(pieces).astype(jnp.bfloat16)
        wait_blocks(*moves)
        land_ref[me] = early_ref[me]
        early_sum[...] = jnp.sum(land_ref[...].astype(jnp.float32), axis=0).astype(jnp.bfloat16)


def bottom_layer(
    state_grad, preact, returned, send_row, own, mean, sums_two, sums_three, early, mesh_sizes, collective
):
    units, nodes = preact.shape
    width = own.shape[0]
    padded = mean.shape[0]
    halo = send_row.shape[1]
    parts = mesh_sizes[0] * mesh_sizes[1]
    rows = units // 128 * (2 * padded + 2) + -(-sums_three.shape[0] // 128)
    rows = -(-rows // 512) * 512
    rows = -(-rows // parts) * parts
    early_blocks = (parts, early.shape[0] // parts, early.shape[1])
    return pl.pallas_call(
        functools.partial(bottom_kernel, mesh_sizes),
        grid=(nodes // BLOCK,),
        in_specs=[
            lanes(units, BLOCK),
            lanes(units, BLOCK),
            whole(returned.shape),
            whole(send_row.shape),
            lanes(width, BLOCK),
            lanes(padded, BLOCK),
            whole(sums_two.shape),
            whole(sums_three.shape),
            whole(early_blocks),
        ],
        out_specs=[whole((rows, 128)), whole(early_blocks[1:])],
        out_shape=[
            jax.ShapeDtypeStruct((rows, 128), jnp.bfloat16),
            jax.ShapeDtypeStruct(early_blocks[1:], jnp.bfloat16),
        ],
        scratch_shapes=[
            pltpu.VMEM((units, halo), jnp.bfloat16),
            pltpu.VMEM((units, 128), jnp.float32),
            pltpu.VMEM((2, padded, units), jnp.float32),
            pltpu.VMEM(early_blocks, jnp.bfloat16),
        ]
        + semaphores(parts),
        compiler_params=params(collective),
        name="bottom_layer",
    )(
        state_grad,
        preact,
        returned,
        send_row,
        own,
        mean,
        sums_two,
        sums_three,
        early.reshape(early_blocks),
    )


def share_kernel(
    mesh_sizes,
    early_ref,
    late_ref,
    early_out,
    late_out,
    early_land,
    late_land,
    late_sum,
    late_all,
    early_send,
    early_recv,
    late_send,
    late_recv,
    last_send,
    last_recv,
):
    me = ring(mesh_sizes)[1]
    first = (mesh_sizes, late_ref, late_land, late_send, late_recv)
    second = (mesh_sizes, early_ref, early_land, early_send, early_recv)
    third = (mesh_sizes, late_sum, late_all, last_send, last_recv)
    greet(mesh_sizes)
    all_greeted(mesh_sizes)
    send_blocks(*first)
    send_all(*second)
    wait_blocks(*first)
    late_land[me] = late_ref[me]
    late_sum[...] = jnp.sum(late_land[...].astype(jnp.float32), axis=0).astype(jnp.bfloat16)
    send_all(*third)
    wait_all(*second)
    early_land[me] = early_ref[...]
    early_out[...] = early_land[...]
    wait_all(*third)
    late_all[me] = late_sum[...]
    late_out[...] = late_all[...]


def share_sums(early_sum, late_rows, mesh_sizes, collective):
    parts = mesh_sizes[0] * mesh_sizes[1]
    early = (parts,) + early_sum.shape
    late_shape = (parts, late_rows.shape[0] // parts, 128)
    vmem = pl.BlockSpec(memory_space=pltpu.VMEM)
    return pl.pallas_call(
        functools.partial(share_kernel, mesh_sizes),
        in_specs=[vmem, vmem],
        out_specs=[vmem, vmem],
        out_shape=[
            jax.ShapeDtypeStruct(early, jnp.bfloat16),
            jax.ShapeDtypeStruct(late_shape, jnp.bfloat16),
        ],
        scratch_shapes=[
            pltpu.VMEM(early, jnp.bfloat16),
            pltpu.VMEM(late_shape, jnp.bfloat16),
            pltpu.VMEM(late_shape[1:], jnp.bfloat16),
            pltpu.VMEM(late_shape, jnp.bfloat16),
        ]
        + semaphores(parts)
        + semaphores(parts)
        + semaphores(parts),
        compiler_params=pltpu.CompilerParams(
            vmem_limit_bytes=VMEM_BYTES, collective_id=collective, has_side_effects=True
        ),
        name="share_sums",
    )(early_sum, late_rows.reshape(late_shape))


def in_two(value):
    high = value.astype(jnp.bfloat16)
    return high, (value - high.astype(jnp.float32)).astype(jnp.bfloat16)


def product(left, right, dims=(((1,), (0,)), ((), ()))):
    if left.dtype == jnp.bfloat16:
        high, low = in_two(right)
        return dot(left, high, dims) + dot(left, low, dims)
    high, low = in_two(left)
    if right.dtype == jnp.bfloat16:
        return dot(high, right, dims) + dot(low, right, dims)
    right_high, right_low = in_two(right)
    return dot(high, right_high, dims) + (
        dot(high, right_low, dims) + dot(low, right_high, dims)
    )


def moments(turned, first, second):
    first = beta_one * first + (1.0 - beta_one) * turned
    second = beta_two * second + (1.0 - beta_two) * turned * turned
    update = first / (1.0 - beta_one**STEP) / (jnp.sqrt(second / (1.0 - beta_two**STEP)) + epsilon)
    return first, second, update


def adam_kernel(
    padded,
    early_ref,
    late_ref,
    notes_ref,
    weight_one,
    weight_two,
    weight_three,
    left_one,
    right_one,
    left_two,
    right_two,
    left_three,
    right_three,
    first_one,
    first_two,
    first_three,
    second_one,
    second_two,
    second_three,
    bias_ref,
    bias_first,
    bias_second,
    *outs,
):
    share = 1.0 / notes_ref[8:9, 0:1]
    units = weight_two.shape[1]
    width = weight_one.shape[0] // 2
    kinds = weight_three.shape[0]

    def step(grad, weight, first, second, left, right, rate, out):
        turned = product(product(left[...], grad, TRANS_LEFT), right[...]) * share
        new_first, new_second, update = moments(turned, first[...], second[...])
        out[1][...] = new_first
        out[2][...] = new_second
        moved = product(product(left[...], update), right[...], TRANS_RIGHT)
        out[0][...] = weight[...] - rate * moved

    step(
        early_ref[:, :units],
        weight_two,
        first_two,
        second_two,
        left_two,
        right_two,
        step_rates[1],
        outs[3:6],
    )
    grad = early_ref[:, units:].astype(jnp.float32).T[:kinds].astype(jnp.bfloat16)
    turned = product(right_three[...], product(grad, left_three[...])) * share
    new_first, new_second, update = moments(turned, first_three[...], second_three[...])
    outs[7][...] = new_first
    outs[8][...] = new_second
    moved = product(update, left_three[...], TRANS_RIGHT)
    moved = product(right_three[...], moved, TRANS_LEFT)
    outs[6][...] = weight_three[...] - step_rates[2] * moved

    late_rows = late_ref[...].astype(jnp.float32)
    columns = []
    for start in range(0, units, 128):
        row = start // 128 * 2 * padded
        columns.append(
            jnp.concatenate(
                [late_rows[row : row + width], late_rows[row + padded : row + padded + width]]
            )
        )
    step(
        jnp.concatenate(columns, axis=1).astype(jnp.bfloat16),
        weight_one,
        first_one,
        second_one,
        left_one,
        right_one,
        step_rates[0],
        outs[0:3],
    )
    row = units // 128 * 2 * padded
    pieces = []
    while len(pieces) * 128 < 2 * units + kinds:
        pieces.append(late_rows[row : row + 1])
        row += 1
    grad = jnp.concatenate(pieces, axis=1)[:, : 2 * units + kinds] * share
    new_first, new_second, update = moments(grad, bias_first[...], bias_second[...])
    bias = bias_ref[...]
    outs[9][...] = bias - bias_rate * (update + weight_decay * bias)
    outs[10][...] = new_first
    outs[11][...] = new_second


def adam(padded, early_all, late_all, notes, *state):
    vmem = pl.BlockSpec(memory_space=pltpu.VMEM)
    order = (0, 9, 12, 1, 10, 13, 2, 11, 14, 15, 16, 17)
    outs = [jax.ShapeDtypeStruct(state[at].shape, jnp.float32) for at in order]
    return pl.pallas_call(
        functools.partial(adam_kernel, padded),
        in_specs=[vmem] * (3 + len(state)),
        out_specs=[vmem] * len(outs),
        out_shape=outs,
        compiler_params=pltpu.CompilerParams(vmem_limit_bytes=VMEM_BYTES),
        name="adam",
    )(early_all, late_all, notes, *state)


def on_device(
    mesh_sizes,
    features,
    labels,
    seed_rows,
    seed_mask,
    send_rows,
    neighbors_one,
    neighbors_two,
    neighbors_three,
    weight_one,
    weight_two,
    weight_three,
    left_one,
    right_one,
    left_two,
    right_two,
    left_three,
    right_three,
    first_one,
    first_two,
    first_three,
    second_one,
    second_two,
    second_three,
    bias_all,
    bias_first,
    bias_second,
):
    units = weight_one.shape[1]
    classes = weight_three.shape[1]
    halo = send_rows.size
    fans = (neighbors_one.shape[1], neighbors_two.shape[1], neighbors_three.shape[1])
    feats = features.T
    send_row = send_rows.reshape(1, halo)
    bias_row = bias_all.reshape(1, -1)
    weight_three = weight_three.T
    padded_classes = -(-classes // 16) * 16
    seed_slots = (
        padded_classes,
        seed_rows.reshape(1, -1),
        labels.reshape(1, -1),
        seed_mask.reshape(1, -1),
    )

    words_one, got = count_words(
        neighbors_one.T, mesh_sizes, 0, halo, feats=feats, send_row=send_row
    )
    state_one, preact_one, sent, mean_one = hidden_layer(
        words_one, feats, got, weight_one, bias_row, 0, send_row, fans[0]
    )
    words_two, got = count_words(neighbors_two.T, mesh_sizes, 1, halo, sent=sent)
    state_two, preact_two, sent, table_two = hidden_layer(
        words_two, state_one, got, weight_two, bias_row, units, send_row, fans[1]
    )
    words_three, got, seeds = count_words(
        neighbors_three.T, mesh_sizes, 2, halo, sent=sent, seeds=seed_slots
    )
    grad_three, rows_three, sums_three, notes, table_three, far, halo_grad = last_layer(
        words_three, state_two, got, weight_three, bias_row, 2 * units, seeds, fans[2]
    )
    state_grad, weight_grad, returned, notes = scatter_layer(
        words_three,
        grad_three,
        rows_three,
        far,
        table_three,
        weight_three,
        halo_grad,
        notes,
        mesh_sizes,
        3,
        fans[2],
    )
    grad_two, rows_two, sums_two, far, halo_grad = middle_layer(
        state_grad, preact_two, returned, send_row, words_two, weight_two, fans[1]
    )
    state_grad, early, returned = scatter_layer(
        words_two,
        grad_two,
        rows_two,
        far,
        table_two,
        weight_two,
        halo_grad,
        weight_grad,
        mesh_sizes,
        4,
        fans[1],
    )
    late_rows, early_sum = bottom_layer(
        state_grad,
        preact_one,
        returned,
        send_row,
        feats,
        mean_one,
        sums_two,
        sums_three,
        early,
        mesh_sizes,
        5,
    )
    early_all, late_all = share_sums(early_sum, late_rows, mesh_sizes, 6)
    out = adam(
        mean_one.shape[0],
        early_all.reshape(early.shape),
        late_all.reshape(late_rows.shape),
        notes,
        weight_one,
        weight_two,
        weight_three,
        left_one,
        right_one,
        left_two,
        right_two,
        left_three,
        right_three.T,
        first_one,
        first_two,
        first_three.T,
        second_one,
        second_two,
        second_three.T,
        bias_row,
        bias_first.reshape(1, -1),
        bias_second.reshape(1, -1),
    )
    biases = [value.reshape(-1) for value in out[9:12]]
    third = [value.T for value in out[6:9]]
    return (*out[:6], *third, *biases, notes[0, 0], notes[8, 0])


def solution(mesh):
    split = P(axes)
    rows = P(axes, None)
    placed = (rows, split, split, split, rows, rows, rows, rows) + (P(),) * 18
    mesh_sizes = (mesh.shape[axes[0]], mesh.shape[axes[1]])
    return jax.shard_map(
        functools.partial(on_device, mesh_sizes),
        mesh=mesh,
        in_specs=placed,
        out_specs=(P(),) * 14,
        check_vma=False,
    )
```

```python
import functools

import jax
import jax.numpy as jnp
from jax import lax
from jax.experimental import pallas as pl
from jax.experimental.pallas import tpu as pltpu
from jax.sharding import PartitionSpec as P

STEP = 10


beta_one = 0.9
beta_two = 0.999
epsilon = 1e-08
step_rates = (0.05, 0.5, 1.0)
bias_rate = 0.05
weight_decay = 0.01

axes = ("dom", "rep")
WORDS = 4
SLOTS = 8
RUN = 48
UNIT = SLOTS * RUN
BLOCK = 512
MIB = 1024 * 1024
TRANS_LEFT = (((0,), (0,)), ((), ()))
TRANS_RIGHT = (((1,), (1,)), ((), ()))


def dot(left, right, dims=(((1,), (0,)), ((), ()))):
    return lax.dot_general(left, right, dims, preferred_element_type=jnp.float32)


def params(limit, collective=None):
    remote = {} if collective is None else dict(collective_id=collective, has_side_effects=True)
    return pltpu.CompilerParams(
        dimension_semantics=("arbitrary",), vmem_limit_bytes=limit * MIB, **remote
    )


def in_hbm(*arrays):
    return [pltpu.with_memory_space_constraint(array, pltpu.HBM) for array in arrays]


def whole(shape):
    return pl.BlockSpec(shape, lambda i: (0,) * len(shape))


def lanes(rows, width):
    return pl.BlockSpec((rows, width), lambda i: (0, i))


def floor_over(value, size):
    return ((value.astype(jnp.float32) + 0.5) * (1.0 / size)).astype(jnp.int32)


def words_layer(near_ref, out_ref, place_ref, field_ref):
    fanout, block = near_ref.shape
    span = out_ref.shape[0] // WORDS
    near = near_ref[...]
    unit = floor_over(near, UNIT)
    rest = near - unit * UNIT
    slot = floor_over(rest, RUN)
    word = floor_over(unit, span // RUN)
    place = (unit - word * (span // RUN)) * RUN + rest - slot * RUN
    bit = jnp.left_shift(jnp.int32(1), slot * 4)
    parts = [jnp.where(word == k, bit, 0) for k in range(WORDS)]
    totals = [jnp.zeros_like(bit) for _ in range(WORDS)]
    for g in range(fanout):
        same = place == place[g : g + 1]
        for k in range(WORDS):
            totals[k] = totals[k] + jnp.where(same, parts[k][g : g + 1], 0)
    place_ref[:fanout, :] = place
    for k in range(WORDS):
        field_ref[k, :fanout, :] = totals[k]
    chunk = RUN
    for tile in range(0, block, 128):
        cols = slice(tile, tile + 128)
        for start in range(0, span, chunk):
            rows = lax.broadcasted_iota(jnp.int32, (chunk, 128), 0) + start
            sums = [jnp.zeros((chunk, 128), jnp.int32) for _ in range(WORDS)]
            for g in range(fanout):
                hit = rows == place_ref[g : g + 1, cols]
                for k in range(WORDS):
                    sums[k] = jnp.where(hit, field_ref[k, g : g + 1, cols], sums[k])
            for k in range(WORDS):
                out_ref[k * span + start : k * span + start + chunk, cols] = sums[k]


def my_index(mesh_sizes):
    return lax.axis_index(axes[0]) * mesh_sizes[1] + lax.axis_index(axes[1])


def each_peer(mesh_sizes, act):
    across, along = mesh_sizes
    row, column = lax.axis_index(axes[0]), lax.axis_index(axes[1])

    def wrapped(value, size):
        return jnp.where(value >= size, value - size, value)

    def line(down, carry):
        other = wrapped(row + down, across)
        for ahead in range(along):
            place = wrapped(column + ahead, along)
            act(other * along + place, (other, place))
        return carry

    for ahead in range(1, along):
        place = wrapped(column + ahead, along)
        act(row * along + place, (row, place))
    lax.fori_loop(1, across, line, 0)


def greet(mesh_sizes):
    barrier = pltpu.get_barrier_semaphore()

    def tell(index, where):
        pl.semaphore_signal(
            barrier, inc=1, device_id=where, device_id_type=pl.DeviceIdType.MESH
        )

    each_peer(mesh_sizes, tell)


def all_greeted(mesh_sizes):
    pl.semaphore_wait(pltpu.get_barrier_semaphore(), mesh_sizes[0] * mesh_sizes[1] - 1)


def send_blocks(mesh_sizes, out_ref, in_ref, send_sem, recv_sem):
    me = my_index(mesh_sizes)

    def send(index, where):
        pltpu.make_async_remote_copy(
            src_ref=out_ref.at[index],
            dst_ref=in_ref.at[me],
            send_sem=send_sem,
            recv_sem=recv_sem,
            device_id=where,
            device_id_type=pl.DeviceIdType.MESH,
        ).start()

    each_peer(mesh_sizes, send)


def send_all(mesh_sizes, own_ref, in_ref, send_sem, recv_sem):
    me = my_index(mesh_sizes)

    def send(index, where):
        pltpu.make_async_remote_copy(
            src_ref=own_ref,
            dst_ref=in_ref.at[me],
            send_sem=send_sem,
            recv_sem=recv_sem,
            device_id=where,
            device_id_type=pl.DeviceIdType.MESH,
        ).start()

    each_peer(mesh_sizes, send)


def wait_moves(mesh_sizes, out_ref, in_ref, send_sem, recv_sem):
    others = pl.ds(0, mesh_sizes[0] * mesh_sizes[1] - 1)
    copy = pltpu.make_async_remote_copy(
        src_ref=in_ref.at[others],
        dst_ref=in_ref.at[others],
        send_sem=send_sem,
        recv_sem=recv_sem,
        device_id=(lax.axis_index(axes[0]), lax.axis_index(axes[1])),
        device_id_type=pl.DeviceIdType.MESH,
    )
    copy.wait_send()
    copy.wait_recv()


def semaphores():
    return [pltpu.SemaphoreType.DMA, pltpu.SemaphoreType.DMA]


def chosen_nodes(send_row, start, count):
    node = lax.broadcasted_iota(jnp.int32, (count, send_row.shape[1]), 0) + start
    return jnp.where(node == send_row, 1.0, 0.0).astype(jnp.bfloat16)


def words_kernel(mesh_sizes, kind, near_ref, *refs):
    refs = list(refs)
    if kind == "features":
        feats_ref, send_ref, out_ref, got_ref, sent_ref = refs[:5]
        refs = refs[5:]
    elif kind == "seeds":
        sent_ref, slots_ref, labels_ref, mask_ref, out_ref, got_ref, seeds_ref = refs[:7]
        refs = refs[7:]
    else:
        sent_ref, out_ref, got_ref = refs[:3]
        refs = refs[3:]
    place_ref, field_ref, land_ref, send_sem, recv_sem = refs
    step = pl.program_id(0)
    block = near_ref.shape[1]
    moves = (mesh_sizes, sent_ref, land_ref, send_sem, recv_sem)

    @pl.when(step == 0)
    def _():
        greet(mesh_sizes)

    if kind == "features":

        @pl.when(step == 0)
        def _():
            width, nodes = feats_ref.shape
            halo = send_ref.shape[1]
            total = jnp.zeros((width, halo), jnp.float32)
            for start in range(0, nodes, block):
                chosen = chosen_nodes(send_ref[...], start, block)
                total = total + dot(feats_ref[:, start : start + block], chosen)
            padded = sent_ref.shape[2]
            total = jnp.concatenate([total, jnp.zeros((padded - width, halo), jnp.float32)])
            sent_ref[...] = total.T.astype(jnp.bfloat16).reshape(sent_ref.shape)

    if kind == "seeds":
        classes = seeds_ref.shape[0]
        slots = slots_ref.shape[1]
        label = lax.broadcasted_iota(jnp.int32, (classes, slots), 0)
        marked = jnp.where((label == labels_ref[...]) & (mask_ref[...] != 0), 1.0, 0.0)
        chosen = chosen_nodes(slots_ref[...], step * block, block)
        seeds_ref[...] = dot(marked.astype(jnp.bfloat16), chosen, TRANS_RIGHT)

    words_layer(near_ref, out_ref, place_ref, field_ref)

    @pl.when(step == 0)
    def _():
        all_greeted(mesh_sizes)
        send_blocks(*moves)

    @pl.when(step == pl.num_programs(0) - 1)
    def _():
        me = my_index(mesh_sizes)
        wait_moves(*moves)
        land_ref[me] = sent_ref[me]
        got_ref[...] = land_ref[...]


def count_words(near, mesh_sizes, collective, halo, sent=None, feats=None, send_row=None, seeds=None):
    fanout, nodes = near.shape
    parts = mesh_sizes[0] * mesh_sizes[1]
    height = (nodes + halo) // SLOTS
    in_specs = [lanes(fanout, BLOCK)]
    operands = [near]
    scratch = []
    if sent is None:
        kind = "features"
        blocks = (parts, halo // parts, -(-feats.shape[0] // 128) * 128)
        in_specs += [whole(feats.shape), whole(send_row.shape)]
        operands += [*in_hbm(feats), send_row]
        scratch.append(pltpu.VMEM(blocks, jnp.bfloat16))
    else:
        kind = "plain"
        blocks = (parts, halo // parts, sent.shape[1])
        in_specs.append(whole(blocks))
        operands.append(sent.reshape(blocks))
    out_specs = [lanes(height, BLOCK), whole(blocks)]
    out_shape = [
        pltpu.HBM((height, nodes), jnp.int32),
        jax.ShapeDtypeStruct(blocks, jnp.bfloat16),
    ]
    if seeds is not None:
        kind = "seeds"
        classes, slots, labels, mask = seeds
        in_specs += [whole(slots.shape)] * 3
        operands += [slots, labels, mask]
        out_specs.append(lanes(classes, BLOCK))
        out_shape.append(jax.ShapeDtypeStruct((classes, nodes), jnp.float32))
    return pl.pallas_call(
        functools.partial(words_kernel, mesh_sizes, kind),
        grid=(nodes // BLOCK,),
        in_specs=in_specs,
        out_specs=out_specs,
        out_shape=out_shape,
        scratch_shapes=scratch
        + [
            pltpu.VMEM((16, BLOCK), jnp.int32),
            pltpu.VMEM((WORDS, 16, BLOCK), jnp.int32),
            pltpu.VMEM(blocks, jnp.bfloat16),
        ]
        + semaphores(),
        compiler_params=params(20, collective),
        name="count_words",
    )(*in_hbm(*operands[:1]), *operands[1:])


def field(words, slot):
    if slot == SLOTS - 1:
        picked = lax.shift_right_logical(words, 4 * slot)
    else:
        picked = words & (15 << (4 * slot))
    return picked.astype(jnp.float32).astype(jnp.bfloat16)


def slot_scale(slot):
    return 1.0 if slot == SLOTS - 1 else 2.0 ** (-4 * slot)


def spread_unit(words_ref, word_row, counts_ref, count_row):
    for start in range(0, RUN, 16):
        for tile in range(0, words_ref.shape[1], 256):
            cols = slice(tile, tile + 256)
            words = words_ref[word_row + start : word_row + start + 16, cols]
            for slot in range(SLOTS):
                row = count_row + slot * RUN + start
                counts_ref[row : row + 16, cols] = field(words, slot)


def gather_product(table_ref, words_ref, counts_ref):
    table = table_ref.shape[1]
    total = None
    for start in range(0, table, 2 * UNIT):
        stop = start + 2 * UNIT
        for row in range(start, stop, UNIT):
            spread_unit(words_ref, row // SLOTS, counts_ref, row)
        term = dot(table_ref[:, start:stop], counts_ref[start:stop, :])
        total = term if total is None else total + term
    return total


def scale_row(table):
    column = lax.broadcasted_iota(jnp.int32, (1, table), 1)
    rest = column - floor_over(column, UNIT) * UNIT
    slot = floor_over(rest, RUN)
    scale = jnp.ones((1, table), jnp.float32)
    for k in range(SLOTS - 1):
        scale = jnp.where(slot == k, slot_scale(k), scale)
    return scale


def column_of(row):
    return jnp.broadcast_to(row, (128, row.shape[1])).T


def late(rows, width):
    return pl.BlockSpec((rows, width), lambda i: (0, jnp.maximum(i - 1, 0)))


def now(rows, width, steps):
    return pl.BlockSpec((rows, width), lambda i: (0, jnp.minimum(i, steps - 1)))


def hidden_kernel(
    fanout,
    bias_start,
    words_ref,
    own_ref,
    own_block,
    got_ref,
    weight_ref,
    bias_ref,
    send_ref,
    state_ref,
    preact_ref,
    sent_ref,
    extra_ref,
    table_ref,
    counts_ref,
    picked_ref,
    mean_ref,
    self_ref,
    near_ref,
    bias_col,
):
    step = pl.program_id(0)
    last = pl.num_programs(0) - 1
    width, nodes = own_ref.shape
    units, block = state_ref.shape
    padded = mean_ref.shape[0]

    @pl.when(step == 0)
    def _():
        if table_ref.shape[0] > width:
            table_ref[...] = jnp.zeros_like(table_ref)
        got = got_ref[...].reshape(-1, got_ref.shape[2]).T[:width]
        scale = scale_row(table_ref.shape[1])
        own = own_ref[...].astype(jnp.float32) * scale[:, :nodes]
        table_ref[:width, :nodes] = own.astype(jnp.bfloat16)
        far = got.astype(jnp.float32) * scale[:, nodes:]
        table_ref[:width, nodes:] = far.astype(jnp.bfloat16)
        mean_ref[...] = jnp.zeros_like(mean_ref)
        picked_ref[...] = jnp.zeros_like(picked_ref)
        self_ref[...] = weight_ref[:width, :].T.astype(jnp.bfloat16)
        if padded > width:
            near_ref[...] = jnp.zeros_like(near_ref)
        near_ref[:, :width] = weight_ref[width:, :].T.astype(jnp.bfloat16)
        bias = bias_ref[...].reshape(1, -1)
        bias_col[...] = column_of(bias[:, bias_start : bias_start + units])

    def finish():
        mean = mean_ref[...]
        extra_ref[...] = mean
        preact = dot(self_ref[...], own_block[...]) + dot(near_ref[...], mean) + bias_col[:, :1]
        preact_ref[...] = preact
        active = preact * jax.nn.sigmoid(preact)
        norm = lax.rsqrt(jnp.sum(active * active, axis=0, keepdims=True) + 1e-06)
        state = (active * norm).astype(jnp.bfloat16)
        state_ref[...] = state
        picked_ref[...] += dot(state, chosen_nodes(send_ref[...], (step - 1) * block, block))

    @pl.when(step < last)
    def _():
        finish()
        total = gather_product(table_ref, words_ref, counts_ref)
        mean_ref[...] = (total / fanout).astype(jnp.bfloat16)

    @pl.when(step == last)
    def _():
        finish()
        sent_ref[...] = picked_ref[...].T.astype(jnp.bfloat16)


def hidden_layer(words, own, got, weight, bias, bias_start, send_row, fanout):
    width, nodes = own.shape
    halo = send_row.shape[1]
    table = nodes + halo
    units = weight.shape[1]
    padded = -(-width // 16) * 16
    steps = nodes // BLOCK
    return pl.pallas_call(
        functools.partial(hidden_kernel, fanout, bias_start),
        grid=(steps + 1,),
        in_specs=[
            now(words.shape[0], BLOCK, steps),
            whole(own.shape),
            late(width, BLOCK),
            whole(got.shape),
            whole(weight.shape),
            whole(bias.shape),
            whole(send_row.shape),
        ],
        out_specs=[
            late(units, BLOCK),
            late(units, BLOCK),
            whole((halo, units)),
            late(padded, BLOCK),
        ],
        out_shape=[
            jax.ShapeDtypeStruct((units, nodes), jnp.bfloat16),
            pltpu.HBM((units, nodes), jnp.float32),
            jax.ShapeDtypeStruct((halo, units), jnp.bfloat16),
            pltpu.HBM((padded, nodes), jnp.bfloat16),
        ],
        scratch_shapes=[
            pltpu.VMEM((padded, table), jnp.bfloat16),
            pltpu.VMEM((table, BLOCK), jnp.bfloat16),
            pltpu.VMEM((units, halo), jnp.float32),
            pltpu.VMEM((padded, BLOCK), jnp.bfloat16),
            pltpu.VMEM((units, width), jnp.bfloat16),
            pltpu.VMEM((units, padded), jnp.bfloat16),
            pltpu.VMEM((units, 128), jnp.float32),
        ],
        compiler_params=params(28),
        name="hidden_layer",
    )(*in_hbm(words), own, own, got, *in_hbm(weight, bias), send_row)


def far_start(nodes):
    return nodes // UNIT * UNIT


def unscaled(sums, fanout):
    pieces = []
    for row in range(0, sums.shape[0], RUN):
        slot = row // RUN % SLOTS
        pieces.append((sums[row : row + RUN] * (slot_scale(slot) / fanout)).astype(jnp.bfloat16))
    return jnp.concatenate(pieces)


def last_kernel(
    fanout,
    bias_start,
    words_ref,
    own_ref,
    own_block,
    got_ref,
    weight_ref,
    bias_ref,
    seeds_ref,
    grad_ref,
    rows_ref,
    sums_ref,
    notes_ref,
    table_out,
    far_ref,
    halo_ref,
    reduced_ref,
    counts_ref,
    both_ref,
    self_ref,
    near_ref,
    bias_col,
    far_sums,
):
    step = pl.program_id(0)
    last = pl.num_programs(0) - 1
    classes = self_ref.shape[0]
    width, nodes = own_ref.shape
    kinds = weight_ref.shape[0]
    halo = far_ref.shape[0]
    first = far_start(nodes)

    @pl.when(step == 0)
    def _():
        table_out[:, :nodes] = own_ref[...]
        table_out[:, nodes:] = got_ref[...].reshape(halo, width).T
        more = jnp.zeros((classes - kinds, 2 * width), jnp.float32)
        weight = jnp.concatenate([weight_ref[...], more]).astype(jnp.bfloat16)
        self_ref[...] = weight[:, :width]
        near_ref[...] = weight[:, width:]
        rest = jnp.full((1, classes - kinds), -1e30, jnp.float32)
        bias = bias_ref[...].reshape(1, -1)
        bias_col[...] = column_of(
            jnp.concatenate([bias[:, bias_start : bias_start + kinds], rest], axis=1)
        )
        reduced = dot(near_ref[...], table_out[...]) * scale_row(table_out.shape[1])
        high = reduced.astype(jnp.bfloat16)
        reduced_ref[:classes, :] = high
        reduced_ref[classes:, :] = (reduced - high.astype(jnp.float32)).astype(jnp.bfloat16)
        both_ref[...] = jnp.zeros_like(both_ref)
        counts_ref[first:, :] = jnp.zeros_like(counts_ref[first:, :])

    @pl.when(step <= 1)
    def _():
        sums_ref[...] = jnp.zeros_like(sums_ref)
        notes_ref[...] = jnp.zeros_like(notes_ref)
        far_sums[...] = jnp.zeros_like(far_sums)

    def finish():
        near_part = (both_ref[:classes, :] + both_ref[classes:, :]) / fanout
        logits = dot(self_ref[...], own_block[...]) + near_part + bias_col[:, :1]
        top = jnp.max(logits, axis=0, keepdims=True)
        powers = jnp.exp(logits - top)
        total = jnp.sum(powers, axis=0, keepdims=True)
        normer = jnp.log(total) + top
        seeds = seeds_ref[...]
        uses = jnp.sum(seeds, axis=0, keepdims=True)
        grad = (powers / total * uses - seeds).astype(jnp.bfloat16)
        grad_ref[...] = grad
        loss = uses * normer - jnp.sum(seeds * logits, axis=0, keepdims=True)
        sums_ref[...] += jnp.sum(grad.astype(jnp.float32), axis=1, keepdims=True)
        notes_ref[:8, :] += jnp.sum(loss)
        notes_ref[8:, :] += jnp.sum(uses)
        rows = grad.T
        rows_ref[...] = rows
        far_sums[...] += dot(counts_ref[first:, :], rows)

    @pl.when(step < last)
    def _():
        finish()
        both_ref[...] = gather_product(reduced_ref, words_ref, counts_ref)

    @pl.when(step == last)
    def _():
        finish()
        sums = unscaled(far_sums[...], fanout)[nodes - first :]
        far_ref[...] = sums
        halo_ref[...] = dot(sums, near_ref[...]).astype(jnp.bfloat16)


def last_layer(words, own, got, weight, bias, bias_start, seeds, fanout):
    width, nodes = own.shape
    halo = got.shape[0] * got.shape[1]
    table = nodes + halo
    classes = seeds.shape[0]
    steps = nodes // BLOCK
    far_height = table - far_start(nodes)
    return pl.pallas_call(
        functools.partial(last_kernel, fanout, bias_start),
        grid=(steps + 1,),
        in_specs=[
            now(words.shape[0], BLOCK, steps),
            whole(own.shape),
            late(width, BLOCK),
            whole(got.shape),
            whole(weight.shape),
            whole(bias.shape),
            late(classes, BLOCK),
        ],
        out_specs=[
            late(classes, BLOCK),
            pl.BlockSpec((BLOCK, classes), lambda i: (jnp.maximum(i - 1, 0), 0)),
            whole((classes, 128)),
            whole((16, 128)),
            whole((width, table)),
            whole((halo, classes)),
            whole((halo, width)),
        ],
        out_shape=[
            jax.ShapeDtypeStruct((classes, nodes), jnp.bfloat16),
            jax.ShapeDtypeStruct((nodes, classes), jnp.bfloat16),
            jax.ShapeDtypeStruct((classes, 128), jnp.float32),
            jax.ShapeDtypeStruct((16, 128), jnp.float32),
            jax.ShapeDtypeStruct((width, table), jnp.bfloat16),
            jax.ShapeDtypeStruct((halo, classes), jnp.bfloat16),
            jax.ShapeDtypeStruct((halo, width), jnp.bfloat16),
        ],
        scratch_shapes=[
            pltpu.VMEM((2 * classes, table), jnp.bfloat16),
            pltpu.VMEM((table, BLOCK), jnp.bfloat16),
            pltpu.VMEM((2 * classes, BLOCK), jnp.float32),
            pltpu.VMEM((classes, width), jnp.bfloat16),
            pltpu.VMEM((classes, width), jnp.bfloat16),
            pltpu.VMEM((classes, 128), jnp.float32),
            pltpu.VMEM((far_height, classes), jnp.float32),
        ],
        compiler_params=params(28),
        name="last_layer",
    )(*in_hbm(words), own, own, got, *in_hbm(weight, bias), seeds)


def scatter_kernel(mesh_sizes, fanout, flipped, words_ref, grad_ref, rows_ref, *refs):
    refs = list(refs)
    if flipped:
        weight_in, halo_ref, far_ref, table_ref, far_table = refs[:5]
        state_ref, got_ref, weight_ref = refs[5:8]
        padded_ref, counts_ref, sums_ref, self_ref, near_ref, land_ref = refs[8:14]
        send_sem, recv_sem = refs[14:]
    else:
        weight_in, halo_ref, early_ref = refs[:3]
        state_ref, got_ref, early_sum, notes_ref = refs[3:7]
        padded_ref, counts_ref, sums_ref, self_ref, near_ref, land_ref = refs[7:13]
        early_land, send_sem, recv_sem, early_send, early_recv = refs[13:]
        early_moves = (mesh_sizes, early_ref, early_land, early_send, early_recv)
    step = pl.program_id(0)
    units, nodes = grad_ref.shape
    width = state_ref.shape[0]
    span = words_ref.shape[0]
    part = span * SLOTS
    steps = -(-nodes // part)
    moves = (mesh_sizes, halo_ref, land_ref, send_sem, recv_sem)

    @pl.when(step == 0)
    def _():
        greet(mesh_sizes)
        for k in range(steps):
            start = k * part
            stop = min(start + part, nodes)
            padded_ref[k, :, : stop - start] = grad_ref[:, start:stop]
            if stop < start + part:
                padded_ref[k, :, stop - start :] = jnp.zeros(
                    (units, start + part - stop), jnp.bfloat16
                )
        weight = weight_in[...]
        if flipped:
            more = jnp.zeros((units - weight.shape[0], 2 * width), jnp.float32)
            weight = jnp.concatenate([weight, more]).T
            weight_ref[:width, :] = jnp.zeros((width, units), jnp.float32)
            weight_ref[width:, :] = dot(far_table[...], far_ref[...])
        self_ref[...] = weight[:width].astype(jnp.bfloat16)
        near_ref[...] = weight[width:].astype(jnp.bfloat16)
        sums_ref[...] = jnp.zeros_like(sums_ref)
        all_greeted(mesh_sizes)
        send_blocks(*moves)
        if not flipped:
            send_blocks(*early_moves)

    def add(row):
        spread_unit(words_ref, row // SLOTS, counts_ref, row)
        added = dot(counts_ref[row : row + UNIT, :], rows_ref[...])
        sums_ref[row : row + UNIT, :] = unscaled(added, fanout)

    beyond = nodes - (steps - 1) * part
    ending = -(-beyond // UNIT) * UNIT
    for row in range(0, ending, UNIT):
        add(row)
    if ending < part:

        @pl.when(step < steps - 1)
        def _():
            for row in range(ending, part, UNIT):
                add(row)

    if flipped and beyond < part:

        @pl.when(step == steps - 1)
        def _():
            sums_ref[beyond:, :] = jnp.zeros((part - beyond, units), jnp.bfloat16)

    sums = sums_ref[...]
    own_grad = padded_ref[step]
    state_ref[...] = dot(near_ref[...], sums, TRANS_RIGHT) + dot(self_ref[...], own_grad)
    if flipped:
        weight_ref[:width, :] += dot(table_ref[...], own_grad, TRANS_RIGHT)
        weight_ref[width:, :] += dot(table_ref[...], sums)

    @pl.when(step == steps - 1)
    def _():
        me = my_index(mesh_sizes)
        wait_moves(*moves)
        land_ref[me] = halo_ref[me]
        got_ref[...] = land_ref[...]
        if not flipped:
            wait_moves(*early_moves)
            early_land[me] = early_ref[me]
            total = jnp.sum(early_land[...].astype(jnp.float32), axis=0)
            early_sum[...] = total.astype(jnp.bfloat16)
            lane = lax.broadcasted_iota(jnp.int32, (8, 128), 1)
            row = lax.broadcasted_iota(jnp.int32, (8, 128), 0)
            last = jnp.broadcast_to(total[:1, -128:], (8, 128))
            for index in range(2):
                mine = (lane >= 120 + 3 * index) & (lane < 123 + 3 * index)
                note = jnp.sum(jnp.where(mine & (row == 0), last, 0.0))
                notes_ref[index] = jnp.full((1, 1), note, jnp.float32)


def scatter_layer(
    words, grad, rows, weight, halo_rows, mesh_sizes, collective, fanout, tables=None, early=None
):
    units, nodes = grad.shape
    halo, width = halo_rows.shape
    parts = mesh_sizes[0] * mesh_sizes[1]
    flipped = tables is not None
    total = nodes + halo
    part = total // WORDS
    span = part // SLOTS
    steps = -(-nodes // part)
    blocks = (parts, halo // parts, width)
    in_specs = [
        pl.BlockSpec((span, nodes), lambda i: (i, 0)),
        whole(grad.shape),
        whole(rows.shape),
        whole(weight.shape),
        whole(blocks),
    ]
    operands = [words, grad, rows, weight, halo_rows.reshape(blocks)]
    out_specs = [lanes(width, part), whole(blocks)]
    out_shape = [
        jax.ShapeDtypeStruct((width, total), jnp.float32),
        jax.ShapeDtypeStruct(blocks, jnp.bfloat16),
    ]
    if flipped:
        far, table = tables
        in_specs += [
            whole(far.shape),
            lanes(width, part),
            pl.BlockSpec((width, halo), lambda i: (0, nodes // halo)),
        ]
        operands += [far, table, table]
        out_specs.append(whole((2 * width, units)))
        out_shape.append(jax.ShapeDtypeStruct((2 * width, units), jnp.float32))
        scratch = semaphores()
    else:
        early_blocks = (parts, early.shape[0] // parts, early.shape[1])
        in_specs.append(whole(early_blocks))
        operands.append(early.reshape(early_blocks))
        out_specs += [whole(early_blocks[1:]), whole((2, 1, 1))]
        out_shape += [
            jax.ShapeDtypeStruct(early_blocks[1:], jnp.bfloat16),
            jax.ShapeDtypeStruct((2, 1, 1), jnp.float32),
        ]
        scratch = [pltpu.VMEM(early_blocks, jnp.bfloat16)] + semaphores() + semaphores()
    return pl.pallas_call(
        functools.partial(scatter_kernel, mesh_sizes, fanout, flipped),
        grid=(steps,),
        in_specs=in_specs,
        out_specs=out_specs,
        out_shape=out_shape,
        scratch_shapes=[
            pltpu.VMEM((steps, units, part), jnp.bfloat16),
            pltpu.VMEM((part, nodes), jnp.bfloat16),
            pltpu.VMEM((part, units), jnp.bfloat16),
            pltpu.VMEM((width, units), jnp.bfloat16),
            pltpu.VMEM((width, units), jnp.bfloat16),
            pltpu.VMEM(blocks, jnp.bfloat16),
        ]
        + scratch,
        compiler_params=params(36, collective),
        name="scatter_layer",
    )(*in_hbm(words), *operands[1:3], *in_hbm(weight), *operands[4:])


def active_grad(step, state_ref, preact_ref, back_ref, send_ref):
    block = state_ref.shape[1]
    chosen = chosen_nodes(send_ref[...], step * block, block)
    upper = state_ref[...] + dot(back_ref[...], chosen, TRANS_RIGHT)
    preact = preact_ref[...]
    gate = jax.nn.sigmoid(preact)
    active = preact * gate
    norm = lax.rsqrt(jnp.sum(active * active, axis=0, keepdims=True) + 1e-06)
    along = jnp.sum(active * upper, axis=0, keepdims=True)
    inner = norm * upper - active * (norm * norm * norm * along)
    return (inner * (gate * (1.0 + preact * (1.0 - gate)))).astype(jnp.bfloat16)


def middle_kernel(
    fanout,
    state_ref,
    preact_ref,
    returned_ref,
    send_ref,
    words_ref,
    weight_ref,
    own_block,
    mean_block,
    above_ref,
    notes_ref,
    grad_ref,
    rows_ref,
    sums_ref,
    halo_ref,
    early_ref,
    back_ref,
    counts_ref,
    far_sums,
    total_ref,
):
    step = pl.program_id(0)
    units, block = state_ref.shape
    halo = halo_ref.shape[0]
    nodes = block * pl.num_programs(0)
    first = far_start(nodes)
    part = (nodes + halo) // WORDS

    @pl.when(step == 0)
    def _():
        back_ref[...] = returned_ref[...].reshape(halo, units).T
        sums_ref[...] = jnp.zeros_like(sums_ref)
        far_sums[...] = jnp.zeros_like(far_sums)
        total_ref[...] = jnp.zeros_like(total_ref)

    base = first // part * part
    for row in range(first, nodes + halo, UNIT):
        spread_unit(words_ref, (row - base) // SLOTS, counts_ref, row - first)
    grad = active_grad(step, state_ref, preact_ref, back_ref, send_ref)
    grad_ref[...] = grad
    sums_ref[...] += jnp.sum(grad.astype(jnp.float32), axis=1, keepdims=True)
    rows = grad.T
    rows_ref[...] = rows
    far_sums[...] += dot(counts_ref[...], rows)
    width = own_block.shape[0]
    total_ref[:width, :] += dot(own_block[...], rows)
    total_ref[width:, :] += dot(mean_block[...], rows)

    @pl.when(step == pl.num_programs(0) - 1)
    def _():
        near = weight_ref[units:, :].T.astype(jnp.bfloat16)
        sums = unscaled(far_sums[...], fanout)[nodes - first :]
        halo_ref[...] = dot(sums, near).astype(jnp.bfloat16)
        early_ref[:, :units] = total_ref[...].astype(jnp.bfloat16)
        height, narrow = above_ref.shape
        above = jnp.concatenate(
            [above_ref[...], jnp.zeros((height, 128 - narrow), jnp.float32)], axis=1
        )
        lane = lax.broadcasted_iota(jnp.int32, above.shape, 1)
        for index in range(2):
            value = notes_ref[8 * index : 8 * index + 1, 0:1]
            for at in range(3):
                term = value.astype(jnp.bfloat16).astype(jnp.float32)
                above = jnp.where(lane == 120 + 3 * index + at, term, above)
                value = value - term
        early_ref[:, units:] = above.astype(jnp.bfloat16)


def middle_layer(
    state_grad, preact, returned, send_row, words, weight, own, mean, above, notes, fanout
):
    units, nodes = preact.shape
    width = own.shape[0]
    wide = units + 128
    halo = send_row.shape[1]
    part = (nodes + halo) // WORDS
    span = part // SLOTS
    far_words = WORDS - far_start(nodes) // part
    far_height = nodes + halo - far_start(nodes)
    return pl.pallas_call(
        functools.partial(middle_kernel, fanout),
        grid=(nodes // BLOCK,),
        in_specs=[
            lanes(units, BLOCK),
            lanes(units, BLOCK),
            whole(returned.shape),
            whole(send_row.shape),
            pl.BlockSpec((far_words * span, BLOCK), lambda i: (WORDS // far_words - 1, i)),
            whole(weight.shape),
            lanes(width, BLOCK),
            lanes(width, BLOCK),
            whole(above.shape),
            whole(notes.shape),
        ],
        out_specs=[
            lanes(units, BLOCK),
            pl.BlockSpec((BLOCK, units), lambda i: (i, 0)),
            whole((units, 128)),
            whole((halo, units)),
            whole((2 * width, wide)),
        ],
        out_shape=[
            jax.ShapeDtypeStruct((units, nodes), jnp.bfloat16),
            jax.ShapeDtypeStruct((nodes, units), jnp.bfloat16),
            jax.ShapeDtypeStruct((units, 128), jnp.float32),
            jax.ShapeDtypeStruct((halo, units), jnp.bfloat16),
            jax.ShapeDtypeStruct((2 * width, wide), jnp.bfloat16),
        ],
        scratch_shapes=[
            pltpu.VMEM((units, halo), jnp.bfloat16),
            pltpu.VMEM((far_height, BLOCK), jnp.bfloat16),
            pltpu.VMEM((far_height, units), jnp.float32),
            pltpu.VMEM((2 * width, units), jnp.float32),
        ],
        compiler_params=params(26),
        name="middle_layer",
    )(
        state_grad,
        *in_hbm(preact),
        returned,
        send_row,
        *in_hbm(words, weight),
        own,
        *in_hbm(mean),
        above,
        notes,
    )


def bottom_kernel(
    mesh_sizes,
    state_ref,
    preact_ref,
    returned_ref,
    send_ref,
    own_block,
    mean_block,
    sums_two,
    sums_three,
    early_ref,
    late_ref,
    early_all,
    back_ref,
    sums_ref,
    weight_ref,
    land_ref,
    send_sem,
    recv_sem,
):
    step = pl.program_id(0)
    units = state_ref.shape[0]
    halo = send_ref.shape[1]
    moves = (mesh_sizes, early_ref, land_ref, send_sem, recv_sem)

    @pl.when(step == 0)
    def _():
        greet(mesh_sizes)
        back_ref[...] = returned_ref[...].reshape(halo, units).T
        sums_ref[...] = jnp.zeros_like(sums_ref)
        weight_ref[...] = jnp.zeros_like(weight_ref)
        all_greeted(mesh_sizes)
        send_all(*moves)

    grad = active_grad(step, state_ref, preact_ref, back_ref, send_ref)
    sums_ref[...] += jnp.sum(grad.astype(jnp.float32), axis=1, keepdims=True)
    width = own_block.shape[0]
    weight_ref[0, :width, :] += dot(own_block[...], grad, TRANS_RIGHT)
    weight_ref[1] += dot(mean_block[...], grad, TRANS_RIGHT)

    @pl.when(step == pl.num_programs(0) - 1)
    def _():
        me = my_index(mesh_sizes)
        padded = weight_ref.shape[1]
        row = 0
        for start in range(0, units, 128):
            for half in range(2):
                late_ref[row : row + padded, :] = weight_ref[half, :, start : start + 128].astype(
                    jnp.bfloat16
                )
                row += padded
        pieces = []
        for sums in (sums_ref, sums_two, sums_three):
            flat = sums[...].T[:1]
            for start in range(0, flat.shape[1], 128):
                piece = flat[:, start : start + 128]
                pieces.append(piece)
        narrow = pieces[-1].shape[1]
        pieces[-1] = jnp.concatenate(
            [pieces[-1], jnp.zeros((1, 128 - narrow), jnp.float32)], axis=1
        )
        rest = late_ref.shape[0] - row
        pieces.append(jnp.zeros((rest - len(pieces), 128), jnp.float32))
        late_ref[row:, :] = jnp.concatenate(pieces).astype(jnp.bfloat16)
        wait_moves(*moves)
        land_ref[me] = early_ref[...]
        early_all[...] = land_ref[...]


def bottom_layer(
    state_grad, preact, returned, send_row, own, mean, sums_two, sums_three, early, mesh_sizes, collective
):
    units, nodes = preact.shape
    width = own.shape[0]
    padded = mean.shape[0]
    halo = send_row.shape[1]
    parts = mesh_sizes[0] * mesh_sizes[1]
    rows = units // 128 * (2 * padded + 2) + -(-sums_three.shape[0] // 128)
    rows = -(-rows // 512) * 512
    rows = -(-rows // parts) * parts
    early_blocks = (parts,) + early.shape
    return pl.pallas_call(
        functools.partial(bottom_kernel, mesh_sizes),
        grid=(nodes // BLOCK,),
        in_specs=[
            lanes(units, BLOCK),
            lanes(units, BLOCK),
            whole(returned.shape),
            whole(send_row.shape),
            lanes(width, BLOCK),
            lanes(padded, BLOCK),
            whole(sums_two.shape),
            whole(sums_three.shape),
            whole(early.shape),
        ],
        out_specs=[whole((rows, 128)), whole(early_blocks)],
        out_shape=[
            jax.ShapeDtypeStruct((rows, 128), jnp.bfloat16),
            jax.ShapeDtypeStruct(early_blocks, jnp.bfloat16),
        ],
        scratch_shapes=[
            pltpu.VMEM((units, halo), jnp.bfloat16),
            pltpu.VMEM((units, 128), jnp.float32),
            pltpu.VMEM((2, padded, units), jnp.float32),
            pltpu.VMEM(early_blocks, jnp.bfloat16),
        ]
        + semaphores(),
        compiler_params=params(24, collective),
        name="bottom_layer",
    )(
        state_grad,
        *in_hbm(preact),
        returned,
        send_row,
        *in_hbm(own, mean),
        sums_two,
        sums_three,
        early,
    )


def in_two(value):
    high = value.astype(jnp.bfloat16)
    return high, (value - high.astype(jnp.float32)).astype(jnp.bfloat16)


def product(left, right, dims=(((1,), (0,)), ((), ()))):
    if left.dtype == jnp.bfloat16:
        high, low = in_two(right)
        return dot(left, high, dims) + dot(left, low, dims)
    high, low = in_two(left)
    if right.dtype == jnp.bfloat16:
        return dot(high, right, dims) + dot(low, right, dims)
    right_high, right_low = in_two(right)
    return dot(high, right_high, dims) + (
        dot(high, right_low, dims) + dot(low, right_high, dims)
    )


def moments(turned, first, second):
    first = beta_one * first + (1.0 - beta_one) * turned
    second = beta_two * second + (1.0 - beta_two) * turned * turned
    update = first / (1.0 - beta_one**STEP) / (jnp.sqrt(second / (1.0 - beta_two**STEP)) + epsilon)
    return first, second, update


def share_kernel(
    mesh_sizes, late_ref, late_out, late_land, late_sum, late_all, send_sem, recv_sem, last_send, last_recv
):
    me = my_index(mesh_sizes)
    inward = (mesh_sizes, late_ref, late_land, send_sem, recv_sem)
    outward = (mesh_sizes, late_sum, late_all, last_send, last_recv)
    greet(mesh_sizes)
    all_greeted(mesh_sizes)
    send_blocks(*inward)
    wait_moves(*inward)
    late_land[me] = late_ref[me]
    late_sum[...] = jnp.sum(late_land[...].astype(jnp.float32), axis=0).astype(jnp.bfloat16)
    send_all(*outward)
    wait_moves(*outward)
    late_all[me] = late_sum[...]
    late_out[...] = late_all[...]


def share_sums(late_rows, mesh_sizes, collective):
    parts = mesh_sizes[0] * mesh_sizes[1]
    late_shape = (parts, late_rows.shape[0] // parts, 128)
    vmem = pl.BlockSpec(memory_space=pltpu.VMEM)
    return pl.pallas_call(
        functools.partial(share_kernel, mesh_sizes),
        in_specs=[vmem],
        out_specs=vmem,
        out_shape=jax.ShapeDtypeStruct(late_shape, jnp.bfloat16),
        scratch_shapes=[
            pltpu.VMEM(late_shape, jnp.bfloat16),
            pltpu.VMEM(late_shape[1:], jnp.bfloat16),
            pltpu.VMEM(late_shape, jnp.bfloat16),
        ]
        + semaphores()
        + semaphores(),
        compiler_params=pltpu.CompilerParams(
            vmem_limit_bytes=8 * MIB, collective_id=collective, has_side_effects=True
        ),
        name="share_sums",
    )(late_rows.reshape(late_shape))


def adam_kernel(
    padded,
    late_ref,
    early_ref,
    notes_ref,
    weight_one,
    weight_two,
    weight_three,
    left_one,
    right_one,
    left_two,
    right_two,
    left_three,
    right_three,
    first_one,
    first_two,
    first_three,
    second_one,
    second_two,
    second_three,
    bias_ref,
    bias_first,
    bias_second,
    *outs,
):
    share = 1.0 / notes_ref[1]
    units = weight_two.shape[1]
    width = weight_one.shape[0] // 2
    kinds = weight_three.shape[0]

    def step(grad, weight, first, second, left, right, rate, out):
        turned = product(product(left[...], grad, TRANS_LEFT), right[...]) * share
        new_first, new_second, update = moments(turned, first[...], second[...])
        out[1][...] = new_first
        out[2][...] = new_second
        moved = product(product(left[...], update), right[...], TRANS_RIGHT)
        out[0][...] = weight[...] - rate * moved

    step(
        early_ref[:, :units],
        weight_two,
        first_two,
        second_two,
        left_two,
        right_two,
        step_rates[1],
        outs[3:6],
    )

    grad = early_ref[:, units:].astype(jnp.float32).T[:kinds].astype(jnp.bfloat16)
    turned = product(right_three[...], product(grad, left_three[...])) * share
    new_first, new_second, update = moments(turned, first_three[...], second_three[...])
    outs[7][...] = new_first
    outs[8][...] = new_second
    moved = product(update, left_three[...], TRANS_RIGHT)
    moved = product(right_three[...], moved, TRANS_LEFT)
    outs[6][...] = weight_three[...] - step_rates[2] * moved

    late_rows = late_ref[...].astype(jnp.float32)
    columns = []
    for start in range(0, units, 128):
        row = start // 128 * 2 * padded
        columns.append(
            jnp.concatenate(
                [late_rows[row : row + width], late_rows[row + padded : row + padded + width]]
            )
        )
    step(
        jnp.concatenate(columns, axis=1).astype(jnp.bfloat16),
        weight_one,
        first_one,
        second_one,
        left_one,
        right_one,
        step_rates[0],
        outs[0:3],
    )
    row = units // 128 * 2 * padded
    pieces = []
    while len(pieces) * 128 < 2 * units + kinds:
        pieces.append(late_rows[row : row + 1])
        row += 1
    grad = jnp.concatenate(pieces, axis=1)[:, : 2 * units + kinds] * share
    flat = bias_ref.shape
    bias, first, second = (ref[...].reshape(grad.shape) for ref in (bias_ref, bias_first, bias_second))
    new_first, new_second, update = moments(grad, first, second)
    outs[9][...] = (bias - bias_rate * (update + weight_decay * bias)).reshape(flat)
    outs[10][...] = new_first.reshape(flat)
    outs[11][...] = new_second.reshape(flat)


def adam(padded, late_all, early_all, notes, *state):
    vmem = pl.BlockSpec(memory_space=pltpu.VMEM)
    order = (0, 9, 12, 1, 10, 13, 2, 11, 14, 15, 16, 17)
    outs = [jax.ShapeDtypeStruct(state[at].shape, jnp.float32) for at in order]
    return pl.pallas_call(
        functools.partial(adam_kernel, padded),
        in_specs=[vmem] * (3 + len(state)),
        out_specs=[vmem] * len(outs),
        out_shape=outs,
        compiler_params=pltpu.CompilerParams(vmem_limit_bytes=32 * MIB),
        name="adam",
    )(late_all, early_all, notes, *in_hbm(*state))


def on_device(
    mesh_sizes,
    features,
    labels,
    seed_rows,
    seed_mask,
    send_rows,
    neighbors_one,
    neighbors_two,
    neighbors_three,
    weight_one,
    weight_two,
    weight_three,
    left_one,
    right_one,
    left_two,
    right_two,
    left_three,
    right_three,
    first_one,
    first_two,
    first_three,
    second_one,
    second_two,
    second_three,
    bias_all,
    bias_first,
    bias_second,
):
    units = weight_one.shape[1]
    classes = weight_three.shape[1]
    halo = send_rows.size
    fans = (neighbors_one.shape[1], neighbors_two.shape[1], neighbors_three.shape[1])
    feats = features.T
    send_row = send_rows.reshape(1, halo)
    weight_three = weight_three.T
    padded_classes = -(-classes // 16) * 16
    seed_slots = (
        padded_classes,
        seed_rows.reshape(1, -1),
        labels.reshape(1, -1),
        seed_mask.reshape(1, -1),
    )

    words_one, got = count_words(
        neighbors_one.T, mesh_sizes, 0, halo, feats=feats, send_row=send_row
    )
    state_one, preact_one, sent, mean_one = hidden_layer(
        words_one, feats, got, weight_one, bias_all, 0, send_row, fans[0]
    )
    words_two, got = count_words(neighbors_two.T, mesh_sizes, 1, halo, sent=sent)
    state_two, preact_two, sent, mean_two = hidden_layer(
        words_two, state_one, got, weight_two, bias_all, units, send_row, fans[1]
    )
    words_three, got, seeds = count_words(
        neighbors_three.T, mesh_sizes, 2, halo, sent=sent, seeds=seed_slots
    )
    grad_three, rows_three, sums_three, notes, table_three, far, halo_grad = last_layer(
        words_three, state_two, got, weight_three, bias_all, 2 * units, seeds, fans[2]
    )
    state_grad, returned, weight_grad = scatter_layer(
        words_three,
        grad_three,
        rows_three,
        weight_three,
        halo_grad,
        mesh_sizes,
        3,
        fans[2],
        tables=(far, table_three),
    )
    grad_two, rows_two, sums_two, halo_grad, early = middle_layer(
        state_grad,
        preact_two,
        returned,
        send_row,
        words_two,
        weight_two,
        state_one,
        mean_two,
        weight_grad,
        notes,
        fans[1],
    )
    state_grad, returned, early_sum, notes = scatter_layer(
        words_two, grad_two, rows_two, weight_two, halo_grad, mesh_sizes, 4, fans[1], early=early
    )
    late_rows, early_all = bottom_layer(
        state_grad,
        preact_one,
        returned,
        send_row,
        feats,
        mean_one,
        sums_two,
        sums_three,
        early_sum,
        mesh_sizes,
        5,
    )
    late_all = share_sums(late_rows, mesh_sizes, 6)
    out = adam(
        mean_one.shape[0],
        late_all.reshape(late_rows.shape),
        early_all.reshape(early.shape),
        notes,
        weight_one,
        weight_two,
        weight_three,
        left_one,
        right_one,
        left_two,
        right_two,
        left_three,
        right_three.T,
        first_one,
        first_two,
        first_three.T,
        second_one,
        second_two,
        second_three.T,
        bias_all,
        bias_first,
        bias_second,
    )
    third = [value.T for value in out[6:9]]
    return (*out[:6], *third, *out[9:12], notes[0, 0, 0], notes[1, 0, 0])


def solution(mesh):
    split = P(axes)
    rows = P(axes, None)
    placed = (rows, split, split, split, rows, rows, rows, rows) + (P(),) * 18
    mesh_sizes = (mesh.shape[axes[0]], mesh.shape[axes[1]])
    return jax.shard_map(
        functools.partial(on_device, mesh_sizes),
        mesh=mesh,
        in_specs=placed,
        out_specs=(P(),) * 14,
        check_vma=False,
    )
```

```python
import functools

import jax
import jax.numpy as jnp
from jax import lax
from jax.experimental import pallas as pl
from jax.experimental.pallas import tpu as pltpu
from jax.sharding import PartitionSpec as P

STEP = 10


beta_one = 0.9
beta_two = 0.999
epsilon = 1e-08
step_rates = (0.05, 0.5, 1.0)
bias_rate = 0.05
weight_decay = 0.01

axes = ("dom", "rep")
WORDS = 4
SLOTS = 8
RUN = 48
UNIT = SLOTS * RUN
BLOCK = 512
MIB = 1024 * 1024
TRANS_LEFT = (((0,), (0,)), ((), ()))
TRANS_RIGHT = (((1,), (1,)), ((), ()))


def dot(left, right, dims=(((1,), (0,)), ((), ()))):
    return lax.dot_general(left, right, dims, preferred_element_type=jnp.float32)


def params(limit, collective=None):
    remote = {} if collective is None else dict(collective_id=collective, has_side_effects=True)
    return pltpu.CompilerParams(
        dimension_semantics=("arbitrary",), vmem_limit_bytes=limit * MIB, **remote
    )


def in_hbm(*arrays):
    return [pltpu.with_memory_space_constraint(array, pltpu.HBM) for array in arrays]


def whole(shape):
    return pl.BlockSpec(shape, lambda i: (0,) * len(shape))


def lanes(rows, width):
    return pl.BlockSpec((rows, width), lambda i: (0, i))


def floor_over(value, size):
    return ((value.astype(jnp.float32) + 0.5) * (1.0 / size)).astype(jnp.int32)


def words_layer(near_ref, out_ref, place_ref, field_ref):
    fanout, block = near_ref.shape
    span = out_ref.shape[0] // WORDS
    near = near_ref[...]
    unit = floor_over(near, UNIT)
    rest = near - unit * UNIT
    slot = floor_over(rest, RUN)
    word = floor_over(unit, span // RUN)
    place = (unit - word * (span // RUN)) * RUN + rest - slot * RUN
    bit = jnp.left_shift(jnp.int32(1), slot * 4)
    parts = [jnp.where(word == k, bit, 0) for k in range(WORDS)]
    totals = [jnp.zeros_like(bit) for _ in range(WORDS)]
    for g in range(fanout):
        same = place == place[g : g + 1]
        for k in range(WORDS):
            totals[k] = totals[k] + jnp.where(same, parts[k][g : g + 1], 0)
    place_ref[:fanout, :] = place
    for k in range(WORDS):
        field_ref[k, :fanout, :] = totals[k]
    chunk = RUN
    for tile in range(0, block, 128):
        cols = slice(tile, tile + 128)
        for start in range(0, span, chunk):
            rows = lax.broadcasted_iota(jnp.int32, (chunk, 128), 0) + start
            sums = [jnp.zeros((chunk, 128), jnp.int32) for _ in range(WORDS)]
            for g in range(fanout):
                hit = rows == place_ref[g : g + 1, cols]
                for k in range(WORDS):
                    sums[k] = jnp.where(hit, field_ref[k, g : g + 1, cols], sums[k])
            for k in range(WORDS):
                out_ref[k * span + start : k * span + start + chunk, cols] = sums[k]


def my_index(mesh_sizes):
    return lax.axis_index(axes[0]) * mesh_sizes[1] + lax.axis_index(axes[1])


def each_peer(mesh_sizes, act):
    across, along = mesh_sizes
    row, column = lax.axis_index(axes[0]), lax.axis_index(axes[1])

    def wrapped(value, size):
        return jnp.where(value >= size, value - size, value)

    def line(down, carry):
        other = wrapped(row + down, across)
        for ahead in range(along):
            place = wrapped(column + ahead, along)
            act(other * along + place, (other, place))
        return carry

    for ahead in range(1, along):
        place = wrapped(column + ahead, along)
        act(row * along + place, (row, place))
    lax.fori_loop(1, across, line, 0)


def greet(mesh_sizes):
    barrier = pltpu.get_barrier_semaphore()

    def tell(index, where):
        pl.semaphore_signal(
            barrier, inc=1, device_id=where, device_id_type=pl.DeviceIdType.MESH
        )

    each_peer(mesh_sizes, tell)


def all_greeted(mesh_sizes):
    pl.semaphore_wait(pltpu.get_barrier_semaphore(), mesh_sizes[0] * mesh_sizes[1] - 1)


def send_blocks(mesh_sizes, out_ref, in_ref, send_sem, recv_sem):
    me = my_index(mesh_sizes)

    def send(index, where):
        pltpu.make_async_remote_copy(
            src_ref=out_ref.at[index],
            dst_ref=in_ref.at[me],
            send_sem=send_sem,
            recv_sem=recv_sem,
            device_id=where,
            device_id_type=pl.DeviceIdType.MESH,
        ).start()

    each_peer(mesh_sizes, send)


def send_all(mesh_sizes, own_ref, in_ref, send_sem, recv_sem):
    me = my_index(mesh_sizes)

    def send(index, where):
        pltpu.make_async_remote_copy(
            src_ref=own_ref,
            dst_ref=in_ref.at[me],
            send_sem=send_sem,
            recv_sem=recv_sem,
            device_id=where,
            device_id_type=pl.DeviceIdType.MESH,
        ).start()

    each_peer(mesh_sizes, send)


def wait_moves(mesh_sizes, out_ref, in_ref, send_sem, recv_sem):
    others = pl.ds(0, mesh_sizes[0] * mesh_sizes[1] - 1)
    copy = pltpu.make_async_remote_copy(
        src_ref=in_ref.at[others],
        dst_ref=in_ref.at[others],
        send_sem=send_sem,
        recv_sem=recv_sem,
        device_id=(lax.axis_index(axes[0]), lax.axis_index(axes[1])),
        device_id_type=pl.DeviceIdType.MESH,
    )
    copy.wait_send()
    copy.wait_recv()


def split_sizes(mesh_sizes):
    across, along = mesh_sizes
    high = 4 if across % 4 == 0 else 1
    return high, across // high, along


def split_place(mesh_sizes):
    _, low, along = split_sizes(mesh_sizes)
    row, column = lax.axis_index(axes[0]), lax.axis_index(axes[1])
    top = row // low
    return top, row - top * low, column, (row - top * low) * along + column


def each_high(mesh_sizes, act):
    high, low, _ = split_sizes(mesh_sizes)
    top, bottom, column, _ = split_place(mesh_sizes)
    for ahead in range(1, high):
        other = top + ahead
        other = jnp.where(other >= high, other - high, other)
        act(other, (other * low + bottom, column))


def each_plane(mesh_sizes, act):
    _, low, along = split_sizes(mesh_sizes)
    top, bottom, column, _ = split_place(mesh_sizes)
    for down in range(low):
        for ahead in range(along):
            if down == 0 and ahead == 0:
                continue
            line = bottom + down
            line = jnp.where(line >= low, line - low, line)
            place = column + ahead
            place = jnp.where(place >= along, place - along, place)
            act(line * along + place, (top * low + line, place))


def greet_split(mesh_sizes):
    barrier = pltpu.get_barrier_semaphore()

    def tell(index, where):
        pl.semaphore_signal(
            barrier, inc=1, device_id=where, device_id_type=pl.DeviceIdType.MESH
        )

    each_high(mesh_sizes, tell)
    each_plane(mesh_sizes, tell)


def split_greeted(mesh_sizes):
    high, low, along = split_sizes(mesh_sizes)
    pl.semaphore_wait(pltpu.get_barrier_semaphore(), high - 1 + low * along - 1)


def push(src_ref, dst_ref, sems, where):
    pltpu.make_async_remote_copy(
        src_ref=src_ref,
        dst_ref=dst_ref,
        send_sem=sems[0],
        recv_sem=sems[1],
        device_id=where,
        device_id_type=pl.DeviceIdType.MESH,
    ).start()


def wait_pushed(ref, sems):
    copy = pltpu.make_async_remote_copy(
        src_ref=ref,
        dst_ref=ref,
        send_sem=sems[0],
        recv_sem=sems[1],
        device_id=(lax.axis_index(axes[0]), lax.axis_index(axes[1])),
        device_id_type=pl.DeviceIdType.MESH,
    )
    copy.wait_send()
    copy.wait_recv()


def high_start(mesh_sizes, sent_ref, relay_ref, sems):
    top = split_place(mesh_sizes)[0]
    each_high(
        mesh_sizes, lambda other, where: push(sent_ref.at[other], relay_ref.at[top], sems, where)
    )


def high_wait(mesh_sizes, relay_ref, sems):
    high = split_sizes(mesh_sizes)[0]
    if high > 1:
        wait_pushed(relay_ref.at[pl.ds(0, high - 1)], sems)


def plane_wait(mesh_sizes, land_ref, sems):
    _, low, along = split_sizes(mesh_sizes)
    wait_pushed(land_ref.at[pl.ds(0, low * along - 1)], sems)


def plane_blocks(mesh_sizes, relay_ref, land_ref, sems):
    me = split_place(mesh_sizes)[3]
    each_plane(
        mesh_sizes,
        lambda other, where: push(relay_ref.at[:, other], land_ref.at[:, me], sems, where),
    )


def plane_blocks_wait(mesh_sizes, land_ref, sems):
    _, low, along = split_sizes(mesh_sizes)
    wait_pushed(land_ref.at[:, pl.ds(0, low * along - 1)], sems)


NOTES = 120


def put_terms(rows, values):
    lane = lax.broadcasted_iota(jnp.int32, rows.shape, 1)
    for index, value in enumerate(values):
        for at in range(3):
            term = value.astype(jnp.bfloat16).astype(jnp.float32)
            rows = jnp.where(lane == NOTES + 3 * index + at, term, rows)
            value = value - term
    return rows


def take_terms(rows):
    lane = lax.broadcasted_iota(jnp.int32, rows.shape, 1)
    values = []
    for index in range(2):
        first = NOTES + 3 * index
        mine = (lane >= first) & (lane < first + 3)
        values.append(jnp.sum(jnp.where(mine, rows, 0.0), axis=1, keepdims=True))
    return values


def semaphores():
    return [pltpu.SemaphoreType.DMA, pltpu.SemaphoreType.DMA]


def chosen_nodes(send_row, start, count):
    node = lax.broadcasted_iota(jnp.int32, (count, send_row.shape[1]), 0) + start
    return jnp.where(node == send_row, 1.0, 0.0).astype(jnp.bfloat16)


def words_kernel(mesh_sizes, kind, near_ref, *refs):
    refs = list(refs)
    if kind == "features":
        feats_ref, send_ref, out_ref, got_ref, sent_ref = refs[:5]
        refs = refs[5:]
    elif kind == "seeds":
        sent_ref, slots_ref, labels_ref, mask_ref, out_ref, got_ref, seeds_ref = refs[:7]
        refs = refs[7:]
    else:
        sent_ref, out_ref, got_ref = refs[:3]
        refs = refs[3:]
    place_ref, field_ref, land_ref, send_sem, recv_sem = refs
    step = pl.program_id(0)
    block = near_ref.shape[1]
    moves = (mesh_sizes, sent_ref, land_ref, send_sem, recv_sem)

    @pl.when(step == 0)
    def _():
        greet(mesh_sizes)

    if kind == "features":

        @pl.when(step == 0)
        def _():
            width, nodes = feats_ref.shape
            halo = send_ref.shape[1]
            total = jnp.zeros((width, halo), jnp.float32)
            for start in range(0, nodes, block):
                chosen = chosen_nodes(send_ref[...], start, block)
                total = total + dot(feats_ref[:, start : start + block], chosen)
            padded = sent_ref.shape[2]
            total = jnp.concatenate([total, jnp.zeros((padded - width, halo), jnp.float32)])
            sent_ref[...] = total.T.astype(jnp.bfloat16).reshape(sent_ref.shape)

    if kind == "seeds":
        classes = seeds_ref.shape[0]
        slots = slots_ref.shape[1]
        label = lax.broadcasted_iota(jnp.int32, (classes, slots), 0)
        marked = jnp.where((label == labels_ref[...]) & (mask_ref[...] != 0), 1.0, 0.0)
        chosen = chosen_nodes(slots_ref[...], step * block, block)
        seeds_ref[...] = dot(marked.astype(jnp.bfloat16), chosen, TRANS_RIGHT)

    words_layer(near_ref, out_ref, place_ref, field_ref)

    @pl.when(step == 0)
    def _():
        all_greeted(mesh_sizes)
        send_blocks(*moves)

    @pl.when(step == pl.num_programs(0) - 1)
    def _():
        me = my_index(mesh_sizes)
        wait_moves(*moves)
        land_ref[me] = sent_ref[me]
        got_ref[...] = land_ref[...]


def count_words(near, mesh_sizes, collective, halo, sent=None, feats=None, send_row=None, seeds=None):
    fanout, nodes = near.shape
    parts = mesh_sizes[0] * mesh_sizes[1]
    height = (nodes + halo) // SLOTS
    in_specs = [lanes(fanout, BLOCK)]
    operands = [near]
    scratch = []
    if sent is None:
        kind = "features"
        blocks = (parts, halo // parts, -(-feats.shape[0] // 128) * 128)
        in_specs += [whole(feats.shape), whole(send_row.shape)]
        operands += [*in_hbm(feats), send_row]
        scratch.append(pltpu.VMEM(blocks, jnp.bfloat16))
    else:
        kind = "plain"
        blocks = (parts, halo // parts, sent.shape[1])
        in_specs.append(whole(blocks))
        operands.append(sent.reshape(blocks))
    out_specs = [lanes(height, BLOCK), whole(blocks)]
    out_shape = [
        pltpu.HBM((height, nodes), jnp.int32),
        jax.ShapeDtypeStruct(blocks, jnp.bfloat16),
    ]
    if seeds is not None:
        kind = "seeds"
        classes, slots, labels, mask = seeds
        in_specs += [whole(slots.shape)] * 3
        operands += [slots, labels, mask]
        out_specs.append(lanes(classes, BLOCK))
        out_shape.append(jax.ShapeDtypeStruct((classes, nodes), jnp.float32))
    return pl.pallas_call(
        functools.partial(words_kernel, mesh_sizes, kind),
        grid=(nodes // BLOCK,),
        in_specs=in_specs,
        out_specs=out_specs,
        out_shape=out_shape,
        scratch_shapes=scratch
        + [
            pltpu.VMEM((16, BLOCK), jnp.int32),
            pltpu.VMEM((WORDS, 16, BLOCK), jnp.int32),
            pltpu.VMEM(blocks, jnp.bfloat16),
        ]
        + semaphores(),
        compiler_params=params(20, collective),
        name="count_words",
    )(*in_hbm(*operands[:1]), *operands[1:])


def field(words, slot):
    if slot == SLOTS - 1:
        picked = lax.shift_right_logical(words, 4 * slot)
    else:
        picked = words & (15 << (4 * slot))
    return picked.astype(jnp.float32).astype(jnp.bfloat16)


def slot_scale(slot):
    return 1.0 if slot == SLOTS - 1 else 2.0 ** (-4 * slot)


def spread_unit(words_ref, word_row, counts_ref, count_row):
    for start in range(0, RUN, 16):
        for tile in range(0, words_ref.shape[1], 256):
            cols = slice(tile, tile + 256)
            words = words_ref[word_row + start : word_row + start + 16, cols]
            for slot in range(SLOTS):
                row = count_row + slot * RUN + start
                counts_ref[row : row + 16, cols] = field(words, slot)


def gather_product(table_ref, words_ref, counts_ref):
    table = table_ref.shape[1]
    total = None
    for start in range(0, table, 2 * UNIT):
        stop = start + 2 * UNIT
        for row in range(start, stop, UNIT):
            spread_unit(words_ref, row // SLOTS, counts_ref, row)
        term = dot(table_ref[:, start:stop], counts_ref[start:stop, :])
        total = term if total is None else total + term
    return total


def scale_row(table):
    column = lax.broadcasted_iota(jnp.int32, (1, table), 1)
    rest = column - floor_over(column, UNIT) * UNIT
    slot = floor_over(rest, RUN)
    scale = jnp.ones((1, table), jnp.float32)
    for k in range(SLOTS - 1):
        scale = jnp.where(slot == k, slot_scale(k), scale)
    return scale


def column_of(row):
    return jnp.broadcast_to(row, (128, row.shape[1])).T


def late(rows, width):
    return pl.BlockSpec((rows, width), lambda i: (0, jnp.maximum(i - 1, 0)))


def now(rows, width, steps):
    return pl.BlockSpec((rows, width), lambda i: (0, jnp.minimum(i, steps - 1)))


def hidden_kernel(
    fanout,
    bias_start,
    words_ref,
    own_ref,
    own_block,
    got_ref,
    weight_ref,
    bias_ref,
    send_ref,
    state_ref,
    preact_ref,
    sent_ref,
    extra_ref,
    table_ref,
    counts_ref,
    picked_ref,
    mean_ref,
    self_ref,
    near_ref,
    bias_col,
):
    step = pl.program_id(0)
    last = pl.num_programs(0) - 1
    width, nodes = own_ref.shape
    units, block = state_ref.shape
    padded = mean_ref.shape[0]

    @pl.when(step == 0)
    def _():
        if table_ref.shape[0] > width:
            table_ref[...] = jnp.zeros_like(table_ref)
        got = got_ref[...].reshape(-1, got_ref.shape[2]).T[:width]
        scale = scale_row(table_ref.shape[1])
        own = own_ref[...].astype(jnp.float32) * scale[:, :nodes]
        table_ref[:width, :nodes] = own.astype(jnp.bfloat16)
        far = got.astype(jnp.float32) * scale[:, nodes:]
        table_ref[:width, nodes:] = far.astype(jnp.bfloat16)
        mean_ref[...] = jnp.zeros_like(mean_ref)
        picked_ref[...] = jnp.zeros_like(picked_ref)
        self_ref[...] = weight_ref[:width, :].T.astype(jnp.bfloat16)
        if padded > width:
            near_ref[...] = jnp.zeros_like(near_ref)
        near_ref[:, :width] = weight_ref[width:, :].T.astype(jnp.bfloat16)
        bias = bias_ref[...].reshape(1, -1)
        bias_col[...] = column_of(bias[:, bias_start : bias_start + units])

    def finish():
        mean = mean_ref[...]
        extra_ref[...] = mean
        preact = dot(self_ref[...], own_block[...]) + dot(near_ref[...], mean) + bias_col[:, :1]
        preact_ref[...] = preact
        active = preact * jax.nn.sigmoid(preact)
        norm = lax.rsqrt(jnp.sum(active * active, axis=0, keepdims=True) + 1e-06)
        state = (active * norm).astype(jnp.bfloat16)
        state_ref[...] = state
        picked_ref[...] += dot(state, chosen_nodes(send_ref[...], (step - 1) * block, block))

    @pl.when(step < last)
    def _():
        finish()
        total = gather_product(table_ref, words_ref, counts_ref)
        mean_ref[...] = (total / fanout).astype(jnp.bfloat16)

    @pl.when(step == last)
    def _():
        finish()
        sent_ref[...] = picked_ref[...].T.astype(jnp.bfloat16)


def hidden_layer(words, own, got, weight, bias, bias_start, send_row, fanout):
    width, nodes = own.shape
    halo = send_row.shape[1]
    table = nodes + halo
    units = weight.shape[1]
    padded = -(-width // 16) * 16
    steps = nodes // BLOCK
    return pl.pallas_call(
        functools.partial(hidden_kernel, fanout, bias_start),
        grid=(steps + 1,),
        in_specs=[
            now(words.shape[0], BLOCK, steps),
            whole(own.shape),
            late(width, BLOCK),
            whole(got.shape),
            whole(weight.shape),
            whole(bias.shape),
            whole(send_row.shape),
        ],
        out_specs=[
            late(units, BLOCK),
            late(units, BLOCK),
            whole((halo, units)),
            late(padded, BLOCK),
        ],
        out_shape=[
            jax.ShapeDtypeStruct((units, nodes), jnp.bfloat16),
            pltpu.HBM((units, nodes), jnp.float32),
            jax.ShapeDtypeStruct((halo, units), jnp.bfloat16),
            pltpu.HBM((padded, nodes), jnp.bfloat16),
        ],
        scratch_shapes=[
            pltpu.VMEM((padded, table), jnp.bfloat16),
            pltpu.VMEM((table, BLOCK), jnp.bfloat16),
            pltpu.VMEM((units, halo), jnp.float32),
            pltpu.VMEM((padded, BLOCK), jnp.bfloat16),
            pltpu.VMEM((units, width), jnp.bfloat16),
            pltpu.VMEM((units, padded), jnp.bfloat16),
            pltpu.VMEM((units, 128), jnp.float32),
        ],
        compiler_params=params(28),
        name="hidden_layer",
    )(*in_hbm(words), own, own, got, *in_hbm(weight, bias), send_row)


def far_start(nodes):
    return nodes // UNIT * UNIT


def unscaled(sums, fanout):
    pieces = []
    for row in range(0, sums.shape[0], RUN):
        slot = row // RUN % SLOTS
        pieces.append((sums[row : row + RUN] * (slot_scale(slot) / fanout)).astype(jnp.bfloat16))
    return jnp.concatenate(pieces)


def last_kernel(
    fanout,
    bias_start,
    words_ref,
    own_ref,
    own_block,
    got_ref,
    weight_ref,
    bias_ref,
    seeds_ref,
    grad_ref,
    rows_ref,
    sums_ref,
    notes_ref,
    table_out,
    far_ref,
    halo_ref,
    reduced_ref,
    counts_ref,
    both_ref,
    self_ref,
    near_ref,
    bias_col,
    far_sums,
):
    step = pl.program_id(0)
    last = pl.num_programs(0) - 1
    classes = self_ref.shape[0]
    width, nodes = own_ref.shape
    kinds = weight_ref.shape[0]
    halo = far_ref.shape[0]
    first = far_start(nodes)

    @pl.when(step == 0)
    def _():
        table_out[:, :nodes] = own_ref[...]
        table_out[:, nodes:] = got_ref[...].reshape(halo, width).T
        more = jnp.zeros((classes - kinds, 2 * width), jnp.float32)
        weight = jnp.concatenate([weight_ref[...], more]).astype(jnp.bfloat16)
        self_ref[...] = weight[:, :width]
        near_ref[...] = weight[:, width:]
        rest = jnp.full((1, classes - kinds), -1e30, jnp.float32)
        bias = bias_ref[...].reshape(1, -1)
        bias_col[...] = column_of(
            jnp.concatenate([bias[:, bias_start : bias_start + kinds], rest], axis=1)
        )
        reduced = dot(near_ref[...], table_out[...]) * scale_row(table_out.shape[1])
        high = reduced.astype(jnp.bfloat16)
        reduced_ref[:classes, :] = high
        reduced_ref[classes:, :] = (reduced - high.astype(jnp.float32)).astype(jnp.bfloat16)
        both_ref[...] = jnp.zeros_like(both_ref)
        counts_ref[first:, :] = jnp.zeros_like(counts_ref[first:, :])

    @pl.when(step <= 1)
    def _():
        sums_ref[...] = jnp.zeros_like(sums_ref)
        notes_ref[...] = jnp.zeros_like(notes_ref)
        far_sums[...] = jnp.zeros_like(far_sums)

    def finish():
        near_part = (both_ref[:classes, :] + both_ref[classes:, :]) / fanout
        logits = dot(self_ref[...], own_block[...]) + near_part + bias_col[:, :1]
        top = jnp.max(logits, axis=0, keepdims=True)
        powers = jnp.exp(logits - top)
        total = jnp.sum(powers, axis=0, keepdims=True)
        normer = jnp.log(total) + top
        seeds = seeds_ref[...]
        uses = jnp.sum(seeds, axis=0, keepdims=True)
        grad = (powers / total * uses - seeds).astype(jnp.bfloat16)
        grad_ref[...] = grad
        loss = uses * normer - jnp.sum(seeds * logits, axis=0, keepdims=True)
        sums_ref[...] += jnp.sum(grad.astype(jnp.float32), axis=1, keepdims=True)
        notes_ref[:8, :] += jnp.sum(loss)
        notes_ref[8:, :] += jnp.sum(uses)
        rows = grad.T
        rows_ref[...] = rows
        far_sums[...] += dot(counts_ref[first:, :], rows)

    @pl.when(step < last)
    def _():
        finish()
        both_ref[...] = gather_product(reduced_ref, words_ref, counts_ref)

    @pl.when(step == last)
    def _():
        finish()
        sums = unscaled(far_sums[...], fanout)[nodes - first :]
        far_ref[...] = sums
        halo_ref[...] = dot(sums, near_ref[...]).astype(jnp.bfloat16)


def last_layer(words, own, got, weight, bias, bias_start, seeds, fanout):
    width, nodes = own.shape
    halo = got.shape[0] * got.shape[1]
    table = nodes + halo
    classes = seeds.shape[0]
    steps = nodes // BLOCK
    far_height = table - far_start(nodes)
    return pl.pallas_call(
        functools.partial(last_kernel, fanout, bias_start),
        grid=(steps + 1,),
        in_specs=[
            now(words.shape[0], BLOCK, steps),
            whole(own.shape),
            late(width, BLOCK),
            whole(got.shape),
            whole(weight.shape),
            whole(bias.shape),
            late(classes, BLOCK),
        ],
        out_specs=[
            late(classes, BLOCK),
            pl.BlockSpec((BLOCK, classes), lambda i: (jnp.maximum(i - 1, 0), 0)),
            whole((classes, 128)),
            whole((16, 128)),
            whole((width, table)),
            whole((halo, classes)),
            whole((halo, width)),
        ],
        out_shape=[
            jax.ShapeDtypeStruct((classes, nodes), jnp.bfloat16),
            jax.ShapeDtypeStruct((nodes, classes), jnp.bfloat16),
            jax.ShapeDtypeStruct((classes, 128), jnp.float32),
            jax.ShapeDtypeStruct((16, 128), jnp.float32),
            jax.ShapeDtypeStruct((width, table), jnp.bfloat16),
            jax.ShapeDtypeStruct((halo, classes), jnp.bfloat16),
            jax.ShapeDtypeStruct((halo, width), jnp.bfloat16),
        ],
        scratch_shapes=[
            pltpu.VMEM((2 * classes, table), jnp.bfloat16),
            pltpu.VMEM((table, BLOCK), jnp.bfloat16),
            pltpu.VMEM((2 * classes, BLOCK), jnp.float32),
            pltpu.VMEM((classes, width), jnp.bfloat16),
            pltpu.VMEM((classes, width), jnp.bfloat16),
            pltpu.VMEM((classes, 128), jnp.float32),
            pltpu.VMEM((far_height, classes), jnp.float32),
        ],
        compiler_params=params(28),
        name="last_layer",
    )(*in_hbm(words), own, own, got, *in_hbm(weight, bias), seeds)


def scatter_kernel(mesh_sizes, fanout, flipped, words_ref, grad_ref, rows_ref, *refs):
    refs = list(refs)
    if flipped:
        weight_in, halo_ref, far_ref, table_ref, far_table = refs[:5]
        state_ref, got_ref, weight_ref = refs[5:8]
        refs = refs[8:]
    else:
        weight_in, halo_ref, early_ref = refs[:3]
        state_ref, got_ref, early_sum, notes_ref = refs[3:7]
        refs = refs[7:]
    padded_ref, counts_ref, sums_ref, self_ref, near_ref, relay_ref, land_ref = refs[:7]
    if flipped:
        high_sems, plane_sems = refs[7:9], refs[9:11]
    else:
        early_relay, early_part, early_land = refs[7:10]
        high_sems, plane_sems = refs[10:12], refs[12:14]
        early_high, early_plane = refs[14:16], refs[16:18]
    step = pl.program_id(0)
    units, nodes = grad_ref.shape
    width = state_ref.shape[0]
    span = words_ref.shape[0]
    part = span * SLOTS
    steps = -(-nodes // part)

    @pl.when(step == 0)
    def _():
        greet_split(mesh_sizes)
        for k in range(steps):
            start = k * part
            stop = min(start + part, nodes)
            padded_ref[k, :, : stop - start] = grad_ref[:, start:stop]
            if stop < start + part:
                padded_ref[k, :, stop - start :] = jnp.zeros(
                    (units, start + part - stop), jnp.bfloat16
                )
        weight = weight_in[...]
        if flipped:
            more = jnp.zeros((units - weight.shape[0], 2 * width), jnp.float32)
            weight = jnp.concatenate([weight, more]).T
            weight_ref[:width, :] = jnp.zeros((width, units), jnp.float32)
            weight_ref[width:, :] = dot(far_table[...], far_ref[...])
        self_ref[...] = weight[:width].astype(jnp.bfloat16)
        near_ref[...] = weight[width:].astype(jnp.bfloat16)
        sums_ref[...] = jnp.zeros_like(sums_ref)
        split_greeted(mesh_sizes)
        high_start(mesh_sizes, halo_ref, relay_ref, high_sems)
        if not flipped:
            plane_blocks(mesh_sizes, early_ref, early_relay, early_plane)

    @pl.when(step == steps // 2)
    def _():
        top, _, _, me = split_place(mesh_sizes)
        high_wait(mesh_sizes, relay_ref, high_sems)
        relay_ref[top] = halo_ref[top]
        plane_blocks(mesh_sizes, relay_ref, land_ref, plane_sems)
        if not flipped:
            plane_blocks_wait(mesh_sizes, early_relay, early_plane)
            early_relay[:, me] = early_ref[:, me]
            total = jnp.sum(early_relay[...].astype(jnp.float32), axis=1)
            shape = total.shape
            total = total.reshape(-1, shape[2])
            last = total[:, -128:]
            total = jnp.concatenate([total[:, :-128], put_terms(last, take_terms(last))], axis=1)
            early_part[...] = total.astype(jnp.bfloat16).reshape(shape)
            high_start(mesh_sizes, early_part, early_land, early_high)

    def add(row):
        spread_unit(words_ref, row // SLOTS, counts_ref, row)
        added = dot(counts_ref[row : row + UNIT, :], rows_ref[...])
        sums_ref[row : row + UNIT, :] = unscaled(added, fanout)

    beyond = nodes - (steps - 1) * part
    ending = -(-beyond // UNIT) * UNIT
    for row in range(0, ending, UNIT):
        add(row)
    if ending < part:

        @pl.when(step < steps - 1)
        def _():
            for row in range(ending, part, UNIT):
                add(row)

    if flipped and beyond < part:

        @pl.when(step == steps - 1)
        def _():
            sums_ref[beyond:, :] = jnp.zeros((part - beyond, units), jnp.bfloat16)

    sums = sums_ref[...]
    own_grad = padded_ref[step]
    state_ref[...] = dot(near_ref[...], sums, TRANS_RIGHT) + dot(self_ref[...], own_grad)
    if flipped:
        weight_ref[:width, :] += dot(table_ref[...], own_grad, TRANS_RIGHT)
        weight_ref[width:, :] += dot(table_ref[...], sums)

    @pl.when(step == steps - 1)
    def _():
        me = split_place(mesh_sizes)[3]
        plane_blocks_wait(mesh_sizes, land_ref, plane_sems)
        land_ref[:, me] = relay_ref[:, me]
        got_ref[...] = land_ref[...]
        if not flipped:
            top = split_place(mesh_sizes)[0]
            high_wait(mesh_sizes, early_land, early_high)
            early_land[top] = early_part[top]
            total = jnp.sum(early_land[...].astype(jnp.float32), axis=0)
            early_sum[...] = total.astype(jnp.bfloat16)
            for index, value in enumerate(take_terms(total[:, -128:])):
                notes_ref[index] = value[:1]


def scatter_layer(
    words, grad, rows, weight, halo_rows, mesh_sizes, collective, fanout, tables=None, early=None
):
    units, nodes = grad.shape
    halo, width = halo_rows.shape
    parts = mesh_sizes[0] * mesh_sizes[1]
    flipped = tables is not None
    total = nodes + halo
    part = total // WORDS
    span = part // SLOTS
    steps = -(-nodes // part)
    high = split_sizes(mesh_sizes)[0]
    blocks = (high, parts // high, halo // parts, width)
    in_specs = [
        pl.BlockSpec((span, nodes), lambda i: (i, 0)),
        whole(grad.shape),
        whole(rows.shape),
        whole(weight.shape),
        whole(blocks),
    ]
    operands = [words, grad, rows, weight, halo_rows.reshape(blocks)]
    out_specs = [lanes(width, part), whole(blocks)]
    out_shape = [
        jax.ShapeDtypeStruct((width, total), jnp.float32),
        jax.ShapeDtypeStruct(blocks, jnp.bfloat16),
    ]
    if flipped:
        far, table = tables
        in_specs += [
            whole(far.shape),
            lanes(width, part),
            pl.BlockSpec((width, halo), lambda i: (0, nodes // halo)),
        ]
        operands += [far, table, table]
        out_specs.append(whole((2 * width, units)))
        out_shape.append(jax.ShapeDtypeStruct((2 * width, units), jnp.float32))
        scratch = semaphores() + semaphores()
    else:
        early_blocks = (high, parts // high, early.shape[0] // parts, early.shape[1])
        in_specs.append(whole(early_blocks))
        operands.append(early.reshape(early_blocks))
        out_specs += [whole(early_blocks[2:]), whole((2, 1, 1))]
        out_shape += [
            jax.ShapeDtypeStruct(early_blocks[2:], jnp.bfloat16),
            jax.ShapeDtypeStruct((2, 1, 1), jnp.float32),
        ]
        scratch = [
            pltpu.VMEM(early_blocks, jnp.bfloat16),
            pltpu.VMEM((high,) + early_blocks[2:], jnp.bfloat16),
            pltpu.VMEM((high,) + early_blocks[2:], jnp.bfloat16),
        ]
        scratch += semaphores() * 4
    return pl.pallas_call(
        functools.partial(scatter_kernel, mesh_sizes, fanout, flipped),
        grid=(steps,),
        in_specs=in_specs,
        out_specs=out_specs,
        out_shape=out_shape,
        scratch_shapes=[
            pltpu.VMEM((steps, units, part), jnp.bfloat16),
            pltpu.VMEM((part, nodes), jnp.bfloat16),
            pltpu.VMEM((part, units), jnp.bfloat16),
            pltpu.VMEM((width, units), jnp.bfloat16),
            pltpu.VMEM((width, units), jnp.bfloat16),
            pltpu.VMEM(blocks, jnp.bfloat16),
            pltpu.VMEM(blocks, jnp.bfloat16),
        ]
        + scratch,
        compiler_params=params(36, collective),
        name="scatter_layer",
    )(*in_hbm(words), *operands[1:3], *in_hbm(weight), *operands[4:])


def active_grad(step, state_ref, preact_ref, back_ref, send_ref):
    block = state_ref.shape[1]
    chosen = chosen_nodes(send_ref[...], step * block, block)
    upper = state_ref[...] + dot(back_ref[...], chosen, TRANS_RIGHT)
    preact = preact_ref[...]
    gate = jax.nn.sigmoid(preact)
    active = preact * gate
    norm = lax.rsqrt(jnp.sum(active * active, axis=0, keepdims=True) + 1e-06)
    along = jnp.sum(active * upper, axis=0, keepdims=True)
    inner = norm * upper - active * (norm * norm * norm * along)
    return (inner * (gate * (1.0 + preact * (1.0 - gate)))).astype(jnp.bfloat16)


def middle_kernel(
    fanout,
    state_ref,
    preact_ref,
    returned_ref,
    send_ref,
    words_ref,
    weight_ref,
    own_block,
    mean_block,
    above_ref,
    notes_ref,
    grad_ref,
    rows_ref,
    sums_ref,
    halo_ref,
    early_ref,
    back_ref,
    counts_ref,
    far_sums,
    total_ref,
):
    step = pl.program_id(0)
    units, block = state_ref.shape
    halo = halo_ref.shape[0]
    nodes = block * pl.num_programs(0)
    first = far_start(nodes)
    part = (nodes + halo) // WORDS

    @pl.when(step == 0)
    def _():
        back_ref[...] = returned_ref[...].reshape(halo, units).T
        sums_ref[...] = jnp.zeros_like(sums_ref)
        far_sums[...] = jnp.zeros_like(far_sums)
        total_ref[...] = jnp.zeros_like(total_ref)

    base = first // part * part
    for row in range(first, nodes + halo, UNIT):
        spread_unit(words_ref, (row - base) // SLOTS, counts_ref, row - first)
    grad = active_grad(step, state_ref, preact_ref, back_ref, send_ref)
    grad_ref[...] = grad
    sums_ref[...] += jnp.sum(grad.astype(jnp.float32), axis=1, keepdims=True)
    rows = grad.T
    rows_ref[...] = rows
    far_sums[...] += dot(counts_ref[...], rows)
    width = own_block.shape[0]
    total_ref[:width, :] += dot(own_block[...], rows)
    total_ref[width:, :] += dot(mean_block[...], rows)

    @pl.when(step == pl.num_programs(0) - 1)
    def _():
        near = weight_ref[units:, :].T.astype(jnp.bfloat16)
        sums = unscaled(far_sums[...], fanout)[nodes - first :]
        halo_ref[...] = dot(sums, near).astype(jnp.bfloat16)
        early_ref[:, :units] = total_ref[...].astype(jnp.bfloat16)
        height, narrow = above_ref.shape
        above = jnp.concatenate(
            [above_ref[...], jnp.zeros((height, 128 - narrow), jnp.float32)], axis=1
        )
        above = put_terms(above, [notes_ref[0:1, 0:1], notes_ref[8:9, 0:1]])
        early_ref[:, units:] = above.astype(jnp.bfloat16)


def middle_layer(
    state_grad, preact, returned, send_row, words, weight, own, mean, above, notes, fanout
):
    units, nodes = preact.shape
    width = own.shape[0]
    wide = units + 128
    halo = send_row.shape[1]
    part = (nodes + halo) // WORDS
    span = part // SLOTS
    far_words = WORDS - far_start(nodes) // part
    far_height = nodes + halo - far_start(nodes)
    return pl.pallas_call(
        functools.partial(middle_kernel, fanout),
        grid=(nodes // BLOCK,),
        in_specs=[
            lanes(units, BLOCK),
            lanes(units, BLOCK),
            whole(returned.shape),
            whole(send_row.shape),
            pl.BlockSpec((far_words * span, BLOCK), lambda i: (WORDS // far_words - 1, i)),
            whole(weight.shape),
            lanes(width, BLOCK),
            lanes(width, BLOCK),
            whole(above.shape),
            whole(notes.shape),
        ],
        out_specs=[
            lanes(units, BLOCK),
            pl.BlockSpec((BLOCK, units), lambda i: (i, 0)),
            whole((units, 128)),
            whole((halo, units)),
            whole((2 * width, wide)),
        ],
        out_shape=[
            jax.ShapeDtypeStruct((units, nodes), jnp.bfloat16),
            jax.ShapeDtypeStruct((nodes, units), jnp.bfloat16),
            jax.ShapeDtypeStruct((units, 128), jnp.float32),
            jax.ShapeDtypeStruct((halo, units), jnp.bfloat16),
            jax.ShapeDtypeStruct((2 * width, wide), jnp.bfloat16),
        ],
        scratch_shapes=[
            pltpu.VMEM((units, halo), jnp.bfloat16),
            pltpu.VMEM((far_height, BLOCK), jnp.bfloat16),
            pltpu.VMEM((far_height, units), jnp.float32),
            pltpu.VMEM((2 * width, units), jnp.float32),
        ],
        compiler_params=params(26),
        name="middle_layer",
    )(
        state_grad,
        *in_hbm(preact),
        returned,
        send_row,
        *in_hbm(words, weight),
        own,
        *in_hbm(mean),
        above,
        notes,
    )


def bottom_kernel(
    mesh_sizes,
    state_ref,
    preact_ref,
    returned_ref,
    send_ref,
    own_block,
    mean_block,
    sums_two,
    sums_three,
    early_ref,
    late_ref,
    early_all,
    back_ref,
    sums_ref,
    weight_ref,
    relay_ref,
    land_ref,
    *sems,
):
    step = pl.program_id(0)
    units = state_ref.shape[0]
    halo = send_ref.shape[1]
    high_sems, plane_sems = sems[:2], sems[2:]

    @pl.when(step == 0)
    def _():
        greet_split(mesh_sizes)
        back_ref[...] = returned_ref[...].reshape(halo, units).T
        sums_ref[...] = jnp.zeros_like(sums_ref)
        weight_ref[...] = jnp.zeros_like(weight_ref)
        split_greeted(mesh_sizes)
        top = split_place(mesh_sizes)[0]
        each_high(
            mesh_sizes,
            lambda other, where: push(early_ref, relay_ref.at[top], high_sems, where),
        )

    @pl.when(step == 3)
    def _():
        top, _, _, me = split_place(mesh_sizes)
        high_wait(mesh_sizes, relay_ref, high_sems)
        relay_ref[top] = early_ref[...]
        each_plane(
            mesh_sizes,
            lambda other, where: push(relay_ref, land_ref.at[:, me], plane_sems, where),
        )

    grad = active_grad(step, state_ref, preact_ref, back_ref, send_ref)
    sums_ref[...] += jnp.sum(grad.astype(jnp.float32), axis=1, keepdims=True)
    width = own_block.shape[0]
    weight_ref[0, :width, :] += dot(own_block[...], grad, TRANS_RIGHT)
    weight_ref[1] += dot(mean_block[...], grad, TRANS_RIGHT)

    @pl.when(step == pl.num_programs(0) - 1)
    def _():
        me = split_place(mesh_sizes)[3]
        padded = weight_ref.shape[1]
        row = 0
        for start in range(0, units, 128):
            for half in range(2):
                late_ref[row : row + padded, :] = weight_ref[half, :, start : start + 128].astype(
                    jnp.bfloat16
                )
                row += padded
        pieces = []
        for sums in (sums_ref, sums_two, sums_three):
            flat = sums[...].T[:1]
            for start in range(0, flat.shape[1], 128):
                piece = flat[:, start : start + 128]
                pieces.append(piece)
        narrow = pieces[-1].shape[1]
        pieces[-1] = jnp.concatenate(
            [pieces[-1], jnp.zeros((1, 128 - narrow), jnp.float32)], axis=1
        )
        rest = late_ref.shape[0] - row
        pieces.append(jnp.zeros((rest - len(pieces), 128), jnp.float32))
        late_ref[row:, :] = jnp.concatenate(pieces).astype(jnp.bfloat16)
        plane_blocks_wait(mesh_sizes, land_ref, plane_sems)
        land_ref[:, me] = relay_ref[...]
        early_all[...] = land_ref[...]


def bottom_layer(
    state_grad, preact, returned, send_row, own, mean, sums_two, sums_three, early, mesh_sizes, collective
):
    units, nodes = preact.shape
    width = own.shape[0]
    padded = mean.shape[0]
    halo = send_row.shape[1]
    parts = mesh_sizes[0] * mesh_sizes[1]
    rows = units // 128 * (2 * padded + 2) + -(-sums_three.shape[0] // 128)
    rows = -(-rows // 512) * 512
    rows = -(-rows // parts) * parts
    high = split_sizes(mesh_sizes)[0]
    early_blocks = (high, parts // high) + early.shape
    return pl.pallas_call(
        functools.partial(bottom_kernel, mesh_sizes),
        grid=(nodes // BLOCK,),
        in_specs=[
            lanes(units, BLOCK),
            lanes(units, BLOCK),
            whole(returned.shape),
            whole(send_row.shape),
            lanes(width, BLOCK),
            lanes(padded, BLOCK),
            whole(sums_two.shape),
            whole(sums_three.shape),
            whole(early.shape),
        ],
        out_specs=[whole((rows, 128)), whole(early_blocks)],
        out_shape=[
            jax.ShapeDtypeStruct((rows, 128), jnp.bfloat16),
            jax.ShapeDtypeStruct(early_blocks, jnp.bfloat16),
        ],
        scratch_shapes=[
            pltpu.VMEM((units, halo), jnp.bfloat16),
            pltpu.VMEM((units, 128), jnp.float32),
            pltpu.VMEM((2, padded, units), jnp.float32),
            pltpu.VMEM((high,) + early.shape, jnp.bfloat16),
            pltpu.VMEM(early_blocks, jnp.bfloat16),
        ]
        + semaphores()
        + semaphores(),
        compiler_params=params(24, collective),
        name="bottom_layer",
    )(
        state_grad,
        *in_hbm(preact),
        returned,
        send_row,
        *in_hbm(own, mean),
        sums_two,
        sums_three,
        early,
    )


def in_two(value):
    high = value.astype(jnp.bfloat16)
    return high, (value - high.astype(jnp.float32)).astype(jnp.bfloat16)


def product(left, right, dims=(((1,), (0,)), ((), ()))):
    if left.dtype == jnp.bfloat16:
        high, low = in_two(right)
        return dot(left, high, dims) + dot(left, low, dims)
    high, low = in_two(left)
    if right.dtype == jnp.bfloat16:
        return dot(high, right, dims) + dot(low, right, dims)
    right_high, right_low = in_two(right)
    return dot(high, right_high, dims) + (
        dot(high, right_low, dims) + dot(low, right_high, dims)
    )


def moments(turned, first, second):
    first = beta_one * first + (1.0 - beta_one) * turned
    second = beta_two * second + (1.0 - beta_two) * turned * turned
    update = first / (1.0 - beta_one**STEP) / (jnp.sqrt(second / (1.0 - beta_two**STEP)) + epsilon)
    return first, second, update


def share_kernel(
    mesh_sizes,
    late_ref,
    early_ref,
    notes_ref,
    left_two,
    right_two,
    left_three,
    right_three,
    first_two,
    first_three,
    second_two,
    second_three,
    late_out,
    turned_two,
    moved_two,
    turned_three,
    moved_three,
    plane_land,
    part_ref,
    high_land,
    whole_ref,
    *sems,
):
    inward, across, outward = sems[:2], sems[2:4], sems[4:]
    top, _, _, me = split_place(mesh_sizes)
    units = right_two.shape[0]
    kinds = right_three.shape[0]
    share = 1.0 / notes_ref[1]
    greet_split(mesh_sizes)
    split_greeted(mesh_sizes)
    each_plane(
        mesh_sizes,
        lambda other, where: push(late_ref.at[other], plane_land.at[me], inward, where),
    )

    grad = early_ref[:, :units]
    turned = product(product(left_two[...], grad, TRANS_LEFT), right_two[...]) * share
    turned_two[...] = turned

    plane_wait(mesh_sizes, plane_land, inward)
    plane_land[me] = late_ref[me]
    part_ref[...] = jnp.sum(plane_land[...].astype(jnp.float32), axis=0).astype(jnp.bfloat16)
    each_high(
        mesh_sizes, lambda other, where: push(part_ref, high_land.at[top], across, where)
    )

    update = moments(turned, first_two[...], second_two[...])[2]
    moved_two[...] = product(product(left_two[...], update), right_two[...], TRANS_RIGHT)

    high_wait(mesh_sizes, high_land, across)
    high_land[top] = part_ref[...]
    whole_ref[...] = jnp.sum(high_land[...].astype(jnp.float32), axis=0).astype(jnp.bfloat16)
    each_plane(
        mesh_sizes, lambda other, where: push(whole_ref, late_out.at[me], outward, where)
    )

    grad = early_ref[:, units:].astype(jnp.float32).T[:kinds].astype(jnp.bfloat16)
    turned = product(right_three[...], product(grad, left_three[...])) * share
    turned_three[...] = turned
    update = moments(turned, first_three[...], second_three[...])[2]
    moved = product(update, left_three[...], TRANS_RIGHT)
    moved_three[...] = product(right_three[...], moved, TRANS_LEFT)

    plane_wait(mesh_sizes, late_out, outward)
    late_out[me] = whole_ref[...]


def share_sums(late_rows, mesh_sizes, collective, early_all, notes, bases, second_state, third_state):
    high, low, along = split_sizes(mesh_sizes)
    blocks = (low * along, late_rows.shape[0] // (low * along), 128)
    vmem = pl.BlockSpec(memory_space=pltpu.VMEM)
    operands = [early_all, notes, *in_hbm(*bases, second_state[0], third_state[0])]
    operands += in_hbm(second_state[1], third_state[1])
    two = jax.ShapeDtypeStruct(second_state[0].shape, jnp.float32)
    three = jax.ShapeDtypeStruct(third_state[0].shape, jnp.float32)
    return pl.pallas_call(
        functools.partial(share_kernel, mesh_sizes),
        in_specs=[vmem] * (1 + len(operands)),
        out_specs=[vmem] * 5,
        out_shape=[jax.ShapeDtypeStruct(blocks, jnp.bfloat16), two, two, three, three],
        scratch_shapes=[
            pltpu.VMEM(blocks, jnp.bfloat16),
            pltpu.VMEM(blocks[1:], jnp.bfloat16),
            pltpu.VMEM((high,) + blocks[1:], jnp.bfloat16),
            pltpu.VMEM(blocks[1:], jnp.bfloat16),
        ]
        + semaphores()
        + semaphores()
        + semaphores(),
        compiler_params=pltpu.CompilerParams(
            vmem_limit_bytes=32 * MIB, collective_id=collective, has_side_effects=True
        ),
        name="share_sums",
    )(late_rows.reshape(blocks), *operands)


def adam_kernel(
    padded,
    late_ref,
    notes_ref,
    turned_two,
    moved_two,
    turned_three,
    moved_three,
    weight_one,
    weight_two,
    weight_three,
    left_one,
    right_one,
    first_one,
    first_two,
    first_three,
    second_one,
    second_two,
    second_three,
    bias_ref,
    bias_first,
    bias_second,
    *outs,
):
    share = 1.0 / notes_ref[1]
    units = weight_two.shape[1]
    width = weight_one.shape[0] // 2
    kinds = weight_three.shape[0]

    late_rows = late_ref[...].astype(jnp.float32)
    columns = []
    for start in range(0, units, 128):
        row = start // 128 * 2 * padded
        columns.append(
            jnp.concatenate(
                [late_rows[row : row + width], late_rows[row + padded : row + padded + width]]
            )
        )
    grad = jnp.concatenate(columns, axis=1).astype(jnp.bfloat16)
    turned = product(product(left_one[...], grad, TRANS_LEFT), right_one[...]) * share
    new_first, new_second, update = moments(turned, first_one[...], second_one[...])
    outs[1][...] = new_first
    outs[2][...] = new_second
    moved = product(product(left_one[...], update), right_one[...], TRANS_RIGHT)
    outs[0][...] = weight_one[...] - step_rates[0] * moved

    new_first, new_second, _ = moments(turned_two[...], first_two[...], second_two[...])
    outs[3][...] = weight_two[...] - step_rates[1] * moved_two[...]
    outs[4][...] = new_first
    outs[5][...] = new_second
    new_first, new_second, _ = moments(turned_three[...], first_three[...], second_three[...])
    outs[6][...] = weight_three[...] - step_rates[2] * moved_three[...]
    outs[7][...] = new_first
    outs[8][...] = new_second

    row = units // 128 * 2 * padded
    pieces = []
    while len(pieces) * 128 < 2 * units + kinds:
        pieces.append(late_rows[row : row + 1])
        row += 1
    grad = jnp.concatenate(pieces, axis=1)[:, : 2 * units + kinds] * share
    flat = bias_ref.shape
    bias, first, second = (ref[...].reshape(grad.shape) for ref in (bias_ref, bias_first, bias_second))
    new_first, new_second, update = moments(grad, first, second)
    outs[9][...] = (bias - bias_rate * (update + weight_decay * bias)).reshape(flat)
    outs[10][...] = new_first.reshape(flat)
    outs[11][...] = new_second.reshape(flat)


def adam(padded, late_all, notes, steps, *state):
    vmem = pl.BlockSpec(memory_space=pltpu.VMEM)
    order = (0, 5, 8, 1, 6, 9, 2, 7, 10, 11, 12, 13)
    outs = [jax.ShapeDtypeStruct(state[at].shape, jnp.float32) for at in order]
    return pl.pallas_call(
        functools.partial(adam_kernel, padded),
        in_specs=[vmem] * (2 + len(steps) + len(state)),
        out_specs=[vmem] * len(outs),
        out_shape=outs,
        compiler_params=pltpu.CompilerParams(vmem_limit_bytes=32 * MIB),
        name="adam",
    )(late_all, notes, *steps, *in_hbm(*state))


def on_device(
    mesh_sizes,
    features,
    labels,
    seed_rows,
    seed_mask,
    send_rows,
    neighbors_one,
    neighbors_two,
    neighbors_three,
    weight_one,
    weight_two,
    weight_three,
    left_one,
    right_one,
    left_two,
    right_two,
    left_three,
    right_three,
    first_one,
    first_two,
    first_three,
    second_one,
    second_two,
    second_three,
    bias_all,
    bias_first,
    bias_second,
):
    units = weight_one.shape[1]
    classes = weight_three.shape[1]
    halo = send_rows.size
    fans = (neighbors_one.shape[1], neighbors_two.shape[1], neighbors_three.shape[1])
    feats = features.T
    send_row = send_rows.reshape(1, halo)
    weight_three = weight_three.T
    padded_classes = -(-classes // 16) * 16
    seed_slots = (
        padded_classes,
        seed_rows.reshape(1, -1),
        labels.reshape(1, -1),
        seed_mask.reshape(1, -1),
    )

    words_one, got = count_words(
        neighbors_one.T, mesh_sizes, 0, halo, feats=feats, send_row=send_row
    )
    state_one, preact_one, sent, mean_one = hidden_layer(
        words_one, feats, got, weight_one, bias_all, 0, send_row, fans[0]
    )
    words_two, got = count_words(neighbors_two.T, mesh_sizes, 1, halo, sent=sent)
    state_two, preact_two, sent, mean_two = hidden_layer(
        words_two, state_one, got, weight_two, bias_all, units, send_row, fans[1]
    )
    words_three, got, seeds = count_words(
        neighbors_three.T, mesh_sizes, 2, halo, sent=sent, seeds=seed_slots
    )
    grad_three, rows_three, sums_three, notes, table_three, far, halo_grad = last_layer(
        words_three, state_two, got, weight_three, bias_all, 2 * units, seeds, fans[2]
    )
    state_grad, returned, weight_grad = scatter_layer(
        words_three,
        grad_three,
        rows_three,
        weight_three,
        halo_grad,
        mesh_sizes,
        3,
        fans[2],
        tables=(far, table_three),
    )
    grad_two, rows_two, sums_two, halo_grad, early = middle_layer(
        state_grad,
        preact_two,
        returned,
        send_row,
        words_two,
        weight_two,
        state_one,
        mean_two,
        weight_grad,
        notes,
        fans[1],
    )
    state_grad, returned, early_sum, notes = scatter_layer(
        words_two, grad_two, rows_two, weight_two, halo_grad, mesh_sizes, 4, fans[1], early=early
    )
    late_rows, early_all = bottom_layer(
        state_grad,
        preact_one,
        returned,
        send_row,
        feats,
        mean_one,
        sums_two,
        sums_three,
        early_sum,
        mesh_sizes,
        5,
    )
    first_three, second_three = first_three.T, second_three.T
    late_all, *steps = share_sums(
        late_rows,
        mesh_sizes,
        6,
        early_all.reshape(early.shape),
        notes,
        (left_two, right_two, left_three, right_three.T),
        (first_two, second_two),
        (first_three, second_three),
    )
    out = adam(
        mean_one.shape[0],
        late_all.reshape(late_rows.shape),
        notes,
        steps,
        weight_one,
        weight_two,
        weight_three,
        left_one,
        right_one,
        first_one,
        first_two,
        first_three,
        second_one,
        second_two,
        second_three,
        bias_all,
        bias_first,
        bias_second,
    )
    third = [value.T for value in out[6:9]]
    return (*out[:6], *third, *out[9:12], notes[0, 0, 0], notes[1, 0, 0])


def solution(mesh):
    split = P(axes)
    rows = P(axes, None)
    placed = (rows, split, split, split, rows, rows, rows, rows) + (P(),) * 18
    mesh_sizes = (mesh.shape[axes[0]], mesh.shape[axes[1]])
    return jax.shard_map(
        functools.partial(on_device, mesh_sizes),
        mesh=mesh,
        in_specs=placed,
        out_specs=(P(),) * 14,
        check_vma=False,
    )
```

```python
import functools

import jax
import jax.numpy as jnp
from jax import lax
from jax.experimental import pallas as pl
from jax.experimental.pallas import tpu as pltpu
from jax.sharding import PartitionSpec as P

STEP = 10


beta_one = 0.9
beta_two = 0.999
epsilon = 1e-08
step_rates = (0.05, 0.5, 1.0)
bias_rate = 0.05
weight_decay = 0.01

axes = ("dom", "rep")
WORDS = 4
SLOTS = 8
RUN = 48
UNIT = SLOTS * RUN
BLOCK = 1024
LIST_BLOCK = 512
MIB = 1024 * 1024
TRANS_LEFT = (((0,), (0,)), ((), ()))
TRANS_RIGHT = (((1,), (1,)), ((), ()))


def dot(left, right, dims=(((1,), (0,)), ((), ()))):
    return lax.dot_general(left, right, dims, preferred_element_type=jnp.float32)


def params(limit, collective=None):
    remote = {} if collective is None else dict(collective_id=collective, has_side_effects=True)
    return pltpu.CompilerParams(
        dimension_semantics=("arbitrary",), vmem_limit_bytes=limit * MIB, **remote
    )


def in_hbm(*arrays):
    return [pltpu.with_memory_space_constraint(array, pltpu.HBM) for array in arrays]


def whole(shape):
    return pl.BlockSpec(shape, lambda i: (0,) * len(shape))


def lanes(rows, width):
    return pl.BlockSpec((rows, width), lambda i: (0, i))


def floor_over(value, size):
    return ((value.astype(jnp.float32) + 0.5) * (1.0 / size)).astype(jnp.int32)


def words_layer(near_ref, out_ref, place_ref, field_ref):
    fanout, block = near_ref.shape
    span = out_ref.shape[0] // WORDS
    near = near_ref[...]
    unit = floor_over(near, UNIT)
    rest = near - unit * UNIT
    slot = floor_over(rest, RUN)
    word = floor_over(unit, span // RUN)
    place = (unit - word * (span // RUN)) * RUN + rest - slot * RUN
    bit = jnp.left_shift(jnp.int32(1), slot * 4)
    parts = [jnp.where(word == k, bit, 0) for k in range(WORDS)]
    totals = [jnp.zeros_like(bit) for _ in range(WORDS)]
    for g in range(fanout):
        same = place == place[g : g + 1]
        for k in range(WORDS):
            totals[k] = totals[k] + jnp.where(same, parts[k][g : g + 1], 0)
    place_ref[:fanout, :] = place
    for k in range(WORDS):
        field_ref[k, :fanout, :] = totals[k]
    chunk = RUN
    for tile in range(0, block, 128):
        cols = slice(tile, tile + 128)
        for start in range(0, span, chunk):
            rows = lax.broadcasted_iota(jnp.int32, (chunk, 128), 0) + start
            sums = [jnp.zeros((chunk, 128), jnp.int32) for _ in range(WORDS)]
            for g in range(fanout):
                hit = rows == place_ref[g : g + 1, cols]
                for k in range(WORDS):
                    sums[k] = jnp.where(hit, field_ref[k, g : g + 1, cols], sums[k])
            for k in range(WORDS):
                out_ref[k * span + start : k * span + start + chunk, cols] = sums[k]


def my_index(mesh_sizes):
    return lax.axis_index(axes[0]) * mesh_sizes[1] + lax.axis_index(axes[1])


def each_peer(mesh_sizes, act):
    across, along = mesh_sizes
    row, column = lax.axis_index(axes[0]), lax.axis_index(axes[1])

    def wrapped(value, size):
        return jnp.where(value >= size, value - size, value)

    def line(down, carry):
        other = wrapped(row + down, across)
        for ahead in range(along):
            place = wrapped(column + ahead, along)
            act(other * along + place, (other, place))
        return carry

    for ahead in range(1, along):
        place = wrapped(column + ahead, along)
        act(row * along + place, (row, place))
    lax.fori_loop(1, across, line, 0)


def greet(mesh_sizes):
    barrier = pltpu.get_barrier_semaphore()

    def tell(index, where):
        pl.semaphore_signal(
            barrier, inc=1, device_id=where, device_id_type=pl.DeviceIdType.MESH
        )

    each_peer(mesh_sizes, tell)


def all_greeted(mesh_sizes):
    pl.semaphore_wait(pltpu.get_barrier_semaphore(), mesh_sizes[0] * mesh_sizes[1] - 1)


def send_blocks(mesh_sizes, out_ref, in_ref, send_sem, recv_sem):
    me = my_index(mesh_sizes)

    def send(index, where):
        pltpu.make_async_remote_copy(
            src_ref=out_ref.at[index],
            dst_ref=in_ref.at[me],
            send_sem=send_sem,
            recv_sem=recv_sem,
            device_id=where,
            device_id_type=pl.DeviceIdType.MESH,
        ).start()

    each_peer(mesh_sizes, send)


def send_all(mesh_sizes, own_ref, in_ref, send_sem, recv_sem):
    me = my_index(mesh_sizes)

    def send(index, where):
        pltpu.make_async_remote_copy(
            src_ref=own_ref,
            dst_ref=in_ref.at[me],
            send_sem=send_sem,
            recv_sem=recv_sem,
            device_id=where,
            device_id_type=pl.DeviceIdType.MESH,
        ).start()

    each_peer(mesh_sizes, send)


def wait_moves(mesh_sizes, out_ref, in_ref, send_sem, recv_sem):
    others = pl.ds(0, mesh_sizes[0] * mesh_sizes[1] - 1)
    copy = pltpu.make_async_remote_copy(
        src_ref=in_ref.at[others],
        dst_ref=in_ref.at[others],
        send_sem=send_sem,
        recv_sem=recv_sem,
        device_id=(lax.axis_index(axes[0]), lax.axis_index(axes[1])),
        device_id_type=pl.DeviceIdType.MESH,
    )
    copy.wait_send()
    copy.wait_recv()


def split_sizes(mesh_sizes):
    across, along = mesh_sizes
    high = 4 if across % 4 == 0 else 1
    return high, across // high, along


def split_place(mesh_sizes):
    _, low, along = split_sizes(mesh_sizes)
    row, column = lax.axis_index(axes[0]), lax.axis_index(axes[1])
    top = row // low
    return top, row - top * low, column, (row - top * low) * along + column


def each_high(mesh_sizes, act):
    high, low, _ = split_sizes(mesh_sizes)
    top, bottom, column, _ = split_place(mesh_sizes)
    for ahead in range(1, high):
        other = top + ahead
        other = jnp.where(other >= high, other - high, other)
        act(other, (other * low + bottom, column))


def each_plane(mesh_sizes, act):
    _, low, along = split_sizes(mesh_sizes)
    top, bottom, column, _ = split_place(mesh_sizes)
    for down in range(low):
        for ahead in range(along):
            if down == 0 and ahead == 0:
                continue
            line = bottom + down
            line = jnp.where(line >= low, line - low, line)
            place = column + ahead
            place = jnp.where(place >= along, place - along, place)
            act(line * along + place, (top * low + line, place))


def greet_split(mesh_sizes):
    barrier = pltpu.get_barrier_semaphore()

    def tell(index, where):
        pl.semaphore_signal(
            barrier, inc=1, device_id=where, device_id_type=pl.DeviceIdType.MESH
        )

    each_high(mesh_sizes, tell)
    each_plane(mesh_sizes, tell)


def split_greeted(mesh_sizes):
    high, low, along = split_sizes(mesh_sizes)
    pl.semaphore_wait(pltpu.get_barrier_semaphore(), high - 1 + low * along - 1)


def push(src_ref, dst_ref, sems, where):
    pltpu.make_async_remote_copy(
        src_ref=src_ref,
        dst_ref=dst_ref,
        send_sem=sems[0],
        recv_sem=sems[1],
        device_id=where,
        device_id_type=pl.DeviceIdType.MESH,
    ).start()


def wait_pushed(ref, sems):
    copy = pltpu.make_async_remote_copy(
        src_ref=ref,
        dst_ref=ref,
        send_sem=sems[0],
        recv_sem=sems[1],
        device_id=(lax.axis_index(axes[0]), lax.axis_index(axes[1])),
        device_id_type=pl.DeviceIdType.MESH,
    )
    copy.wait_send()
    copy.wait_recv()


def high_start(mesh_sizes, sent_ref, relay_ref, sems):
    top = split_place(mesh_sizes)[0]
    each_high(
        mesh_sizes, lambda other, where: push(sent_ref.at[other], relay_ref.at[top], sems, where)
    )


def high_wait(mesh_sizes, relay_ref, sems):
    high = split_sizes(mesh_sizes)[0]
    if high > 1:
        wait_pushed(relay_ref.at[pl.ds(0, high - 1)], sems)


def plane_wait(mesh_sizes, land_ref, sems):
    _, low, along = split_sizes(mesh_sizes)
    wait_pushed(land_ref.at[pl.ds(0, low * along - 1)], sems)


def plane_blocks(mesh_sizes, relay_ref, land_ref, sems):
    me = split_place(mesh_sizes)[3]
    each_plane(
        mesh_sizes,
        lambda other, where: push(relay_ref.at[:, other], land_ref.at[:, me], sems, where),
    )


def plane_blocks_wait(mesh_sizes, land_ref, sems):
    _, low, along = split_sizes(mesh_sizes)
    wait_pushed(land_ref.at[:, pl.ds(0, low * along - 1)], sems)


NOTES = 120


def put_terms(rows, values):
    lane = lax.broadcasted_iota(jnp.int32, rows.shape, 1)
    for index, value in enumerate(values):
        for at in range(3):
            term = value.astype(jnp.bfloat16).astype(jnp.float32)
            rows = jnp.where(lane == NOTES + 3 * index + at, term, rows)
            value = value - term
    return rows


def take_terms(rows):
    lane = lax.broadcasted_iota(jnp.int32, rows.shape, 1)
    values = []
    for index in range(2):
        first = NOTES + 3 * index
        mine = (lane >= first) & (lane < first + 3)
        values.append(jnp.sum(jnp.where(mine, rows, 0.0), axis=1, keepdims=True))
    return values


def semaphores():
    return [pltpu.SemaphoreType.DMA, pltpu.SemaphoreType.DMA]


def chosen_nodes(send_row, start, count):
    node = lax.broadcasted_iota(jnp.int32, (count, send_row.shape[1]), 0) + start
    return jnp.where(node == send_row, 1.0, 0.0).astype(jnp.bfloat16)


def words_kernel(mesh_sizes, kind, near_ref, *refs):
    refs = list(refs)
    if kind == "features":
        feats_ref, send_ref, out_ref, got_ref, sent_ref = refs[:5]
        refs = refs[5:]
    elif kind == "seeds":
        sent_ref, slots_ref, labels_ref, mask_ref, out_ref, got_ref, seeds_ref = refs[:7]
        refs = refs[7:]
    else:
        sent_ref, out_ref, got_ref = refs[:3]
        refs = refs[3:]
    place_ref, field_ref, land_ref, send_sem, recv_sem = refs
    step = pl.program_id(0)
    block = near_ref.shape[1]
    moves = (mesh_sizes, sent_ref, land_ref, send_sem, recv_sem)

    @pl.when(step == 0)
    def _():
        greet(mesh_sizes)

    if kind == "features":

        @pl.when(step == 0)
        def _():
            width, nodes = feats_ref.shape
            halo = send_ref.shape[1]
            total = jnp.zeros((width, halo), jnp.float32)
            for start in range(0, nodes, block):
                chosen = chosen_nodes(send_ref[...], start, block)
                total = total + dot(feats_ref[:, start : start + block], chosen)
            padded = sent_ref.shape[2]
            total = jnp.concatenate([total, jnp.zeros((padded - width, halo), jnp.float32)])
            sent_ref[...] = total.T.astype(jnp.bfloat16).reshape(sent_ref.shape)

    if kind == "seeds":
        classes = seeds_ref.shape[0]
        slots = slots_ref.shape[1]
        label = lax.broadcasted_iota(jnp.int32, (classes, slots), 0)
        marked = jnp.where((label == labels_ref[...]) & (mask_ref[...] != 0), 1.0, 0.0)
        chosen = chosen_nodes(slots_ref[...], step * block, block)
        seeds_ref[...] = dot(marked.astype(jnp.bfloat16), chosen, TRANS_RIGHT)

    words_layer(near_ref, out_ref, place_ref, field_ref)

    @pl.when(step == 0)
    def _():
        all_greeted(mesh_sizes)
        send_blocks(*moves)

    @pl.when(step == pl.num_programs(0) - 1)
    def _():
        me = my_index(mesh_sizes)
        wait_moves(*moves)
        land_ref[me] = sent_ref[me]
        got_ref[...] = land_ref[...]


def count_words(near, mesh_sizes, collective, halo, sent=None, feats=None, send_row=None, seeds=None):
    fanout, nodes = near.shape
    parts = mesh_sizes[0] * mesh_sizes[1]
    height = (nodes + halo) // SLOTS
    in_specs = [lanes(fanout, LIST_BLOCK)]
    operands = [near]
    scratch = []
    if sent is None:
        kind = "features"
        blocks = (parts, halo // parts, -(-feats.shape[0] // 128) * 128)
        in_specs += [whole(feats.shape), whole(send_row.shape)]
        operands += [*in_hbm(feats), send_row]
        scratch.append(pltpu.VMEM(blocks, jnp.bfloat16))
    else:
        kind = "plain"
        blocks = (parts, halo // parts, sent.shape[1])
        in_specs.append(whole(blocks))
        operands.append(sent.reshape(blocks))
    out_specs = [lanes(height, LIST_BLOCK), whole(blocks)]
    out_shape = [
        pltpu.HBM((height, nodes), jnp.int32),
        jax.ShapeDtypeStruct(blocks, jnp.bfloat16),
    ]
    if seeds is not None:
        kind = "seeds"
        classes, slots, labels, mask = seeds
        in_specs += [whole(slots.shape)] * 3
        operands += [slots, labels, mask]
        out_specs.append(lanes(classes, LIST_BLOCK))
        out_shape.append(jax.ShapeDtypeStruct((classes, nodes), jnp.float32))
    return pl.pallas_call(
        functools.partial(words_kernel, mesh_sizes, kind),
        grid=(nodes // LIST_BLOCK,),
        in_specs=in_specs,
        out_specs=out_specs,
        out_shape=out_shape,
        scratch_shapes=scratch
        + [
            pltpu.VMEM((16, LIST_BLOCK), jnp.int32),
            pltpu.VMEM((WORDS, 16, LIST_BLOCK), jnp.int32),
            pltpu.VMEM(blocks, jnp.bfloat16),
        ]
        + semaphores(),
        compiler_params=params(20, collective),
        name="count_words",
    )(*in_hbm(*operands[:1]), *operands[1:])


def field(words, slot):
    if slot == SLOTS - 1:
        picked = lax.shift_right_logical(words, 4 * slot)
    else:
        picked = words & (15 << (4 * slot))
    return picked.astype(jnp.float32).astype(jnp.bfloat16)


def slot_scale(slot):
    return 1.0 if slot == SLOTS - 1 else 2.0 ** (-4 * slot)


def spread_unit(words_ref, word_row, counts_ref, count_row):
    for start in range(0, RUN, 16):
        for tile in range(0, words_ref.shape[1], 256):
            cols = slice(tile, tile + 256)
            words = words_ref[word_row + start : word_row + start + 16, cols]
            for slot in range(SLOTS):
                row = count_row + slot * RUN + start
                counts_ref[row : row + 16, cols] = field(words, slot)


def gather_product(table_ref, words_ref, counts_ref):
    table = table_ref.shape[1]
    total = None
    for start in range(0, table, 2 * UNIT):
        stop = start + 2 * UNIT
        for row in range(start, stop, UNIT):
            spread_unit(words_ref, row // SLOTS, counts_ref, row)
        term = dot(table_ref[:, start:stop], counts_ref[start:stop, :])
        total = term if total is None else total + term
    return total


def scale_row(table):
    column = lax.broadcasted_iota(jnp.int32, (1, table), 1)
    rest = column - floor_over(column, UNIT) * UNIT
    slot = floor_over(rest, RUN)
    scale = jnp.ones((1, table), jnp.float32)
    for k in range(SLOTS - 1):
        scale = jnp.where(slot == k, slot_scale(k), scale)
    return scale


def column_of(row):
    return jnp.broadcast_to(row, (128, row.shape[1])).T


def late(rows, width):
    return pl.BlockSpec((rows, width), lambda i: (0, jnp.maximum(i - 1, 0)))


def now(rows, width, steps):
    return pl.BlockSpec((rows, width), lambda i: (0, jnp.minimum(i, steps - 1)))


def hidden_kernel(
    fanout,
    bias_start,
    words_ref,
    own_ref,
    own_block,
    got_ref,
    weight_ref,
    bias_ref,
    send_ref,
    state_ref,
    preact_ref,
    sent_ref,
    extra_ref,
    table_ref,
    counts_ref,
    picked_ref,
    mean_ref,
    self_ref,
    near_ref,
    bias_col,
):
    step = pl.program_id(0)
    last = pl.num_programs(0) - 1
    width, nodes = own_ref.shape
    units, block = state_ref.shape
    padded = mean_ref.shape[0]

    @pl.when(step == 0)
    def _():
        if table_ref.shape[0] > width:
            table_ref[...] = jnp.zeros_like(table_ref)
        got = got_ref[...].reshape(-1, got_ref.shape[2]).T[:width]
        scale = scale_row(table_ref.shape[1])
        own = own_ref[...].astype(jnp.float32) * scale[:, :nodes]
        table_ref[:width, :nodes] = own.astype(jnp.bfloat16)
        far = got.astype(jnp.float32) * scale[:, nodes:]
        table_ref[:width, nodes:] = far.astype(jnp.bfloat16)
        mean_ref[...] = jnp.zeros_like(mean_ref)
        picked_ref[...] = jnp.zeros_like(picked_ref)
        self_ref[...] = weight_ref[:width, :].T.astype(jnp.bfloat16)
        if padded > width:
            near_ref[...] = jnp.zeros_like(near_ref)
        near_ref[:, :width] = weight_ref[width:, :].T.astype(jnp.bfloat16)
        bias = bias_ref[...].reshape(1, -1)
        bias_col[...] = column_of(bias[:, bias_start : bias_start + units])

    def finish():
        mean = mean_ref[...]
        extra_ref[...] = mean
        preact = dot(self_ref[...], own_block[...]) + dot(near_ref[...], mean) + bias_col[:, :1]
        preact_ref[...] = preact
        active = preact * jax.nn.sigmoid(preact)
        norm = lax.rsqrt(jnp.sum(active * active, axis=0, keepdims=True) + 1e-06)
        state = (active * norm).astype(jnp.bfloat16)
        state_ref[...] = state
        picked_ref[...] += dot(state, chosen_nodes(send_ref[...], (step - 1) * block, block))

    @pl.when(step < last)
    def _():
        finish()
        total = gather_product(table_ref, words_ref, counts_ref)
        mean_ref[...] = (total / fanout).astype(jnp.bfloat16)

    @pl.when(step == last)
    def _():
        finish()
        sent_ref[...] = picked_ref[...].T.astype(jnp.bfloat16)


def hidden_layer(words, own, got, weight, bias, bias_start, send_row, fanout):
    width, nodes = own.shape
    halo = send_row.shape[1]
    table = nodes + halo
    units = weight.shape[1]
    padded = -(-width // 16) * 16
    steps = nodes // BLOCK
    return pl.pallas_call(
        functools.partial(hidden_kernel, fanout, bias_start),
        grid=(steps + 1,),
        in_specs=[
            now(words.shape[0], BLOCK, steps),
            whole(own.shape),
            late(width, BLOCK),
            whole(got.shape),
            whole(weight.shape),
            whole(bias.shape),
            whole(send_row.shape),
        ],
        out_specs=[
            late(units, BLOCK),
            late(units, BLOCK),
            whole((halo, units)),
            late(padded, BLOCK),
        ],
        out_shape=[
            jax.ShapeDtypeStruct((units, nodes), jnp.bfloat16),
            pltpu.HBM((units, nodes), jnp.float32),
            jax.ShapeDtypeStruct((halo, units), jnp.bfloat16),
            pltpu.HBM((padded, nodes), jnp.bfloat16),
        ],
        scratch_shapes=[
            pltpu.VMEM((padded, table), jnp.bfloat16),
            pltpu.VMEM((table, BLOCK), jnp.bfloat16),
            pltpu.VMEM((units, halo), jnp.float32),
            pltpu.VMEM((padded, BLOCK), jnp.bfloat16),
            pltpu.VMEM((units, width), jnp.bfloat16),
            pltpu.VMEM((units, padded), jnp.bfloat16),
            pltpu.VMEM((units, 128), jnp.float32),
        ],
        compiler_params=params(40),
        name="hidden_layer",
    )(*in_hbm(words), own, own, got, *in_hbm(weight, bias), send_row)


def far_start(nodes):
    return nodes // UNIT * UNIT


def unscaled(sums, fanout):
    pieces = []
    for row in range(0, sums.shape[0], RUN):
        slot = row // RUN % SLOTS
        pieces.append((sums[row : row + RUN] * (slot_scale(slot) / fanout)).astype(jnp.bfloat16))
    return jnp.concatenate(pieces)


def last_kernel(
    fanout,
    bias_start,
    words_ref,
    own_ref,
    own_block,
    got_ref,
    weight_ref,
    bias_ref,
    seeds_ref,
    grad_ref,
    rows_ref,
    sums_ref,
    notes_ref,
    table_out,
    far_ref,
    halo_ref,
    reduced_ref,
    counts_ref,
    both_ref,
    self_ref,
    near_ref,
    bias_col,
    far_sums,
):
    step = pl.program_id(0)
    last = pl.num_programs(0) - 1
    classes = self_ref.shape[0]
    width, nodes = own_ref.shape
    kinds = weight_ref.shape[0]
    halo = far_ref.shape[0]
    first = far_start(nodes)

    @pl.when(step == 0)
    def _():
        table_out[:, :nodes] = own_ref[...]
        table_out[:, nodes:] = got_ref[...].reshape(halo, width).T
        more = jnp.zeros((classes - kinds, 2 * width), jnp.float32)
        weight = jnp.concatenate([weight_ref[...], more]).astype(jnp.bfloat16)
        self_ref[...] = weight[:, :width]
        near_ref[...] = weight[:, width:]
        rest = jnp.full((1, classes - kinds), -1e30, jnp.float32)
        bias = bias_ref[...].reshape(1, -1)
        bias_col[...] = column_of(
            jnp.concatenate([bias[:, bias_start : bias_start + kinds], rest], axis=1)
        )
        reduced = dot(near_ref[...], table_out[...]) * scale_row(table_out.shape[1])
        high = reduced.astype(jnp.bfloat16)
        reduced_ref[:classes, :] = high
        reduced_ref[classes:, :] = (reduced - high.astype(jnp.float32)).astype(jnp.bfloat16)
        both_ref[...] = jnp.zeros_like(both_ref)
        counts_ref[first:, :] = jnp.zeros_like(counts_ref[first:, :])

    @pl.when(step <= 1)
    def _():
        sums_ref[...] = jnp.zeros_like(sums_ref)
        notes_ref[...] = jnp.zeros_like(notes_ref)
        far_sums[...] = jnp.zeros_like(far_sums)

    def finish():
        near_part = (both_ref[:classes, :] + both_ref[classes:, :]) / fanout
        logits = dot(self_ref[...], own_block[...]) + near_part + bias_col[:, :1]
        top = jnp.max(logits, axis=0, keepdims=True)
        powers = jnp.exp(logits - top)
        total = jnp.sum(powers, axis=0, keepdims=True)
        normer = jnp.log(total) + top
        seeds = seeds_ref[...]
        uses = jnp.sum(seeds, axis=0, keepdims=True)
        grad = (powers / total * uses - seeds).astype(jnp.bfloat16)
        grad_ref[...] = grad
        loss = uses * normer - jnp.sum(seeds * logits, axis=0, keepdims=True)
        sums_ref[...] += jnp.sum(grad.astype(jnp.float32), axis=1, keepdims=True)
        notes_ref[:8, :] += jnp.sum(loss)
        notes_ref[8:, :] += jnp.sum(uses)
        rows = grad.T
        rows_ref[...] = rows
        far_sums[...] += dot(counts_ref[first:, :], rows)

    @pl.when(step < last)
    def _():
        finish()
        both_ref[...] = gather_product(reduced_ref, words_ref, counts_ref)

    @pl.when(step == last)
    def _():
        finish()
        sums = unscaled(far_sums[...], fanout)[nodes - first :]
        far_ref[...] = sums
        halo_ref[...] = dot(sums, near_ref[...]).astype(jnp.bfloat16)


def last_layer(words, own, got, weight, bias, bias_start, seeds, fanout):
    width, nodes = own.shape
    halo = got.shape[0] * got.shape[1]
    table = nodes + halo
    classes = seeds.shape[0]
    steps = nodes // BLOCK
    far_height = table - far_start(nodes)
    return pl.pallas_call(
        functools.partial(last_kernel, fanout, bias_start),
        grid=(steps + 1,),
        in_specs=[
            now(words.shape[0], BLOCK, steps),
            whole(own.shape),
            late(width, BLOCK),
            whole(got.shape),
            whole(weight.shape),
            whole(bias.shape),
            late(classes, BLOCK),
        ],
        out_specs=[
            late(classes, BLOCK),
            pl.BlockSpec((BLOCK, classes), lambda i: (jnp.maximum(i - 1, 0), 0)),
            whole((classes, 128)),
            whole((16, 128)),
            whole((width, table)),
            whole((halo, classes)),
            whole((halo, width)),
        ],
        out_shape=[
            jax.ShapeDtypeStruct((classes, nodes), jnp.bfloat16),
            jax.ShapeDtypeStruct((nodes, classes), jnp.bfloat16),
            jax.ShapeDtypeStruct((classes, 128), jnp.float32),
            jax.ShapeDtypeStruct((16, 128), jnp.float32),
            jax.ShapeDtypeStruct((width, table), jnp.bfloat16),
            jax.ShapeDtypeStruct((halo, classes), jnp.bfloat16),
            jax.ShapeDtypeStruct((halo, width), jnp.bfloat16),
        ],
        scratch_shapes=[
            pltpu.VMEM((2 * classes, table), jnp.bfloat16),
            pltpu.VMEM((table, BLOCK), jnp.bfloat16),
            pltpu.VMEM((2 * classes, BLOCK), jnp.float32),
            pltpu.VMEM((classes, width), jnp.bfloat16),
            pltpu.VMEM((classes, width), jnp.bfloat16),
            pltpu.VMEM((classes, 128), jnp.float32),
            pltpu.VMEM((far_height, classes), jnp.float32),
        ],
        compiler_params=params(40),
        name="last_layer",
    )(*in_hbm(words), own, own, got, *in_hbm(weight, bias), seeds)


def scatter_kernel(mesh_sizes, fanout, flipped, words_ref, grad_ref, rows_ref, *refs):
    refs = list(refs)
    if flipped:
        weight_in, halo_ref, far_ref, table_ref, far_table = refs[:5]
        state_ref, got_ref, weight_ref = refs[5:8]
        refs = refs[8:]
    else:
        weight_in, halo_ref, early_ref = refs[:3]
        state_ref, got_ref, early_sum, loss_ref, count_ref = refs[3:8]
        refs = refs[8:]
    padded_ref, counts_ref, sums_ref, self_ref, near_ref, relay_ref, land_ref = refs[:7]
    if flipped:
        high_sems, plane_sems = refs[7:9], refs[9:11]
    else:
        early_relay, early_part, early_land, early_own, early_back = refs[7:12]
        high_sems, plane_sems = refs[12:14], refs[14:16]
        early_high, early_plane, back_sems = refs[16:18], refs[18:20], refs[20:22]
    step = pl.program_id(0)
    units, nodes = grad_ref.shape
    width = state_ref.shape[0]
    span = words_ref.shape[0]
    part = span * SLOTS
    steps = -(-nodes // part)

    @pl.when(step == 0)
    def _():
        greet_split(mesh_sizes)
        for k in range(steps):
            start = k * part
            stop = min(start + part, nodes)
            padded_ref[k, :, : stop - start] = grad_ref[:, start:stop]
            if stop < start + part:
                padded_ref[k, :, stop - start :] = jnp.zeros(
                    (units, start + part - stop), jnp.bfloat16
                )
        weight = weight_in[...]
        if flipped:
            more = jnp.zeros((units - weight.shape[0], 2 * width), jnp.float32)
            weight = jnp.concatenate([weight, more]).T
            weight_ref[:width, :] = jnp.zeros((width, units), jnp.float32)
            weight_ref[width:, :] = dot(far_table[...], far_ref[...])
        self_ref[...] = weight[:width].astype(jnp.bfloat16)
        near_ref[...] = weight[width:].astype(jnp.bfloat16)
        sums_ref[...] = jnp.zeros_like(sums_ref)
        split_greeted(mesh_sizes)
        high_start(mesh_sizes, halo_ref, relay_ref, high_sems)
        if not flipped:
            plane_blocks(mesh_sizes, early_ref, early_relay, early_plane)

    @pl.when(step == steps // 2)
    def _():
        top, _, _, me = split_place(mesh_sizes)
        high_wait(mesh_sizes, relay_ref, high_sems)
        relay_ref[top] = halo_ref[top]
        plane_blocks(mesh_sizes, relay_ref, land_ref, plane_sems)
        if not flipped:
            plane_blocks_wait(mesh_sizes, early_relay, early_plane)
            early_relay[:, me] = early_ref[:, me]
            total = jnp.sum(early_relay[...].astype(jnp.float32), axis=1)
            shape = total.shape
            total = total.reshape(-1, shape[2])
            last = total[:, -128:]
            total = jnp.concatenate([total[:, :-128], put_terms(last, take_terms(last))], axis=1)
            early_part[...] = total.astype(jnp.bfloat16).reshape(shape)
            high_start(mesh_sizes, early_part, early_land, early_high)

    if not flipped:

        @pl.when(step == steps - 1)
        def _():
            top = split_place(mesh_sizes)[0]
            high_wait(mesh_sizes, early_land, early_high)
            early_land[top] = early_part[top]
            total = jnp.sum(early_land[...].astype(jnp.float32), axis=0)
            early_own[...] = total.astype(jnp.bfloat16)
            loss, count = take_terms(total[:, -128:])
            loss_ref[...] = loss[:1]
            count_ref[...] = count[:1]
            each_high(
                mesh_sizes,
                lambda other, where: push(early_own, early_back.at[top], back_sems, where),
            )

    def add(row):
        spread_unit(words_ref, row // SLOTS, counts_ref, row)
        added = dot(counts_ref[row : row + UNIT, :], rows_ref[...])
        sums_ref[row : row + UNIT, :] = unscaled(added, fanout)

    beyond = nodes - (steps - 1) * part
    ending = -(-beyond // UNIT) * UNIT
    for row in range(0, ending, UNIT):
        add(row)
    if ending < part:

        @pl.when(step < steps - 1)
        def _():
            for row in range(ending, part, UNIT):
                add(row)

    if flipped and beyond < part:

        @pl.when(step == steps - 1)
        def _():
            sums_ref[beyond:, :] = jnp.zeros((part - beyond, units), jnp.bfloat16)

    sums = sums_ref[...]
    own_grad = padded_ref[step]
    state_ref[...] = dot(near_ref[...], sums, TRANS_RIGHT) + dot(self_ref[...], own_grad)
    if flipped:
        weight_ref[:width, :] += dot(table_ref[...], own_grad, TRANS_RIGHT)
        weight_ref[width:, :] += dot(table_ref[...], sums)

    @pl.when(step == steps - 1)
    def _():
        me = split_place(mesh_sizes)[3]
        plane_blocks_wait(mesh_sizes, land_ref, plane_sems)
        land_ref[:, me] = relay_ref[:, me]
        got_ref[...] = land_ref[...]
        if not flipped:
            top = split_place(mesh_sizes)[0]
            high_wait(mesh_sizes, early_back, back_sems)
            early_back[top] = early_own[...]
            early_sum[...] = early_back[...]


def scatter_layer(
    words, grad, rows, weight, halo_rows, mesh_sizes, collective, fanout, tables=None, early=None
):
    units, nodes = grad.shape
    halo, width = halo_rows.shape
    parts = mesh_sizes[0] * mesh_sizes[1]
    flipped = tables is not None
    total = nodes + halo
    part = total // WORDS
    span = part // SLOTS
    steps = -(-nodes // part)
    high = split_sizes(mesh_sizes)[0]
    blocks = (high, parts // high, halo // parts, width)
    in_specs = [
        pl.BlockSpec((span, nodes), lambda i: (i, 0)),
        whole(grad.shape),
        whole(rows.shape),
        whole(weight.shape),
        whole(blocks),
    ]
    operands = [words, grad, rows, weight, halo_rows.reshape(blocks)]
    out_specs = [lanes(width, part), whole(blocks)]
    out_shape = [
        jax.ShapeDtypeStruct((width, total), jnp.float32),
        jax.ShapeDtypeStruct(blocks, jnp.bfloat16),
    ]
    if flipped:
        far, table = tables
        in_specs += [
            whole(far.shape),
            lanes(width, part),
            pl.BlockSpec((width, halo), lambda i: (0, nodes // halo)),
        ]
        operands += [far, table, table]
        out_specs.append(whole((2 * width, units)))
        out_shape.append(jax.ShapeDtypeStruct((2 * width, units), jnp.float32))
        scratch = semaphores() + semaphores()
    else:
        early_blocks = (high, parts // high, early.shape[0] // parts, early.shape[1])
        in_specs.append(whole(early_blocks))
        operands.append(early.reshape(early_blocks))
        summed = (high,) + early_blocks[2:]
        out_specs += [whole(summed), whole((1, 1)), whole((1, 1))]
        out_shape += [
            jax.ShapeDtypeStruct(summed, jnp.bfloat16),
            jax.ShapeDtypeStruct((1, 1), jnp.float32),
            jax.ShapeDtypeStruct((1, 1), jnp.float32),
        ]
        scratch = [
            pltpu.VMEM(early_blocks, jnp.bfloat16),
            pltpu.VMEM(summed, jnp.bfloat16),
            pltpu.VMEM(summed, jnp.bfloat16),
            pltpu.VMEM(summed[1:], jnp.bfloat16),
            pltpu.VMEM(summed, jnp.bfloat16),
        ]
        scratch += semaphores() * 5
    return pl.pallas_call(
        functools.partial(scatter_kernel, mesh_sizes, fanout, flipped),
        grid=(steps,),
        in_specs=in_specs,
        out_specs=out_specs,
        out_shape=out_shape,
        scratch_shapes=[
            pltpu.VMEM((steps, units, part), jnp.bfloat16),
            pltpu.VMEM((part, nodes), jnp.bfloat16),
            pltpu.VMEM((part, units), jnp.bfloat16),
            pltpu.VMEM((width, units), jnp.bfloat16),
            pltpu.VMEM((width, units), jnp.bfloat16),
            pltpu.VMEM(blocks, jnp.bfloat16),
            pltpu.VMEM(blocks, jnp.bfloat16),
        ]
        + scratch,
        compiler_params=params(36, collective),
        name="scatter_layer",
    )(*in_hbm(words), *operands[1:3], *in_hbm(weight), *operands[4:])


def active_grad(step, state_ref, preact_ref, back_ref, send_ref):
    block = state_ref.shape[1]
    chosen = chosen_nodes(send_ref[...], step * block, block)
    upper = state_ref[...] + dot(back_ref[...], chosen, TRANS_RIGHT)
    preact = preact_ref[...]
    gate = jax.nn.sigmoid(preact)
    active = preact * gate
    norm = lax.rsqrt(jnp.sum(active * active, axis=0, keepdims=True) + 1e-06)
    along = jnp.sum(active * upper, axis=0, keepdims=True)
    inner = norm * upper - active * (norm * norm * norm * along)
    return (inner * (gate * (1.0 + preact * (1.0 - gate)))).astype(jnp.bfloat16)


def middle_kernel(
    fanout,
    state_ref,
    preact_ref,
    returned_ref,
    send_ref,
    words_ref,
    weight_ref,
    own_block,
    mean_block,
    above_ref,
    notes_ref,
    grad_ref,
    rows_ref,
    sums_ref,
    halo_ref,
    early_ref,
    back_ref,
    counts_ref,
    far_sums,
    total_ref,
):
    step = pl.program_id(0)
    units, block = state_ref.shape
    halo = halo_ref.shape[0]
    nodes = block * pl.num_programs(0)
    first = far_start(nodes)
    part = (nodes + halo) // WORDS

    @pl.when(step == 0)
    def _():
        back_ref[...] = returned_ref[...].reshape(halo, units).T
        sums_ref[...] = jnp.zeros_like(sums_ref)
        far_sums[...] = jnp.zeros_like(far_sums)
        total_ref[...] = jnp.zeros_like(total_ref)

    base = first // part * part
    for row in range(first, nodes + halo, UNIT):
        spread_unit(words_ref, (row - base) // SLOTS, counts_ref, row - first)
    grad = active_grad(step, state_ref, preact_ref, back_ref, send_ref)
    grad_ref[...] = grad
    sums_ref[...] += jnp.sum(grad.astype(jnp.float32), axis=1, keepdims=True)
    rows = grad.T
    rows_ref[...] = rows
    far_sums[...] += dot(counts_ref[...], rows)
    width = own_block.shape[0]
    total_ref[:width, :] += dot(own_block[...], rows)
    total_ref[width:, :] += dot(mean_block[...], rows)

    @pl.when(step == pl.num_programs(0) - 1)
    def _():
        near = weight_ref[units:, :].T.astype(jnp.bfloat16)
        sums = unscaled(far_sums[...], fanout)[nodes - first :]
        halo_ref[...] = dot(sums, near).astype(jnp.bfloat16)
        early_ref[:, :units] = total_ref[...].astype(jnp.bfloat16)
        height, narrow = above_ref.shape
        above = jnp.concatenate(
            [above_ref[...], jnp.zeros((height, 128 - narrow), jnp.float32)], axis=1
        )
        above = put_terms(above, [notes_ref[0:1, 0:1], notes_ref[8:9, 0:1]])
        early_ref[:, units:] = above.astype(jnp.bfloat16)


def middle_layer(
    state_grad, preact, returned, send_row, words, weight, own, mean, above, notes, fanout
):
    units, nodes = preact.shape
    width = own.shape[0]
    wide = units + 128
    halo = send_row.shape[1]
    part = (nodes + halo) // WORDS
    span = part // SLOTS
    far_words = WORDS - far_start(nodes) // part
    far_height = nodes + halo - far_start(nodes)
    return pl.pallas_call(
        functools.partial(middle_kernel, fanout),
        grid=(nodes // BLOCK,),
        in_specs=[
            lanes(units, BLOCK),
            lanes(units, BLOCK),
            whole(returned.shape),
            whole(send_row.shape),
            pl.BlockSpec((far_words * span, BLOCK), lambda i: (WORDS // far_words - 1, i)),
            whole(weight.shape),
            lanes(width, BLOCK),
            lanes(width, BLOCK),
            whole(above.shape),
            whole(notes.shape),
        ],
        out_specs=[
            lanes(units, BLOCK),
            pl.BlockSpec((BLOCK, units), lambda i: (i, 0)),
            whole((units, 128)),
            whole((halo, units)),
            whole((2 * width, wide)),
        ],
        out_shape=[
            jax.ShapeDtypeStruct((units, nodes), jnp.bfloat16),
            jax.ShapeDtypeStruct((nodes, units), jnp.bfloat16),
            jax.ShapeDtypeStruct((units, 128), jnp.float32),
            jax.ShapeDtypeStruct((halo, units), jnp.bfloat16),
            jax.ShapeDtypeStruct((2 * width, wide), jnp.bfloat16),
        ],
        scratch_shapes=[
            pltpu.VMEM((units, halo), jnp.bfloat16),
            pltpu.VMEM((far_height, BLOCK), jnp.bfloat16),
            pltpu.VMEM((far_height, units), jnp.float32),
            pltpu.VMEM((2 * width, units), jnp.float32),
        ],
        compiler_params=params(30),
        name="middle_layer",
    )(
        state_grad,
        *in_hbm(preact),
        returned,
        send_row,
        *in_hbm(words, weight),
        own,
        *in_hbm(mean),
        above,
        notes,
    )


def in_two(value):
    high = value.astype(jnp.bfloat16)
    return high, (value - high.astype(jnp.float32)).astype(jnp.bfloat16)


def product(left, right, dims=(((1,), (0,)), ((), ()))):
    if left.dtype == jnp.bfloat16:
        high, low = in_two(right)
        return dot(left, high, dims) + dot(left, low, dims)
    high, low = in_two(left)
    if right.dtype == jnp.bfloat16:
        return dot(high, right, dims) + dot(low, right, dims)
    right_high, right_low = in_two(right)
    return dot(high, right_high, dims) + (
        dot(high, right_low, dims) + dot(low, right_high, dims)
    )


def moments(turned, first, second):
    first = beta_one * first + (1.0 - beta_one) * turned
    second = beta_two * second + (1.0 - beta_two) * turned * turned
    update = first / (1.0 - beta_one**STEP) / (jnp.sqrt(second / (1.0 - beta_two**STEP)) + epsilon)
    return first, second, update


def bottom_kernel(
    mesh_sizes,
    state_ref,
    preact_ref,
    returned_ref,
    send_ref,
    own_block,
    mean_block,
    sums_two,
    sums_three,
    early_ref,
    count_ref,
    *refs,
):
    refs = list(refs)
    kept, refs = refs[:10], refs[10:]
    late_out, *new, back_ref, sums_ref, weight_ref, late_ref = refs[:11]
    land_ref, plane_land, part_ref, high_land, whole_ref, last_land = refs[11:17]
    fetched, refs = refs[17:27], refs[27:]
    plane_sems, inward, across, outward = refs[:2], refs[2:4], refs[4:6], refs[6:8]
    fetch_sem = refs[8]
    step = pl.program_id(0)
    units = state_ref.shape[0]
    halo = send_ref.shape[1]
    top, _, _, me = split_place(mesh_sizes)

    @pl.when(step == 0)
    def _():
        greet_split(mesh_sizes)
        for index, (source, target) in enumerate(zip(kept, fetched)):
            pltpu.make_async_copy(source, target, fetch_sem.at[index]).start()
        back_ref[...] = returned_ref[...].reshape(halo, units).T
        sums_ref[...] = jnp.zeros_like(sums_ref)
        weight_ref[...] = jnp.zeros_like(weight_ref)
        split_greeted(mesh_sizes)
        each_plane(
            mesh_sizes,
            lambda other, where: push(early_ref, land_ref.at[:, me], plane_sems, where),
        )

    grad = active_grad(step, state_ref, preact_ref, back_ref, send_ref)
    sums_ref[...] += jnp.sum(grad.astype(jnp.float32), axis=1, keepdims=True)
    width = own_block.shape[0]
    weight_ref[0, :width, :] += dot(own_block[...], grad, TRANS_RIGHT)
    weight_ref[1] += dot(mean_block[...], grad, TRANS_RIGHT)

    @pl.when(step == pl.num_programs(0) - 1)
    def _():
        padded = weight_ref.shape[1]
        row = 0
        for start in range(0, units, 128):
            for half in range(2):
                late_ref[row : row + padded, :] = weight_ref[half, :, start : start + 128].astype(
                    jnp.bfloat16
                )
                row += padded
        pieces = []
        for sums in (sums_ref, sums_two, sums_three):
            flat = sums[...].T[:1]
            for start in range(0, flat.shape[1], 128):
                pieces.append(flat[:, start : start + 128])
        narrow = pieces[-1].shape[1]
        pieces[-1] = jnp.concatenate(
            [pieces[-1], jnp.zeros((1, 128 - narrow), jnp.float32)], axis=1
        )
        rest = late_ref.shape[0] - row
        pieces.append(jnp.zeros((rest - len(pieces), 128), jnp.float32))
        late_ref[row:, :] = jnp.concatenate(pieces).astype(jnp.bfloat16)

        tall = part_ref.shape[0]

        def rows_of(place):
            return late_ref.at[pl.ds(pl.multiple_of(place * tall, tall), tall)]

        each_plane(
            mesh_sizes,
            lambda other, where: push(rows_of(other), plane_land.at[me], inward, where),
        )
        for index, (source, target) in enumerate(zip(kept, fetched)):
            pltpu.make_async_copy(source, target, fetch_sem.at[index]).wait()
        left_two, right_two, left_three, right_three = fetched[:4]
        weight_two, first_two, second_two = fetched[4:7]
        weight_three, first_three, second_three = fetched[7:]
        share = 1.0 / count_ref[...]
        plane_blocks_wait(mesh_sizes, land_ref, plane_sems)
        land_ref[:, me] = early_ref[...]
        early = land_ref[...].reshape(-1, land_ref.shape[3])
        grad = early[:, :units]
        turned = product(product(left_two[...], grad, TRANS_LEFT), right_two[...]) * share
        new_first, new_second, update = moments(turned, first_two[...], second_two[...])
        new[1][...] = new_first
        new[2][...] = new_second

        plane_wait(mesh_sizes, plane_land, inward)
        plane_land[me] = late_ref[pl.ds(pl.multiple_of(me * tall, tall), tall), :]
        part_ref[...] = jnp.sum(plane_land[...].astype(jnp.float32), axis=0).astype(jnp.bfloat16)
        each_high(
            mesh_sizes, lambda other, where: push(part_ref, high_land.at[top], across, where)
        )

        moved = product(product(left_two[...], update), right_two[...], TRANS_RIGHT)
        new[0][...] = weight_two[...] - step_rates[1] * moved

        high_wait(mesh_sizes, high_land, across)
        high_land[top] = part_ref[...]
        whole_ref[...] = jnp.sum(high_land[...].astype(jnp.float32), axis=0).astype(jnp.bfloat16)
        each_plane(
            mesh_sizes, lambda other, where: push(whole_ref, last_land.at[me], outward, where)
        )

        kinds = right_three.shape[0]
        grad = early[:, units:].astype(jnp.float32).T[:kinds].astype(jnp.bfloat16)
        turned = product(right_three[...], product(grad, left_three[...]), TRANS_LEFT) * share
        new_first, new_second, update = moments(turned, first_three[...], second_three[...])
        new[4][...] = new_first
        new[5][...] = new_second
        moved = product(right_three[...], product(update, left_three[...], TRANS_RIGHT))
        new[3][...] = weight_three[...] - step_rates[2] * moved

        plane_wait(mesh_sizes, last_land, outward)
        last_land[me] = whole_ref[...]
        late_out[...] = last_land[...]


def bottom_layer(
    state_grad,
    preact,
    returned,
    send_row,
    own,
    mean,
    sums_two,
    sums_three,
    early,
    count,
    kept,
    mesh_sizes,
    collective,
):
    units, nodes = preact.shape
    width = own.shape[0]
    padded = mean.shape[0]
    halo = send_row.shape[1]
    rows = units // 128 * (2 * padded + 2) + -(-sums_three.shape[0] // 128)
    rows = -(-rows // 512) * 512
    high, low, along = split_sizes(mesh_sizes)
    plane = low * along
    early_blocks = (high, plane) + early.shape[1:]
    late_blocks = (plane, rows // plane, 128)
    hbm = pl.BlockSpec(memory_space=pl.ANY)
    new = [jax.ShapeDtypeStruct(array.shape, jnp.float32) for array in kept[4:]]
    return pl.pallas_call(
        functools.partial(bottom_kernel, mesh_sizes),
        grid=(nodes // BLOCK,),
        in_specs=[
            lanes(units, BLOCK),
            lanes(units, BLOCK),
            whole(returned.shape),
            whole(send_row.shape),
            lanes(width, BLOCK),
            lanes(padded, BLOCK),
            whole(sums_two.shape),
            whole(sums_three.shape),
            whole(early.shape),
            whole(count.shape),
        ]
        + [hbm] * len(kept),
        out_specs=[whole(late_blocks)] + [whole(array.shape) for array in new],
        out_shape=[jax.ShapeDtypeStruct(late_blocks, jnp.bfloat16)] + new,
        scratch_shapes=[
            pltpu.VMEM((units, halo), jnp.bfloat16),
            pltpu.VMEM((units, 128), jnp.float32),
            pltpu.VMEM((2, padded, units), jnp.float32),
            pltpu.VMEM((rows, 128), jnp.bfloat16),
            pltpu.VMEM(early_blocks, jnp.bfloat16),
            pltpu.VMEM(late_blocks, jnp.bfloat16),
            pltpu.VMEM(late_blocks[1:], jnp.bfloat16),
            pltpu.VMEM((high,) + late_blocks[1:], jnp.bfloat16),
            pltpu.VMEM(late_blocks[1:], jnp.bfloat16),
            pltpu.VMEM(late_blocks, jnp.bfloat16),
        ]
        + [pltpu.VMEM(array.shape, array.dtype) for array in kept]
        + semaphores() * 4
        + [pltpu.SemaphoreType.DMA((len(kept),))],
        compiler_params=params(34, collective),
        name="bottom_layer",
    )(
        state_grad,
        *in_hbm(preact),
        returned,
        send_row,
        *in_hbm(own, mean),
        sums_two,
        sums_three,
        early,
        count,
        *in_hbm(*kept),
    )


def adam_kernel(
    padded,
    late_ref,
    count_ref,
    weight_one,
    left_one,
    right_one,
    first_one,
    second_one,
    bias_ref,
    bias_first,
    bias_second,
    *refs,
):
    ready, refs = refs[:6], refs[6:]
    outs, sem = refs[:12], refs[12]
    for index in range(6):
        pltpu.make_async_copy(ready[index], outs[3 + index], sem.at[index]).start()
    share = 1.0 / count_ref[...]
    units = weight_one.shape[1]
    width = weight_one.shape[0] // 2

    late_rows = late_ref[...].astype(jnp.float32)
    columns = []
    for start in range(0, units, 128):
        row = start // 128 * 2 * padded
        columns.append(
            jnp.concatenate(
                [late_rows[row : row + width], late_rows[row + padded : row + padded + width]]
            )
        )
    grad = jnp.concatenate(columns, axis=1).astype(jnp.bfloat16)
    turned = product(product(left_one[...], grad, TRANS_LEFT), right_one[...]) * share
    new_first, new_second, update = moments(turned, first_one[...], second_one[...])
    outs[1][...] = new_first
    outs[2][...] = new_second
    moved = product(product(left_one[...], update), right_one[...], TRANS_RIGHT)
    outs[0][...] = weight_one[...] - step_rates[0] * moved

    row = units // 128 * 2 * padded
    size = bias_ref.shape[0]
    pieces = []
    while len(pieces) * 128 < size:
        pieces.append(late_rows[row : row + 1])
        row += 1
    grad = jnp.concatenate(pieces, axis=1)[:, :size] * share
    flat = bias_ref.shape
    bias, first, second = (ref[...].reshape(grad.shape) for ref in (bias_ref, bias_first, bias_second))
    new_first, new_second, update = moments(grad, first, second)
    outs[9][...] = (bias - bias_rate * (update + weight_decay * bias)).reshape(flat)
    outs[10][...] = new_first.reshape(flat)
    outs[11][...] = new_second.reshape(flat)
    for index in range(6):
        pltpu.make_async_copy(ready[index], outs[3 + index], sem.at[index]).wait()


def adam(padded, late_all, count, state, ready):
    vmem = pl.BlockSpec(memory_space=pltpu.VMEM)
    hbm = pl.BlockSpec(memory_space=pl.ANY)
    one, bias = state[0], state[5]
    shapes = [one.shape] * 3 + [array.shape for array in ready] + [bias.shape] * 3
    return pl.pallas_call(
        functools.partial(adam_kernel, padded),
        in_specs=[vmem] * (2 + len(state)) + [hbm] * len(ready),
        out_specs=[vmem] * 3 + [hbm] * 6 + [vmem] * 3,
        out_shape=[jax.ShapeDtypeStruct(shape, jnp.float32) for shape in shapes],
        scratch_shapes=[pltpu.SemaphoreType.DMA((6,))],
        compiler_params=pltpu.CompilerParams(vmem_limit_bytes=24 * MIB),
        name="adam",
    )(late_all, count, *in_hbm(*state), *ready)


def on_device(
    mesh_sizes,
    features,
    labels,
    seed_rows,
    seed_mask,
    send_rows,
    neighbors_one,
    neighbors_two,
    neighbors_three,
    weight_one,
    weight_two,
    weight_three,
    left_one,
    right_one,
    left_two,
    right_two,
    left_three,
    right_three,
    first_one,
    first_two,
    first_three,
    second_one,
    second_two,
    second_three,
    bias_all,
    bias_first,
    bias_second,
):
    units = weight_one.shape[1]
    classes = weight_three.shape[1]
    halo = send_rows.size
    fans = (neighbors_one.shape[1], neighbors_two.shape[1], neighbors_three.shape[1])
    feats = features.T
    send_row = send_rows.reshape(1, halo)
    weight_three = weight_three.T
    padded_classes = -(-classes // 16) * 16
    seed_slots = (
        padded_classes,
        seed_rows.reshape(1, -1),
        labels.reshape(1, -1),
        seed_mask.reshape(1, -1),
    )

    words_one, got = count_words(
        neighbors_one.T, mesh_sizes, 0, halo, feats=feats, send_row=send_row
    )
    feats = in_hbm(feats)[0]
    state_one, preact_one, sent, mean_one = hidden_layer(
        words_one, feats, got, weight_one, bias_all, 0, send_row, fans[0]
    )
    words_two, got = count_words(neighbors_two.T, mesh_sizes, 1, halo, sent=sent)
    state_two, preact_two, sent, mean_two = hidden_layer(
        words_two, state_one, got, weight_two, bias_all, units, send_row, fans[1]
    )
    words_three, got, seeds = count_words(
        neighbors_three.T, mesh_sizes, 2, halo, sent=sent, seeds=seed_slots
    )
    grad_three, rows_three, sums_three, notes, table_three, far, halo_grad = last_layer(
        words_three, state_two, got, weight_three, bias_all, 2 * units, seeds, fans[2]
    )
    state_grad, returned, weight_grad = scatter_layer(
        words_three,
        grad_three,
        rows_three,
        weight_three,
        halo_grad,
        mesh_sizes,
        3,
        fans[2],
        tables=(far, table_three),
    )
    grad_two, rows_two, sums_two, halo_grad, early = middle_layer(
        state_grad,
        preact_two,
        returned,
        send_row,
        words_two,
        weight_two,
        state_one,
        mean_two,
        weight_grad,
        notes,
        fans[1],
    )
    state_grad, returned, early_sum, loss, count = scatter_layer(
        words_two, grad_two, rows_two, weight_two, halo_grad, mesh_sizes, 4, fans[1], early=early
    )
    late_all, *ready = bottom_layer(
        state_grad,
        preact_one,
        returned,
        send_row,
        feats,
        mean_one,
        sums_two,
        sums_three,
        early_sum,
        count,
        (
            left_two,
            right_two,
            left_three,
            right_three,
            weight_two,
            first_two,
            second_two,
            weight_three,
            first_three.T,
            second_three.T,
        ),
        mesh_sizes,
        5,
    )
    out = adam(
        mean_one.shape[0],
        late_all.reshape(-1, 128),
        count,
        (
            weight_one,
            left_one,
            right_one,
            first_one,
            second_one,
            bias_all,
            bias_first,
            bias_second,
        ),
        ready,
    )
    third = [value.T for value in out[6:9]]
    return (*out[:6], *third, *out[9:12], loss.reshape(()), count.reshape(()))


def solution(mesh):
    split = P(axes)
    rows = P(axes, None)
    placed = (rows, split, split, split, rows, rows, rows, rows) + (P(),) * 18
    mesh_sizes = (mesh.shape[axes[0]], mesh.shape[axes[1]])
    return jax.shard_map(
        functools.partial(on_device, mesh_sizes),
        mesh=mesh,
        in_specs=placed,
        out_specs=(P(),) * 14,
        check_vma=False,
    )
```

```python
import functools

import jax
import jax.numpy as jnp
from jax import lax
from jax.experimental import pallas as pl
from jax.experimental.pallas import tpu as pltpu
from jax.sharding import PartitionSpec as P

STEP = 10


beta_one = 0.9
beta_two = 0.999
epsilon = 1e-08
step_rates = (0.05, 0.5, 1.0)
bias_rate = 0.05
weight_decay = 0.01

axes = ("dom", "rep")
WORDS = 4
SLOTS = 8
RUN = 48
UNIT = SLOTS * RUN
BLOCK = 1024
LIST_BLOCK = 512
MIB = 1024 * 1024
TRANS_LEFT = (((0,), (0,)), ((), ()))
TRANS_RIGHT = (((1,), (1,)), ((), ()))


def dot(left, right, dims=(((1,), (0,)), ((), ()))):
    return lax.dot_general(left, right, dims, preferred_element_type=jnp.float32)


def params(limit, collective=None):
    remote = {} if collective is None else dict(collective_id=collective, has_side_effects=True)
    return pltpu.CompilerParams(
        dimension_semantics=("arbitrary",), vmem_limit_bytes=limit * MIB, **remote
    )


def in_hbm(*arrays):
    return [pltpu.with_memory_space_constraint(array, pltpu.HBM) for array in arrays]


def whole(shape):
    return pl.BlockSpec(shape, lambda i: (0,) * len(shape))


def lanes(rows, width):
    return pl.BlockSpec((rows, width), lambda i: (0, i))


def floor_over(value, size):
    return ((value.astype(jnp.float32) + 0.5) * (1.0 / size)).astype(jnp.int32)


def words_layer(near_ref, out_ref, place_ref, field_ref):
    fanout, block = near_ref.shape
    span = out_ref.shape[0] // WORDS
    near = near_ref[...]
    unit = floor_over(near, UNIT)
    rest = near - unit * UNIT
    slot = floor_over(rest, RUN)
    word = floor_over(unit, span // RUN)
    place = (unit - word * (span // RUN)) * RUN + rest - slot * RUN
    bit = jnp.left_shift(jnp.int32(1), slot * 4)
    parts = [jnp.where(word == k, bit, 0) for k in range(WORDS)]
    totals = [jnp.zeros_like(bit) for _ in range(WORDS)]
    for g in range(fanout):
        same = place == place[g : g + 1]
        for k in range(WORDS):
            totals[k] = totals[k] + jnp.where(same, parts[k][g : g + 1], 0)
    place_ref[:fanout, :] = place
    for k in range(WORDS):
        field_ref[k, :fanout, :] = totals[k]
    chunk = RUN
    for tile in range(0, block, 128):
        cols = slice(tile, tile + 128)
        for start in range(0, span, chunk):
            rows = lax.broadcasted_iota(jnp.int32, (chunk, 128), 0) + start
            sums = [jnp.zeros((chunk, 128), jnp.int32) for _ in range(WORDS)]
            for g in range(fanout):
                hit = rows == place_ref[g : g + 1, cols]
                for k in range(WORDS):
                    sums[k] = jnp.where(hit, field_ref[k, g : g + 1, cols], sums[k])
            for k in range(WORDS):
                out_ref[k * span + start : k * span + start + chunk, cols] = sums[k]


def my_index(mesh_sizes):
    return lax.axis_index(axes[0]) * mesh_sizes[1] + lax.axis_index(axes[1])


def each_peer(mesh_sizes, act):
    across, along = mesh_sizes
    row, column = lax.axis_index(axes[0]), lax.axis_index(axes[1])

    def wrapped(value, size):
        return jnp.where(value >= size, value - size, value)

    def line(down, carry):
        other = wrapped(row + down, across)
        for ahead in range(along):
            place = wrapped(column + ahead, along)
            act(other * along + place, (other, place))
        return carry

    for ahead in range(1, along):
        place = wrapped(column + ahead, along)
        act(row * along + place, (row, place))
    lax.fori_loop(1, across, line, 0)


def greet(mesh_sizes):
    barrier = pltpu.get_barrier_semaphore()

    def tell(index, where):
        pl.semaphore_signal(
            barrier, inc=1, device_id=where, device_id_type=pl.DeviceIdType.MESH
        )

    each_peer(mesh_sizes, tell)


def all_greeted(mesh_sizes):
    pl.semaphore_wait(pltpu.get_barrier_semaphore(), mesh_sizes[0] * mesh_sizes[1] - 1)


def send_blocks(mesh_sizes, out_ref, in_ref, send_sem, recv_sem):
    me = my_index(mesh_sizes)

    def send(index, where):
        pltpu.make_async_remote_copy(
            src_ref=out_ref.at[index],
            dst_ref=in_ref.at[me],
            send_sem=send_sem,
            recv_sem=recv_sem,
            device_id=where,
            device_id_type=pl.DeviceIdType.MESH,
        ).start()

    each_peer(mesh_sizes, send)


def send_all(mesh_sizes, own_ref, in_ref, send_sem, recv_sem):
    me = my_index(mesh_sizes)

    def send(index, where):
        pltpu.make_async_remote_copy(
            src_ref=own_ref,
            dst_ref=in_ref.at[me],
            send_sem=send_sem,
            recv_sem=recv_sem,
            device_id=where,
            device_id_type=pl.DeviceIdType.MESH,
        ).start()

    each_peer(mesh_sizes, send)


def wait_moves(mesh_sizes, out_ref, in_ref, send_sem, recv_sem):
    others = pl.ds(0, mesh_sizes[0] * mesh_sizes[1] - 1)
    copy = pltpu.make_async_remote_copy(
        src_ref=in_ref.at[others],
        dst_ref=in_ref.at[others],
        send_sem=send_sem,
        recv_sem=recv_sem,
        device_id=(lax.axis_index(axes[0]), lax.axis_index(axes[1])),
        device_id_type=pl.DeviceIdType.MESH,
    )
    copy.wait_send()
    copy.wait_recv()


def split_sizes(mesh_sizes):
    across, along = mesh_sizes
    high = 4 if across % 4 == 0 else 1
    return high, across // high, along


def split_place(mesh_sizes):
    _, low, along = split_sizes(mesh_sizes)
    row, column = lax.axis_index(axes[0]), lax.axis_index(axes[1])
    top = row // low
    return top, row - top * low, column, (row - top * low) * along + column


def each_high(mesh_sizes, act):
    high, low, _ = split_sizes(mesh_sizes)
    top, bottom, column, _ = split_place(mesh_sizes)
    for ahead in range(1, high):
        other = top + ahead
        other = jnp.where(other >= high, other - high, other)
        act(other, (other * low + bottom, column))


def each_plane(mesh_sizes, act):
    _, low, along = split_sizes(mesh_sizes)
    top, bottom, column, _ = split_place(mesh_sizes)
    for down in range(low):
        for ahead in range(along):
            if down == 0 and ahead == 0:
                continue
            line = bottom + down
            line = jnp.where(line >= low, line - low, line)
            place = column + ahead
            place = jnp.where(place >= along, place - along, place)
            act(line * along + place, (top * low + line, place))


def greet_split(mesh_sizes):
    barrier = pltpu.get_barrier_semaphore()

    def tell(index, where):
        pl.semaphore_signal(
            barrier, inc=1, device_id=where, device_id_type=pl.DeviceIdType.MESH
        )

    each_high(mesh_sizes, tell)
    each_plane(mesh_sizes, tell)


def split_greeted(mesh_sizes):
    high, low, along = split_sizes(mesh_sizes)
    pl.semaphore_wait(pltpu.get_barrier_semaphore(), high - 1 + low * along - 1)


def push(src_ref, dst_ref, sems, where):
    pltpu.make_async_remote_copy(
        src_ref=src_ref,
        dst_ref=dst_ref,
        send_sem=sems[0],
        recv_sem=sems[1],
        device_id=where,
        device_id_type=pl.DeviceIdType.MESH,
    ).start()


def wait_pushed(ref, sems):
    copy = pltpu.make_async_remote_copy(
        src_ref=ref,
        dst_ref=ref,
        send_sem=sems[0],
        recv_sem=sems[1],
        device_id=(lax.axis_index(axes[0]), lax.axis_index(axes[1])),
        device_id_type=pl.DeviceIdType.MESH,
    )
    copy.wait_send()
    copy.wait_recv()


def high_start(mesh_sizes, sent_ref, relay_ref, sems):
    top = split_place(mesh_sizes)[0]
    each_high(
        mesh_sizes, lambda other, where: push(sent_ref.at[other], relay_ref.at[top], sems, where)
    )


def high_wait(mesh_sizes, relay_ref, sems):
    high = split_sizes(mesh_sizes)[0]
    if high > 1:
        wait_pushed(relay_ref.at[pl.ds(0, high - 1)], sems)


def plane_wait(mesh_sizes, land_ref, sems):
    _, low, along = split_sizes(mesh_sizes)
    wait_pushed(land_ref.at[pl.ds(0, low * along - 1)], sems)


def plane_blocks(mesh_sizes, relay_ref, land_ref, sems):
    me = split_place(mesh_sizes)[3]
    each_plane(
        mesh_sizes,
        lambda other, where: push(relay_ref.at[:, other], land_ref.at[:, me], sems, where),
    )


def plane_blocks_wait(mesh_sizes, land_ref, sems):
    _, low, along = split_sizes(mesh_sizes)
    wait_pushed(land_ref.at[:, pl.ds(0, low * along - 1)], sems)


NOTES = 120


def put_terms(rows, values):
    lane = lax.broadcasted_iota(jnp.int32, rows.shape, 1)
    for index, value in enumerate(values):
        for at in range(3):
            term = value.astype(jnp.bfloat16).astype(jnp.float32)
            rows = jnp.where(lane == NOTES + 3 * index + at, term, rows)
            value = value - term
    return rows


def take_terms(rows):
    lane = lax.broadcasted_iota(jnp.int32, rows.shape, 1)
    values = []
    for index in range(2):
        first = NOTES + 3 * index
        mine = (lane >= first) & (lane < first + 3)
        values.append(jnp.sum(jnp.where(mine, rows, 0.0), axis=1, keepdims=True))
    return values


def semaphores():
    return [pltpu.SemaphoreType.DMA, pltpu.SemaphoreType.DMA]


def one_row(rows):
    per, parts = rows.shape
    column = lax.broadcasted_iota(jnp.int32, (parts, parts * per), 1)
    owner = lax.broadcasted_iota(jnp.int32, (parts, parts * per), 0)
    rest = column - owner * per
    mine = jnp.where((rest >= 0) & (rest < per), 1.0, 0.0).astype(jnp.bfloat16)
    high = (rows >> 7).astype(jnp.float32).astype(jnp.bfloat16)
    low = (rows & 127).astype(jnp.float32).astype(jnp.bfloat16)
    wide = dot(high, mine) * 128.0 + dot(low, mine)
    column = lax.broadcasted_iota(jnp.int32, wide.shape, 1)
    at = lax.broadcasted_iota(jnp.int32, wide.shape, 0)
    picked = jnp.where(column - floor_over(column, per) * per == at, wide, 0.0)
    return jnp.sum(picked, axis=0, keepdims=True).astype(jnp.int32)


def chosen_nodes(send_row, start, count):
    node = lax.broadcasted_iota(jnp.int32, (count, send_row.shape[1]), 0) + start
    return jnp.where(node == send_row, 1.0, 0.0).astype(jnp.bfloat16)


def words_kernel(mesh_sizes, kind, near_ref, *refs):
    refs = list(refs)
    if kind == "features":
        feats_ref, send_ref, out_ref, got_ref, row_ref, sent_ref = refs[:6]
        refs = refs[6:]
    elif kind == "seeds":
        sent_ref, slots_ref, labels_ref, mask_ref, out_ref, got_ref, seeds_ref = refs[:7]
        refs = refs[7:]
    else:
        sent_ref, out_ref, got_ref = refs[:3]
        refs = refs[3:]
    place_ref, field_ref, land_ref, send_sem, recv_sem = refs
    step = pl.program_id(0)
    block = near_ref.shape[1]
    moves = (mesh_sizes, sent_ref, land_ref, send_sem, recv_sem)

    @pl.when(step == 0)
    def _():
        greet(mesh_sizes)

    if kind == "features":

        @pl.when(step == 0)
        def _():
            width, nodes = feats_ref.shape
            halo = row_ref.shape[1]
            row_ref[...] = one_row(send_ref[...])
            total = jnp.zeros((width, halo), jnp.float32)
            for start in range(0, nodes, block):
                chosen = chosen_nodes(row_ref[...], start, block)
                total = total + dot(feats_ref[:, start : start + block], chosen)
            padded = sent_ref.shape[2]
            total = jnp.concatenate([total, jnp.zeros((padded - width, halo), jnp.float32)])
            sent_ref[...] = total.T.astype(jnp.bfloat16).reshape(sent_ref.shape)

    if kind == "seeds":
        classes = seeds_ref.shape[0]
        slots = slots_ref.shape[1]
        label = lax.broadcasted_iota(jnp.int32, (classes, slots), 0)
        marked = jnp.where((label == labels_ref[...]) & (mask_ref[...] != 0), 1.0, 0.0)
        chosen = chosen_nodes(slots_ref[...], step * block, block)
        seeds_ref[...] = dot(marked.astype(jnp.bfloat16), chosen, TRANS_RIGHT)

    words_layer(near_ref, out_ref, place_ref, field_ref)

    @pl.when(step == 0)
    def _():
        all_greeted(mesh_sizes)
        send_blocks(*moves)

    @pl.when(step == pl.num_programs(0) - 1)
    def _():
        me = my_index(mesh_sizes)
        wait_moves(*moves)
        land_ref[me] = sent_ref[me]
        got_ref[...] = land_ref[...]


def words_space(table, near):
    return pltpu.VMEM if near and table <= 5120 else pltpu.HBM


def place_words(words, near):
    return pltpu.with_memory_space_constraint(words, words_space(words.shape[0] * SLOTS, near))


def count_words(
    near, mesh_sizes, collective, halo, sent=None, feats=None, send_rows=None, seeds=None
):
    fanout, nodes = near.shape
    parts = mesh_sizes[0] * mesh_sizes[1]
    height = (nodes + halo) // SLOTS
    in_specs = [lanes(fanout, LIST_BLOCK)]
    operands = [near]
    scratch = []
    if sent is None:
        kind = "features"
        blocks = (parts, halo // parts, -(-feats.shape[0] // 128) * 128)
        in_specs += [whole(feats.shape), whole(send_rows.shape)]
        operands += in_hbm(feats, send_rows)
        scratch.append(pltpu.VMEM(blocks, jnp.bfloat16))
    else:
        kind = "plain"
        blocks = (parts, halo // parts, sent.shape[1])
        in_specs.append(whole(blocks))
        operands.append(sent.reshape(blocks))
    out_specs = [lanes(height, LIST_BLOCK), whole(blocks)]
    out_shape = [
        words_space(nodes + halo, sent is None)(
            (height, nodes), jnp.int32
        ),
        jax.ShapeDtypeStruct(blocks, jnp.bfloat16),
    ]
    if sent is None:
        out_specs.append(whole((1, halo)))
        out_shape.append(jax.ShapeDtypeStruct((1, halo), jnp.int32))
    if seeds is not None:
        kind = "seeds"
        classes, slots, labels, mask = seeds
        in_specs += [whole(slots.shape)] * 3
        operands += [slots, labels, mask]
        out_specs.append(lanes(classes, LIST_BLOCK))
        out_shape.append(jax.ShapeDtypeStruct((classes, nodes), jnp.float32))
    return pl.pallas_call(
        functools.partial(words_kernel, mesh_sizes, kind),
        grid=(nodes // LIST_BLOCK,),
        in_specs=in_specs,
        out_specs=out_specs,
        out_shape=out_shape,
        scratch_shapes=scratch
        + [
            pltpu.VMEM((16, LIST_BLOCK), jnp.int32),
            pltpu.VMEM((WORDS, 16, LIST_BLOCK), jnp.int32),
            pltpu.VMEM(blocks, jnp.bfloat16),
        ]
        + semaphores(),
        compiler_params=params(20, collective),
        name="count_words",
    )(*in_hbm(*operands[:1]), *operands[1:])


def field(words, slot):
    if slot == SLOTS - 1:
        picked = lax.shift_right_logical(words, 4 * slot)
    else:
        picked = words & (15 << (4 * slot))
    return picked.astype(jnp.float32).astype(jnp.bfloat16)


def slot_scale(slot):
    return 1.0 if slot == SLOTS - 1 else 2.0 ** (-4 * slot)


def spread_unit(words_ref, word_row, counts_ref, count_row):
    for start in range(0, RUN, 16):
        for tile in range(0, words_ref.shape[1], 256):
            cols = slice(tile, tile + 256)
            words = words_ref[word_row + start : word_row + start + 16, cols]
            for slot in range(SLOTS):
                row = count_row + slot * RUN + start
                counts_ref[row : row + 16, cols] = field(words, slot)


def gather_product(table_ref, words_ref, counts_ref):
    table = table_ref.shape[1]
    total = None
    for start in range(0, table, 2 * UNIT):
        stop = start + 2 * UNIT
        for row in range(start, stop, UNIT):
            spread_unit(words_ref, row // SLOTS, counts_ref, row)
        term = dot(table_ref[:, start:stop], counts_ref[start:stop, :])
        total = term if total is None else total + term
    return total


def scale_row(table):
    column = lax.broadcasted_iota(jnp.int32, (1, table), 1)
    rest = column - floor_over(column, UNIT) * UNIT
    slot = floor_over(rest, RUN)
    scale = jnp.ones((1, table), jnp.float32)
    for k in range(SLOTS - 1):
        scale = jnp.where(slot == k, slot_scale(k), scale)
    return scale


def column_of(row):
    return jnp.broadcast_to(row, (128, row.shape[1])).T


def late(rows, width):
    return pl.BlockSpec((rows, width), lambda i: (0, jnp.maximum(i - 1, 0)))


def now(rows, width, steps):
    return pl.BlockSpec((rows, width), lambda i: (0, jnp.minimum(i, steps - 1)))


def hidden_kernel(
    fanout,
    bias_start,
    words_ref,
    own_ref,
    own_block,
    got_ref,
    weight_ref,
    bias_ref,
    send_ref,
    state_ref,
    preact_ref,
    sent_ref,
    extra_ref,
    table_ref,
    counts_ref,
    picked_ref,
    mean_ref,
    self_ref,
    near_ref,
    bias_col,
):
    step = pl.program_id(0)
    last = pl.num_programs(0) - 1
    width, nodes = own_ref.shape
    units, block = state_ref.shape
    padded = mean_ref.shape[0]

    @pl.when(step == 0)
    def _():
        if table_ref.shape[0] > width:
            table_ref[...] = jnp.zeros_like(table_ref)
        got = got_ref[...].reshape(-1, got_ref.shape[2]).T[:width]
        scale = scale_row(table_ref.shape[1])
        own = own_ref[...].astype(jnp.float32) * scale[:, :nodes]
        table_ref[:width, :nodes] = own.astype(jnp.bfloat16)
        far = got.astype(jnp.float32) * scale[:, nodes:]
        table_ref[:width, nodes:] = far.astype(jnp.bfloat16)
        mean_ref[...] = jnp.zeros_like(mean_ref)
        picked_ref[...] = jnp.zeros_like(picked_ref)
        self_ref[...] = weight_ref[:width, :].T.astype(jnp.bfloat16)
        if padded > width:
            near_ref[...] = jnp.zeros_like(near_ref)
        near_ref[:, :width] = weight_ref[width:, :].T.astype(jnp.bfloat16)
        bias = bias_ref[...].reshape(1, -1)
        bias_col[...] = column_of(bias[:, bias_start : bias_start + units])

    def finish():
        mean = mean_ref[...]
        extra_ref[...] = mean
        if padded > width:
            extra_ref[width : width + 1, :] = jnp.ones((1, block), jnp.bfloat16)
        preact = dot(self_ref[...], own_block[...]) + dot(near_ref[...], mean) + bias_col[:, :1]
        preact_ref[...] = preact
        active = preact * jax.nn.sigmoid(preact)
        norm = lax.rsqrt(jnp.sum(active * active, axis=0, keepdims=True) + 1e-06)
        state = (active * norm).astype(jnp.bfloat16)
        state_ref[...] = state
        picked_ref[...] += dot(state, chosen_nodes(send_ref[...], (step - 1) * block, block))

    @pl.when(step < last)
    def _():
        finish()
        total = gather_product(table_ref, words_ref, counts_ref)
        mean_ref[...] = (total / fanout).astype(jnp.bfloat16)

    @pl.when(step == last)
    def _():
        finish()
        sent_ref[...] = picked_ref[...].T.astype(jnp.bfloat16)


def hidden_layer(words, own, got, weight, bias, bias_start, send_row, fanout):
    width, nodes = own.shape
    halo = send_row.shape[1]
    table = nodes + halo
    units = weight.shape[1]
    padded = width if width == units else (width // 16 + 1) * 16
    steps = nodes // BLOCK
    return pl.pallas_call(
        functools.partial(hidden_kernel, fanout, bias_start),
        grid=(steps + 1,),
        in_specs=[
            now(words.shape[0], BLOCK, steps),
            whole(own.shape),
            late(width, BLOCK),
            whole(got.shape),
            whole(weight.shape),
            whole(bias.shape),
            whole(send_row.shape),
        ],
        out_specs=[
            late(units, BLOCK),
            late(units, BLOCK),
            whole((halo, units)),
            late(padded, BLOCK),
        ],
        out_shape=[
            jax.ShapeDtypeStruct((units, nodes), jnp.bfloat16),
            pltpu.HBM((units, nodes), jnp.float32),
            jax.ShapeDtypeStruct((halo, units), jnp.bfloat16),
            pltpu.HBM((padded, nodes), jnp.bfloat16),
        ],
        scratch_shapes=[
            pltpu.VMEM((padded, table), jnp.bfloat16),
            pltpu.VMEM((table, BLOCK), jnp.bfloat16),
            pltpu.VMEM((units, halo), jnp.float32),
            pltpu.VMEM((padded, BLOCK), jnp.bfloat16),
            pltpu.VMEM((units, width), jnp.bfloat16),
            pltpu.VMEM((units, padded), jnp.bfloat16),
            pltpu.VMEM((units, 128), jnp.float32),
        ],
        compiler_params=params(40),
        name="hidden_layer",
    )(place_words(words, width != units), own, own, got, *in_hbm(weight, bias), send_row)


def far_start(nodes):
    return nodes // UNIT * UNIT


def column_sums(rows):
    return dot(jnp.ones((16, rows.shape[0]), jnp.bfloat16), rows)


def unscaled(sums, fanout):
    pieces = []
    for row in range(0, sums.shape[0], RUN):
        slot = row // RUN % SLOTS
        pieces.append((sums[row : row + RUN] * (slot_scale(slot) / fanout)).astype(jnp.bfloat16))
    return jnp.concatenate(pieces)


def last_kernel(
    fanout,
    bias_start,
    words_ref,
    own_ref,
    own_block,
    got_ref,
    weight_ref,
    bias_ref,
    seeds_ref,
    grad_ref,
    rows_ref,
    sums_ref,
    notes_ref,
    table_out,
    far_ref,
    halo_ref,
    reduced_ref,
    counts_ref,
    both_ref,
    self_ref,
    near_ref,
    bias_col,
    far_sums,
):
    step = pl.program_id(0)
    last = pl.num_programs(0) - 1
    classes = self_ref.shape[0]
    width, nodes = own_ref.shape
    kinds = weight_ref.shape[0]
    halo = far_ref.shape[0]
    first = far_start(nodes)

    @pl.when(step == 0)
    def _():
        table_out[:, :nodes] = own_ref[...]
        table_out[:, nodes:] = got_ref[...].reshape(halo, width).T
        more = jnp.zeros((classes - kinds, 2 * width), jnp.float32)
        weight = jnp.concatenate([weight_ref[...], more]).astype(jnp.bfloat16)
        self_ref[...] = weight[:, :width]
        near_ref[...] = weight[:, width:]
        rest = jnp.full((1, classes - kinds), -1e30, jnp.float32)
        bias = bias_ref[...].reshape(1, -1)
        bias_col[...] = column_of(
            jnp.concatenate([bias[:, bias_start : bias_start + kinds], rest], axis=1)
        )
        reduced = dot(near_ref[...], table_out[...]) * scale_row(table_out.shape[1])
        high = reduced.astype(jnp.bfloat16)
        reduced_ref[:classes, :] = high
        reduced_ref[classes:, :] = (reduced - high.astype(jnp.float32)).astype(jnp.bfloat16)
        both_ref[...] = jnp.zeros_like(both_ref)
        counts_ref[first:, :] = jnp.zeros_like(counts_ref[first:, :])

    @pl.when(step <= 1)
    def _():
        sums_ref[...] = jnp.zeros_like(sums_ref)
        notes_ref[...] = jnp.zeros_like(notes_ref)
        far_sums[...] = jnp.zeros_like(far_sums)

    def finish():
        near_part = (both_ref[:classes, :] + both_ref[classes:, :]) / fanout
        logits = dot(self_ref[...], own_block[...]) + near_part + bias_col[:, :1]
        top = jnp.max(logits, axis=0, keepdims=True)
        powers = jnp.exp(logits - top)
        total = jnp.sum(powers, axis=0, keepdims=True)
        normer = jnp.log(total) + top
        seeds = seeds_ref[...]
        uses = jnp.sum(seeds, axis=0, keepdims=True)
        grad = (powers / total * uses - seeds).astype(jnp.bfloat16)
        grad_ref[...] = grad
        loss = uses * normer - jnp.sum(seeds * logits, axis=0, keepdims=True)
        notes_ref[:8, :] += jnp.sum(loss)
        notes_ref[8:, :] += jnp.sum(uses)
        rows = grad.T
        rows_ref[...] = rows
        sums_ref[...] += column_sums(rows)
        far_sums[...] += dot(counts_ref[first:, :], rows)

    @pl.when(step < last)
    def _():
        finish()
        both_ref[...] = gather_product(reduced_ref, words_ref, counts_ref)

    @pl.when(step == last)
    def _():
        finish()
        sums = unscaled(far_sums[...], fanout)[nodes - first :]
        far_ref[...] = sums
        halo_ref[...] = dot(sums, near_ref[...]).astype(jnp.bfloat16)


def last_layer(words, own, got, weight, bias, bias_start, seeds, fanout):
    width, nodes = own.shape
    halo = got.shape[0] * got.shape[1]
    table = nodes + halo
    classes = seeds.shape[0]
    steps = nodes // BLOCK
    far_height = table - far_start(nodes)
    return pl.pallas_call(
        functools.partial(last_kernel, fanout, bias_start),
        grid=(steps + 1,),
        in_specs=[
            now(words.shape[0], BLOCK, steps),
            whole(own.shape),
            late(width, BLOCK),
            whole(got.shape),
            whole(weight.shape),
            whole(bias.shape),
            late(classes, BLOCK),
        ],
        out_specs=[
            late(classes, BLOCK),
            pl.BlockSpec((BLOCK, classes), lambda i: (jnp.maximum(i - 1, 0), 0)),
            whole((16, classes)),
            whole((16, 128)),
            whole((width, table)),
            whole((halo, classes)),
            whole((halo, width)),
        ],
        out_shape=[
            jax.ShapeDtypeStruct((classes, nodes), jnp.bfloat16),
            jax.ShapeDtypeStruct((nodes, classes), jnp.bfloat16),
            jax.ShapeDtypeStruct((16, classes), jnp.float32),
            jax.ShapeDtypeStruct((16, 128), jnp.float32),
            jax.ShapeDtypeStruct((width, table), jnp.bfloat16),
            jax.ShapeDtypeStruct((halo, classes), jnp.bfloat16),
            jax.ShapeDtypeStruct((halo, width), jnp.bfloat16),
        ],
        scratch_shapes=[
            pltpu.VMEM((2 * classes, table), jnp.bfloat16),
            pltpu.VMEM((table, BLOCK), jnp.bfloat16),
            pltpu.VMEM((2 * classes, BLOCK), jnp.float32),
            pltpu.VMEM((classes, width), jnp.bfloat16),
            pltpu.VMEM((classes, width), jnp.bfloat16),
            pltpu.VMEM((classes, 128), jnp.float32),
            pltpu.VMEM((far_height, classes), jnp.float32),
        ],
        compiler_params=params(40),
        name="last_layer",
    )(*in_hbm(words), own, own, got, *in_hbm(weight, bias), seeds)


def scatter_kernel(mesh_sizes, fanout, flipped, words_ref, grad_ref, rows_ref, *refs):
    refs = list(refs)
    if flipped:
        weight_in, halo_ref, far_ref, table_ref, far_table = refs[:5]
        state_ref, got_ref, weight_ref = refs[5:8]
        refs = refs[8:]
    else:
        weight_in, halo_ref, early_ref = refs[:3]
        state_ref, got_ref, early_sum, loss_ref, count_ref = refs[3:8]
        refs = refs[8:]
    padded_ref, counts_ref, sums_ref, self_ref, near_ref, relay_ref, land_ref = refs[:7]
    if flipped:
        high_sems, plane_sems = refs[7:9], refs[9:11]
    else:
        early_relay, early_part, early_land, early_own, early_back = refs[7:12]
        high_sems, plane_sems = refs[12:14], refs[14:16]
        early_high, early_plane, back_sems = refs[16:18], refs[18:20], refs[20:22]
    step = pl.program_id(0)
    units, nodes = grad_ref.shape
    width = state_ref.shape[0]
    span = words_ref.shape[0]
    part = span * SLOTS
    steps = -(-nodes // part)

    @pl.when(step == 0)
    def _():
        greet_split(mesh_sizes)
        for k in range(steps):
            start = k * part
            stop = min(start + part, nodes)
            padded_ref[k, :, : stop - start] = grad_ref[:, start:stop]
            if stop < start + part:
                padded_ref[k, :, stop - start :] = jnp.zeros(
                    (units, start + part - stop), jnp.bfloat16
                )
        weight = weight_in[...]
        if flipped:
            more = jnp.zeros((units - weight.shape[0], 2 * width), jnp.float32)
            weight = jnp.concatenate([weight, more]).T
            weight_ref[:width, :] = jnp.zeros((width, units), jnp.float32)
            weight_ref[width:, :] = dot(far_table[...], far_ref[...])
        self_ref[...] = weight[:width].astype(jnp.bfloat16)
        near_ref[...] = weight[width:].astype(jnp.bfloat16)
        sums_ref[...] = jnp.zeros_like(sums_ref)
        split_greeted(mesh_sizes)
        high_start(mesh_sizes, halo_ref, relay_ref, high_sems)
        if not flipped:
            plane_blocks(mesh_sizes, early_ref, early_relay, early_plane)

    @pl.when(step == steps // 2)
    def _():
        top, _, _, me = split_place(mesh_sizes)
        high_wait(mesh_sizes, relay_ref, high_sems)
        relay_ref[top] = halo_ref[top]
        plane_blocks(mesh_sizes, relay_ref, land_ref, plane_sems)
        if not flipped:
            plane_blocks_wait(mesh_sizes, early_relay, early_plane)
            early_relay[:, me] = early_ref[:, me]
            total = jnp.sum(early_relay[...].astype(jnp.float32), axis=1)
            shape = total.shape
            total = total.reshape(-1, shape[2])
            last = total[:, -128:]
            total = jnp.concatenate([total[:, :-128], put_terms(last, take_terms(last))], axis=1)
            early_part[...] = total.astype(jnp.bfloat16).reshape(shape)
            high_start(mesh_sizes, early_part, early_land, early_high)

    if not flipped:

        @pl.when(step == steps - 1)
        def _():
            top = split_place(mesh_sizes)[0]
            high_wait(mesh_sizes, early_land, early_high)
            early_land[top] = early_part[top]
            total = jnp.sum(early_land[...].astype(jnp.float32), axis=0)
            early_own[...] = total.astype(jnp.bfloat16)
            loss, count = take_terms(total[:, -128:])
            loss_ref[...] = loss[:1]
            count_ref[...] = count[:1]
            each_high(
                mesh_sizes,
                lambda other, where: push(early_own, early_back.at[top], back_sems, where),
            )

    def add(row):
        spread_unit(words_ref, row // SLOTS, counts_ref, row)
        added = dot(counts_ref[row : row + UNIT, :], rows_ref[...])
        sums_ref[row : row + UNIT, :] = unscaled(added, fanout)

    beyond = nodes - (steps - 1) * part
    ending = -(-beyond // UNIT) * UNIT
    for row in range(0, ending, UNIT):
        add(row)
    if ending < part:

        @pl.when(step < steps - 1)
        def _():
            for row in range(ending, part, UNIT):
                add(row)

    if flipped and beyond < part:

        @pl.when(step == steps - 1)
        def _():
            sums_ref[beyond:, :] = jnp.zeros((part - beyond, units), jnp.bfloat16)

    sums = sums_ref[...]
    own_grad = padded_ref[step]
    state_ref[...] = dot(near_ref[...], sums, TRANS_RIGHT) + dot(self_ref[...], own_grad)
    if flipped:
        weight_ref[:width, :] += dot(table_ref[...], own_grad, TRANS_RIGHT)
        weight_ref[width:, :] += dot(table_ref[...], sums)

    @pl.when(step == steps - 1)
    def _():
        me = split_place(mesh_sizes)[3]
        plane_blocks_wait(mesh_sizes, land_ref, plane_sems)
        land_ref[:, me] = relay_ref[:, me]
        got_ref[...] = land_ref[...]
        if not flipped:
            top = split_place(mesh_sizes)[0]
            high_wait(mesh_sizes, early_back, back_sems)
            early_back[top] = early_own[...]
            early_sum[...] = early_back[...]


def scatter_layer(
    words, grad, rows, weight, halo_rows, mesh_sizes, collective, fanout, tables=None, early=None
):
    units, nodes = grad.shape
    halo, width = halo_rows.shape
    parts = mesh_sizes[0] * mesh_sizes[1]
    flipped = tables is not None
    total = nodes + halo
    part = total // WORDS
    span = part // SLOTS
    steps = -(-nodes // part)
    high = split_sizes(mesh_sizes)[0]
    blocks = (high, parts // high, halo // parts, width)
    in_specs = [
        pl.BlockSpec((span, nodes), lambda i: (i, 0)),
        whole(grad.shape),
        whole(rows.shape),
        whole(weight.shape),
        whole(blocks),
    ]
    operands = [words, grad, rows, weight, halo_rows.reshape(blocks)]
    out_specs = [lanes(width, part), whole(blocks)]
    out_shape = [
        jax.ShapeDtypeStruct((width, total), jnp.float32),
        jax.ShapeDtypeStruct(blocks, jnp.bfloat16),
    ]
    if flipped:
        far, table = tables
        in_specs += [
            whole(far.shape),
            lanes(width, part),
            pl.BlockSpec((width, halo), lambda i: (0, nodes // halo)),
        ]
        operands += [far, table, table]
        out_specs.append(whole((2 * width, units)))
        out_shape.append(jax.ShapeDtypeStruct((2 * width, units), jnp.float32))
        scratch = semaphores() + semaphores()
    else:
        early_blocks = (high, parts // high, early.shape[0] // parts, early.shape[1])
        in_specs.append(whole(early_blocks))
        operands.append(early.reshape(early_blocks))
        summed = (high,) + early_blocks[2:]
        out_specs += [whole(summed), whole((1, 1)), whole((1, 1))]
        out_shape += [
            jax.ShapeDtypeStruct(summed, jnp.bfloat16),
            jax.ShapeDtypeStruct((1, 1), jnp.float32),
            jax.ShapeDtypeStruct((1, 1), jnp.float32),
        ]
        scratch = [
            pltpu.VMEM(early_blocks, jnp.bfloat16),
            pltpu.VMEM(summed, jnp.bfloat16),
            pltpu.VMEM(summed, jnp.bfloat16),
            pltpu.VMEM(summed[1:], jnp.bfloat16),
            pltpu.VMEM(summed, jnp.bfloat16),
        ]
        scratch += semaphores() * 5
    return pl.pallas_call(
        functools.partial(scatter_kernel, mesh_sizes, fanout, flipped),
        grid=(steps,),
        in_specs=in_specs,
        out_specs=out_specs,
        out_shape=out_shape,
        scratch_shapes=[
            pltpu.VMEM((steps, units, part), jnp.bfloat16),
            pltpu.VMEM((part, nodes), jnp.bfloat16),
            pltpu.VMEM((part, units), jnp.bfloat16),
            pltpu.VMEM((width, units), jnp.bfloat16),
            pltpu.VMEM((width, units), jnp.bfloat16),
            pltpu.VMEM(blocks, jnp.bfloat16),
            pltpu.VMEM(blocks, jnp.bfloat16),
        ]
        + scratch,
        compiler_params=params(36, collective),
        name="scatter_layer",
    )(*in_hbm(words), *operands[1:3], *in_hbm(weight), *operands[4:])


def active_grad(step, state_ref, preact_ref, back_ref, send_ref):
    block = state_ref.shape[1]
    chosen = chosen_nodes(send_ref[...], step * block, block)
    upper = state_ref[...] + dot(back_ref[...], chosen, TRANS_RIGHT)
    preact = preact_ref[...]
    gate = jax.nn.sigmoid(preact)
    active = preact * gate
    norm = lax.rsqrt(jnp.sum(active * active, axis=0, keepdims=True) + 1e-06)
    along = jnp.sum(active * upper, axis=0, keepdims=True)
    inner = norm * upper - active * (norm * norm * norm * along)
    return (inner * (gate * (1.0 + preact * (1.0 - gate)))).astype(jnp.bfloat16)


def middle_kernel(
    fanout,
    state_ref,
    preact_ref,
    returned_ref,
    send_ref,
    words_ref,
    weight_ref,
    own_block,
    mean_block,
    above_ref,
    notes_ref,
    grad_ref,
    rows_ref,
    sums_ref,
    halo_ref,
    early_ref,
    back_ref,
    counts_ref,
    far_sums,
    total_ref,
):
    step = pl.program_id(0)
    units, block = state_ref.shape
    halo = halo_ref.shape[0]
    nodes = block * pl.num_programs(0)
    first = far_start(nodes)
    part = (nodes + halo) // WORDS

    @pl.when(step == 0)
    def _():
        back_ref[...] = returned_ref[...].reshape(halo, units).T
        sums_ref[...] = jnp.zeros_like(sums_ref)
        far_sums[...] = jnp.zeros_like(far_sums)
        total_ref[...] = jnp.zeros_like(total_ref)

    base = first // part * part
    for row in range(first, nodes + halo, UNIT):
        spread_unit(words_ref, (row - base) // SLOTS, counts_ref, row - first)
    grad = active_grad(step, state_ref, preact_ref, back_ref, send_ref)
    grad_ref[...] = grad
    rows = grad.T
    rows_ref[...] = rows
    sums_ref[...] += column_sums(rows)
    far_sums[...] += dot(counts_ref[...], rows)
    width = own_block.shape[0]
    total_ref[:width, :] += dot(own_block[...], rows)
    total_ref[width:, :] += dot(mean_block[...], rows)

    @pl.when(step == pl.num_programs(0) - 1)
    def _():
        near = weight_ref[units:, :].T.astype(jnp.bfloat16)
        sums = unscaled(far_sums[...], fanout)[nodes - first :]
        halo_ref[...] = dot(sums, near).astype(jnp.bfloat16)
        early_ref[:, :units] = total_ref[...].astype(jnp.bfloat16)
        height, narrow = above_ref.shape
        above = jnp.concatenate(
            [above_ref[...], jnp.zeros((height, 128 - narrow), jnp.float32)], axis=1
        )
        above = put_terms(above, [notes_ref[0:1, 0:1], notes_ref[8:9, 0:1]])
        early_ref[:, units:] = above.astype(jnp.bfloat16)


def middle_layer(
    state_grad, preact, returned, send_row, words, weight, own, mean, above, notes, fanout
):
    units, nodes = preact.shape
    width = own.shape[0]
    wide = units + 128
    halo = send_row.shape[1]
    part = (nodes + halo) // WORDS
    span = part // SLOTS
    far_words = WORDS - far_start(nodes) // part
    far_height = nodes + halo - far_start(nodes)
    return pl.pallas_call(
        functools.partial(middle_kernel, fanout),
        grid=(nodes // BLOCK,),
        in_specs=[
            lanes(units, BLOCK),
            lanes(units, BLOCK),
            whole(returned.shape),
            whole(send_row.shape),
            pl.BlockSpec((far_words * span, BLOCK), lambda i: (WORDS // far_words - 1, i)),
            whole(weight.shape),
            lanes(width, BLOCK),
            lanes(width, BLOCK),
            whole(above.shape),
            whole(notes.shape),
        ],
        out_specs=[
            lanes(units, BLOCK),
            pl.BlockSpec((BLOCK, units), lambda i: (i, 0)),
            whole((16, units)),
            whole((halo, units)),
            whole((2 * width, wide)),
        ],
        out_shape=[
            jax.ShapeDtypeStruct((units, nodes), jnp.bfloat16),
            jax.ShapeDtypeStruct((nodes, units), jnp.bfloat16),
            jax.ShapeDtypeStruct((16, units), jnp.float32),
            jax.ShapeDtypeStruct((halo, units), jnp.bfloat16),
            jax.ShapeDtypeStruct((2 * width, wide), jnp.bfloat16),
        ],
        scratch_shapes=[
            pltpu.VMEM((units, halo), jnp.bfloat16),
            pltpu.VMEM((far_height, BLOCK), jnp.bfloat16),
            pltpu.VMEM((far_height, units), jnp.float32),
            pltpu.VMEM((2 * width, units), jnp.float32),
        ],
        compiler_params=params(30),
        name="middle_layer",
    )(
        state_grad,
        *in_hbm(preact),
        returned,
        send_row,
        *in_hbm(words, weight),
        own,
        *in_hbm(mean),
        above,
        notes,
    )


def in_two(value):
    high = value.astype(jnp.bfloat16)
    return high, (value - high.astype(jnp.float32)).astype(jnp.bfloat16)


def product(left, right, dims=(((1,), (0,)), ((), ()))):
    if left.dtype == jnp.bfloat16:
        high, low = in_two(right)
        return dot(left, high, dims) + dot(left, low, dims)
    high, low = in_two(left)
    if right.dtype == jnp.bfloat16:
        return dot(high, right, dims) + dot(low, right, dims)
    right_high, right_low = in_two(right)
    return dot(high, right_high, dims) + (
        dot(high, right_low, dims) + dot(low, right_high, dims)
    )


def moments(turned, first, second):
    first = beta_one * first + (1.0 - beta_one) * turned
    second = beta_two * second + (1.0 - beta_two) * turned * turned
    update = first / (1.0 - beta_one**STEP) / (jnp.sqrt(second / (1.0 - beta_two**STEP)) + epsilon)
    return first, second, update


def bottom_kernel(
    mesh_sizes,
    state_ref,
    preact_ref,
    returned_ref,
    send_ref,
    own_block,
    mean_block,
    sums_two,
    sums_three,
    early_ref,
    count_ref,
    *refs,
):
    refs = list(refs)
    kept, refs = refs[:10], refs[10:]
    late_out, *new, back_ref, weight_ref, late_ref = refs[:10]
    land_ref, plane_land, part_ref, high_land, whole_ref, last_land = refs[10:16]
    fetched, refs = refs[16:26], refs[26:]
    plane_sems, inward, across, outward = refs[:2], refs[2:4], refs[4:6], refs[6:8]
    fetch_sem = refs[8]
    step = pl.program_id(0)
    units = state_ref.shape[0]
    halo = send_ref.shape[1]
    top, _, _, me = split_place(mesh_sizes)

    @pl.when(step == 0)
    def _():
        greet_split(mesh_sizes)
        for index, (source, target) in enumerate(zip(kept, fetched)):
            pltpu.make_async_copy(source, target, fetch_sem.at[index]).start()
        back_ref[...] = returned_ref[...].reshape(halo, units).T
        weight_ref[...] = jnp.zeros_like(weight_ref)
        pieces = []
        for sums in (sums_two, sums_three):
            for start in range(0, sums.shape[1], 128):
                pieces.append(sums[:1, start : start + 128])
        narrow = pieces[-1].shape[1]
        pieces[-1] = jnp.concatenate(
            [pieces[-1], jnp.zeros((1, 128 - narrow), jnp.float32)], axis=1
        )
        row = units // 128 * 2 * weight_ref.shape[1]
        rest = late_ref.shape[0] - row
        pieces.append(jnp.zeros((rest - len(pieces), 128), jnp.float32))
        late_ref[row:, :] = jnp.concatenate(pieces).astype(jnp.bfloat16)
        split_greeted(mesh_sizes)
        each_plane(
            mesh_sizes,
            lambda other, where: push(early_ref, land_ref.at[:, me], plane_sems, where),
        )

    grad = active_grad(step, state_ref, preact_ref, back_ref, send_ref)
    width = own_block.shape[0]
    weight_ref[0, :width, :] += dot(own_block[...], grad, TRANS_RIGHT)
    weight_ref[1] += dot(mean_block[...], grad, TRANS_RIGHT)

    @pl.when(step == pl.num_programs(0) - 1)
    def _():
        padded = weight_ref.shape[1]
        row = 0
        for start in range(0, units, 128):
            for half in range(2):
                late_ref[row : row + padded, :] = weight_ref[half, :, start : start + 128].astype(
                    jnp.bfloat16
                )
                row += padded
        tall = part_ref.shape[0]

        def rows_of(place):
            return late_ref.at[pl.ds(pl.multiple_of(place * tall, tall), tall)]

        each_plane(
            mesh_sizes,
            lambda other, where: push(rows_of(other), plane_land.at[me], inward, where),
        )
        for index, (source, target) in enumerate(zip(kept, fetched)):
            pltpu.make_async_copy(source, target, fetch_sem.at[index]).wait()
        left_two, right_two, left_three, right_three = fetched[:4]
        weight_two, first_two, second_two = fetched[4:7]
        weight_three, first_three, second_three = fetched[7:]
        share = 1.0 / count_ref[...]
        plane_blocks_wait(mesh_sizes, land_ref, plane_sems)
        land_ref[:, me] = early_ref[...]
        early = land_ref[...].reshape(-1, land_ref.shape[3])
        grad = early[:, :units]
        turned = product(product(left_two[...], grad, TRANS_LEFT), right_two[...]) * share
        new_first, new_second, update = moments(turned, first_two[...], second_two[...])
        new[1][...] = new_first
        new[2][...] = new_second

        plane_wait(mesh_sizes, plane_land, inward)
        plane_land[me] = late_ref[pl.ds(pl.multiple_of(me * tall, tall), tall), :]
        part_ref[...] = jnp.sum(plane_land[...].astype(jnp.float32), axis=0).astype(jnp.bfloat16)
        each_high(
            mesh_sizes, lambda other, where: push(part_ref, high_land.at[top], across, where)
        )

        moved = product(product(left_two[...], update), right_two[...], TRANS_RIGHT)
        new[0][...] = weight_two[...] - step_rates[1] * moved

        high_wait(mesh_sizes, high_land, across)
        high_land[top] = part_ref[...]
        whole_ref[...] = jnp.sum(high_land[...].astype(jnp.float32), axis=0).astype(jnp.bfloat16)
        each_plane(
            mesh_sizes, lambda other, where: push(whole_ref, last_land.at[me], outward, where)
        )

        kinds = right_three.shape[0]
        grad = early[:, units:].astype(jnp.float32).T[:kinds].astype(jnp.bfloat16)
        turned = product(right_three[...], product(grad, left_three[...]), TRANS_LEFT) * share
        new_first, new_second, update = moments(turned, first_three[...], second_three[...])
        new[4][...] = new_first
        new[5][...] = new_second
        moved = product(right_three[...], product(update, left_three[...], TRANS_RIGHT))
        new[3][...] = weight_three[...] - step_rates[2] * moved

        plane_wait(mesh_sizes, last_land, outward)
        last_land[me] = whole_ref[...]
        late_out[...] = last_land[...]


def bottom_layer(
    state_grad,
    preact,
    returned,
    send_row,
    own,
    mean,
    sums_two,
    sums_three,
    early,
    count,
    kept,
    mesh_sizes,
    collective,
):
    units, nodes = preact.shape
    width = own.shape[0]
    padded = mean.shape[0]
    halo = send_row.shape[1]
    rows = units // 128 * (2 * padded + 1) + -(-sums_three.shape[1] // 128)
    rows = -(-rows // 512) * 512
    high, low, along = split_sizes(mesh_sizes)
    plane = low * along
    early_blocks = (high, plane) + early.shape[1:]
    late_blocks = (plane, rows // plane, 128)
    hbm = pl.BlockSpec(memory_space=pl.ANY)
    new = [jax.ShapeDtypeStruct(array.shape, jnp.float32) for array in kept[4:]]
    return pl.pallas_call(
        functools.partial(bottom_kernel, mesh_sizes),
        grid=(nodes // BLOCK,),
        in_specs=[
            lanes(units, BLOCK),
            lanes(units, BLOCK),
            whole(returned.shape),
            whole(send_row.shape),
            lanes(width, BLOCK),
            lanes(padded, BLOCK),
            whole(sums_two.shape),
            whole(sums_three.shape),
            whole(early.shape),
            whole(count.shape),
        ]
        + [hbm] * len(kept),
        out_specs=[whole(late_blocks)] + [whole(array.shape) for array in new],
        out_shape=[jax.ShapeDtypeStruct(late_blocks, jnp.bfloat16)] + new,
        scratch_shapes=[
            pltpu.VMEM((units, halo), jnp.bfloat16),
            pltpu.VMEM((2, padded, units), jnp.float32),
            pltpu.VMEM((rows, 128), jnp.bfloat16),
            pltpu.VMEM(early_blocks, jnp.bfloat16),
            pltpu.VMEM(late_blocks, jnp.bfloat16),
            pltpu.VMEM(late_blocks[1:], jnp.bfloat16),
            pltpu.VMEM((high,) + late_blocks[1:], jnp.bfloat16),
            pltpu.VMEM(late_blocks[1:], jnp.bfloat16),
            pltpu.VMEM(late_blocks, jnp.bfloat16),
        ]
        + [pltpu.VMEM(array.shape, array.dtype) for array in kept]
        + semaphores() * 4
        + [pltpu.SemaphoreType.DMA((len(kept),))],
        compiler_params=params(34, collective),
        name="bottom_layer",
    )(
        state_grad,
        *in_hbm(preact),
        returned,
        send_row,
        *in_hbm(own, mean),
        sums_two,
        sums_three,
        early,
        count,
        *in_hbm(*kept),
    )


def adam_kernel(
    padded,
    late_ref,
    count_ref,
    weight_one,
    left_one,
    right_one,
    first_one,
    second_one,
    bias_ref,
    bias_first,
    bias_second,
    *refs,
):
    ready, refs = refs[:6], refs[6:]
    outs, sem = refs[:12], refs[12]
    for index in range(6):
        pltpu.make_async_copy(ready[index], outs[3 + index], sem.at[index]).start()
    share = 1.0 / count_ref[...]
    units = weight_one.shape[1]
    width = weight_one.shape[0] // 2

    late_rows = late_ref[...].astype(jnp.float32)
    columns = []
    for start in range(0, units, 128):
        row = start // 128 * 2 * padded
        columns.append(
            jnp.concatenate(
                [late_rows[row : row + width], late_rows[row + padded : row + padded + width]]
            )
        )
    grad = jnp.concatenate(columns, axis=1).astype(jnp.bfloat16)
    turned = product(product(left_one[...], grad, TRANS_LEFT), right_one[...]) * share
    new_first, new_second, update = moments(turned, first_one[...], second_one[...])
    outs[1][...] = new_first
    outs[2][...] = new_second
    moved = product(product(left_one[...], update), right_one[...], TRANS_RIGHT)
    outs[0][...] = weight_one[...] - step_rates[0] * moved

    size = bias_ref.shape[0]
    pieces = []
    for start in range(0, units, 128):
        row = start // 128 * 2 * padded + padded + width
        pieces.append(late_rows[row : row + 1])
    row = units // 128 * 2 * padded
    while len(pieces) * 128 < size:
        pieces.append(late_rows[row : row + 1])
        row += 1
    grad = jnp.concatenate(pieces, axis=1)[:, :size] * share
    flat = bias_ref.shape
    bias, first, second = (ref[...].reshape(grad.shape) for ref in (bias_ref, bias_first, bias_second))
    new_first, new_second, update = moments(grad, first, second)
    outs[9][...] = (bias - bias_rate * (update + weight_decay * bias)).reshape(flat)
    outs[10][...] = new_first.reshape(flat)
    outs[11][...] = new_second.reshape(flat)
    for index in range(6):
        pltpu.make_async_copy(ready[index], outs[3 + index], sem.at[index]).wait()


def adam(padded, late_all, count, state, ready):
    vmem = pl.BlockSpec(memory_space=pltpu.VMEM)
    hbm = pl.BlockSpec(memory_space=pl.ANY)
    one, bias = state[0], state[5]
    shapes = [one.shape] * 3 + [array.shape for array in ready] + [bias.shape] * 3
    return pl.pallas_call(
        functools.partial(adam_kernel, padded),
        in_specs=[vmem] * (2 + len(state)) + [hbm] * len(ready),
        out_specs=[vmem] * 3 + [hbm] * 6 + [vmem] * 3,
        out_shape=[jax.ShapeDtypeStruct(shape, jnp.float32) for shape in shapes],
        scratch_shapes=[pltpu.SemaphoreType.DMA((6,))],
        compiler_params=pltpu.CompilerParams(vmem_limit_bytes=24 * MIB),
        name="adam",
    )(late_all, count, *in_hbm(*state), *ready)


def on_device(
    mesh_sizes,
    features,
    labels,
    seed_rows,
    seed_mask,
    send_rows,
    neighbors_one,
    neighbors_two,
    neighbors_three,
    weight_one,
    weight_two,
    weight_three,
    left_one,
    right_one,
    left_two,
    right_two,
    left_three,
    right_three,
    first_one,
    first_two,
    first_three,
    second_one,
    second_two,
    second_three,
    bias_all,
    bias_first,
    bias_second,
):
    units = weight_one.shape[1]
    classes = weight_three.shape[1]
    halo = send_rows.size
    fans = (neighbors_one.shape[1], neighbors_two.shape[1], neighbors_three.shape[1])
    feats = features.T
    weight_three = weight_three.T
    padded_classes = -(-classes // 16) * 16
    seed_slots = (
        padded_classes,
        seed_rows.reshape(1, -1),
        labels.reshape(1, -1),
        seed_mask.reshape(1, -1),
    )

    words_one, got, send_row = count_words(
        neighbors_one.T, mesh_sizes, 0, halo, feats=feats, send_rows=send_rows.T
    )
    feats = in_hbm(feats)[0]
    state_one, preact_one, sent, mean_one = hidden_layer(
        words_one, feats, got, weight_one, bias_all, 0, send_row, fans[0]
    )
    words_two, got = count_words(neighbors_two.T, mesh_sizes, 1, halo, sent=sent)
    state_two, preact_two, sent, mean_two = hidden_layer(
        words_two, state_one, got, weight_two, bias_all, units, send_row, fans[1]
    )
    words_three, got, seeds = count_words(
        neighbors_three.T, mesh_sizes, 2, halo, sent=sent, seeds=seed_slots
    )
    grad_three, rows_three, sums_three, notes, table_three, far, halo_grad = last_layer(
        words_three, state_two, got, weight_three, bias_all, 2 * units, seeds, fans[2]
    )
    state_grad, returned, weight_grad = scatter_layer(
        words_three,
        grad_three,
        rows_three,
        weight_three,
        halo_grad,
        mesh_sizes,
        3,
        fans[2],
        tables=(far, table_three),
    )
    grad_two, rows_two, sums_two, halo_grad, early = middle_layer(
        state_grad,
        preact_two,
        returned,
        send_row,
        words_two,
        weight_two,
        state_one,
        mean_two,
        weight_grad,
        notes,
        fans[1],
    )
    state_grad, returned, early_sum, loss, count = scatter_layer(
        words_two, grad_two, rows_two, weight_two, halo_grad, mesh_sizes, 4, fans[1], early=early
    )
    late_all, *ready = bottom_layer(
        state_grad,
        preact_one,
        returned,
        send_row,
        feats,
        mean_one,
        sums_two,
        sums_three,
        early_sum,
        count,
        (
            left_two,
            right_two,
            left_three,
            right_three,
            weight_two,
            first_two,
            second_two,
            weight_three,
            first_three.T,
            second_three.T,
        ),
        mesh_sizes,
        5,
    )
    out = adam(
        mean_one.shape[0],
        late_all.reshape(-1, 128),
        count,
        (
            weight_one,
            left_one,
            right_one,
            first_one,
            second_one,
            bias_all,
            bias_first,
            bias_second,
        ),
        ready,
    )
    third = [value.T for value in out[6:9]]
    return (*out[:6], *third, *out[9:12], loss.reshape(()), count.reshape(()))


def solution(mesh):
    split = P(axes)
    rows = P(axes, None)
    placed = (rows, split, split, split, rows, rows, rows, rows) + (P(),) * 18
    mesh_sizes = (mesh.shape[axes[0]], mesh.shape[axes[1]])
    return jax.shard_map(
        functools.partial(on_device, mesh_sizes),
        mesh=mesh,
        in_specs=placed,
        out_specs=(P(),) * 14,
        check_vma=False,
    )
```

```python
import functools

import jax
import jax.numpy as jnp
from jax import lax
from jax.experimental import pallas as pl
from jax.experimental.pallas import tpu as pltpu
from jax.sharding import PartitionSpec as P

STEP = 10


beta_one = 0.9
beta_two = 0.999
epsilon = 1e-08
step_rates = (0.05, 0.5, 1.0)
bias_rate = 0.05
weight_decay = 0.01

axes = ("dom", "rep")
WORDS = 4
SLOTS = 8
RUN = 48
UNIT = SLOTS * RUN
BLOCK = 1024
LIST_BLOCK = 512
MIB = 1024 * 1024
TRANS_LEFT = (((0,), (0,)), ((), ()))
TRANS_RIGHT = (((1,), (1,)), ((), ()))


def dot(left, right, dims=(((1,), (0,)), ((), ()))):
    return lax.dot_general(left, right, dims, preferred_element_type=jnp.float32)


def params(limit, collective=None):
    remote = {} if collective is None else dict(collective_id=collective, has_side_effects=True)
    return pltpu.CompilerParams(
        dimension_semantics=("arbitrary",), vmem_limit_bytes=limit * MIB, **remote
    )


def in_hbm(*arrays):
    return [pltpu.with_memory_space_constraint(array, pltpu.HBM) for array in arrays]


def whole(shape):
    return pl.BlockSpec(shape, lambda i: (0,) * len(shape))


def lanes(rows, width):
    return pl.BlockSpec((rows, width), lambda i: (0, i))


def floor_over(value, size):
    return ((value.astype(jnp.float32) + 0.5) * (1.0 / size)).astype(jnp.int32)


def words_layer(near_ref, out_ref, place_ref, field_ref):
    fanout, block = near_ref.shape
    span = out_ref.shape[0] // WORDS
    near = near_ref[...]
    unit = floor_over(near, UNIT)
    rest = near - unit * UNIT
    slot = floor_over(rest, RUN)
    word = floor_over(unit, span // RUN)
    place = (unit - word * (span // RUN)) * RUN + rest - slot * RUN
    bit = jnp.left_shift(jnp.int32(1), slot * 4)
    parts = [jnp.where(word == k, bit, 0) for k in range(WORDS)]
    totals = [jnp.zeros_like(bit) for _ in range(WORDS)]
    for g in range(fanout):
        same = place == place[g : g + 1]
        for k in range(WORDS):
            totals[k] = totals[k] + jnp.where(same, parts[k][g : g + 1], 0)
    place_ref[:fanout, :] = place
    for k in range(WORDS):
        field_ref[k, :fanout, :] = totals[k]
    chunk = RUN
    for tile in range(0, block, 128):
        cols = slice(tile, tile + 128)
        for start in range(0, span, chunk):
            rows = lax.broadcasted_iota(jnp.int32, (chunk, 128), 0) + start
            sums = [jnp.zeros((chunk, 128), jnp.int32) for _ in range(WORDS)]
            for g in range(fanout):
                hit = rows == place_ref[g : g + 1, cols]
                for k in range(WORDS):
                    sums[k] = jnp.where(hit, field_ref[k, g : g + 1, cols], sums[k])
            for k in range(WORDS):
                out_ref[k * span + start : k * span + start + chunk, cols] = sums[k]


def my_index(mesh_sizes):
    return lax.axis_index(axes[0]) * mesh_sizes[1] + lax.axis_index(axes[1])


def each_peer(mesh_sizes, act):
    across, along = mesh_sizes
    row, column = lax.axis_index(axes[0]), lax.axis_index(axes[1])

    def wrapped(value, size):
        return jnp.where(value >= size, value - size, value)

    def line(down, carry):
        other = wrapped(row + down, across)
        for ahead in range(along):
            place = wrapped(column + ahead, along)
            act(other * along + place, (other, place))
        return carry

    for ahead in range(1, along):
        place = wrapped(column + ahead, along)
        act(row * along + place, (row, place))
    for down in range(1, across):
        line(down, 0)


def greet(mesh_sizes):
    barrier = pltpu.get_barrier_semaphore()

    def tell(index, where):
        pl.semaphore_signal(
            barrier, inc=1, device_id=where, device_id_type=pl.DeviceIdType.MESH
        )

    each_peer(mesh_sizes, tell)


def all_greeted(mesh_sizes):
    pl.semaphore_wait(pltpu.get_barrier_semaphore(), mesh_sizes[0] * mesh_sizes[1] - 1)


def send_blocks(mesh_sizes, out_ref, in_ref, send_sem, recv_sem):
    me = my_index(mesh_sizes)

    def send(index, where):
        pltpu.make_async_remote_copy(
            src_ref=out_ref.at[index],
            dst_ref=in_ref.at[me],
            send_sem=send_sem,
            recv_sem=recv_sem,
            device_id=where,
            device_id_type=pl.DeviceIdType.MESH,
        ).start()

    each_peer(mesh_sizes, send)


def send_all(mesh_sizes, own_ref, in_ref, send_sem, recv_sem):
    me = my_index(mesh_sizes)

    def send(index, where):
        pltpu.make_async_remote_copy(
            src_ref=own_ref,
            dst_ref=in_ref.at[me],
            send_sem=send_sem,
            recv_sem=recv_sem,
            device_id=where,
            device_id_type=pl.DeviceIdType.MESH,
        ).start()

    each_peer(mesh_sizes, send)


def wait_moves(mesh_sizes, out_ref, in_ref, send_sem, recv_sem):
    others = pl.ds(0, mesh_sizes[0] * mesh_sizes[1] - 1)
    copy = pltpu.make_async_remote_copy(
        src_ref=in_ref.at[others],
        dst_ref=in_ref.at[others],
        send_sem=send_sem,
        recv_sem=recv_sem,
        device_id=(lax.axis_index(axes[0]), lax.axis_index(axes[1])),
        device_id_type=pl.DeviceIdType.MESH,
    )
    copy.wait_send()
    copy.wait_recv()


def split_sizes(mesh_sizes):
    across, along = mesh_sizes
    high = 4 if across % 4 == 0 else 1
    return high, across // high, along


def split_place(mesh_sizes):
    _, low, along = split_sizes(mesh_sizes)
    row, column = lax.axis_index(axes[0]), lax.axis_index(axes[1])
    top = row // low
    return top, row - top * low, column, (row - top * low) * along + column


def each_high(mesh_sizes, act):
    high, low, _ = split_sizes(mesh_sizes)
    top, bottom, column, _ = split_place(mesh_sizes)
    for ahead in range(1, high):
        other = top + ahead
        other = jnp.where(other >= high, other - high, other)
        act(other, (other * low + bottom, column))


def each_plane(mesh_sizes, act):
    _, low, along = split_sizes(mesh_sizes)
    top, bottom, column, _ = split_place(mesh_sizes)
    for down in range(low):
        for ahead in range(along):
            if down == 0 and ahead == 0:
                continue
            line = bottom + down
            line = jnp.where(line >= low, line - low, line)
            place = column + ahead
            place = jnp.where(place >= along, place - along, place)
            act(line * along + place, (top * low + line, place))


def greet_split(mesh_sizes):
    barrier = pltpu.get_barrier_semaphore()

    def tell(index, where):
        pl.semaphore_signal(
            barrier, inc=1, device_id=where, device_id_type=pl.DeviceIdType.MESH
        )

    each_high(mesh_sizes, tell)
    each_plane(mesh_sizes, tell)


def split_greeted(mesh_sizes):
    high, low, along = split_sizes(mesh_sizes)
    pl.semaphore_wait(pltpu.get_barrier_semaphore(), high - 1 + low * along - 1)


def push(src_ref, dst_ref, sems, where):
    pltpu.make_async_remote_copy(
        src_ref=src_ref,
        dst_ref=dst_ref,
        send_sem=sems[0],
        recv_sem=sems[1],
        device_id=where,
        device_id_type=pl.DeviceIdType.MESH,
    ).start()


def wait_pushed(ref, sems):
    copy = pltpu.make_async_remote_copy(
        src_ref=ref,
        dst_ref=ref,
        send_sem=sems[0],
        recv_sem=sems[1],
        device_id=(lax.axis_index(axes[0]), lax.axis_index(axes[1])),
        device_id_type=pl.DeviceIdType.MESH,
    )
    copy.wait_send()
    copy.wait_recv()


def high_start(mesh_sizes, sent_ref, relay_ref, sems):
    top = split_place(mesh_sizes)[0]
    each_high(
        mesh_sizes, lambda other, where: push(sent_ref.at[other], relay_ref.at[top], sems, where)
    )


def high_wait(mesh_sizes, relay_ref, sems):
    high = split_sizes(mesh_sizes)[0]
    if high > 1:
        wait_pushed(relay_ref.at[pl.ds(0, high - 1)], sems)


def plane_wait(mesh_sizes, land_ref, sems):
    _, low, along = split_sizes(mesh_sizes)
    wait_pushed(land_ref.at[pl.ds(0, low * along - 1)], sems)


def plane_blocks(mesh_sizes, relay_ref, land_ref, sems):
    me = split_place(mesh_sizes)[3]
    each_plane(
        mesh_sizes,
        lambda other, where: push(relay_ref.at[:, other], land_ref.at[:, me], sems, where),
    )


def plane_blocks_wait(mesh_sizes, land_ref, sems):
    _, low, along = split_sizes(mesh_sizes)
    wait_pushed(land_ref.at[:, pl.ds(0, low * along - 1)], sems)


NOTES = 120


def put_terms(rows, values):
    lane = lax.broadcasted_iota(jnp.int32, rows.shape, 1)
    for index, value in enumerate(values):
        for at in range(3):
            term = value.astype(jnp.bfloat16).astype(jnp.float32)
            rows = jnp.where(lane == NOTES + 3 * index + at, term, rows)
            value = value - term
    return rows


def take_terms(rows):
    lane = lax.broadcasted_iota(jnp.int32, rows.shape, 1)
    values = []
    for index in range(2):
        first = NOTES + 3 * index
        mine = (lane >= first) & (lane < first + 3)
        values.append(jnp.sum(jnp.where(mine, rows, 0.0), axis=1, keepdims=True))
    return values


def semaphores():
    return [pltpu.SemaphoreType.DMA, pltpu.SemaphoreType.DMA]


def one_row(rows):
    per, parts = rows.shape
    column = lax.broadcasted_iota(jnp.int32, (parts, parts * per), 1)
    owner = lax.broadcasted_iota(jnp.int32, (parts, parts * per), 0)
    rest = column - owner * per
    mine = jnp.where((rest >= 0) & (rest < per), 1.0, 0.0).astype(jnp.bfloat16)
    high = (rows >> 7).astype(jnp.float32).astype(jnp.bfloat16)
    low = (rows & 127).astype(jnp.float32).astype(jnp.bfloat16)
    wide = dot(high, mine) * 128.0 + dot(low, mine)
    column = lax.broadcasted_iota(jnp.int32, wide.shape, 1)
    at = lax.broadcasted_iota(jnp.int32, wide.shape, 0)
    picked = jnp.where(column - floor_over(column, per) * per == at, wide, 0.0)
    return jnp.sum(picked, axis=0, keepdims=True).astype(jnp.int32)


def chosen_nodes(send_row, start, count):
    node = (lax.broadcasted_iota(jnp.int32, (count, 128), 0) + start).astype(jnp.int16)
    one = jnp.ones((count, 128), jnp.bfloat16)
    pieces = []
    for tile in range(0, send_row.shape[1], 128):
        wanted = jnp.broadcast_to(send_row[:, tile : tile + 128], (16, 128)).astype(jnp.int16)
        wanted = jnp.concatenate([wanted] * (count // 16))
        pieces.append(jnp.where(node == wanted, one, jnp.zeros_like(one)))
    return jnp.concatenate(pieces, axis=1)


def words_kernel(mesh_sizes, kind, near_ref, *refs):
    refs = list(refs)
    if kind == "features":
        feats_ref, send_ref, out_ref, got_ref, row_ref, sent_ref = refs[:6]
        refs = refs[6:]
    elif kind == "seeds":
        sent_ref, slots_ref, labels_ref, mask_ref, out_ref, got_ref, seeds_ref = refs[:7]
        refs = refs[7:]
    else:
        sent_ref, out_ref, got_ref = refs[:3]
        refs = refs[3:]
    place_ref, field_ref, land_ref, send_sem, recv_sem = refs
    step = pl.program_id(0)
    block = near_ref.shape[1]
    moves = (mesh_sizes, sent_ref, land_ref, send_sem, recv_sem)

    @pl.when(step == 0)
    def _():
        greet(mesh_sizes)

    if kind == "features":

        @pl.when(step == 0)
        def _():
            width, nodes = feats_ref.shape
            halo = row_ref.shape[1]
            row_ref[...] = one_row(send_ref[...])
            total = jnp.zeros((width, halo), jnp.float32)
            for start in range(0, nodes, block):
                chosen = chosen_nodes(row_ref[...], start, block)
                total = total + dot(feats_ref[:, start : start + block], chosen)
            padded = sent_ref.shape[2]
            total = jnp.concatenate([total, jnp.zeros((padded - width, halo), jnp.float32)])
            sent_ref[...] = total.T.astype(jnp.bfloat16).reshape(sent_ref.shape)

    if kind == "seeds":
        classes = seeds_ref.shape[0]
        slots = slots_ref.shape[1]
        label = lax.broadcasted_iota(jnp.int32, (classes, slots), 0)
        marked = jnp.where((label == labels_ref[...]) & (mask_ref[...] != 0), 1.0, 0.0)
        chosen = chosen_nodes(slots_ref[...], step * block, block)
        seeds_ref[...] = dot(marked.astype(jnp.bfloat16), chosen, TRANS_RIGHT)

    words_layer(near_ref, out_ref, place_ref, field_ref)

    @pl.when(step == 0)
    def _():
        all_greeted(mesh_sizes)
        send_blocks(*moves)

    @pl.when(step == pl.num_programs(0) - 1)
    def _():
        me = my_index(mesh_sizes)
        wait_moves(*moves)
        land_ref[me] = sent_ref[me]
        got_ref[...] = land_ref[...]


def words_space(table, near):
    return pltpu.VMEM if near and table <= 5120 else pltpu.HBM


def place_words(words, near):
    return pltpu.with_memory_space_constraint(words, words_space(words.shape[0] * SLOTS, near))


def count_words(
    near, mesh_sizes, collective, halo, sent=None, feats=None, send_rows=None, seeds=None
):
    fanout, nodes = near.shape
    parts = mesh_sizes[0] * mesh_sizes[1]
    height = (nodes + halo) // SLOTS
    in_specs = [lanes(fanout, LIST_BLOCK)]
    operands = [near]
    scratch = []
    if sent is None:
        kind = "features"
        blocks = (parts, halo // parts, -(-feats.shape[0] // 128) * 128)
        in_specs += [whole(feats.shape), whole(send_rows.shape)]
        operands += in_hbm(feats, send_rows)
        scratch.append(pltpu.VMEM(blocks, jnp.bfloat16))
    else:
        kind = "plain"
        blocks = (parts, halo // parts, sent.shape[1])
        in_specs.append(whole(blocks))
        operands.append(sent.reshape(blocks))
    out_specs = [lanes(height, LIST_BLOCK), whole(blocks)]
    out_shape = [
        words_space(nodes + halo, sent is None)(
            (height, nodes), jnp.int32
        ),
        jax.ShapeDtypeStruct(blocks, jnp.bfloat16),
    ]
    if sent is None:
        out_specs.append(whole((1, halo)))
        out_shape.append(jax.ShapeDtypeStruct((1, halo), jnp.int32))
    if seeds is not None:
        kind = "seeds"
        classes, slots, labels, mask = seeds
        in_specs += [whole(slots.shape)] * 3
        operands += [slots, labels, mask]
        out_specs.append(lanes(classes, LIST_BLOCK))
        out_shape.append(jax.ShapeDtypeStruct((classes, nodes), jnp.float32))
    return pl.pallas_call(
        functools.partial(words_kernel, mesh_sizes, kind),
        grid=(nodes // LIST_BLOCK,),
        in_specs=in_specs,
        out_specs=out_specs,
        out_shape=out_shape,
        scratch_shapes=scratch
        + [
            pltpu.VMEM((16, LIST_BLOCK), jnp.int32),
            pltpu.VMEM((WORDS, 16, LIST_BLOCK), jnp.int32),
            pltpu.VMEM(blocks, jnp.bfloat16),
        ]
        + semaphores(),
        compiler_params=params(20, collective),
        name="count_words",
    )(*in_hbm(*operands[:1]), *operands[1:])


def field(words, slot):
    if slot == SLOTS - 1:
        picked = lax.shift_right_logical(words, 4 * slot)
    else:
        picked = words & (15 << (4 * slot))
    return picked.astype(jnp.float32).astype(jnp.bfloat16)


def slot_scale(slot):
    return 1.0 if slot == SLOTS - 1 else 2.0 ** (-4 * slot)


def spread_unit(words_ref, word_row, counts_ref, count_row):
    for start in range(0, RUN, 16):
        for tile in range(0, words_ref.shape[1], 256):
            cols = slice(tile, tile + 256)
            words = words_ref[word_row + start : word_row + start + 16, cols]
            for slot in range(SLOTS):
                row = count_row + slot * RUN + start
                counts_ref[row : row + 16, cols] = field(words, slot)


def gather_product(table_ref, words_ref, counts_ref):
    table = table_ref.shape[1]
    total = None
    for start in range(0, table, 2 * UNIT):
        stop = start + 2 * UNIT
        for row in range(start, stop, UNIT):
            spread_unit(words_ref, row // SLOTS, counts_ref, row)
        term = dot(table_ref[:, start:stop], counts_ref[start:stop, :])
        total = term if total is None else total + term
    return total


def scale_row(table):
    column = lax.broadcasted_iota(jnp.int32, (1, table), 1)
    rest = column - floor_over(column, UNIT) * UNIT
    slot = floor_over(rest, RUN)
    scale = jnp.ones((1, table), jnp.float32)
    for k in range(SLOTS - 1):
        scale = jnp.where(slot == k, slot_scale(k), scale)
    return scale


def column_of(row):
    return jnp.broadcast_to(row, (128, row.shape[1])).T


def late(rows, width):
    return pl.BlockSpec((rows, width), lambda i: (0, jnp.maximum(i - 1, 0)))


def now(rows, width, steps):
    return pl.BlockSpec((rows, width), lambda i: (0, jnp.minimum(i, steps - 1)))


def hidden_kernel(
    fanout,
    bias_start,
    words_ref,
    own_ref,
    own_block,
    got_ref,
    weight_ref,
    bias_ref,
    send_ref,
    state_ref,
    preact_ref,
    sent_ref,
    extra_ref,
    table_ref,
    counts_ref,
    picked_ref,
    mean_ref,
    self_ref,
    near_ref,
    bias_col,
):
    step = pl.program_id(0)
    last = pl.num_programs(0) - 1
    width, nodes = own_ref.shape
    units, block = state_ref.shape
    padded = mean_ref.shape[0]

    @pl.when(step == 0)
    def _():
        if table_ref.shape[0] > width:
            table_ref[...] = jnp.zeros_like(table_ref)
        got = got_ref[...].reshape(-1, got_ref.shape[2]).T[:width]
        scale = scale_row(table_ref.shape[1])
        own = own_ref[...].astype(jnp.float32) * scale[:, :nodes]
        table_ref[:width, :nodes] = own.astype(jnp.bfloat16)
        far = got.astype(jnp.float32) * scale[:, nodes:]
        table_ref[:width, nodes:] = far.astype(jnp.bfloat16)
        mean_ref[...] = jnp.zeros_like(mean_ref)
        picked_ref[...] = jnp.zeros_like(picked_ref)
        self_ref[...] = weight_ref[:width, :].T.astype(jnp.bfloat16)
        if padded > width:
            near_ref[...] = jnp.zeros_like(near_ref)
        near_ref[:, :width] = weight_ref[width:, :].T.astype(jnp.bfloat16)
        bias = bias_ref[...].reshape(1, -1)
        bias_col[...] = column_of(bias[:, bias_start : bias_start + units])

    def finish():
        mean = mean_ref[...]
        extra_ref[...] = mean
        if padded > width:
            extra_ref[width : width + 1, :] = jnp.ones((1, block), jnp.bfloat16)
        preact = dot(self_ref[...], own_block[...]) + dot(near_ref[...], mean) + bias_col[:, :1]
        preact_ref[...] = preact
        active = preact * jax.nn.sigmoid(preact)
        norm = lax.rsqrt(jnp.sum(active * active, axis=0, keepdims=True) + 1e-06)
        state = (active * norm).astype(jnp.bfloat16)
        state_ref[...] = state
        picked_ref[...] += dot(state, chosen_nodes(send_ref[...], (step - 1) * block, block))

    @pl.when(step < last)
    def _():
        finish()
        total = gather_product(table_ref, words_ref, counts_ref)
        mean_ref[...] = (total / fanout).astype(jnp.bfloat16)

    @pl.when(step == last)
    def _():
        finish()
        sent_ref[...] = picked_ref[...].T.astype(jnp.bfloat16)


def hidden_layer(words, own, got, weight, bias, bias_start, send_row, fanout):
    width, nodes = own.shape
    halo = send_row.shape[1]
    table = nodes + halo
    units = weight.shape[1]
    padded = width if width == units else (width // 16 + 1) * 16
    steps = nodes // BLOCK
    return pl.pallas_call(
        functools.partial(hidden_kernel, fanout, bias_start),
        grid=(steps + 1,),
        in_specs=[
            now(words.shape[0], BLOCK, steps),
            whole(own.shape),
            late(width, BLOCK),
            whole(got.shape),
            whole(weight.shape),
            whole(bias.shape),
            whole(send_row.shape),
        ],
        out_specs=[
            late(units, BLOCK),
            late(units, BLOCK),
            whole((halo, units)),
            late(padded, BLOCK),
        ],
        out_shape=[
            jax.ShapeDtypeStruct((units, nodes), jnp.bfloat16),
            pltpu.HBM((units, nodes), jnp.float32),
            jax.ShapeDtypeStruct((halo, units), jnp.bfloat16),
            pltpu.HBM((padded, nodes), jnp.bfloat16),
        ],
        scratch_shapes=[
            pltpu.VMEM((padded, table), jnp.bfloat16),
            pltpu.VMEM((table, BLOCK), jnp.bfloat16),
            pltpu.VMEM((units, halo), jnp.float32),
            pltpu.VMEM((padded, BLOCK), jnp.bfloat16),
            pltpu.VMEM((units, width), jnp.bfloat16),
            pltpu.VMEM((units, padded), jnp.bfloat16),
            pltpu.VMEM((units, 128), jnp.float32),
        ],
        compiler_params=params(40),
        name="hidden_layer",
    )(place_words(words, width != units), own, own, got, *in_hbm(weight, bias), send_row)


def far_start(nodes):
    return nodes // UNIT * UNIT


def column_sums(rows):
    return dot(jnp.ones((16, rows.shape[0]), jnp.bfloat16), rows)


def unscaled(sums, fanout):
    pieces = []
    for row in range(0, sums.shape[0], RUN):
        slot = row // RUN % SLOTS
        pieces.append((sums[row : row + RUN] * (slot_scale(slot) / fanout)).astype(jnp.bfloat16))
    return jnp.concatenate(pieces)


def last_kernel(
    fanout,
    bias_start,
    words_ref,
    own_ref,
    own_block,
    got_ref,
    weight_ref,
    bias_ref,
    seeds_ref,
    grad_ref,
    rows_ref,
    sums_ref,
    notes_ref,
    table_out,
    far_ref,
    halo_ref,
    reduced_ref,
    counts_ref,
    both_ref,
    self_ref,
    near_ref,
    bias_col,
    far_sums,
):
    step = pl.program_id(0)
    last = pl.num_programs(0) - 1
    classes = self_ref.shape[0]
    width, nodes = own_ref.shape
    kinds = weight_ref.shape[0]
    halo = far_ref.shape[0]
    first = far_start(nodes)

    @pl.when(step == 0)
    def _():
        table_out[:, :nodes] = own_ref[...]
        table_out[:, nodes:] = got_ref[...].reshape(halo, width).T
        more = jnp.zeros((classes - kinds, 2 * width), jnp.float32)
        weight = jnp.concatenate([weight_ref[...], more]).astype(jnp.bfloat16)
        self_ref[...] = weight[:, :width]
        near_ref[...] = weight[:, width:]
        rest = jnp.full((1, classes - kinds), -1e30, jnp.float32)
        bias = bias_ref[...].reshape(1, -1)
        bias_col[...] = column_of(
            jnp.concatenate([bias[:, bias_start : bias_start + kinds], rest], axis=1)
        )
        reduced = dot(near_ref[...], table_out[...]) * scale_row(table_out.shape[1])
        high = reduced.astype(jnp.bfloat16)
        reduced_ref[:classes, :] = high
        reduced_ref[classes:, :] = (reduced - high.astype(jnp.float32)).astype(jnp.bfloat16)
        both_ref[...] = jnp.zeros_like(both_ref)
        counts_ref[first:, :] = jnp.zeros_like(counts_ref[first:, :])

    @pl.when(step <= 1)
    def _():
        sums_ref[...] = jnp.zeros_like(sums_ref)
        notes_ref[...] = jnp.zeros_like(notes_ref)
        far_sums[...] = jnp.zeros_like(far_sums)

    def finish():
        near_part = (both_ref[:classes, :] + both_ref[classes:, :]) / fanout
        logits = dot(self_ref[...], own_block[...]) + near_part + bias_col[:, :1]
        top = jnp.max(logits, axis=0, keepdims=True)
        powers = jnp.exp(logits - top)
        total = jnp.sum(powers, axis=0, keepdims=True)
        normer = jnp.log(total) + top
        seeds = seeds_ref[...]
        uses = jnp.sum(seeds, axis=0, keepdims=True)
        grad = (powers / total * uses - seeds).astype(jnp.bfloat16)
        grad_ref[...] = grad
        loss = uses * normer - jnp.sum(seeds * logits, axis=0, keepdims=True)
        notes_ref[:8, :] += jnp.sum(loss)
        notes_ref[8:, :] += jnp.sum(uses)
        rows = grad.T
        rows_ref[...] = rows
        sums_ref[...] += column_sums(rows)
        far_sums[...] += dot(counts_ref[first:, :], rows)

    @pl.when(step < last)
    def _():
        finish()
        both_ref[...] = gather_product(reduced_ref, words_ref, counts_ref)

    @pl.when(step == last)
    def _():
        finish()
        sums = unscaled(far_sums[...], fanout)[nodes - first :]
        far_ref[...] = sums
        halo_ref[...] = dot(sums, near_ref[...]).astype(jnp.bfloat16)


def last_layer(words, own, got, weight, bias, bias_start, seeds, fanout):
    width, nodes = own.shape
    halo = got.shape[0] * got.shape[1]
    table = nodes + halo
    classes = seeds.shape[0]
    steps = nodes // BLOCK
    far_height = table - far_start(nodes)
    return pl.pallas_call(
        functools.partial(last_kernel, fanout, bias_start),
        grid=(steps + 1,),
        in_specs=[
            now(words.shape[0], BLOCK, steps),
            whole(own.shape),
            late(width, BLOCK),
            whole(got.shape),
            whole(weight.shape),
            whole(bias.shape),
            late(classes, BLOCK),
        ],
        out_specs=[
            late(classes, BLOCK),
            pl.BlockSpec((BLOCK, classes), lambda i: (jnp.maximum(i - 1, 0), 0)),
            whole((16, classes)),
            whole((16, 128)),
            whole((width, table)),
            whole((halo, classes)),
            whole((halo, width)),
        ],
        out_shape=[
            jax.ShapeDtypeStruct((classes, nodes), jnp.bfloat16),
            jax.ShapeDtypeStruct((nodes, classes), jnp.bfloat16),
            jax.ShapeDtypeStruct((16, classes), jnp.float32),
            jax.ShapeDtypeStruct((16, 128), jnp.float32),
            jax.ShapeDtypeStruct((width, table), jnp.bfloat16),
            jax.ShapeDtypeStruct((halo, classes), jnp.bfloat16),
            jax.ShapeDtypeStruct((halo, width), jnp.bfloat16),
        ],
        scratch_shapes=[
            pltpu.VMEM((2 * classes, table), jnp.bfloat16),
            pltpu.VMEM((table, BLOCK), jnp.bfloat16),
            pltpu.VMEM((2 * classes, BLOCK), jnp.float32),
            pltpu.VMEM((classes, width), jnp.bfloat16),
            pltpu.VMEM((classes, width), jnp.bfloat16),
            pltpu.VMEM((classes, 128), jnp.float32),
            pltpu.VMEM((far_height, classes), jnp.float32),
        ],
        compiler_params=params(40),
        name="last_layer",
    )(*in_hbm(words), own, own, got, *in_hbm(weight, bias), seeds)


def scatter_kernel(mesh_sizes, fanout, flipped, words_ref, grad_ref, rows_ref, *refs):
    refs = list(refs)
    if flipped:
        weight_in, halo_ref, far_ref, table_ref, far_table = refs[:5]
        state_ref, got_ref, weight_ref = refs[5:8]
        refs = refs[8:]
    else:
        weight_in, halo_ref, early_ref = refs[:3]
        state_ref, got_ref, early_sum, loss_ref, count_ref = refs[3:8]
        refs = refs[8:]
    padded_ref, counts_ref, sums_ref, self_ref, near_ref, relay_ref, land_ref = refs[:7]
    if flipped:
        high_sems, plane_sems = refs[7:9], refs[9:11]
    else:
        early_relay, early_part, early_land, early_own, early_back = refs[7:12]
        high_sems, plane_sems = refs[12:14], refs[14:16]
        early_high, early_plane, back_sems = refs[16:18], refs[18:20], refs[20:22]
    step = pl.program_id(0)
    units, nodes = grad_ref.shape
    width = state_ref.shape[0]
    span = words_ref.shape[0]
    part = span * SLOTS
    steps = -(-nodes // part)

    @pl.when(step == 0)
    def _():
        greet_split(mesh_sizes)
        for k in range(steps):
            start = k * part
            stop = min(start + part, nodes)
            padded_ref[k, :, : stop - start] = grad_ref[:, start:stop]
            if stop < start + part:
                padded_ref[k, :, stop - start :] = jnp.zeros(
                    (units, start + part - stop), jnp.bfloat16
                )
        weight = weight_in[...]
        if flipped:
            more = jnp.zeros((units - weight.shape[0], 2 * width), jnp.float32)
            weight = jnp.concatenate([weight, more]).T
            weight_ref[:width, :] = jnp.zeros((width, units), jnp.float32)
            weight_ref[width:, :] = dot(far_table[...], far_ref[...])
        self_ref[...] = weight[:width].astype(jnp.bfloat16)
        near_ref[...] = weight[width:].astype(jnp.bfloat16)
        sums_ref[...] = jnp.zeros_like(sums_ref)
        split_greeted(mesh_sizes)
        high_start(mesh_sizes, halo_ref, relay_ref, high_sems)
        if not flipped:
            plane_blocks(mesh_sizes, early_ref, early_relay, early_plane)

    @pl.when(step == steps // 2)
    def _():
        top, _, _, me = split_place(mesh_sizes)
        high_wait(mesh_sizes, relay_ref, high_sems)
        relay_ref[top] = halo_ref[top]
        plane_blocks(mesh_sizes, relay_ref, land_ref, plane_sems)
        if not flipped:
            plane_blocks_wait(mesh_sizes, early_relay, early_plane)
            early_relay[:, me] = early_ref[:, me]
            total = jnp.sum(early_relay[...].astype(jnp.float32), axis=1)
            shape = total.shape
            total = total.reshape(-1, shape[2])
            last = total[:, -128:]
            total = jnp.concatenate([total[:, :-128], put_terms(last, take_terms(last))], axis=1)
            early_part[...] = total.astype(jnp.bfloat16).reshape(shape)
            high_start(mesh_sizes, early_part, early_land, early_high)

    if not flipped:

        @pl.when(step == steps - 1)
        def _():
            top = split_place(mesh_sizes)[0]
            high_wait(mesh_sizes, early_land, early_high)
            early_land[top] = early_part[top]
            total = jnp.sum(early_land[...].astype(jnp.float32), axis=0)
            early_own[...] = total.astype(jnp.bfloat16)
            loss, count = take_terms(total[:, -128:])
            loss_ref[...] = loss[:1]
            count_ref[...] = count[:1]
            each_high(
                mesh_sizes,
                lambda other, where: push(early_own, early_back.at[top], back_sems, where),
            )

    def add(row):
        spread_unit(words_ref, row // SLOTS, counts_ref, row)
        added = dot(counts_ref[row : row + UNIT, :], rows_ref[...])
        sums_ref[row : row + UNIT, :] = unscaled(added, fanout)

    beyond = nodes - (steps - 1) * part
    ending = -(-beyond // UNIT) * UNIT
    for row in range(0, ending, UNIT):
        add(row)
    if ending < part:

        @pl.when(step < steps - 1)
        def _():
            for row in range(ending, part, UNIT):
                add(row)

    if flipped and beyond < part:

        @pl.when(step == steps - 1)
        def _():
            sums_ref[beyond:, :] = jnp.zeros((part - beyond, units), jnp.bfloat16)

    sums = sums_ref[...]
    own_grad = padded_ref[step]
    state_ref[...] = dot(near_ref[...], sums, TRANS_RIGHT) + dot(self_ref[...], own_grad)
    if flipped:
        weight_ref[:width, :] += dot(table_ref[...], own_grad, TRANS_RIGHT)
        weight_ref[width:, :] += dot(table_ref[...], sums)

    @pl.when(step == steps - 1)
    def _():
        me = split_place(mesh_sizes)[3]
        plane_blocks_wait(mesh_sizes, land_ref, plane_sems)
        land_ref[:, me] = relay_ref[:, me]
        got_ref[...] = land_ref[...]
        if not flipped:
            top = split_place(mesh_sizes)[0]
            high_wait(mesh_sizes, early_back, back_sems)
            early_back[top] = early_own[...]
            early_sum[...] = early_back[...]


def scatter_layer(
    words, grad, rows, weight, halo_rows, mesh_sizes, collective, fanout, tables=None, early=None
):
    units, nodes = grad.shape
    halo, width = halo_rows.shape
    parts = mesh_sizes[0] * mesh_sizes[1]
    flipped = tables is not None
    total = nodes + halo
    part = total // WORDS
    span = part // SLOTS
    steps = -(-nodes // part)
    high = split_sizes(mesh_sizes)[0]
    blocks = (high, parts // high, halo // parts, width)
    in_specs = [
        pl.BlockSpec((span, nodes), lambda i: (i, 0)),
        whole(grad.shape),
        whole(rows.shape),
        whole(weight.shape),
        whole(blocks),
    ]
    operands = [words, grad, rows, weight, halo_rows.reshape(blocks)]
    out_specs = [lanes(width, part), whole(blocks)]
    out_shape = [
        jax.ShapeDtypeStruct((width, total), jnp.float32),
        jax.ShapeDtypeStruct(blocks, jnp.bfloat16),
    ]
    if flipped:
        far, table = tables
        in_specs += [
            whole(far.shape),
            lanes(width, part),
            pl.BlockSpec((width, halo), lambda i: (0, nodes // halo)),
        ]
        operands += [far, table, table]
        out_specs.append(whole((2 * width, units)))
        out_shape.append(jax.ShapeDtypeStruct((2 * width, units), jnp.float32))
        scratch = semaphores() + semaphores()
    else:
        early_blocks = (high, parts // high, early.shape[0] // parts, early.shape[1])
        in_specs.append(whole(early_blocks))
        operands.append(early.reshape(early_blocks))
        summed = (high,) + early_blocks[2:]
        out_specs += [whole(summed), whole((1, 1)), whole((1, 1))]
        out_shape += [
            jax.ShapeDtypeStruct(summed, jnp.bfloat16),
            jax.ShapeDtypeStruct((1, 1), jnp.float32),
            jax.ShapeDtypeStruct((1, 1), jnp.float32),
        ]
        scratch = [
            pltpu.VMEM(early_blocks, jnp.bfloat16),
            pltpu.VMEM(summed, jnp.bfloat16),
            pltpu.VMEM(summed, jnp.bfloat16),
            pltpu.VMEM(summed[1:], jnp.bfloat16),
            pltpu.VMEM(summed, jnp.bfloat16),
        ]
        scratch += semaphores() * 5
    return pl.pallas_call(
        functools.partial(scatter_kernel, mesh_sizes, fanout, flipped),
        grid=(steps,),
        in_specs=in_specs,
        out_specs=out_specs,
        out_shape=out_shape,
        scratch_shapes=[
            pltpu.VMEM((steps, units, part), jnp.bfloat16),
            pltpu.VMEM((part, nodes), jnp.bfloat16),
            pltpu.VMEM((part, units), jnp.bfloat16),
            pltpu.VMEM((width, units), jnp.bfloat16),
            pltpu.VMEM((width, units), jnp.bfloat16),
            pltpu.VMEM(blocks, jnp.bfloat16),
            pltpu.VMEM(blocks, jnp.bfloat16),
        ]
        + scratch,
        compiler_params=params(36, collective),
        name="scatter_layer",
    )(*in_hbm(words), *operands[1:3], *in_hbm(weight), *operands[4:])


def active_grad(step, state_ref, preact_ref, back_ref, send_ref):
    block = state_ref.shape[1]
    chosen = chosen_nodes(send_ref[...], step * block, block)
    upper = state_ref[...] + dot(back_ref[...], chosen, TRANS_RIGHT)
    preact = preact_ref[...]
    gate = jax.nn.sigmoid(preact)
    active = preact * gate
    norm = lax.rsqrt(jnp.sum(active * active, axis=0, keepdims=True) + 1e-06)
    along = jnp.sum(active * upper, axis=0, keepdims=True)
    inner = norm * upper - active * (norm * norm * norm * along)
    return (inner * (gate * (1.0 + preact * (1.0 - gate)))).astype(jnp.bfloat16)


def middle_kernel(
    fanout,
    state_ref,
    preact_ref,
    returned_ref,
    send_ref,
    words_ref,
    weight_ref,
    own_block,
    mean_block,
    above_ref,
    notes_ref,
    grad_ref,
    rows_ref,
    sums_ref,
    halo_ref,
    early_ref,
    back_ref,
    counts_ref,
    far_sums,
    total_ref,
):
    step = pl.program_id(0)
    units, block = state_ref.shape
    halo = halo_ref.shape[0]
    nodes = block * pl.num_programs(0)
    first = far_start(nodes)
    part = (nodes + halo) // WORDS

    @pl.when(step == 0)
    def _():
        back_ref[...] = returned_ref[...].reshape(halo, units).T
        sums_ref[...] = jnp.zeros_like(sums_ref)
        far_sums[...] = jnp.zeros_like(far_sums)
        total_ref[...] = jnp.zeros_like(total_ref)

    base = first // part * part
    for row in range(first, nodes + halo, UNIT):
        spread_unit(words_ref, (row - base) // SLOTS, counts_ref, row - first)
    grad = active_grad(step, state_ref, preact_ref, back_ref, send_ref)
    grad_ref[...] = grad
    rows = grad.T
    rows_ref[...] = rows
    sums_ref[...] += column_sums(rows)
    far_sums[...] += dot(counts_ref[...], rows)
    width = own_block.shape[0]
    total_ref[:width, :] += dot(own_block[...], rows)
    total_ref[width:, :] += dot(mean_block[...], rows)

    @pl.when(step == pl.num_programs(0) - 1)
    def _():
        near = weight_ref[units:, :].T.astype(jnp.bfloat16)
        sums = unscaled(far_sums[...], fanout)[nodes - first :]
        halo_ref[...] = dot(sums, near).astype(jnp.bfloat16)
        early_ref[:, :units] = total_ref[...].astype(jnp.bfloat16)
        height, narrow = above_ref.shape
        above = jnp.concatenate(
            [above_ref[...], jnp.zeros((height, 128 - narrow), jnp.float32)], axis=1
        )
        above = put_terms(above, [notes_ref[0:1, 0:1], notes_ref[8:9, 0:1]])
        early_ref[:, units:] = above.astype(jnp.bfloat16)


def middle_layer(
    state_grad, preact, returned, send_row, words, weight, own, mean, above, notes, fanout
):
    units, nodes = preact.shape
    width = own.shape[0]
    wide = units + 128
    halo = send_row.shape[1]
    part = (nodes + halo) // WORDS
    span = part // SLOTS
    far_words = WORDS - far_start(nodes) // part
    far_height = nodes + halo - far_start(nodes)
    return pl.pallas_call(
        functools.partial(middle_kernel, fanout),
        grid=(nodes // BLOCK,),
        in_specs=[
            lanes(units, BLOCK),
            lanes(units, BLOCK),
            whole(returned.shape),
            whole(send_row.shape),
            pl.BlockSpec((far_words * span, BLOCK), lambda i: (WORDS // far_words - 1, i)),
            whole(weight.shape),
            lanes(width, BLOCK),
            lanes(width, BLOCK),
            whole(above.shape),
            whole(notes.shape),
        ],
        out_specs=[
            lanes(units, BLOCK),
            pl.BlockSpec((BLOCK, units), lambda i: (i, 0)),
            whole((16, units)),
            whole((halo, units)),
            whole((2 * width, wide)),
        ],
        out_shape=[
            jax.ShapeDtypeStruct((units, nodes), jnp.bfloat16),
            jax.ShapeDtypeStruct((nodes, units), jnp.bfloat16),
            jax.ShapeDtypeStruct((16, units), jnp.float32),
            jax.ShapeDtypeStruct((halo, units), jnp.bfloat16),
            jax.ShapeDtypeStruct((2 * width, wide), jnp.bfloat16),
        ],
        scratch_shapes=[
            pltpu.VMEM((units, halo), jnp.bfloat16),
            pltpu.VMEM((far_height, BLOCK), jnp.bfloat16),
            pltpu.VMEM((far_height, units), jnp.float32),
            pltpu.VMEM((2 * width, units), jnp.float32),
        ],
        compiler_params=params(30),
        name="middle_layer",
    )(
        state_grad,
        *in_hbm(preact),
        returned,
        send_row,
        *in_hbm(words, weight),
        own,
        *in_hbm(mean),
        above,
        notes,
    )


def in_two(value):
    high = value.astype(jnp.bfloat16)
    return high, (value - high.astype(jnp.float32)).astype(jnp.bfloat16)


def product(left, right, dims=(((1,), (0,)), ((), ()))):
    if left.dtype == jnp.bfloat16:
        high, low = in_two(right)
        return dot(left, high, dims) + dot(left, low, dims)
    high, low = in_two(left)
    if right.dtype == jnp.bfloat16:
        return dot(high, right, dims) + dot(low, right, dims)
    right_high, right_low = in_two(right)
    return dot(high, right_high, dims) + (
        dot(high, right_low, dims) + dot(low, right_high, dims)
    )


def moments(turned, first, second):
    first = beta_one * first + (1.0 - beta_one) * turned
    second = beta_two * second + (1.0 - beta_two) * turned * turned
    update = first / (1.0 - beta_one**STEP) / (jnp.sqrt(second / (1.0 - beta_two**STEP)) + epsilon)
    return first, second, update


def bottom_kernel(
    mesh_sizes,
    state_ref,
    preact_ref,
    returned_ref,
    send_ref,
    own_block,
    mean_block,
    sums_two,
    sums_three,
    early_ref,
    count_ref,
    *refs,
):
    refs = list(refs)
    kept, refs = refs[:10], refs[10:]
    late_out, *new, back_ref, weight_ref, late_ref = refs[:10]
    land_ref, plane_land, part_ref, high_land, whole_ref, last_land = refs[10:16]
    fetched, refs = refs[16:26], refs[26:]
    plane_sems, inward, across, outward = refs[:2], refs[2:4], refs[4:6], refs[6:8]
    fetch_sem = refs[8]
    step = pl.program_id(0)
    units = state_ref.shape[0]
    halo = send_ref.shape[1]
    top, _, _, me = split_place(mesh_sizes)

    @pl.when(step == 0)
    def _():
        greet_split(mesh_sizes)
        for index, (source, target) in enumerate(zip(kept, fetched)):
            pltpu.make_async_copy(source, target, fetch_sem.at[index]).start()
        back_ref[...] = returned_ref[...].reshape(halo, units).T
        weight_ref[...] = jnp.zeros_like(weight_ref)
        pieces = []
        for sums in (sums_two, sums_three):
            for start in range(0, sums.shape[1], 128):
                pieces.append(sums[:1, start : start + 128])
        narrow = pieces[-1].shape[1]
        pieces[-1] = jnp.concatenate(
            [pieces[-1], jnp.zeros((1, 128 - narrow), jnp.float32)], axis=1
        )
        row = units // 128 * 2 * weight_ref.shape[1]
        rest = late_ref.shape[0] - row
        pieces.append(jnp.zeros((rest - len(pieces), 128), jnp.float32))
        late_ref[row:, :] = jnp.concatenate(pieces).astype(jnp.bfloat16)
        split_greeted(mesh_sizes)
        each_plane(
            mesh_sizes,
            lambda other, where: push(early_ref, land_ref.at[:, me], plane_sems, where),
        )

    grad = active_grad(step, state_ref, preact_ref, back_ref, send_ref)
    width = own_block.shape[0]
    weight_ref[0, :width, :] += dot(own_block[...], grad, TRANS_RIGHT)
    weight_ref[1] += dot(mean_block[...], grad, TRANS_RIGHT)

    @pl.when(step == pl.num_programs(0) - 1)
    def _():
        padded = weight_ref.shape[1]
        row = 0
        for start in range(0, units, 128):
            for half in range(2):
                late_ref[row : row + padded, :] = weight_ref[half, :, start : start + 128].astype(
                    jnp.bfloat16
                )
                row += padded
        tall = part_ref.shape[0]

        def rows_of(place):
            return late_ref.at[pl.ds(pl.multiple_of(place * tall, tall), tall)]

        each_plane(
            mesh_sizes,
            lambda other, where: push(rows_of(other), plane_land.at[me], inward, where),
        )
        for index, (source, target) in enumerate(zip(kept, fetched)):
            pltpu.make_async_copy(source, target, fetch_sem.at[index]).wait()
        left_two, right_two, left_three, right_three = fetched[:4]
        weight_two, first_two, second_two = fetched[4:7]
        weight_three, first_three, second_three = fetched[7:]
        share = 1.0 / count_ref[...]
        plane_blocks_wait(mesh_sizes, land_ref, plane_sems)
        land_ref[:, me] = early_ref[...]
        early = land_ref[...].reshape(-1, land_ref.shape[3])
        grad = early[:, :units]
        turned = product(product(left_two[...], grad, TRANS_LEFT), right_two[...]) * share
        new_first, new_second, update = moments(turned, first_two[...], second_two[...])
        new[1][...] = new_first
        new[2][...] = new_second

        plane_wait(mesh_sizes, plane_land, inward)
        plane_land[me] = late_ref[pl.ds(pl.multiple_of(me * tall, tall), tall), :]
        part_ref[...] = jnp.sum(plane_land[...].astype(jnp.float32), axis=0).astype(jnp.bfloat16)
        each_high(
            mesh_sizes, lambda other, where: push(part_ref, high_land.at[top], across, where)
        )

        moved = product(product(left_two[...], update), right_two[...], TRANS_RIGHT)
        new[0][...] = weight_two[...] - step_rates[1] * moved

        high_wait(mesh_sizes, high_land, across)
        high_land[top] = part_ref[...]
        whole_ref[...] = jnp.sum(high_land[...].astype(jnp.float32), axis=0).astype(jnp.bfloat16)
        each_plane(
            mesh_sizes, lambda other, where: push(whole_ref, last_land.at[me], outward, where)
        )

        kinds = right_three.shape[0]
        grad = early[:, units:].astype(jnp.float32).T[:kinds].astype(jnp.bfloat16)
        turned = product(right_three[...], product(grad, left_three[...]), TRANS_LEFT) * share
        new_first, new_second, update = moments(turned, first_three[...], second_three[...])
        new[4][...] = new_first
        new[5][...] = new_second
        moved = product(right_three[...], product(update, left_three[...], TRANS_RIGHT))
        new[3][...] = weight_three[...] - step_rates[2] * moved

        plane_wait(mesh_sizes, last_land, outward)
        last_land[me] = whole_ref[...]
        late_out[...] = last_land[...]


def bottom_layer(
    state_grad,
    preact,
    returned,
    send_row,
    own,
    mean,
    sums_two,
    sums_three,
    early,
    count,
    kept,
    mesh_sizes,
    collective,
):
    units, nodes = preact.shape
    width = own.shape[0]
    padded = mean.shape[0]
    halo = send_row.shape[1]
    rows = units // 128 * (2 * padded + 1) + -(-sums_three.shape[1] // 128)
    rows = -(-rows // 512) * 512
    high, low, along = split_sizes(mesh_sizes)
    plane = low * along
    early_blocks = (high, plane) + early.shape[1:]
    late_blocks = (plane, rows // plane, 128)
    hbm = pl.BlockSpec(memory_space=pl.ANY)
    new = [jax.ShapeDtypeStruct(array.shape, jnp.float32) for array in kept[4:]]
    return pl.pallas_call(
        functools.partial(bottom_kernel, mesh_sizes),
        grid=(nodes // BLOCK,),
        in_specs=[
            lanes(units, BLOCK),
            lanes(units, BLOCK),
            whole(returned.shape),
            whole(send_row.shape),
            lanes(width, BLOCK),
            lanes(padded, BLOCK),
            whole(sums_two.shape),
            whole(sums_three.shape),
            whole(early.shape),
            whole(count.shape),
        ]
        + [hbm] * len(kept),
        out_specs=[whole(late_blocks)] + [whole(array.shape) for array in new],
        out_shape=[jax.ShapeDtypeStruct(late_blocks, jnp.bfloat16)] + new,
        scratch_shapes=[
            pltpu.VMEM((units, halo), jnp.bfloat16),
            pltpu.VMEM((2, padded, units), jnp.float32),
            pltpu.VMEM((rows, 128), jnp.bfloat16),
            pltpu.VMEM(early_blocks, jnp.bfloat16),
            pltpu.VMEM(late_blocks, jnp.bfloat16),
            pltpu.VMEM(late_blocks[1:], jnp.bfloat16),
            pltpu.VMEM((high,) + late_blocks[1:], jnp.bfloat16),
            pltpu.VMEM(late_blocks[1:], jnp.bfloat16),
            pltpu.VMEM(late_blocks, jnp.bfloat16),
        ]
        + [pltpu.VMEM(array.shape, array.dtype) for array in kept]
        + semaphores() * 4
        + [pltpu.SemaphoreType.DMA((len(kept),))],
        compiler_params=params(34, collective),
        name="bottom_layer",
    )(
        state_grad,
        *in_hbm(preact),
        returned,
        send_row,
        *in_hbm(own, mean),
        sums_two,
        sums_three,
        early,
        count,
        *in_hbm(*kept),
    )


def adam_kernel(
    padded,
    late_ref,
    count_ref,
    weight_one,
    left_one,
    right_one,
    first_one,
    second_one,
    bias_ref,
    bias_first,
    bias_second,
    *refs,
):
    ready, refs = refs[:6], refs[6:]
    outs, sem = refs[:12], refs[12]
    for index in range(6):
        pltpu.make_async_copy(ready[index], outs[3 + index], sem.at[index]).start()
    share = 1.0 / count_ref[...]
    units = weight_one.shape[1]
    width = weight_one.shape[0] // 2

    late_rows = late_ref[...].astype(jnp.float32)
    columns = []
    for start in range(0, units, 128):
        row = start // 128 * 2 * padded
        columns.append(
            jnp.concatenate(
                [late_rows[row : row + width], late_rows[row + padded : row + padded + width]]
            )
        )
    grad = jnp.concatenate(columns, axis=1).astype(jnp.bfloat16)
    turned = product(product(left_one[...], grad, TRANS_LEFT), right_one[...]) * share
    new_first, new_second, update = moments(turned, first_one[...], second_one[...])
    outs[1][...] = new_first
    outs[2][...] = new_second
    moved = product(product(left_one[...], update), right_one[...], TRANS_RIGHT)
    outs[0][...] = weight_one[...] - step_rates[0] * moved

    size = bias_ref.shape[0]
    pieces = []
    for start in range(0, units, 128):
        row = start // 128 * 2 * padded + padded + width
        pieces.append(late_rows[row : row + 1])
    row = units // 128 * 2 * padded
    while len(pieces) * 128 < size:
        pieces.append(late_rows[row : row + 1])
        row += 1
    grad = jnp.concatenate(pieces, axis=1)[:, :size] * share
    flat = bias_ref.shape
    bias, first, second = (ref[...].reshape(grad.shape) for ref in (bias_ref, bias_first, bias_second))
    new_first, new_second, update = moments(grad, first, second)
    outs[9][...] = (bias - bias_rate * (update + weight_decay * bias)).reshape(flat)
    outs[10][...] = new_first.reshape(flat)
    outs[11][...] = new_second.reshape(flat)
    for index in range(6):
        pltpu.make_async_copy(ready[index], outs[3 + index], sem.at[index]).wait()


def adam(padded, late_all, count, state, ready):
    vmem = pl.BlockSpec(memory_space=pltpu.VMEM)
    hbm = pl.BlockSpec(memory_space=pl.ANY)
    one, bias = state[0], state[5]
    shapes = [one.shape] * 3 + [array.shape for array in ready] + [bias.shape] * 3
    return pl.pallas_call(
        functools.partial(adam_kernel, padded),
        in_specs=[vmem] * (2 + len(state)) + [hbm] * len(ready),
        out_specs=[vmem] * 3 + [hbm] * 6 + [vmem] * 3,
        out_shape=[jax.ShapeDtypeStruct(shape, jnp.float32) for shape in shapes],
        scratch_shapes=[pltpu.SemaphoreType.DMA((6,))],
        compiler_params=pltpu.CompilerParams(vmem_limit_bytes=24 * MIB),
        name="adam",
    )(late_all, count, *in_hbm(*state), *ready)


def on_device(
    mesh_sizes,
    features,
    labels,
    seed_rows,
    seed_mask,
    send_rows,
    neighbors_one,
    neighbors_two,
    neighbors_three,
    weight_one,
    weight_two,
    weight_three,
    left_one,
    right_one,
    left_two,
    right_two,
    left_three,
    right_three,
    first_one,
    first_two,
    first_three,
    second_one,
    second_two,
    second_three,
    bias_all,
    bias_first,
    bias_second,
):
    units = weight_one.shape[1]
    classes = weight_three.shape[1]
    halo = send_rows.size
    fans = (neighbors_one.shape[1], neighbors_two.shape[1], neighbors_three.shape[1])
    feats = features.T
    weight_three = weight_three.T
    padded_classes = -(-classes // 16) * 16
    seed_slots = (
        padded_classes,
        seed_rows.reshape(1, -1),
        labels.reshape(1, -1),
        seed_mask.reshape(1, -1),
    )

    words_one, got, send_row = count_words(
        neighbors_one.T, mesh_sizes, 0, halo, feats=feats, send_rows=send_rows.T
    )
    feats = in_hbm(feats)[0]
    state_one, preact_one, sent, mean_one = hidden_layer(
        words_one, feats, got, weight_one, bias_all, 0, send_row, fans[0]
    )
    words_two, got = count_words(neighbors_two.T, mesh_sizes, 1, halo, sent=sent)
    state_two, preact_two, sent, mean_two = hidden_layer(
        words_two, state_one, got, weight_two, bias_all, units, send_row, fans[1]
    )
    words_three, got, seeds = count_words(
        neighbors_three.T, mesh_sizes, 2, halo, sent=sent, seeds=seed_slots
    )
    grad_three, rows_three, sums_three, notes, table_three, far, halo_grad = last_layer(
        words_three, state_two, got, weight_three, bias_all, 2 * units, seeds, fans[2]
    )
    state_grad, returned, weight_grad = scatter_layer(
        words_three,
        grad_three,
        rows_three,
        weight_three,
        halo_grad,
        mesh_sizes,
        3,
        fans[2],
        tables=(far, table_three),
    )
    grad_two, rows_two, sums_two, halo_grad, early = middle_layer(
        state_grad,
        preact_two,
        returned,
        send_row,
        words_two,
        weight_two,
        state_one,
        mean_two,
        weight_grad,
        notes,
        fans[1],
    )
    state_grad, returned, early_sum, loss, count = scatter_layer(
        words_two, grad_two, rows_two, weight_two, halo_grad, mesh_sizes, 4, fans[1], early=early
    )
    late_all, *ready = bottom_layer(
        state_grad,
        preact_one,
        returned,
        send_row,
        feats,
        mean_one,
        sums_two,
        sums_three,
        early_sum,
        count,
        (
            left_two,
            right_two,
            left_three,
            right_three,
            weight_two,
            first_two,
            second_two,
            weight_three,
            first_three.T,
            second_three.T,
        ),
        mesh_sizes,
        5,
    )
    out = adam(
        mean_one.shape[0],
        late_all.reshape(-1, 128),
        count,
        (
            weight_one,
            left_one,
            right_one,
            first_one,
            second_one,
            bias_all,
            bias_first,
            bias_second,
        ),
        ready,
    )
    third = [value.T for value in out[6:9]]
    return (*out[:6], *third, *out[9:12], loss.reshape(()), count.reshape(()))


def solution(mesh):
    split = P(axes)
    rows = P(axes, None)
    placed = (rows, split, split, split, rows, rows, rows, rows) + (P(),) * 18
    mesh_sizes = (mesh.shape[axes[0]], mesh.shape[axes[1]])
    return jax.shard_map(
        functools.partial(on_device, mesh_sizes),
        mesh=mesh,
        in_specs=placed,
        out_specs=(P(),) * 14,
        check_vma=False,
    )
```

```python
import functools

import jax
import jax.numpy as jnp
from jax import lax
from jax.experimental import pallas as pl
from jax.experimental.pallas import tpu as pltpu
from jax.sharding import PartitionSpec as P

STEP = 10


beta_one = 0.9
beta_two = 0.999
epsilon = 1e-08
step_rates = (0.05, 0.5, 1.0)
bias_rate = 0.05
weight_decay = 0.01

axes = ("dom", "rep")
WORDS = 4
SLOTS = 8
RUN = 48
UNIT = SLOTS * RUN
BLOCK = 1024
LIST_BLOCK = 512
MIB = 1024 * 1024
TRANS_LEFT = (((0,), (0,)), ((), ()))
TRANS_RIGHT = (((1,), (1,)), ((), ()))


def dot(left, right, dims=(((1,), (0,)), ((), ()))):
    return lax.dot_general(left, right, dims, preferred_element_type=jnp.float32)


def params(limit, collective=None):
    remote = {} if collective is None else dict(collective_id=collective, has_side_effects=True)
    return pltpu.CompilerParams(
        dimension_semantics=("arbitrary",), vmem_limit_bytes=limit * MIB, **remote
    )


def in_hbm(*arrays):
    return [pltpu.with_memory_space_constraint(array, pltpu.HBM) for array in arrays]


def whole(shape):
    return pl.BlockSpec(shape, lambda i: (0,) * len(shape))


def lanes(rows, width):
    return pl.BlockSpec((rows, width), lambda i: (0, i))


def floor_over(value, size):
    return ((value.astype(jnp.float32) + 0.5) * (1.0 / size)).astype(jnp.int32)


def words_layer(near_ref, out_ref, place_ref, field_ref):
    fanout, block = near_ref.shape
    span = out_ref.shape[0] // WORDS
    near = near_ref[...]
    unit = floor_over(near, UNIT)
    rest = near - unit * UNIT
    slot = floor_over(rest, RUN)
    word = floor_over(unit, span // RUN)
    place = (unit - word * (span // RUN)) * RUN + rest - slot * RUN
    bit = jnp.left_shift(jnp.int32(1), slot * 4)
    parts = [jnp.where(word == k, bit, 0) for k in range(WORDS)]
    totals = [jnp.zeros_like(bit) for _ in range(WORDS)]
    for g in range(fanout):
        same = place == place[g : g + 1]
        for k in range(WORDS):
            totals[k] = totals[k] + jnp.where(same, parts[k][g : g + 1], 0)
    place_ref[:fanout, :] = place
    for k in range(WORDS):
        field_ref[k, :fanout, :] = totals[k]
    chunk = RUN
    for tile in range(0, block, 128):
        cols = slice(tile, tile + 128)
        for start in range(0, span, chunk):
            rows = lax.broadcasted_iota(jnp.int32, (chunk, 128), 0) + start
            sums = [jnp.zeros((chunk, 128), jnp.int32) for _ in range(WORDS)]
            for g in range(fanout):
                hit = rows == place_ref[g : g + 1, cols]
                for k in range(WORDS):
                    sums[k] = jnp.where(hit, field_ref[k, g : g + 1, cols], sums[k])
            for k in range(WORDS):
                out_ref[k * span + start : k * span + start + chunk, cols] = sums[k]


def my_index(mesh_sizes):
    return lax.axis_index(axes[0]) * mesh_sizes[1] + lax.axis_index(axes[1])


def each_peer(mesh_sizes, act):
    across, along = mesh_sizes
    row, column = lax.axis_index(axes[0]), lax.axis_index(axes[1])

    def wrapped(value, size):
        return jnp.where(value >= size, value - size, value)

    def line(down, carry):
        other = wrapped(row + down, across)
        for ahead in range(along):
            place = wrapped(column + ahead, along)
            act(other * along + place, (other, place))
        return carry

    for ahead in range(1, along):
        place = wrapped(column + ahead, along)
        act(row * along + place, (row, place))
    for down in range(1, across):
        line(down, 0)


def greet(mesh_sizes):
    barrier = pltpu.get_barrier_semaphore()

    def tell(index, where):
        pl.semaphore_signal(
            barrier, inc=1, device_id=where, device_id_type=pl.DeviceIdType.MESH
        )

    each_peer(mesh_sizes, tell)


def all_greeted(mesh_sizes):
    pl.semaphore_wait(pltpu.get_barrier_semaphore(), mesh_sizes[0] * mesh_sizes[1] - 1)


def send_blocks(mesh_sizes, out_ref, in_ref, send_sem, recv_sem):
    me = my_index(mesh_sizes)

    def send(index, where):
        pltpu.make_async_remote_copy(
            src_ref=out_ref.at[index],
            dst_ref=in_ref.at[me],
            send_sem=send_sem,
            recv_sem=recv_sem,
            device_id=where,
            device_id_type=pl.DeviceIdType.MESH,
        ).start()

    each_peer(mesh_sizes, send)


def send_all(mesh_sizes, own_ref, in_ref, send_sem, recv_sem):
    me = my_index(mesh_sizes)

    def send(index, where):
        pltpu.make_async_remote_copy(
            src_ref=own_ref,
            dst_ref=in_ref.at[me],
            send_sem=send_sem,
            recv_sem=recv_sem,
            device_id=where,
            device_id_type=pl.DeviceIdType.MESH,
        ).start()

    each_peer(mesh_sizes, send)


def wait_moves(mesh_sizes, out_ref, in_ref, send_sem, recv_sem):
    others = pl.ds(0, mesh_sizes[0] * mesh_sizes[1] - 1)
    copy = pltpu.make_async_remote_copy(
        src_ref=in_ref.at[others],
        dst_ref=in_ref.at[others],
        send_sem=send_sem,
        recv_sem=recv_sem,
        device_id=(lax.axis_index(axes[0]), lax.axis_index(axes[1])),
        device_id_type=pl.DeviceIdType.MESH,
    )
    copy.wait_send()
    copy.wait_recv()


def split_sizes(mesh_sizes):
    across, along = mesh_sizes
    high = 4 if across % 4 == 0 else 1
    return high, across // high, along


def split_place(mesh_sizes):
    _, low, along = split_sizes(mesh_sizes)
    row, column = lax.axis_index(axes[0]), lax.axis_index(axes[1])
    top = row // low
    return top, row - top * low, column, (row - top * low) * along + column


def each_high(mesh_sizes, act):
    high, low, _ = split_sizes(mesh_sizes)
    top, bottom, column, _ = split_place(mesh_sizes)
    for ahead in range(1, high):
        other = top + ahead
        other = jnp.where(other >= high, other - high, other)
        act(other, (other * low + bottom, column))


def each_plane(mesh_sizes, act):
    _, low, along = split_sizes(mesh_sizes)
    top, bottom, column, _ = split_place(mesh_sizes)
    for down in range(low):
        for ahead in range(along):
            if down == 0 and ahead == 0:
                continue
            line = bottom + down
            line = jnp.where(line >= low, line - low, line)
            place = column + ahead
            place = jnp.where(place >= along, place - along, place)
            act(line * along + place, (top * low + line, place))


def greet_split(mesh_sizes):
    barrier = pltpu.get_barrier_semaphore()

    def tell(index, where):
        pl.semaphore_signal(
            barrier, inc=1, device_id=where, device_id_type=pl.DeviceIdType.MESH
        )

    each_high(mesh_sizes, tell)
    each_plane(mesh_sizes, tell)


def split_greeted(mesh_sizes):
    high, low, along = split_sizes(mesh_sizes)
    pl.semaphore_wait(pltpu.get_barrier_semaphore(), high - 1 + low * along - 1)


def push(src_ref, dst_ref, sems, where):
    pltpu.make_async_remote_copy(
        src_ref=src_ref,
        dst_ref=dst_ref,
        send_sem=sems[0],
        recv_sem=sems[1],
        device_id=where,
        device_id_type=pl.DeviceIdType.MESH,
    ).start()


def wait_pushed(ref, sems):
    copy = pltpu.make_async_remote_copy(
        src_ref=ref,
        dst_ref=ref,
        send_sem=sems[0],
        recv_sem=sems[1],
        device_id=(lax.axis_index(axes[0]), lax.axis_index(axes[1])),
        device_id_type=pl.DeviceIdType.MESH,
    )
    copy.wait_send()
    copy.wait_recv()


def high_start(mesh_sizes, sent_ref, relay_ref, sems):
    top = split_place(mesh_sizes)[0]
    each_high(
        mesh_sizes, lambda other, where: push(sent_ref.at[other], relay_ref.at[top], sems, where)
    )


def high_wait(mesh_sizes, relay_ref, sems):
    high = split_sizes(mesh_sizes)[0]
    if high > 1:
        wait_pushed(relay_ref.at[pl.ds(0, high - 1)], sems)


def plane_wait(mesh_sizes, land_ref, sems):
    _, low, along = split_sizes(mesh_sizes)
    wait_pushed(land_ref.at[pl.ds(0, low * along - 1)], sems)


def plane_blocks(mesh_sizes, relay_ref, land_ref, sems):
    me = split_place(mesh_sizes)[3]
    each_plane(
        mesh_sizes,
        lambda other, where: push(relay_ref.at[:, other], land_ref.at[:, me], sems, where),
    )


def plane_blocks_wait(mesh_sizes, land_ref, sems):
    _, low, along = split_sizes(mesh_sizes)
    wait_pushed(land_ref.at[:, pl.ds(0, low * along - 1)], sems)


NOTES = 120


def put_terms(rows, values):
    lane = lax.broadcasted_iota(jnp.int32, rows.shape, 1)
    for index, value in enumerate(values):
        for at in range(3):
            term = value.astype(jnp.bfloat16).astype(jnp.float32)
            rows = jnp.where(lane == NOTES + 3 * index + at, term, rows)
            value = value - term
    return rows


def take_terms(rows):
    lane = lax.broadcasted_iota(jnp.int32, rows.shape, 1)
    values = []
    for index in range(2):
        first = NOTES + 3 * index
        mine = (lane >= first) & (lane < first + 3)
        values.append(jnp.sum(jnp.where(mine, rows, 0.0), axis=1, keepdims=True))
    return values


def semaphores():
    return [pltpu.SemaphoreType.DMA, pltpu.SemaphoreType.DMA]


def one_row(rows):
    per, parts = rows.shape
    column = lax.broadcasted_iota(jnp.int32, (parts, parts * per), 1)
    owner = lax.broadcasted_iota(jnp.int32, (parts, parts * per), 0)
    rest = column - owner * per
    mine = jnp.where((rest >= 0) & (rest < per), 1.0, 0.0).astype(jnp.bfloat16)
    high = (rows >> 7).astype(jnp.float32).astype(jnp.bfloat16)
    low = (rows & 127).astype(jnp.float32).astype(jnp.bfloat16)
    wide = dot(high, mine) * 128.0 + dot(low, mine)
    column = lax.broadcasted_iota(jnp.int32, wide.shape, 1)
    at = lax.broadcasted_iota(jnp.int32, wide.shape, 0)
    picked = jnp.where(column - floor_over(column, per) * per == at, wide, 0.0)
    return jnp.sum(picked, axis=0, keepdims=True).astype(jnp.int32)


def chosen_nodes(send_row, start, count):
    node = (lax.broadcasted_iota(jnp.int32, (count, 128), 0) + start).astype(jnp.int16)
    one = jnp.ones((count, 128), jnp.bfloat16)
    pieces = []
    for tile in range(0, send_row.shape[1], 128):
        wanted = jnp.broadcast_to(send_row[:, tile : tile + 128], (16, 128)).astype(jnp.int16)
        wanted = jnp.concatenate([wanted] * (count // 16))
        pieces.append(jnp.where(node == wanted, one, jnp.zeros_like(one)))
    return jnp.concatenate(pieces, axis=1)


def words_kernel(mesh_sizes, kind, near_ref, *refs):
    refs = list(refs)
    if kind == "features":
        feats_ref, send_ref, out_ref, got_ref, row_ref, sent_ref = refs[:6]
        refs = refs[6:]
    elif kind == "seeds":
        sent_ref, slots_ref, labels_ref, mask_ref, out_ref, got_ref, seeds_ref = refs[:7]
        refs = refs[7:]
    else:
        sent_ref, out_ref, got_ref = refs[:3]
        refs = refs[3:]
    place_ref, field_ref, land_ref, send_sem, recv_sem = refs
    step = pl.program_id(0)
    block = near_ref.shape[1]
    moves = (mesh_sizes, sent_ref, land_ref, send_sem, recv_sem)

    @pl.when(step == 0)
    def _():
        greet(mesh_sizes)

    if kind == "features":

        @pl.when(step == 0)
        def _():
            width, nodes = feats_ref.shape
            halo = row_ref.shape[1]
            row_ref[...] = one_row(send_ref[...])
            total = jnp.zeros((width, halo), jnp.float32)
            for start in range(0, nodes, block):
                chosen = chosen_nodes(row_ref[...], start, block)
                total = total + dot(feats_ref[:, start : start + block], chosen)
            padded = sent_ref.shape[2]
            total = jnp.concatenate([total, jnp.zeros((padded - width, halo), jnp.float32)])
            sent_ref[...] = total.T.astype(jnp.bfloat16).reshape(sent_ref.shape)

    if kind == "seeds":
        classes = seeds_ref.shape[0]
        slots = slots_ref.shape[1]
        label = lax.broadcasted_iota(jnp.int32, (classes, slots), 0)
        marked = jnp.where((label == labels_ref[...]) & (mask_ref[...] != 0), 1.0, 0.0)
        chosen = chosen_nodes(slots_ref[...], step * block, block)
        seeds_ref[...] = dot(marked.astype(jnp.bfloat16), chosen, TRANS_RIGHT)

    words_layer(near_ref, out_ref, place_ref, field_ref)

    @pl.when(step == 0)
    def _():
        all_greeted(mesh_sizes)
        send_blocks(*moves)

    @pl.when(step == pl.num_programs(0) - 1)
    def _():
        me = my_index(mesh_sizes)
        wait_moves(*moves)
        land_ref[me] = sent_ref[me]
        got_ref[...] = land_ref[...]


def words_space(table, near):
    return pltpu.VMEM if near and table <= 5120 else pltpu.HBM


def place_words(words, near):
    return pltpu.with_memory_space_constraint(words, words_space(words.shape[0] * SLOTS, near))


def count_words(
    near, mesh_sizes, collective, halo, sent=None, feats=None, send_rows=None, seeds=None
):
    fanout, nodes = near.shape
    parts = mesh_sizes[0] * mesh_sizes[1]
    height = (nodes + halo) // SLOTS
    in_specs = [lanes(fanout, LIST_BLOCK)]
    operands = [near]
    scratch = []
    if sent is None:
        kind = "features"
        blocks = (parts, halo // parts, -(-feats.shape[0] // 128) * 128)
        in_specs += [whole(feats.shape), whole(send_rows.shape)]
        operands += in_hbm(feats, send_rows)
        scratch.append(pltpu.VMEM(blocks, jnp.bfloat16))
    else:
        kind = "plain"
        blocks = (parts, halo // parts, sent.shape[1])
        in_specs.append(whole(blocks))
        operands.append(sent.reshape(blocks))
    out_specs = [lanes(height, LIST_BLOCK), whole(blocks)]
    out_shape = [
        words_space(nodes + halo, sent is None)(
            (height, nodes), jnp.int32
        ),
        jax.ShapeDtypeStruct(blocks, jnp.bfloat16),
    ]
    if sent is None:
        out_specs.append(whole((1, halo)))
        out_shape.append(jax.ShapeDtypeStruct((1, halo), jnp.int32))
    if seeds is not None:
        kind = "seeds"
        classes, slots, labels, mask = seeds
        in_specs += [whole(slots.shape)] * 3
        operands += [slots, labels, mask]
        out_specs.append(lanes(classes, LIST_BLOCK))
        out_shape.append(jax.ShapeDtypeStruct((classes, nodes), jnp.float32))
    return pl.pallas_call(
        functools.partial(words_kernel, mesh_sizes, kind),
        grid=(nodes // LIST_BLOCK,),
        in_specs=in_specs,
        out_specs=out_specs,
        out_shape=out_shape,
        scratch_shapes=scratch
        + [
            pltpu.VMEM((16, LIST_BLOCK), jnp.int32),
            pltpu.VMEM((WORDS, 16, LIST_BLOCK), jnp.int32),
            pltpu.VMEM(blocks, jnp.bfloat16),
        ]
        + semaphores(),
        compiler_params=params(20, collective),
        name="count_words",
    )(*in_hbm(*operands[:1]), *operands[1:])


def field(words, slot):
    if slot == SLOTS - 1:
        picked = lax.shift_right_logical(words, 4 * slot)
    else:
        picked = words & (15 << (4 * slot))
    return picked.astype(jnp.float32).astype(jnp.bfloat16)


def slot_scale(slot):
    return 1.0 if slot == SLOTS - 1 else 2.0 ** (-4 * slot)


def spread_unit(words_ref, word_row, counts_ref, count_row):
    for start in range(0, RUN, 16):
        for tile in range(0, words_ref.shape[1], 256):
            cols = slice(tile, tile + 256)
            words = words_ref[word_row + start : word_row + start + 16, cols]
            for slot in range(SLOTS):
                row = count_row + slot * RUN + start
                counts_ref[row : row + 16, cols] = field(words, slot)


def gather_product(table_ref, words_ref, counts_ref):
    table = table_ref.shape[1]
    total = None
    for start in range(0, table, 2 * UNIT):
        stop = start + 2 * UNIT
        for row in range(start, stop, UNIT):
            spread_unit(words_ref, row // SLOTS, counts_ref, row)
        term = dot(table_ref[:, start:stop], counts_ref[start:stop, :])
        total = term if total is None else total + term
    return total


def scale_row(table):
    column = lax.broadcasted_iota(jnp.int32, (1, table), 1)
    rest = column - floor_over(column, UNIT) * UNIT
    slot = floor_over(rest, RUN)
    scale = jnp.ones((1, table), jnp.float32)
    for k in range(SLOTS - 1):
        scale = jnp.where(slot == k, slot_scale(k), scale)
    return scale


def column_of(row):
    return jnp.broadcast_to(row, (128, row.shape[1])).T


def late(rows, width):
    return pl.BlockSpec((rows, width), lambda i: (0, jnp.maximum(i - 1, 0)))


def now(rows, width, steps):
    return pl.BlockSpec((rows, width), lambda i: (0, jnp.minimum(i, steps - 1)))


def hidden_kernel(
    fanout,
    bias_start,
    words_ref,
    own_ref,
    own_block,
    got_ref,
    weight_ref,
    bias_ref,
    send_ref,
    state_ref,
    preact_ref,
    sent_ref,
    extra_ref,
    table_ref,
    counts_ref,
    picked_ref,
    mean_ref,
    self_ref,
    near_ref,
    bias_col,
):
    step = pl.program_id(0)
    last = pl.num_programs(0) - 1
    width, nodes = own_ref.shape
    units, block = state_ref.shape
    padded = mean_ref.shape[0]

    @pl.when(step == 0)
    def _():
        if table_ref.shape[0] > width:
            table_ref[...] = jnp.zeros_like(table_ref)
        got = got_ref[...].reshape(-1, got_ref.shape[2]).T[:width]
        scale = scale_row(table_ref.shape[1])
        own = own_ref[...].astype(jnp.float32) * scale[:, :nodes]
        table_ref[:width, :nodes] = own.astype(jnp.bfloat16)
        far = got.astype(jnp.float32) * scale[:, nodes:]
        table_ref[:width, nodes:] = far.astype(jnp.bfloat16)
        mean_ref[...] = jnp.zeros_like(mean_ref)
        picked_ref[...] = jnp.zeros_like(picked_ref)
        self_ref[...] = weight_ref[:width, :].T.astype(jnp.bfloat16)
        if padded > width:
            near_ref[...] = jnp.zeros_like(near_ref)
        near_ref[:, :width] = weight_ref[width:, :].T.astype(jnp.bfloat16)
        bias = bias_ref[...].reshape(1, -1)
        bias_col[...] = column_of(bias[:, bias_start : bias_start + units])

    def finish():
        mean = mean_ref[...]
        extra_ref[...] = mean
        if padded > width:
            extra_ref[width : width + 1, :] = jnp.ones((1, block), jnp.bfloat16)
        preact = dot(self_ref[...], own_block[...]) + dot(near_ref[...], mean) + bias_col[:, :1]
        preact_ref[...] = preact
        active = preact * jax.nn.sigmoid(preact)
        norm = lax.rsqrt(jnp.sum(active * active, axis=0, keepdims=True) + 1e-06)
        state = (active * norm).astype(jnp.bfloat16)
        state_ref[...] = state
        picked_ref[...] += dot(state, chosen_nodes(send_ref[...], (step - 1) * block, block))

    @pl.when(step < last)
    def _():
        finish()
        total = gather_product(table_ref, words_ref, counts_ref)
        mean_ref[...] = (total * (1.0 / fanout)).astype(jnp.bfloat16)

    @pl.when(step == last)
    def _():
        finish()
        sent_ref[...] = picked_ref[...].T.astype(jnp.bfloat16)


def hidden_layer(words, own, got, weight, bias, bias_start, send_row, fanout):
    width, nodes = own.shape
    halo = send_row.shape[1]
    table = nodes + halo
    units = weight.shape[1]
    padded = width if width == units else (width // 16 + 1) * 16
    steps = nodes // BLOCK
    return pl.pallas_call(
        functools.partial(hidden_kernel, fanout, bias_start),
        grid=(steps + 1,),
        in_specs=[
            now(words.shape[0], BLOCK, steps),
            whole(own.shape),
            late(width, BLOCK),
            whole(got.shape),
            whole(weight.shape),
            whole(bias.shape),
            whole(send_row.shape),
        ],
        out_specs=[
            late(units, BLOCK),
            late(units, BLOCK),
            whole((halo, units)),
            late(padded, BLOCK),
        ],
        out_shape=[
            jax.ShapeDtypeStruct((units, nodes), jnp.bfloat16),
            pltpu.HBM((units, nodes), jnp.float32),
            jax.ShapeDtypeStruct((halo, units), jnp.bfloat16),
            pltpu.HBM((padded, nodes), jnp.bfloat16),
        ],
        scratch_shapes=[
            pltpu.VMEM((padded, table), jnp.bfloat16),
            pltpu.VMEM((table, BLOCK), jnp.bfloat16),
            pltpu.VMEM((units, halo), jnp.float32),
            pltpu.VMEM((padded, BLOCK), jnp.bfloat16),
            pltpu.VMEM((units, width), jnp.bfloat16),
            pltpu.VMEM((units, padded), jnp.bfloat16),
            pltpu.VMEM((units, 128), jnp.float32),
        ],
        compiler_params=params(40),
        name="hidden_layer",
    )(place_words(words, width != units), own, own, got, *in_hbm(weight, bias), send_row)


def far_start(nodes):
    return nodes // UNIT * UNIT


def column_sums(rows):
    return dot(jnp.ones((16, rows.shape[0]), jnp.bfloat16), rows)


def unscaled(sums, fanout):
    pieces = []
    for row in range(0, sums.shape[0], RUN):
        slot = row // RUN % SLOTS
        pieces.append((sums[row : row + RUN] * (slot_scale(slot) / fanout)).astype(jnp.bfloat16))
    return jnp.concatenate(pieces)


def last_kernel(
    fanout,
    bias_start,
    words_ref,
    own_ref,
    own_block,
    got_ref,
    weight_ref,
    bias_ref,
    seeds_ref,
    grad_ref,
    rows_ref,
    sums_ref,
    notes_ref,
    table_out,
    far_ref,
    halo_ref,
    reduced_ref,
    counts_ref,
    both_ref,
    self_ref,
    near_ref,
    bias_col,
    far_sums,
):
    step = pl.program_id(0)
    last = pl.num_programs(0) - 1
    classes = self_ref.shape[0]
    width, nodes = own_ref.shape
    kinds = weight_ref.shape[0]
    halo = far_ref.shape[0]
    first = far_start(nodes)

    @pl.when(step == 0)
    def _():
        table_out[:, :nodes] = own_ref[...]
        table_out[:, nodes:] = got_ref[...].reshape(halo, width).T
        more = jnp.zeros((classes - kinds, 2 * width), jnp.float32)
        weight = jnp.concatenate([weight_ref[...], more]).astype(jnp.bfloat16)
        self_ref[...] = weight[:, :width]
        near_ref[...] = weight[:, width:]
        rest = jnp.full((1, classes - kinds), -1e30, jnp.float32)
        bias = bias_ref[...].reshape(1, -1)
        bias_col[...] = column_of(
            jnp.concatenate([bias[:, bias_start : bias_start + kinds], rest], axis=1)
        )
        reduced = dot(near_ref[...], table_out[...]) * scale_row(table_out.shape[1])
        high = reduced.astype(jnp.bfloat16)
        reduced_ref[:classes, :] = high
        reduced_ref[classes:, :] = (reduced - high.astype(jnp.float32)).astype(jnp.bfloat16)
        both_ref[...] = jnp.zeros_like(both_ref)
        counts_ref[first:, :] = jnp.zeros_like(counts_ref[first:, :])

    @pl.when(step <= 1)
    def _():
        sums_ref[...] = jnp.zeros_like(sums_ref)
        notes_ref[...] = jnp.zeros_like(notes_ref)
        far_sums[...] = jnp.zeros_like(far_sums)

    def finish():
        near_part = (both_ref[:classes, :] + both_ref[classes:, :]) * (1.0 / fanout)
        logits = dot(self_ref[...], own_block[...]) + near_part + bias_col[:, :1]
        top = jnp.max(logits, axis=0, keepdims=True)
        powers = jnp.exp(logits - top)
        total = jnp.sum(powers, axis=0, keepdims=True)
        normer = jnp.log(total) + top
        seeds = seeds_ref[...]
        uses = jnp.sum(seeds, axis=0, keepdims=True)
        grad = (powers * (uses / total) - seeds).astype(jnp.bfloat16)
        grad_ref[...] = grad
        loss = uses * normer - jnp.sum(seeds * logits, axis=0, keepdims=True)
        notes_ref[:8, :] += jnp.sum(loss)
        notes_ref[8:, :] += jnp.sum(uses)
        rows = grad.T
        rows_ref[...] = rows
        sums_ref[...] += column_sums(rows)
        far_sums[...] += dot(counts_ref[first:, :], rows)

    @pl.when(step < last)
    def _():
        finish()
        both_ref[...] = gather_product(reduced_ref, words_ref, counts_ref)

    @pl.when(step == last)
    def _():
        finish()
        sums = unscaled(far_sums[...], fanout)[nodes - first :]
        far_ref[...] = sums
        halo_ref[...] = dot(sums, near_ref[...]).astype(jnp.bfloat16)


def last_layer(words, own, got, weight, bias, bias_start, seeds, fanout):
    width, nodes = own.shape
    halo = got.shape[0] * got.shape[1]
    table = nodes + halo
    classes = seeds.shape[0]
    steps = nodes // BLOCK
    far_height = table - far_start(nodes)
    return pl.pallas_call(
        functools.partial(last_kernel, fanout, bias_start),
        grid=(steps + 1,),
        in_specs=[
            now(words.shape[0], BLOCK, steps),
            whole(own.shape),
            late(width, BLOCK),
            whole(got.shape),
            whole(weight.shape),
            whole(bias.shape),
            late(classes, BLOCK),
        ],
        out_specs=[
            late(classes, BLOCK),
            pl.BlockSpec((BLOCK, classes), lambda i: (jnp.maximum(i - 1, 0), 0)),
            whole((16, classes)),
            whole((16, 128)),
            whole((width, table)),
            whole((halo, classes)),
            whole((halo, width)),
        ],
        out_shape=[
            jax.ShapeDtypeStruct((classes, nodes), jnp.bfloat16),
            jax.ShapeDtypeStruct((nodes, classes), jnp.bfloat16),
            jax.ShapeDtypeStruct((16, classes), jnp.float32),
            jax.ShapeDtypeStruct((16, 128), jnp.float32),
            jax.ShapeDtypeStruct((width, table), jnp.bfloat16),
            jax.ShapeDtypeStruct((halo, classes), jnp.bfloat16),
            jax.ShapeDtypeStruct((halo, width), jnp.bfloat16),
        ],
        scratch_shapes=[
            pltpu.VMEM((2 * classes, table), jnp.bfloat16),
            pltpu.VMEM((table, BLOCK), jnp.bfloat16),
            pltpu.VMEM((2 * classes, BLOCK), jnp.float32),
            pltpu.VMEM((classes, width), jnp.bfloat16),
            pltpu.VMEM((classes, width), jnp.bfloat16),
            pltpu.VMEM((classes, 128), jnp.float32),
            pltpu.VMEM((far_height, classes), jnp.float32),
        ],
        compiler_params=params(40),
        name="last_layer",
    )(*in_hbm(words), own, own, got, *in_hbm(weight, bias), seeds)


def scatter_kernel(mesh_sizes, fanout, flipped, words_ref, grad_ref, rows_ref, *refs):
    refs = list(refs)
    if flipped:
        weight_in, halo_ref, far_ref, table_ref, far_table = refs[:5]
        state_ref, got_ref, weight_ref = refs[5:8]
        refs = refs[8:]
    else:
        weight_in, halo_ref, early_ref = refs[:3]
        state_ref, got_ref, early_sum, loss_ref, count_ref = refs[3:8]
        refs = refs[8:]
    padded_ref, counts_ref, sums_ref, self_ref, near_ref, relay_ref, land_ref = refs[:7]
    if flipped:
        high_sems, plane_sems = refs[7:9], refs[9:11]
    else:
        early_relay, early_part, early_land, early_own, early_back = refs[7:12]
        high_sems, plane_sems = refs[12:14], refs[14:16]
        early_high, early_plane, back_sems = refs[16:18], refs[18:20], refs[20:22]
    step = pl.program_id(0)
    units, nodes = grad_ref.shape
    width = state_ref.shape[0]
    span = words_ref.shape[0]
    part = span * SLOTS
    steps = -(-nodes // part)

    @pl.when(step == 0)
    def _():
        greet_split(mesh_sizes)
        for k in range(steps):
            start = k * part
            stop = min(start + part, nodes)
            padded_ref[k, :, : stop - start] = grad_ref[:, start:stop]
            if stop < start + part:
                padded_ref[k, :, stop - start :] = jnp.zeros(
                    (units, start + part - stop), jnp.bfloat16
                )
        weight = weight_in[...]
        if flipped:
            more = jnp.zeros((units - weight.shape[0], 2 * width), jnp.float32)
            weight = jnp.concatenate([weight, more]).T
            weight_ref[:width, :] = jnp.zeros((width, units), jnp.float32)
            weight_ref[width:, :] = dot(far_table[...], far_ref[...])
        self_ref[...] = weight[:width].astype(jnp.bfloat16)
        near_ref[...] = weight[width:].astype(jnp.bfloat16)
        sums_ref[...] = jnp.zeros_like(sums_ref)
        split_greeted(mesh_sizes)
        high_start(mesh_sizes, halo_ref, relay_ref, high_sems)
        if not flipped:
            plane_blocks(mesh_sizes, early_ref, early_relay, early_plane)

    @pl.when(step == steps // 2)
    def _():
        top, _, _, me = split_place(mesh_sizes)
        high_wait(mesh_sizes, relay_ref, high_sems)
        relay_ref[top] = halo_ref[top]
        plane_blocks(mesh_sizes, relay_ref, land_ref, plane_sems)
        if not flipped:
            plane_blocks_wait(mesh_sizes, early_relay, early_plane)
            early_relay[:, me] = early_ref[:, me]
            total = jnp.sum(early_relay[...].astype(jnp.float32), axis=1)
            shape = total.shape
            total = total.reshape(-1, shape[2])
            last = total[:, -128:]
            total = jnp.concatenate([total[:, :-128], put_terms(last, take_terms(last))], axis=1)
            early_part[...] = total.astype(jnp.bfloat16).reshape(shape)
            high_start(mesh_sizes, early_part, early_land, early_high)

    if not flipped:

        @pl.when(step == steps - 1)
        def _():
            top = split_place(mesh_sizes)[0]
            high_wait(mesh_sizes, early_land, early_high)
            early_land[top] = early_part[top]
            total = jnp.sum(early_land[...].astype(jnp.float32), axis=0)
            early_own[...] = total.astype(jnp.bfloat16)
            loss, count = take_terms(total[:, -128:])
            loss_ref[...] = loss[:1]
            count_ref[...] = count[:1]
            each_high(
                mesh_sizes,
                lambda other, where: push(early_own, early_back.at[top], back_sems, where),
            )

    def add(row):
        spread_unit(words_ref, row // SLOTS, counts_ref, row)
        added = dot(counts_ref[row : row + UNIT, :], rows_ref[...])
        sums_ref[row : row + UNIT, :] = unscaled(added, fanout)

    beyond = nodes - (steps - 1) * part
    ending = -(-beyond // UNIT) * UNIT
    for row in range(0, ending, UNIT):
        add(row)
    if ending < part:

        @pl.when(step < steps - 1)
        def _():
            for row in range(ending, part, UNIT):
                add(row)

    if flipped and beyond < part:

        @pl.when(step == steps - 1)
        def _():
            sums_ref[beyond:, :] = jnp.zeros((part - beyond, units), jnp.bfloat16)

    sums = sums_ref[...]
    own_grad = padded_ref[step]
    state_ref[...] = dot(near_ref[...], sums, TRANS_RIGHT) + dot(self_ref[...], own_grad)
    if flipped:
        weight_ref[:width, :] += dot(table_ref[...], own_grad, TRANS_RIGHT)
        weight_ref[width:, :] += dot(table_ref[...], sums)

    @pl.when(step == steps - 1)
    def _():
        me = split_place(mesh_sizes)[3]
        plane_blocks_wait(mesh_sizes, land_ref, plane_sems)
        land_ref[:, me] = relay_ref[:, me]
        got_ref[...] = land_ref[...]
        if not flipped:
            top = split_place(mesh_sizes)[0]
            high_wait(mesh_sizes, early_back, back_sems)
            early_back[top] = early_own[...]
            early_sum[...] = early_back[...]


def scatter_layer(
    words, grad, rows, weight, halo_rows, mesh_sizes, collective, fanout, tables=None, early=None
):
    units, nodes = grad.shape
    halo, width = halo_rows.shape
    parts = mesh_sizes[0] * mesh_sizes[1]
    flipped = tables is not None
    total = nodes + halo
    part = total // WORDS
    span = part // SLOTS
    steps = -(-nodes // part)
    high = split_sizes(mesh_sizes)[0]
    blocks = (high, parts // high, halo // parts, width)
    in_specs = [
        pl.BlockSpec((span, nodes), lambda i: (i, 0)),
        whole(grad.shape),
        whole(rows.shape),
        whole(weight.shape),
        whole(blocks),
    ]
    operands = [words, grad, rows, weight, halo_rows.reshape(blocks)]
    out_specs = [lanes(width, part), whole(blocks)]
    out_shape = [
        jax.ShapeDtypeStruct((width, total), jnp.float32),
        jax.ShapeDtypeStruct(blocks, jnp.bfloat16),
    ]
    if flipped:
        far, table = tables
        in_specs += [
            whole(far.shape),
            lanes(width, part),
            pl.BlockSpec((width, halo), lambda i: (0, nodes // halo)),
        ]
        operands += [far, table, table]
        out_specs.append(whole((2 * width, units)))
        out_shape.append(jax.ShapeDtypeStruct((2 * width, units), jnp.float32))
        scratch = semaphores() + semaphores()
    else:
        early_blocks = (high, parts // high, early.shape[0] // parts, early.shape[1])
        in_specs.append(whole(early_blocks))
        operands.append(early.reshape(early_blocks))
        summed = (high,) + early_blocks[2:]
        out_specs += [whole(summed), whole((1, 1)), whole((1, 1))]
        out_shape += [
            jax.ShapeDtypeStruct(summed, jnp.bfloat16),
            jax.ShapeDtypeStruct((1, 1), jnp.float32),
            jax.ShapeDtypeStruct((1, 1), jnp.float32),
        ]
        scratch = [
            pltpu.VMEM(early_blocks, jnp.bfloat16),
            pltpu.VMEM(summed, jnp.bfloat16),
            pltpu.VMEM(summed, jnp.bfloat16),
            pltpu.VMEM(summed[1:], jnp.bfloat16),
            pltpu.VMEM(summed, jnp.bfloat16),
        ]
        scratch += semaphores() * 5
    return pl.pallas_call(
        functools.partial(scatter_kernel, mesh_sizes, fanout, flipped),
        grid=(steps,),
        in_specs=in_specs,
        out_specs=out_specs,
        out_shape=out_shape,
        scratch_shapes=[
            pltpu.VMEM((steps, units, part), jnp.bfloat16),
            pltpu.VMEM((part, nodes), jnp.bfloat16),
            pltpu.VMEM((part, units), jnp.bfloat16),
            pltpu.VMEM((width, units), jnp.bfloat16),
            pltpu.VMEM((width, units), jnp.bfloat16),
            pltpu.VMEM(blocks, jnp.bfloat16),
            pltpu.VMEM(blocks, jnp.bfloat16),
        ]
        + scratch,
        compiler_params=params(36, collective),
        name="scatter_layer",
    )(*in_hbm(words), *operands[1:3], *in_hbm(weight), *operands[4:])


def active_grad(step, state_ref, preact_ref, back_ref, send_ref):
    block = state_ref.shape[1]
    chosen = chosen_nodes(send_ref[...], step * block, block)
    upper = state_ref[...] + dot(back_ref[...], chosen, TRANS_RIGHT)
    preact = preact_ref[...]
    gate = jax.nn.sigmoid(preact)
    active = preact * gate
    norm = lax.rsqrt(jnp.sum(active * active, axis=0, keepdims=True) + 1e-06)
    along = jnp.sum(active * upper, axis=0, keepdims=True)
    inner = norm * upper - active * (norm * norm * norm * along)
    return (inner * (gate + active * (1.0 - gate))).astype(jnp.bfloat16)


def middle_kernel(
    fanout,
    state_ref,
    preact_ref,
    returned_ref,
    send_ref,
    words_ref,
    weight_ref,
    own_block,
    mean_block,
    above_ref,
    notes_ref,
    grad_ref,
    rows_ref,
    sums_ref,
    halo_ref,
    early_ref,
    back_ref,
    counts_ref,
    far_sums,
    total_ref,
):
    step = pl.program_id(0)
    units, block = state_ref.shape
    halo = halo_ref.shape[0]
    nodes = block * pl.num_programs(0)
    first = far_start(nodes)
    part = (nodes + halo) // WORDS

    @pl.when(step == 0)
    def _():
        back_ref[...] = returned_ref[...].reshape(halo, units).T
        sums_ref[...] = jnp.zeros_like(sums_ref)
        far_sums[...] = jnp.zeros_like(far_sums)
        total_ref[...] = jnp.zeros_like(total_ref)

    base = first // part * part
    for row in range(first, nodes + halo, UNIT):
        spread_unit(words_ref, (row - base) // SLOTS, counts_ref, row - first)
    grad = active_grad(step, state_ref, preact_ref, back_ref, send_ref)
    grad_ref[...] = grad
    rows = grad.T
    rows_ref[...] = rows
    sums_ref[...] += column_sums(rows)
    far_sums[...] += dot(counts_ref[...], rows)
    width = own_block.shape[0]
    total_ref[:width, :] += dot(own_block[...], rows)
    total_ref[width:, :] += dot(mean_block[...], rows)

    @pl.when(step == pl.num_programs(0) - 1)
    def _():
        near = weight_ref[units:, :].T.astype(jnp.bfloat16)
        sums = unscaled(far_sums[...], fanout)[nodes - first :]
        halo_ref[...] = dot(sums, near).astype(jnp.bfloat16)
        early_ref[:, :units] = total_ref[...].astype(jnp.bfloat16)
        height, narrow = above_ref.shape
        above = jnp.concatenate(
            [above_ref[...], jnp.zeros((height, 128 - narrow), jnp.float32)], axis=1
        )
        above = put_terms(above, [notes_ref[0:1, 0:1], notes_ref[8:9, 0:1]])
        early_ref[:, units:] = above.astype(jnp.bfloat16)


def middle_layer(
    state_grad, preact, returned, send_row, words, weight, own, mean, above, notes, fanout
):
    units, nodes = preact.shape
    width = own.shape[0]
    wide = units + 128
    halo = send_row.shape[1]
    part = (nodes + halo) // WORDS
    span = part // SLOTS
    far_words = WORDS - far_start(nodes) // part
    far_height = nodes + halo - far_start(nodes)
    return pl.pallas_call(
        functools.partial(middle_kernel, fanout),
        grid=(nodes // BLOCK,),
        in_specs=[
            lanes(units, BLOCK),
            lanes(units, BLOCK),
            whole(returned.shape),
            whole(send_row.shape),
            pl.BlockSpec((far_words * span, BLOCK), lambda i: (WORDS // far_words - 1, i)),
            whole(weight.shape),
            lanes(width, BLOCK),
            lanes(width, BLOCK),
            whole(above.shape),
            whole(notes.shape),
        ],
        out_specs=[
            lanes(units, BLOCK),
            pl.BlockSpec((BLOCK, units), lambda i: (i, 0)),
            whole((16, units)),
            whole((halo, units)),
            whole((2 * width, wide)),
        ],
        out_shape=[
            jax.ShapeDtypeStruct((units, nodes), jnp.bfloat16),
            jax.ShapeDtypeStruct((nodes, units), jnp.bfloat16),
            jax.ShapeDtypeStruct((16, units), jnp.float32),
            jax.ShapeDtypeStruct((halo, units), jnp.bfloat16),
            jax.ShapeDtypeStruct((2 * width, wide), jnp.bfloat16),
        ],
        scratch_shapes=[
            pltpu.VMEM((units, halo), jnp.bfloat16),
            pltpu.VMEM((far_height, BLOCK), jnp.bfloat16),
            pltpu.VMEM((far_height, units), jnp.float32),
            pltpu.VMEM((2 * width, units), jnp.float32),
        ],
        compiler_params=params(30),
        name="middle_layer",
    )(
        state_grad,
        *in_hbm(preact),
        returned,
        send_row,
        *in_hbm(words, weight),
        own,
        *in_hbm(mean),
        above,
        notes,
    )


def in_two(value):
    high = value.astype(jnp.bfloat16)
    return high, (value - high.astype(jnp.float32)).astype(jnp.bfloat16)


def product(left, right, dims=(((1,), (0,)), ((), ()))):
    if left.dtype == jnp.bfloat16:
        high, low = in_two(right)
        return dot(left, high, dims) + dot(left, low, dims)
    high, low = in_two(left)
    if right.dtype == jnp.bfloat16:
        return dot(high, right, dims) + dot(low, right, dims)
    right_high, right_low = in_two(right)
    return dot(high, right_high, dims) + (
        dot(high, right_low, dims) + dot(low, right_high, dims)
    )


def moments(turned, first, second):
    first = beta_one * first + (1.0 - beta_one) * turned
    second = beta_two * second + (1.0 - beta_two) * turned * turned
    update = first / (1.0 - beta_one**STEP) / (jnp.sqrt(second / (1.0 - beta_two**STEP)) + epsilon)
    return first, second, update


def bottom_kernel(
    mesh_sizes,
    state_ref,
    preact_ref,
    returned_ref,
    send_ref,
    own_block,
    mean_block,
    sums_two,
    sums_three,
    early_ref,
    count_ref,
    *refs,
):
    refs = list(refs)
    kept, refs = refs[:10], refs[10:]
    late_out, *new, back_ref, weight_ref, late_ref = refs[:10]
    land_ref, plane_land, part_ref, high_land, whole_ref, last_land = refs[10:16]
    fetched, refs = refs[16:26], refs[26:]
    plane_sems, inward, across, outward = refs[:2], refs[2:4], refs[4:6], refs[6:8]
    fetch_sem = refs[8]
    step = pl.program_id(0)
    units = state_ref.shape[0]
    halo = send_ref.shape[1]
    top, _, _, me = split_place(mesh_sizes)

    @pl.when(step == 0)
    def _():
        greet_split(mesh_sizes)
        for index, (source, target) in enumerate(zip(kept, fetched)):
            pltpu.make_async_copy(source, target, fetch_sem.at[index]).start()
        back_ref[...] = returned_ref[...].reshape(halo, units).T
        weight_ref[...] = jnp.zeros_like(weight_ref)
        pieces = []
        for sums in (sums_two, sums_three):
            for start in range(0, sums.shape[1], 128):
                pieces.append(sums[:1, start : start + 128])
        narrow = pieces[-1].shape[1]
        pieces[-1] = jnp.concatenate(
            [pieces[-1], jnp.zeros((1, 128 - narrow), jnp.float32)], axis=1
        )
        row = units // 128 * 2 * weight_ref.shape[1]
        rest = late_ref.shape[0] - row
        pieces.append(jnp.zeros((rest - len(pieces), 128), jnp.float32))
        late_ref[row:, :] = jnp.concatenate(pieces).astype(jnp.bfloat16)
        split_greeted(mesh_sizes)
        each_plane(
            mesh_sizes,
            lambda other, where: push(early_ref, land_ref.at[:, me], plane_sems, where),
        )

    grad = active_grad(step, state_ref, preact_ref, back_ref, send_ref)
    width = own_block.shape[0]
    weight_ref[0, :width, :] += dot(own_block[...], grad, TRANS_RIGHT)
    weight_ref[1] += dot(mean_block[...], grad, TRANS_RIGHT)

    @pl.when(step == pl.num_programs(0) - 1)
    def _():
        padded = weight_ref.shape[1]
        row = 0
        for start in range(0, units, 128):
            for half in range(2):
                late_ref[row : row + padded, :] = weight_ref[half, :, start : start + 128].astype(
                    jnp.bfloat16
                )
                row += padded
        tall = part_ref.shape[0]

        def rows_of(place):
            return late_ref.at[pl.ds(pl.multiple_of(place * tall, tall), tall)]

        each_plane(
            mesh_sizes,
            lambda other, where: push(rows_of(other), plane_land.at[me], inward, where),
        )
        for index, (source, target) in enumerate(zip(kept, fetched)):
            pltpu.make_async_copy(source, target, fetch_sem.at[index]).wait()
        left_two, right_two, left_three, right_three = fetched[:4]
        weight_two, first_two, second_two = fetched[4:7]
        weight_three, first_three, second_three = fetched[7:]
        share = 1.0 / count_ref[...]
        plane_blocks_wait(mesh_sizes, land_ref, plane_sems)
        land_ref[:, me] = early_ref[...]
        early = land_ref[...].reshape(-1, land_ref.shape[3])
        grad = early[:, :units]
        turned = product(product(left_two[...], grad, TRANS_LEFT), right_two[...]) * share
        new_first, new_second, update = moments(turned, first_two[...], second_two[...])
        new[1][...] = new_first
        new[2][...] = new_second

        plane_wait(mesh_sizes, plane_land, inward)
        plane_land[me] = late_ref[pl.ds(pl.multiple_of(me * tall, tall), tall), :]
        part_ref[...] = jnp.sum(plane_land[...].astype(jnp.float32), axis=0).astype(jnp.bfloat16)
        each_high(
            mesh_sizes, lambda other, where: push(part_ref, high_land.at[top], across, where)
        )

        moved = product(product(left_two[...], update), right_two[...], TRANS_RIGHT)
        new[0][...] = weight_two[...] - step_rates[1] * moved

        high_wait(mesh_sizes, high_land, across)
        high_land[top] = part_ref[...]
        whole_ref[...] = jnp.sum(high_land[...].astype(jnp.float32), axis=0).astype(jnp.bfloat16)
        each_plane(
            mesh_sizes, lambda other, where: push(whole_ref, last_land.at[me], outward, where)
        )

        kinds = right_three.shape[0]
        grad = early[:, units:].astype(jnp.float32).T[:kinds].astype(jnp.bfloat16)
        turned = product(right_three[...], product(grad, left_three[...]), TRANS_LEFT) * share
        new_first, new_second, update = moments(turned, first_three[...], second_three[...])
        new[4][...] = new_first
        new[5][...] = new_second
        moved = product(right_three[...], product(update, left_three[...], TRANS_RIGHT))
        new[3][...] = weight_three[...] - step_rates[2] * moved

        plane_wait(mesh_sizes, last_land, outward)
        last_land[me] = whole_ref[...]
        late_out[...] = last_land[...]


def bottom_layer(
    state_grad,
    preact,
    returned,
    send_row,
    own,
    mean,
    sums_two,
    sums_three,
    early,
    count,
    kept,
    mesh_sizes,
    collective,
):
    units, nodes = preact.shape
    width = own.shape[0]
    padded = mean.shape[0]
    halo = send_row.shape[1]
    rows = units // 128 * (2 * padded + 1) + -(-sums_three.shape[1] // 128)
    rows = -(-rows // 512) * 512
    high, low, along = split_sizes(mesh_sizes)
    plane = low * along
    early_blocks = (high, plane) + early.shape[1:]
    late_blocks = (plane, rows // plane, 128)
    hbm = pl.BlockSpec(memory_space=pl.ANY)
    new = [jax.ShapeDtypeStruct(array.shape, jnp.float32) for array in kept[4:]]
    return pl.pallas_call(
        functools.partial(bottom_kernel, mesh_sizes),
        grid=(nodes // BLOCK,),
        in_specs=[
            lanes(units, BLOCK),
            lanes(units, BLOCK),
            whole(returned.shape),
            whole(send_row.shape),
            lanes(width, BLOCK),
            lanes(padded, BLOCK),
            whole(sums_two.shape),
            whole(sums_three.shape),
            whole(early.shape),
            whole(count.shape),
        ]
        + [hbm] * len(kept),
        out_specs=[whole(late_blocks)] + [whole(array.shape) for array in new],
        out_shape=[jax.ShapeDtypeStruct(late_blocks, jnp.bfloat16)] + new,
        scratch_shapes=[
            pltpu.VMEM((units, halo), jnp.bfloat16),
            pltpu.VMEM((2, padded, units), jnp.float32),
            pltpu.VMEM((rows, 128), jnp.bfloat16),
            pltpu.VMEM(early_blocks, jnp.bfloat16),
            pltpu.VMEM(late_blocks, jnp.bfloat16),
            pltpu.VMEM(late_blocks[1:], jnp.bfloat16),
            pltpu.VMEM((high,) + late_blocks[1:], jnp.bfloat16),
            pltpu.VMEM(late_blocks[1:], jnp.bfloat16),
            pltpu.VMEM(late_blocks, jnp.bfloat16),
        ]
        + [pltpu.VMEM(array.shape, array.dtype) for array in kept]
        + semaphores() * 4
        + [pltpu.SemaphoreType.DMA((len(kept),))],
        compiler_params=params(34, collective),
        name="bottom_layer",
    )(
        state_grad,
        *in_hbm(preact),
        returned,
        send_row,
        *in_hbm(own, mean),
        sums_two,
        sums_three,
        early,
        count,
        *in_hbm(*kept),
    )


def adam_kernel(
    padded,
    late_ref,
    count_ref,
    weight_one,
    left_one,
    right_one,
    first_one,
    second_one,
    bias_ref,
    bias_first,
    bias_second,
    *refs,
):
    ready, refs = refs[:6], refs[6:]
    outs, sem = refs[:12], refs[12]
    for index in range(6):
        pltpu.make_async_copy(ready[index], outs[3 + index], sem.at[index]).start()
    share = 1.0 / count_ref[...]
    units = weight_one.shape[1]
    width = weight_one.shape[0] // 2

    late_rows = late_ref[...].astype(jnp.float32)
    columns = []
    for start in range(0, units, 128):
        row = start // 128 * 2 * padded
        columns.append(
            jnp.concatenate(
                [late_rows[row : row + width], late_rows[row + padded : row + padded + width]]
            )
        )
    grad = jnp.concatenate(columns, axis=1).astype(jnp.bfloat16)
    turned = product(product(left_one[...], grad, TRANS_LEFT), right_one[...]) * share
    new_first, new_second, update = moments(turned, first_one[...], second_one[...])
    outs[1][...] = new_first
    outs[2][...] = new_second
    moved = product(product(left_one[...], update), right_one[...], TRANS_RIGHT)
    outs[0][...] = weight_one[...] - step_rates[0] * moved

    size = bias_ref.shape[0]
    pieces = []
    for start in range(0, units, 128):
        row = start // 128 * 2 * padded + padded + width
        pieces.append(late_rows[row : row + 1])
    row = units // 128 * 2 * padded
    while len(pieces) * 128 < size:
        pieces.append(late_rows[row : row + 1])
        row += 1
    grad = jnp.concatenate(pieces, axis=1)[:, :size] * share
    flat = bias_ref.shape
    bias, first, second = (ref[...].reshape(grad.shape) for ref in (bias_ref, bias_first, bias_second))
    new_first, new_second, update = moments(grad, first, second)
    outs[9][...] = (bias - bias_rate * (update + weight_decay * bias)).reshape(flat)
    outs[10][...] = new_first.reshape(flat)
    outs[11][...] = new_second.reshape(flat)
    for index in range(6):
        pltpu.make_async_copy(ready[index], outs[3 + index], sem.at[index]).wait()


def adam(padded, late_all, count, state, ready):
    vmem = pl.BlockSpec(memory_space=pltpu.VMEM)
    hbm = pl.BlockSpec(memory_space=pl.ANY)
    one, bias = state[0], state[5]
    shapes = [one.shape] * 3 + [array.shape for array in ready] + [bias.shape] * 3
    return pl.pallas_call(
        functools.partial(adam_kernel, padded),
        in_specs=[vmem] * (2 + len(state)) + [hbm] * len(ready),
        out_specs=[vmem] * 3 + [hbm] * 6 + [vmem] * 3,
        out_shape=[jax.ShapeDtypeStruct(shape, jnp.float32) for shape in shapes],
        scratch_shapes=[pltpu.SemaphoreType.DMA((6,))],
        compiler_params=pltpu.CompilerParams(vmem_limit_bytes=24 * MIB),
        name="adam",
    )(late_all, count, *in_hbm(*state), *ready)


def on_device(
    mesh_sizes,
    features,
    labels,
    seed_rows,
    seed_mask,
    send_rows,
    neighbors_one,
    neighbors_two,
    neighbors_three,
    weight_one,
    weight_two,
    weight_three,
    left_one,
    right_one,
    left_two,
    right_two,
    left_three,
    right_three,
    first_one,
    first_two,
    first_three,
    second_one,
    second_two,
    second_three,
    bias_all,
    bias_first,
    bias_second,
):
    units = weight_one.shape[1]
    classes = weight_three.shape[1]
    halo = send_rows.size
    fans = (neighbors_one.shape[1], neighbors_two.shape[1], neighbors_three.shape[1])
    feats = features.T
    weight_three = weight_three.T
    padded_classes = -(-classes // 16) * 16
    seed_slots = (
        padded_classes,
        seed_rows.reshape(1, -1),
        labels.reshape(1, -1),
        seed_mask.reshape(1, -1),
    )

    words_one, got, send_row = count_words(
        neighbors_one.T, mesh_sizes, 0, halo, feats=feats, send_rows=send_rows.T
    )
    feats = in_hbm(feats)[0]
    state_one, preact_one, sent, mean_one = hidden_layer(
        words_one, feats, got, weight_one, bias_all, 0, send_row, fans[0]
    )
    words_two, got = count_words(neighbors_two.T, mesh_sizes, 1, halo, sent=sent)
    state_two, preact_two, sent, mean_two = hidden_layer(
        words_two, state_one, got, weight_two, bias_all, units, send_row, fans[1]
    )
    words_three, got, seeds = count_words(
        neighbors_three.T, mesh_sizes, 2, halo, sent=sent, seeds=seed_slots
    )
    grad_three, rows_three, sums_three, notes, table_three, far, halo_grad = last_layer(
        words_three, state_two, got, weight_three, bias_all, 2 * units, seeds, fans[2]
    )
    state_grad, returned, weight_grad = scatter_layer(
        words_three,
        grad_three,
        rows_three,
        weight_three,
        halo_grad,
        mesh_sizes,
        3,
        fans[2],
        tables=(far, table_three),
    )
    grad_two, rows_two, sums_two, halo_grad, early = middle_layer(
        state_grad,
        preact_two,
        returned,
        send_row,
        words_two,
        weight_two,
        state_one,
        mean_two,
        weight_grad,
        notes,
        fans[1],
    )
    state_grad, returned, early_sum, loss, count = scatter_layer(
        words_two, grad_two, rows_two, weight_two, halo_grad, mesh_sizes, 4, fans[1], early=early
    )
    late_all, *ready = bottom_layer(
        state_grad,
        preact_one,
        returned,
        send_row,
        feats,
        mean_one,
        sums_two,
        sums_three,
        early_sum,
        count,
        (
            left_two,
            right_two,
            left_three,
            right_three,
            weight_two,
            first_two,
            second_two,
            weight_three,
            first_three.T,
            second_three.T,
        ),
        mesh_sizes,
        5,
    )
    out = adam(
        mean_one.shape[0],
        late_all.reshape(-1, 128),
        count,
        (
            weight_one,
            left_one,
            right_one,
            first_one,
            second_one,
            bias_all,
            bias_first,
            bias_second,
        ),
        ready,
    )
    third = [value.T for value in out[6:9]]
    return (*out[:6], *third, *out[9:12], loss.reshape(()), count.reshape(()))


def solution(mesh):
    split = P(axes)
    rows = P(axes, None)
    placed = (rows, split, split, split, rows, rows, rows, rows) + (P(),) * 18
    mesh_sizes = (mesh.shape[axes[0]], mesh.shape[axes[1]])
    return jax.shard_map(
        functools.partial(on_device, mesh_sizes),
        mesh=mesh,
        in_specs=placed,
        out_specs=(P(),) * 14,
        check_vma=False,
    )
```
